128 devices in a mesh: blk: 128 (over x, z, y, core).
Axes of the slice: x: 4, y: 4, z: 4, core: 2. Of those that a mesh axis runs over, the one named last changes fastest.
Arguments:
- x_points: bfloat16 [262144, 512], P('blk'), may hold values from -0.375 to 0.375
- y_points: bfloat16 [262144, 512], P('blk'), may hold values from -0.375 to 0.375
- x_start: bfloat16 [262144], P('blk'), may hold values from -1 to 16
- y_start: bfloat16 [262144], P('blk'), may hold values from -1 to 16
- x_order: int32 [262144], P('blk'), may hold values from 0 to 262143, as said below
- y_order: int32 [262144], P('blk'), may hold values from 0 to 262143, as said below
- partners: int32 [256, 6], P('blk'), may hold values from 0 to 255, as said below
- counts: int32 [256], P('blk'), may hold values from 1 to 6, as said below
Outputs:
- f_out: float32 [262144], P('blk')
- g_out: float32 [262144], P('blk')
The draws below stay inside these ranges and needn't reach their ends.
Inputs may be any that keep to these rules, and one draw needn't show every extreme that they name: x_order is a permutation; every device's points are sent in equal numbers, 2 * 1024 / 128, to the cluster positions of every device. y_order is a permutation; every device's points are sent in equal numbers, 2 * 1024 / 128, to the cluster positions of every device. `partners`: slot 0 of row b is b itself; the first counts[b] slots of row b are distinct blocks held by devices within 3 of the device that holds block b; of the blocks held by any one other device, the rows of all blocks held by one device name at most one; the other slots repeat b. `counts`: 6 is reached in every draw.
All inputs are finite; a program needn't handle non-finite values.
Results may differ from the reference program's by a relative error of at most 0.0003.
Values may be sent and summed in bfloat16 or wider, within the bound.
No kernel may reach another device: no remote copies, remote signals or barrier semaphores. Data moves between devices by JAX's collectives and lax.ppermute only.
A program may use at most 128 MiB of HBM per device.

```python
import math
import jax
import jax.numpy as jnp
from jax import lax

DIM = 512
BS = 1024
BPD = 2
PMAX = 6
REACH = 3
ITERS = 2
NBLK = 256
NPTS = 262144


def balanced_order(key):
    devices = NBLK // BPD
    local = BPD * BS
    share = local // devices
    key_source, key_target = jax.random.split(key)
    source_perm = jax.vmap(lambda sub: jax.random.permutation(sub, local))(jax.random.split(key_source, devices))
    target_perm = jax.vmap(lambda sub: jax.random.permutation(sub, local))(jax.random.split(key_target, devices))
    source = jnp.arange(devices, dtype=jnp.int32)[:, None]
    target = source_perm // share
    within = source_perm % share
    place = target * local + target_perm[target, source * share + within]
    return place.reshape(NPTS).astype(jnp.int32)


def pair_lists(key):
    devices = NBLK // BPD
    width = 2 * REACH + BPD
    block = jnp.arange(NBLK, dtype=jnp.int32)
    device_of = block // BPD
    offsets = jnp.concatenate([jnp.arange(-REACH, 0, dtype=jnp.int32), jnp.arange(1, REACH + 1, dtype=jnp.int32)])
    pick = jax.random.randint(jax.random.fold_in(key, 5), (devices, 2 * REACH), 0, BPD)
    neighbour = device_of[:, None] + offsets[None, :]
    inside = (neighbour >= 0) & (neighbour < devices)
    safe = jnp.clip(neighbour, 0, devices - 1)
    remote = safe * BPD + pick[device_of]
    local_blocks = device_of[:, None] * BPD + jnp.arange(BPD, dtype=jnp.int32)[None, :]
    candidate = jnp.concatenate([remote, local_blocks], axis=1)
    usable = jnp.concatenate([inside, local_blocks != block[:, None]], axis=1)
    available = jnp.sum(usable.astype(jnp.int32), axis=1)
    dense = jax.random.randint(jax.random.fold_in(key, 1), (devices,), 0, 4) == 0
    dense_block = jnp.repeat(dense, BPD)
    high = jax.random.randint(jax.random.fold_in(key, 2), (NBLK,), PMAX - 2, PMAX + 1)
    light = jax.random.randint(jax.random.fold_in(key, 3), (NBLK,), 1, 4)
    count_list = jnp.minimum(jnp.where(dense_block, high, light), 1 + available)
    count_list = count_list.at[REACH * BPD].set(PMAX)
    score = jax.random.randint(jax.random.fold_in(key, 4), (NBLK, width), 0, 1 << 20) * width + jnp.arange(width, dtype=jnp.int32)[None, :]
    score = jnp.where(usable, score, -1)
    unused, picked = lax.top_k(score, PMAX - 1)
    chosen = jnp.take_along_axis(candidate, picked, axis=1)
    slots = jnp.concatenate([block[:, None], chosen], axis=1)
    live = jnp.arange(PMAX, dtype=jnp.int32)[None, :] < count_list[:, None]
    partner_list = jnp.where(live, slots, block[:, None])
    return (partner_list.astype(jnp.int32), count_list.astype(jnp.int32))


def embedding(key, spread, bound):
    return jnp.clip(spread * jax.random.normal(key, (NPTS, DIM), jnp.float32), -bound, bound)


def draw_x_points(key, part):
    key = jax.random.fold_in(key, 41)
    return embedding(key, 0.0625, 0.375).astype(jnp.bfloat16)


def draw_y_points(key, part):
    key = jax.random.fold_in(key, 42)
    return embedding(key, 0.0625, 0.375).astype(jnp.bfloat16)


def draw_x_order(key, part):
    key = jax.random.fold_in(key, 11)
    return balanced_order(key)


def draw_y_order(key, part):
    key = jax.random.fold_in(key, 12)
    return balanced_order(key)


def draw_partners(key, part):
    return pair_lists(jax.random.fold_in(key, 31))[0]


def draw_counts(key, part):
    return pair_lists(jax.random.fold_in(key, 31))[1]


def draw_x_start(key, part):
    key = jax.random.fold_in(key, 21)
    return jnp.clip(0.02 * jax.random.normal(key, (NPTS,), jnp.float32), -1.0, 1.0).astype(jnp.bfloat16)


def draw_y_start(key, part):
    key = jax.random.fold_in(key, 22)
    return jnp.clip(0.02 * jax.random.normal(key, (NPTS,), jnp.float32), -1.0, 1.0).astype(jnp.bfloat16)


def setup_inputs(seed: int = 0) -> dict:
    seeds = jax.random.split(jax.random.key(seed), 9)
    return {
        "x_points": draw_x_points(jax.random.fold_in(seeds[8], 71), 0),
        "y_points": draw_y_points(jax.random.fold_in(seeds[8], 71), 0),
        "x_start": draw_x_start(jax.random.fold_in(seeds[8], 71), 0),
        "y_start": draw_y_start(jax.random.fold_in(seeds[8], 71), 0),
        "x_order": draw_x_order(jax.random.fold_in(seeds[8], 71), 0),
        "y_order": draw_y_order(jax.random.fold_in(seeds[8], 71), 0),
        "partners": draw_partners(jax.random.fold_in(seeds[8], 71), 0),
        "counts": draw_counts(jax.random.fold_in(seeds[8], 71), 0),
    }


entropy_weight = 0.05
lowest_value = -1e30


def merge_pair(first_max, first_sum, second_max, second_sum):
    top = jnp.maximum(first_max, second_max)
    return top, first_sum * jnp.exp(first_max - top) + second_sum * jnp.exp(second_max - top)


def block_terms(x_block, x_sq, f_block, y_block, y_sq, g_block):
    inner = lax.dot_general(x_block, y_block, (((1,), (1,)), ((), ())), preferred_element_type=jnp.float32)
    cost = 0.5 * x_sq[:, None] + 0.5 * y_sq[None, :] - inner
    row_terms = (g_block[None, :] - cost) / entropy_weight
    row_top = jnp.max(row_terms, axis=1)
    row_total = jnp.sum(jnp.exp(row_terms - row_top[:, None]), axis=1)
    col_terms = (f_block[:, None] - cost) / entropy_weight
    col_top = jnp.max(col_terms, axis=0)
    col_total = jnp.sum(jnp.exp(col_terms - col_top[None, :]), axis=0)
    return row_top, row_total, col_top, col_total


def reference(x_points, y_points, x_start, y_start, x_order, y_order, partners, counts):
    x_cluster = jnp.zeros((NPTS, DIM), jnp.bfloat16).at[x_order].set(x_points)
    y_cluster = jnp.zeros((NPTS, DIM), jnp.bfloat16).at[y_order].set(y_points)
    f_now = jnp.zeros((NPTS,), jnp.float32).at[x_order].set(x_start.astype(jnp.float32)).reshape(NBLK, BS)
    g_now = jnp.zeros((NPTS,), jnp.float32).at[y_order].set(y_start.astype(jnp.float32)).reshape(NBLK, BS)
    x_blocks = x_cluster.reshape(NBLK, BS, DIM)
    y_blocks = y_cluster.reshape(NBLK, BS, DIM)
    x_norm = jnp.sum(jnp.square(x_blocks.astype(jnp.float32)), axis=-1)
    y_norm = jnp.sum(jnp.square(y_blocks.astype(jnp.float32)), axis=-1)
    log_count = math.log(NPTS)
    for sweep_index in range(ITERS):
        def per_block(carry, block_id):
            col_max, col_sum = carry

            def per_slot(slot, inner_state):
                row_max, row_sum, col_max, col_sum = inner_state
                other = partners[block_id, slot]
                row_top, row_total, col_top, col_total = block_terms(
                    x_blocks[block_id], x_norm[block_id], f_now[block_id],
                    y_blocks[other], y_norm[other], g_now[other])
                row_max, row_sum = merge_pair(row_max, row_sum, row_top, row_total)
                new_max, new_sum = merge_pair(col_max[other], col_sum[other], col_top, col_total)
                col_max = col_max.at[other].set(new_max)
                col_sum = col_sum.at[other].set(new_sum)
                return row_max, row_sum, col_max, col_sum

            start_state = (jnp.full((BS,), lowest_value, jnp.float32), jnp.zeros((BS,), jnp.float32), col_max, col_sum)
            row_max, row_sum, col_max, col_sum = lax.fori_loop(0, counts[block_id], per_slot, start_state)
            return (col_max, col_sum), (row_max, row_sum)

        start_cols = (jnp.full((NBLK, BS), lowest_value, jnp.float32), jnp.zeros((NBLK, BS), jnp.float32))
        (col_max, col_sum), (row_max, row_sum) = lax.scan(per_block, start_cols, jnp.arange(NBLK, dtype=jnp.int32))
        row_lse = row_max + jnp.log(row_sum)
        col_lse = col_max + jnp.log(col_sum)
        f_next = 0.5 * (f_now - entropy_weight * (row_lse - log_count))
        g_next = 0.5 * (g_now - entropy_weight * (col_lse - log_count))
        f_now, g_now = f_next, g_next
    return f_now.reshape(NPTS), g_now.reshape(NPTS)
```

```python
import functools
import math

import jax
import jax.numpy as jnp
from jax import lax
from jax.experimental import pallas as pl
from jax.experimental.pallas import tpu as pltpu
from jax.sharding import PartitionSpec as P

DIM = 512
BS = 1024
BPD = 2
REACH = 3
LOCAL = BPD * BS
EXTRA = 128
WIDE = DIM + EXTRA
TAIL = 16
ROWS = BS + TAIL
CHUNK = 256
OFFSETS = (-1, 1, -2, 2, -3, 3)
YBLOCKS = BPD + len(OFFSETS)
SLOTS = BPD * YBLOCKS
GROUP = 8

entropy_weight = 0.05
scale = math.log2(math.e) / entropy_weight
lowest = -1e30
exponent_room = 115.0
vmem_bytes = 56 * 1024 * 1024

f32 = jnp.float32
bf16 = jnp.bfloat16
i32 = jnp.int32


def iota(shape, dim):
    return lax.broadcasted_iota(i32, shape, dim)


def nt_dot(a, b):
    return lax.dot_general(a, b, (((1,), (1,)), ((), ())), preferred_element_type=f32)


def params():
    return pltpu.CompilerParams(vmem_limit_bytes=vmem_bytes)


def pack_kernel(info_ref, order_ref, start_ref, points_ref, out_ref, pos_ref, extra_ref, *, devices):
    step = pl.program_id(0)
    share = LOCAL // devices

    @pl.when(step == 0)
    def _():
        dev = iota((devices, 128), 0)
        sub = iota((128, 128), 0)
        before = jnp.where(sub < iota((128, 128), 1), 1.0, 0.0).astype(bf16)
        every = jnp.ones((128, 128), bf16)
        seen = jnp.zeros((devices, 128), f32)
        for c in range(LOCAL // 128):
            part = slice(c * 128, (c + 1) * 128)
            order = order_ref[0:1, part]
            target = lax.shift_right_logical(order, 11)
            hit = dev == target
            hot = jnp.where(hit, 1.0, 0.0).astype(bf16)
            earlier = jnp.dot(hot, before, preferred_element_type=f32) + seen
            rank = jnp.sum(jnp.where(hit, earlier, 0.0), axis=0, keepdims=True)
            seen = seen + jnp.dot(hot, every, preferred_element_type=f32)
            pos_ref[0:1, part] = target * share + rank.astype(i32)
            within = jnp.bitwise_and(order, LOCAL - 1)
            high = lax.shift_right_logical(within, 6).astype(f32)
            low = jnp.bitwise_and(within, 63).astype(f32)
            rows = jnp.where(sub == 0, high, jnp.where(sub == 1, low, jnp.where(sub == 2, start_ref[0:1, part], 0.0)))
            extra_ref[part, :] = rows.T.astype(bf16)

    base = step * CHUNK
    hot = jnp.where(iota((CHUNK, LOCAL), 0) + base == pos_ref[...], 1.0, 0.0).astype(bf16)
    out_ref[:, :DIM] = jnp.dot(hot, points_ref[...], preferred_element_type=f32).astype(bf16)
    tail = jnp.dot(hot, extra_ref[...], preferred_element_type=f32)
    row = iota((CHUNK, EXTRA), 0) + base
    lane = iota((CHUNK, EXTRA), 1)
    for k in range(len(OFFSETS)):
        here = (row == info_ref[k]) & (lane == 3)
        tail = jnp.where(here, info_ref[len(OFFSETS) + k].astype(f32), tail)
    out_ref[:, DIM:] = tail.astype(bf16)


def pack(info, order, start, points, devices):
    whole = lambda s: pl.BlockSpec(s, lambda t: (0, 0))
    return pl.pallas_call(
        functools.partial(pack_kernel, devices=devices),
        grid=(LOCAL // CHUNK,),
        in_specs=[
            pl.BlockSpec(memory_space=pltpu.SMEM),
            whole((1, LOCAL)),
            whole((1, LOCAL)),
            whole((LOCAL, DIM)),
        ],
        out_specs=pl.BlockSpec((CHUNK, WIDE), lambda t: (t, 0)),
        out_shape=jax.ShapeDtypeStruct((LOCAL, WIDE), bf16),
        scratch_shapes=[pltpu.VMEM((1, LOCAL), i32), pltpu.VMEM((LOCAL, EXTRA), bf16)],
        compiler_params=params(),
        name="pack",
    )(info, order, start, points)


def fields(came_ref):
    parts = []
    for c in range(LOCAL // 128):
        piece = came_ref[c * 128 : (c + 1) * 128, DIM:].astype(f32)
        parts.append(piece.T[0:8, :])
    return jnp.concatenate(parts, axis=1)


def placed(came_ref, place, base):
    hot = jnp.where(iota((CHUNK, LOCAL), 0) + base == place, 1.0, 0.0).astype(bf16)
    points = jnp.dot(hot, came_ref[:, :DIM], preferred_element_type=f32)
    tail = jnp.dot(hot, came_ref[:, DIM:], preferred_element_type=f32)
    half = 0.5 * jnp.sum(points * points, axis=1, keepdims=True)
    return points, tail[:, 2:3], half


def position(rows):
    return (rows[0:1, :] * 64.0 + rows[1:2, :]).astype(i32)


def unpack_x_kernel(came_ref, points_ref, cols_ref, place_ref):
    step = pl.program_id(0)

    @pl.when(step == 0)
    def _():
        place_ref[...] = position(fields(came_ref))

    points, start, half = placed(came_ref, place_ref[...], step * CHUNK)
    points_ref[...] = points.astype(bf16)
    lane = iota((CHUNK, 128), 1)
    cols_ref[...] = jnp.where(lane == 0, start, half)


def unpack_x(came):
    return pl.pallas_call(
        unpack_x_kernel,
        grid=(LOCAL // CHUNK,),
        in_specs=[pl.BlockSpec((LOCAL, WIDE), lambda t: (0, 0))],
        out_specs=[pl.BlockSpec((CHUNK, DIM), lambda t: (t, 0)), pl.BlockSpec((CHUNK, 128), lambda t: (t, 0))],
        out_shape=[jax.ShapeDtypeStruct((LOCAL, DIM), bf16), jax.ShapeDtypeStruct((LOCAL, 128), f32)],
        scratch_shapes=[pltpu.VMEM((1, LOCAL), i32)],
        compiler_params=params(),
        name="unpack_x",
    )(came)


def unpack_y_kernel(info_ref, came_ref, rows_ref, own_ref, *rest):
    sends = rest[: len(OFFSETS)]
    held, sems, own_sem = rest[len(OFFSETS) :]
    got = fields(came_ref)
    place = position(got)
    spot = iota((1, LOCAL), 1)
    picks = []
    for k in range(len(OFFSETS)):
        pick = jnp.sum(jnp.where(spot == info_ref[2 * len(OFFSETS) + k], got[3:4, :], 0.0))
        picks.append(pick > 0.5)
    lane = iota((CHUNK, 128), 1)
    for j in range(BPD):
        for c in range(BS // CHUNK):
            span = slice(c * CHUNK, (c + 1) * CHUNK)
            points, start, half = placed(came_ref, place, j * BS + c * CHUNK)
            held[j, span, :] = points.astype(bf16)
            both = jnp.where(lane == 0, start, half)
            rows_ref[j, :, span] = both.T[0:8, :]
        g_row = rows_ref[j, 0:1, :]
        half_row = rows_ref[j, 1:2, :]
        beta = g_row - half_row
        first = beta.astype(bf16).astype(f32)
        second = (beta - first).astype(bf16).astype(f32)
        third = beta - first - second
        most = jnp.max(half_row, axis=1, keepdims=True) * 1.01
        sub = iota((TAIL, DIM), 0)
        tail = jnp.zeros((TAIL, DIM), f32) + most
        for n, piece in enumerate((first, second, third)):
            tail = jnp.where(sub == 2 * n, piece[:, :DIM], tail)
            tail = jnp.where(sub == 2 * n + 1, piece[:, DIM:], tail)
        held[j, BS:, :] = tail.astype(bf16)
        pltpu.make_async_copy(held.at[j], own_ref.at[j], own_sem.at[j]).start()
        for k in range(len(OFFSETS)):
            wanted = picks[k] if j == 1 else jnp.logical_not(picks[k])

            @pl.when(wanted)
            def _():
                pltpu.make_async_copy(held.at[j], sends[k], sems.at[k]).start()

    for j in range(BPD):
        pltpu.make_async_copy(held.at[j], own_ref.at[j], own_sem.at[j]).wait()
    for k in range(len(OFFSETS)):
        pltpu.make_async_copy(held.at[0], sends[k], sems.at[k]).wait()


def unpack_y(info, came):
    count = len(OFFSETS)
    return pl.pallas_call(
        unpack_y_kernel,
        in_specs=[pl.BlockSpec(memory_space=pltpu.SMEM), pl.BlockSpec(memory_space=pltpu.VMEM)],
        out_specs=[pl.BlockSpec(memory_space=pltpu.VMEM)] + [pl.BlockSpec(memory_space=pl.ANY)] * (1 + count),
        out_shape=[jax.ShapeDtypeStruct((BPD, 8, BS), f32), jax.ShapeDtypeStruct((BPD, ROWS, DIM), bf16)]
        + [jax.ShapeDtypeStruct((ROWS, DIM), bf16)] * count,
        scratch_shapes=[
            pltpu.VMEM((BPD, ROWS, DIM), bf16),
            pltpu.SemaphoreType.DMA((count,)),
            pltpu.SemaphoreType.DMA((BPD,)),
        ],
        compiler_params=params(),
        name="unpack_y",
    )(info, came)


def merge(top, total, other_top, other_total):
    new = jnp.maximum(top, other_top)
    return new, total * jnp.exp2(top - new) + other_total * jnp.exp2(other_top - new)


def fold_lanes(values):
    total = values[:, 0:128]
    for c in range(1, values.shape[1] // 128):
        total = total + values[:, c * 128 : (c + 1) * 128]
    return jnp.sum(total, axis=1, keepdims=True)


def fold_rows(values):
    return jnp.sum(values.reshape(values.shape[0] // 8, 8, values.shape[1]), axis=0)


def scalar(one):
    return one[0, 0]


def put_rows(state_ref, base, part_top, part_total):
    size = part_total.shape[0]
    span = pl.ds(base, size)
    top, total = merge(state_ref[span, 0:1], state_ref[span, 1:2], part_top, part_total)
    lane = iota((size, 128), 1)
    state_ref[span, :] = jnp.where(lane == 0, top, total)


def put_cols(col_ref, part_top, part_total):
    top, total = merge(col_ref[0:1, :], col_ref[1:2, :], part_top, part_total)
    col_ref[0:1, :] = top
    col_ref[1:2, :] = total


def shifted_rows(x_ref, y_ref, beta, state_ref, base):
    def body(c, carry):
        inner = nt_dot(x_ref[pl.ds(c * CHUNK, CHUNK), :], y_ref[0:BS, :])
        terms = inner * scale + beta
        top = jnp.max(terms, axis=1, keepdims=True)
        put_rows(state_ref, base + c * CHUNK, top, fold_lanes(jnp.exp2(terms - top)))
        return carry

    lax.fori_loop(0, BS // CHUNK, body, 0)


def shifted_cols(x_ref, y_ref, alpha_ref, col_ref):
    def body(c, carry):
        span = pl.ds(c * CHUNK, CHUNK)
        inner = nt_dot(x_ref[span, :], y_ref[0:BS, :])
        terms = inner * scale + alpha_ref[span, 0:1]
        top = jnp.max(terms, axis=0, keepdims=True)
        put_cols(col_ref, top, jnp.sum(jnp.exp2(terms - top), axis=0, keepdims=True))
        return carry

    lax.fori_loop(0, BS // CHUNK, body, 0)


def beta_of(y_ref):
    tail = y_ref[BS:ROWS, :].astype(f32)
    left = tail[0:1, :] + tail[2:3, :] + tail[4:5, :]
    right = tail[1:2, :] + tail[3:4, :] + tail[5:6, :]
    return jnp.concatenate([left, right], axis=1) * scale, tail[6:7, 0:1]


def spread(values):
    top = jnp.max(jnp.max(values, axis=1, keepdims=True), axis=0, keepdims=True)
    bottom = jnp.min(jnp.min(values, axis=1, keepdims=True), axis=0, keepdims=True)
    return top, bottom


def sweep_kernel(*refs, count, first):
    use_ref, x_ref, cols_ref = refs[:3]
    refs = refs[3:]
    if first:
        state_in = None
    else:
        state_in = refs[0]
        refs = refs[2:]
    y_refs = refs[:1] if first else refs[:count]
    refs = refs[len(y_refs) :]
    state_ref, out_ref, good_ref, kept_ref = refs[:4]
    y_buf, sems, col_ref, alpha_ref, stat_ref = refs[4:]
    step = pl.program_id(0)
    y, b = step // BPD, step % BPD

    def copies(which):
        if first:
            return [pltpu.make_async_copy(y_refs[0].at[n], y_buf.at[n % 2], sems.at[n % 2]) for n in which]
        return [pltpu.make_async_copy(y_refs[n], y_buf.at[n % 2], sems.at[n % 2]) for n in which]

    @pl.when(step == 0)
    def _():
        copies([0])[0].start()
        if state_in is None:
            lane = iota((LOCAL, 128), 1)
            state_ref[...] = jnp.where(lane == 0, lowest, 0.0)
        else:
            state_ref[...] = state_in[...]
        for n in range(BPD):
            alpha = (cols_ref[n * BS : (n + 1) * BS, 0:1] - cols_ref[n * BS : (n + 1) * BS, 1:2]) * scale
            top, bottom = spread(alpha)
            most = jnp.max(cols_ref[n * BS : (n + 1) * BS, 1:2], axis=0, keepdims=True)
            alpha_ref[n * BS : (n + 1) * BS, :] = jnp.where(iota((BS, 128), 1) == 0, alpha, jnp.exp2(alpha - top))
            lane = iota((1, 128), 1)
            stat_ref[n, :, :] = jnp.where(lane == 0, top, jnp.where(lane == 1, bottom, most))

    for n in range(count):

        @pl.when(step == BPD * n)
        def _():
            copies([n])[0].wait()
            if n + 1 < count:
                copies([n + 1])[0].start()

    @pl.when(b == 0)
    def _():
        col_ref[0:1, :] = jnp.full((1, BS), lowest, f32)
        col_ref[1:2, :] = jnp.zeros((1, BS), f32)

    now = y_buf.at[y % 2]
    good_ref[step] = 0

    @pl.when(use_ref[step] > 0)
    def _():
        beta, y_most = beta_of(now)
        beta_top, beta_bottom = spread(beta)
        a_top, a_bottom = stat_ref[b, :, 0:1], stat_ref[b, :, 1:2]
        bound = 2.0 * scale * jnp.sqrt(y_most * stat_ref[b, :, 2:3])
        room = bound + jnp.maximum(beta_top - beta_bottom, a_top - a_bottom)
        fits = scalar(room) <= exponent_room
        x_now = x_ref.at[pl.ds(b * BS, BS), :]
        alpha_now = alpha_ref.at[pl.ds(b * BS, BS), :]

        @pl.when(fits)
        def _():
            good_ref[step] = 1
            weight = jnp.exp2(beta - beta_top)
            sums = jnp.zeros((8, BS), f32)
            for c in range(BS // CHUNK):
                span = slice(c * CHUNK, (c + 1) * CHUNK)
                kernel = jnp.exp2(nt_dot(x_now[span, :], now[0:BS, :]) * scale)
                kept_ref[0, span, :] = kernel.astype(bf16)
                put_rows(state_ref, b * BS + c * CHUNK, beta_top, fold_lanes(kernel * weight))
                sums = sums + fold_rows(kernel * alpha_now[span, 1:2])
            put_cols(col_ref, a_top, jnp.sum(sums, axis=0, keepdims=True))

        @pl.when(jnp.logical_not(fits))
        def _():
            shifted_rows(x_now, now, beta, state_ref, b * BS)
            shifted_cols(x_now, now, alpha_now, col_ref)

    @pl.when(b == BPD - 1)
    def _():
        out_ref[y] = jnp.where(col_ref[1:2, :] > 0.0, col_ref[0:1, :] + jnp.log2(col_ref[1:2, :]), lowest)


def sweep(use, x_blocks, x_cols, y_list, base, carried):
    first = carried is None
    count = BPD if first else len(y_list)
    steps = count * BPD
    whole = lambda s: pl.BlockSpec(s, lambda t: (0,) * len(s))
    smem = pl.BlockSpec(memory_space=pltpu.SMEM)
    anyw = pl.BlockSpec(memory_space=pl.ANY)
    in_specs = [smem, whole((LOCAL, DIM)), whole((LOCAL, 128))]
    operands = [use[base * BPD : base * BPD + steps], x_blocks, x_cols]
    aliases = {}
    if not first:
        in_specs += [whole((LOCAL, 128)), anyw]
        operands += list(carried)
        aliases = {4: 3}
    in_specs += [anyw] * len(y_list)
    operands += y_list
    return pl.pallas_call(
        functools.partial(sweep_kernel, count=count, first=first),
        grid=(steps,),
        in_specs=in_specs,
        out_specs=[
            whole((LOCAL, 128)),
            whole((count, 1, BS)),
            smem,
            pl.BlockSpec((1, BS, BS), lambda t: (base * BPD + t, 0, 0)),
        ],
        out_shape=[
            jax.ShapeDtypeStruct((LOCAL, 128), f32),
            jax.ShapeDtypeStruct((count, 1, BS), f32),
            jax.ShapeDtypeStruct((steps,), i32),
            jax.ShapeDtypeStruct((SLOTS, BS, BS), bf16),
        ],
        scratch_shapes=[
            pltpu.VMEM((2, ROWS, DIM), bf16),
            pltpu.SemaphoreType.DMA((2,)),
            pltpu.VMEM((8, BS), f32),
            pltpu.VMEM((LOCAL, 128), f32),
            pltpu.VMEM((BPD, 1, 128), f32),
        ],
        input_output_aliases=aliases,
        compiler_params=params(),
        name=f"sweep_{base}",
    )(*operands)


def load_pair(slot, x_ref, y_refs, x_buf, y_buf, sems):
    copy = pltpu.make_async_copy(x_ref.at[pl.ds((slot % BPD) * BS, BS), :], x_buf, sems.at[0])
    copy.start()
    copy.wait()
    for n in range(YBLOCKS):
        source = y_refs[0].at[n] if n < BPD else y_refs[n - BPD + 1]

        @pl.when(slot // BPD == n)
        def _():
            copy = pltpu.make_async_copy(source, y_buf, sems.at[1])
            copy.start()
            copy.wait()


def next_potential(col, state, log_count):
    total = state[:, 0:1] + jnp.log2(state[:, 1:2])
    return 0.5 * (col[:, 0:1] + col[:, 1:2] + entropy_weight * (log_count - math.log(2.0) * total))


def columns_kernel(src_ref, use_ref, good_ref, *refs, log_count):
    cols_ref, state_ref, kept_ref, x_ref = refs[:4]
    y_refs = refs[4 : 4 + 1 + len(OFFSETS)]
    next_ref, out_ref, col_ref, alpha_ref, stat_ref, x_buf, y_buf, sems = refs[5 + len(OFFSETS) :]
    slot = pl.program_id(0)
    y, b = slot // BPD, slot % BPD

    @pl.when(slot == 0)
    def _():
        lane = iota((BS, 128), 1)
        for n in range(BPD):
            span = slice(n * BS, (n + 1) * BS)
            f_next = next_potential(cols_ref[span, :], state_ref[span, :], log_count)
            half = cols_ref[span, 1:2]
            next_ref[span, :] = jnp.where(lane == 0, f_next, half)
            alpha = (f_next - half) * scale
            top, bottom = spread(alpha)
            alpha_ref[span, :] = jnp.where(lane == 0, alpha, jnp.exp2(alpha - top))
            most = jnp.max(half, axis=0, keepdims=True)
            lane1 = iota((1, 128), 1)
            stat_ref[n, :, :] = jnp.where(lane1 == 0, top, jnp.where(lane1 == 1, bottom, most))

    @pl.when(b == 0)
    def _():
        col_ref[0:1, :] = jnp.full((1, BS), lowest, f32)
        col_ref[1:2, :] = jnp.zeros((1, BS), f32)

    @pl.when(use_ref[slot] > 0)
    def _():
        top, bottom = stat_ref[b, :, 0:1], stat_ref[b, :, 1:2]
        fits = (scalar(top - bottom) <= good_ref[slot, 0]) & (good_ref[slot, 1] > 0.5)
        alpha_now = alpha_ref.at[pl.ds(b * BS, BS), :]

        @pl.when(fits)
        def _():
            sums = jnp.zeros((8, BS), f32)
            for c in range(BS // CHUNK):
                span = slice(c * CHUNK, (c + 1) * CHUNK)
                sums = sums + fold_rows(kept_ref[0, span, :].astype(f32) * alpha_now[span, 1:2])
            put_cols(col_ref, top, jnp.sum(sums, axis=0, keepdims=True))

        @pl.when(jnp.logical_not(fits))
        def _():
            load_pair(slot, x_ref, y_refs, x_buf, y_buf, sems)
            shifted_cols(x_buf, y_buf, alpha_now, col_ref)

    @pl.when(b == BPD - 1)
    def _():
        out_ref[y] = jnp.where(col_ref[1:2, :] > 0.0, col_ref[0:1, :] + jnp.log2(col_ref[1:2, :]), lowest)


def rows_kernel(src_ref, use_ref, good_ref, *refs, log_count):
    beta_ref, cols_ref, kept_ref, x_ref = refs[:4]
    y_refs = refs[4 : 4 + 1 + len(OFFSETS)]
    out_ref, state_ref, x_buf, y_buf, sems = refs[5 + len(OFFSETS) :]
    slot = pl.program_id(0)
    y, b = slot // BPD, slot % BPD

    @pl.when(slot == 0)
    def _():
        lane = iota((LOCAL, 128), 1)
        state_ref[...] = jnp.where(lane == 0, lowest, 0.0)

    @pl.when(use_ref[slot] > 0)
    def _():
        beta = beta_ref[y] * scale
        top, bottom = spread(beta)
        fits = (scalar(top - bottom) <= good_ref[slot, 0]) & (good_ref[slot, 1] > 0.5)

        @pl.when(fits)
        def _():
            weight = jnp.exp2(beta - top)
            for c in range(BS // CHUNK):
                span = slice(c * CHUNK, (c + 1) * CHUNK)
                put_rows(state_ref, b * BS + c * CHUNK, top, fold_lanes(kept_ref[0, span, :].astype(f32) * weight))

        @pl.when(jnp.logical_not(fits))
        def _():
            load_pair(slot, x_ref, y_refs, x_buf, y_buf, sems)
            shifted_rows(x_buf, y_buf, beta, state_ref, b * BS)

    @pl.when(slot == SLOTS - 1)
    def _():
        for c in range(LOCAL // 128):
            span = slice(c * 128, (c + 1) * 128)
            f_next = next_potential(cols_ref[span, :], state_ref[span, :], log_count)
            out_ref[0:1, span] = jnp.broadcast_to(f_next, (128, 128)).T[0:1, :]


def kept_spec():
    return pl.BlockSpec((1, BS, BS), lambda t, src, use: (src[t], 0, 0))


def slots_call(kernel, src, use, good, front, kept, x_blocks, y_list, outs, scratch, name):
    whole = lambda s: pl.BlockSpec(s, lambda t, src, use: (0,) * len(s))
    anyw = pl.BlockSpec(memory_space=pl.ANY)
    return pl.pallas_call(
        kernel,
        grid_spec=pltpu.PrefetchScalarGridSpec(
            num_scalar_prefetch=2,
            grid=(SLOTS,),
            in_specs=[pl.BlockSpec(memory_space=pltpu.SMEM)]
            + [whole(a.shape) for a in front]
            + [kept_spec(), anyw]
            + [anyw] * len(y_list),
            out_specs=[whole(o.shape) for o in outs],
            scratch_shapes=scratch
            + [pltpu.VMEM((BS, DIM), bf16), pltpu.VMEM((ROWS, DIM), bf16), pltpu.SemaphoreType.DMA((2,))],
        ),
        out_shape=outs,
        compiler_params=params(),
        name=name,
    )(src, use, good, *front, kept, x_blocks, *y_list)


def groups(devices):
    even = [list(range(GROUP * k, GROUP * (k + 1))) for k in range(devices // GROUP)]
    odd = [[(GROUP * k + GROUP // 2 + j) % devices for j in range(GROUP)] for k in range(devices // GROUP)]
    return even, odd


def swap(rows, axis_groups):
    return lax.all_to_all(rows, "blk", split_axis=0, concat_axis=0, tiled=True, axis_index_groups=axis_groups)


def on_device(x_points, y_points, x_start, y_start, x_order, y_order, partners, counts):
    devices = lax.axis_size("blk")
    me = lax.axis_index("blk")
    share = LOCAL // devices
    log_count = math.log(LOCAL * devices)
    offsets = jnp.array(OFFSETS, i32)

    live = jnp.arange(partners.shape[1], dtype=i32)[None, :] < counts[:, None]
    away = jnp.where(live, partners // BPD - me, devices)
    inner = partners % BPD
    local_use = [((away == 0) & (inner == j)).any(axis=1) for j in range(BPD)]
    far = away[None, :, :] == offsets[:, None, None]
    use = jnp.concatenate([jnp.stack(local_use), far.any(axis=2)]).astype(i32).reshape(SLOTS)
    need = jnp.max(jnp.where(far, inner[None], 0), axis=(1, 2))
    info = jnp.concatenate([(me + offsets) * share, need, (me - offsets) * share]).astype(i32)

    y_sent = pack(info, y_order[None, :], y_start.astype(f32)[None, :], y_points, devices)
    y_came = lax.all_to_all(y_sent, "blk", split_axis=0, concat_axis=0, tiled=True)
    x_sent = pack(info, x_order[None, :], x_start.astype(f32)[None, :], x_points, devices)
    x_came = lax.all_to_all(x_sent, "blk", split_axis=0, concat_axis=0, tiled=True)

    y_rows, y_own, *y_sends = unpack_y(info, y_came)
    y_far = []
    for off, block in zip(OFFSETS, y_sends):
        pairs = [(i, i - off) for i in range(devices) if 0 <= i - off < devices]
        y_far.append(lax.ppermute(block, "blk", pairs))
    x_blocks, x_cols = unpack_x(x_came)

    state, col_a, good_a, kept = sweep(use, x_blocks, x_cols, [y_own], 0, None)
    state, col_b, good_b, kept = sweep(use, x_blocks, x_cols, y_far[:4], 2, (state, kept))
    state, col_c, good_c, kept = sweep(use, x_blocks, x_cols, y_far[4:], 6, (state, kept))
    y_all = [y_own] + y_far

    y_most = jnp.concatenate([y_own[:, BS + 6, 0], jnp.stack([v[BS + 6, 0] for v in y_far])]).astype(f32)
    x_most = jnp.max(x_cols[:, 1].reshape(BPD, BS), axis=1)
    room = exponent_room - 2.0 * scale * jnp.sqrt(y_most[:, None] * x_most[None, :])
    good = jnp.stack([room.reshape(SLOTS), jnp.concatenate([good_a, good_b, good_c]).astype(f32)], axis=1)
    slots = jnp.arange(SLOTS, dtype=i32)
    src = lax.cummax(jnp.where(use > 0, slots, 0))

    even, odd = groups(devices)
    seat_even = me % GROUP
    seat_odd = (me + GROUP // 2) % GROUP
    base_even = me - seat_even
    base_odd = (me - seat_odd) % devices
    flags = y_came.reshape(devices, share, WIDE)[:, 0, DIM + 3]
    pick_even = lax.dynamic_slice(flags, (base_even,), (GROUP,)) > 0.5
    pick_odd = lax.dynamic_slice(jnp.concatenate([flags, flags]), (base_odd,), (GROUP,)) > 0.5
    ids_odd = (base_odd + jnp.arange(GROUP, dtype=i32)) % devices
    twice = ids_odd // GROUP == me // GROUP
    by_offset = [OFFSETS.index(o) if o else None for o in range(-REACH, REACH + 1)]

    def outgoing(far_rows, seat):
        none = jnp.full((1, BS), lowest, f32)
        table = jnp.concatenate([none if k is None else far_rows[k : k + 1] for k in by_offset])
        table = jnp.pad(table, ((GROUP, GROUP), (0, 0)), constant_values=lowest)
        return lax.dynamic_slice(table, (GROUP + REACH - seat, 0), (GROUP, BS))

    def gathered(own_rows, from_even, from_odd):
        from_odd = jnp.where(twice[:, None], lowest, from_odd)
        out = []
        for j in range(BPD):
            terms = jnp.concatenate(
                [
                    own_rows[j : j + 1],
                    jnp.where((pick_even == bool(j))[:, None], from_even, lowest),
                    jnp.where((pick_odd == bool(j))[:, None], from_odd, lowest),
                ]
            )
            top = jnp.max(terms, axis=0)
            out.append(top + jnp.log2(jnp.sum(jnp.exp2(terms - top), axis=0)))
        return jnp.stack(out)

    cols_first = jnp.concatenate([col_a, col_b, col_c]).reshape(YBLOCKS, BS)
    back_even = swap(outgoing(cols_first[BPD:], seat_even), even)
    back_odd = swap(outgoing(cols_first[BPD:], seat_odd), odd)

    x_next, cols_second = slots_call(
        functools.partial(columns_kernel, log_count=log_count),
        src,
        use,
        good,
        [x_cols, state],
        kept,
        x_blocks,
        y_all,
        [jax.ShapeDtypeStruct((LOCAL, 128), f32), jax.ShapeDtypeStruct((YBLOCKS, 1, BS), f32)],
        [pltpu.VMEM((8, BS), f32), pltpu.VMEM((LOCAL, 128), f32), pltpu.VMEM((BPD, 1, 128), f32)],
        "columns",
    )
    cols_second = cols_second.reshape(YBLOCKS, BS)

    g_start, y_half = y_rows[:, 0], y_rows[:, 1]

    def next_g(g_now, total):
        return 0.5 * (g_now + y_half + entropy_weight * (log_count - math.log(2.0) * total))

    g_one = next_g(g_start, gathered(cols_first[:BPD], back_even, back_odd))
    beta = g_one - y_half
    chosen = lambda picks: jnp.where(picks[:, None], beta[1][None], beta[0][None])
    both_even = swap(jnp.stack([chosen(pick_even), outgoing(cols_second[BPD:], seat_even)], axis=1), even)
    both_odd = swap(jnp.stack([chosen(pick_odd), outgoing(cols_second[BPD:], seat_odd)], axis=1), odd)

    g_two = next_g(g_one, gathered(cols_second[:BPD], both_even[:, 1], both_odd[:, 1]))

    def window(rows, seat):
        return lax.dynamic_slice(jnp.pad(rows, ((REACH, REACH), (0, 0))), (seat, 0), (2 * REACH + 1, BS))

    reach = jnp.arange(-REACH, REACH + 1, dtype=i32) + seat_even
    in_even = (reach >= 0) & (reach < GROUP)
    near = jnp.where(in_even[:, None], window(both_even[:, 0], seat_even), window(both_odd[:, 0], seat_odd))
    betas = jnp.concatenate([beta] + [near[o + REACH : o + REACH + 1] for o in OFFSETS])[:, None, :]

    (f_two,) = slots_call(
        functools.partial(rows_kernel, log_count=log_count),
        src,
        use,
        good,
        [betas, x_next],
        kept,
        x_blocks,
        y_all,
        [jax.ShapeDtypeStruct((1, LOCAL), f32)],
        [pltpu.VMEM((LOCAL, 128), f32)],
        "rows",
    )
    return f_two.reshape(LOCAL), g_two.reshape(LOCAL)


def solution(mesh):
    placed_as = (
        P("blk", None),
        P("blk", None),
        P("blk"),
        P("blk"),
        P("blk"),
        P("blk"),
        P("blk", None),
        P("blk"),
    )
    return jax.shard_map(
        on_device, mesh=mesh, in_specs=placed_as, out_specs=(P("blk"), P("blk")), check_vma=False
    )
```

```python
import functools
import math

import jax
import jax.numpy as jnp
import numpy as np
from jax import lax
from jax.experimental import pallas as pl
from jax.experimental.pallas import tpu as pltpu
from jax.sharding import PartitionSpec as P

DIM = 512
BS = 1024
BPD = 2
REACH = 3
LOCAL = BPD * BS
EXTRA = 128
WIDE = DIM + EXTRA
TAIL = 16
ROWS = BS + TAIL
CHUNK = 512
PART = 256
OFFSETS = (-1, 1, -2, 2, -3, 3)
FAR = len(OFFSETS)
YBLOCKS = BPD + FAR
SLOTS = BPD * YBLOCKS
MOST = 12
GROUP = 8
PEERS = GROUP + 3
X_LANES = EXTRA // 2

entropy_weight = 0.05
scale = math.log2(math.e) / entropy_weight
log_two = math.log(2.0)
lowest = -1e30
exponent_room = 112.0
vmem_bytes = 56 * 1024 * 1024

f32 = jnp.float32
bf16 = jnp.bfloat16
i32 = jnp.int32

SMEM = pl.BlockSpec(memory_space=pltpu.SMEM)
ANY = pl.BlockSpec(memory_space=pl.ANY)


def iota(shape, dim):
    return lax.broadcasted_iota(i32, shape, dim)


def dot(a, b):
    return jnp.dot(a, b, preferred_element_type=f32)


def nt_dot(a, b):
    return lax.dot_general(a, b, (((1,), (1,)), ((), ())), preferred_element_type=f32)


def ones_where(mask):
    return jnp.where(mask, 1.0, 0.0).astype(bf16)


def params():
    return pltpu.CompilerParams(vmem_limit_bytes=vmem_bytes)


def whole(shape):
    return pl.BlockSpec(shape, lambda *t: (0,) * len(shape))


def laid_out(square):
    return jnp.concatenate([square[n : n + 1, :] for n in range(square.shape[0])], axis=1)


def down(row):
    parts = [jnp.broadcast_to(row[:, c : c + 128], (128, 128)).T for c in range(0, row.shape[1], 128)]
    return jnp.concatenate(parts, axis=0)


def moved(values, place):
    high = iota((16, LOCAL), 0) == lax.shift_right_logical(place, 7)
    low = ones_where(iota((128, LOCAL), 0) == jnp.bitwise_and(place, 127))
    stack = jnp.concatenate([jnp.where(high, v, 0.0) for v in values], axis=0).astype(bf16)
    out = nt_dot(stack, low)
    return [laid_out(out[16 * n : 16 * n + 16, :]) for n in range(len(values))]


def moved_exact(value, place):
    first = value.astype(bf16).astype(f32)
    second = (value - first).astype(bf16).astype(f32)
    parts = moved([first, second, value - first - second], place)
    return parts[0] + parts[1] + parts[2]


def before_matrix():
    return ones_where(iota((128, 128), 0) < iota((128, 128), 1))


def plan(order, start, devices, first_lane):
    share = LOCAL // devices
    target = lax.shift_right_logical(order, 11)
    hit = iota((devices, LOCAL), 0) == target
    hot = ones_where(hit)
    before = before_matrix()
    every = jnp.ones((128, 128), bf16)
    seen = jnp.zeros((devices, 128), f32)
    earlier = []
    for c in range(0, LOCAL, 128):
        piece = hot[:, c : c + 128]
        earlier.append(dot(piece, before) + seen)
        seen = seen + dot(piece, every)
    earlier = jnp.concatenate(earlier, axis=1)
    rank = jnp.sum(jnp.where(hit, earlier, 0.0), axis=0, keepdims=True).astype(i32)
    within = jnp.bitwise_and(order, LOCAL - 1)
    high = lax.shift_right_logical(within, 6).astype(f32)
    low = jnp.bitwise_and(within, 63).astype(f32)
    row = iota((EXTRA, LOCAL), 0) - first_lane
    field = row // share
    value = jnp.where(field == 0, high, jnp.where(field == 1, low, start))
    mine = (row >= 0) & (row < 3 * share) & (row % share == rank)
    return target * share + rank, nt_dot(hot, jnp.where(mine, value, 0.0).astype(bf16))


def pack_y_kernel(
    me_ref, partners_ref, counts_ref, y_order, y_start, x_order, x_start, points_ref, out_ref, x_pos_ref, pos_ref, table_ref,
    *, devices
):
    step = pl.program_id(0)
    share = LOCAL // devices

    @pl.when(step == 0)
    def _():
        pos, y_table = plan(y_order[...], y_start[...], devices, 0)
        pos_ref[...] = pos
        x_pos, x_table = plan(x_order[...], x_start[...], devices, X_LANES)
        x_pos_ref[...] = x_pos
        me = me_ref[0]
        need = [jnp.int32(0)] * FAR
        for b in range(BPD):
            for s in range(partners_ref.shape[1]):
                block = partners_ref[b, s]
                away = lax.shift_right_logical(block, 1) - me
                for k in range(FAR):
                    listed = (s < counts_ref[b]) & (away == OFFSETS[k])
                    need[k] = jnp.where(listed, jnp.bitwise_and(block, 1), need[k])
        table = y_table + x_table
        row, lane = iota(table.shape, 0), iota(table.shape, 1)
        for k in range(FAR):
            table = jnp.where((row == me + OFFSETS[k]) & (lane == 3 * share), need[k].astype(f32), table)
        table_ref[...] = table

    base = step * CHUNK
    hot = ones_where(iota((CHUNK, LOCAL), 0) + base == pos_ref[...])
    out_ref[:, :DIM] = dot(hot, points_ref[...]).astype(bf16)
    some = CHUNK // share
    table = table_ref[pl.ds(pl.multiple_of(step * some, some), some), :]
    out_ref[:, DIM:] = jnp.broadcast_to(table[:, None, :], (some, share, EXTRA)).reshape(CHUNK, EXTRA).astype(bf16)


def pack_y(me, partners, counts, y_order, y_start, x_order, x_start, points, devices):
    row = whole((1, LOCAL))
    return pl.pallas_call(
        functools.partial(pack_y_kernel, devices=devices),
        grid=(LOCAL // CHUNK,),
        in_specs=[SMEM, SMEM, SMEM, row, row, row, row, whole((LOCAL, DIM))],
        out_specs=[pl.BlockSpec((CHUNK, WIDE), lambda t: (t, 0)), row],
        out_shape=[jax.ShapeDtypeStruct((LOCAL, WIDE), bf16), jax.ShapeDtypeStruct((1, LOCAL), i32)],
        scratch_shapes=[pltpu.VMEM((1, LOCAL), i32), pltpu.VMEM((devices, EXTRA), f32)],
        compiler_params=params(),
        name="pack_y",
    )(me, partners, counts, y_order, y_start, x_order, x_start, points)


def pack_x_kernel(pos_ref, points_ref, out_ref):
    base = pl.program_id(0) * CHUNK
    hot = ones_where(iota((CHUNK, LOCAL), 0) + base == pos_ref[...])
    out_ref[...] = dot(hot, points_ref[...]).astype(bf16)


def pack_x(pos, points):
    return pl.pallas_call(
        pack_x_kernel,
        grid=(LOCAL // CHUNK,),
        in_specs=[whole((1, LOCAL)), whole((LOCAL, DIM))],
        out_specs=pl.BlockSpec((CHUNK, DIM), lambda t: (t, 0)),
        out_shape=jax.ShapeDtypeStruct((LOCAL, DIM), bf16),
        compiler_params=params(),
        name="pack_x",
    )(pos, points)


WINDOW = PART + 16
HELD = BS + WINDOW + 16


def unpack_y_kernel(me_ref, came_ref, rows_ref, fields_ref, table_ref, own_ref, *rest, devices):
    sends = rest[:FAR]
    held, sems, own_sem = rest[FAR:]
    share = LOCAL // devices
    me = me_ref[0]
    row, lane = iota((devices, LOCAL), 0), iota((devices, LOCAL), 1)
    table = dot(ones_where(lane == row * share), came_ref[:, DIM:])
    table_ref[...] = table
    held[...] = jnp.zeros(held.shape, bf16)
    table = table.astype(bf16)
    mine = lane // share == row
    spot = lane % share

    def field(base, with_low):
        pick = jnp.where(row == base + spot, 64.0 if with_low else 1.0, 0.0)
        if with_low:
            pick = jnp.where(row == base + share + spot, 1.0, pick)
        return jnp.sum(jnp.where(mine, dot(table, pick.astype(bf16)), 0.0), axis=0, keepdims=True)

    place = field(0, True)
    start = field(2 * share, False)
    fields_ref[0:1, :] = field(X_LANES, True)
    fields_ref[1:2, :] = field(X_LANES + 2 * share, False)
    fields_ref[2:8, :] = jnp.zeros((6, LOCAL), f32)

    picks = []
    small_row, small_lane = iota((devices, EXTRA), 0), iota((devices, EXTRA), 1)
    for k in range(FAR):
        here = (small_row == me - OFFSETS[k]) & (small_lane == 3 * share)
        picks.append(jnp.sum(jnp.where(here, table_ref[...], 0.0)) > 0.5)

    second = place >= float(BS)
    bits = jnp.where(second, 1.0, 0.0)
    square = jnp.concatenate([bits[:, c : c + 128] for c in range(0, LOCAL, 128)], axis=0).astype(bf16)
    totals = dot(square, jnp.ones((128, 128), bf16)).astype(bf16)
    earlier = dot(square, before_matrix()) + dot(ones_where(iota((16, 16), 1) < iota((16, 16), 0)), totals)
    ones_before = laid_out(earlier)
    dest = jnp.where(second, ones_before, iota((1, LOCAL), 1).astype(f32) - ones_before).astype(i32)
    seat = jnp.where(second, dest + BS, dest)
    position = place.astype(i32)
    start_row, high_row, low_row = moved(
        [start, lax.shift_right_logical(position, 6).astype(f32), jnp.bitwise_and(position, 63).astype(f32)], seat
    )
    rows_ref[0:1, :] = start_row
    rows_ref[2:3, :] = high_row * 64.0 + low_row
    rows_ref[3:8, :] = jnp.zeros((5, LOCAL), f32)
    sixteen, lane16 = iota((16, 128), 0), iota((16, 128), 1)

    for j in range(BPD):
        here = jnp.where(second if j else jnp.logical_not(second), dest, -1)
        for c in range(LOCAL // PART):
            span = slice(c * PART, (c + 1) * PART)
            begin = jnp.sum(jnp.where((sixteen == c * PART // 128) & (lane16 == 0), earlier, 0.0)).astype(i32)
            if j == 0:
                begin = c * PART - begin
            begin = pl.multiple_of(lax.shift_left(lax.shift_right_logical(begin, 4), 4), 16)
            hot = ones_where(iota((WINDOW, PART), 0) + begin == here[:, span])
            part = dot(hot, came_ref[span, :DIM]).astype(bf16)
            held[j, pl.ds(begin, WINDOW), :] = held[j, pl.ds(begin, WINDOW), :] + part
        half = []
        for c in range(0, BS, PART):
            points = held[j, c : c + PART, :].astype(f32)
            total = 0.5 * jnp.sum(points * points, axis=1, keepdims=True)
            half.append(jnp.broadcast_to(total, (PART, 128)).T[0:1, :])
        half = jnp.concatenate(half, axis=1)
        block = slice(j * BS, (j + 1) * BS)
        rows_ref[1:2, block] = half
        beta = start_row[:, block] - half
        first = beta.astype(bf16).astype(f32)
        next_part = (beta - first).astype(bf16).astype(f32)
        most = jnp.max(half, axis=1, keepdims=True) * 1.01
        sub = iota((TAIL, DIM), 0)
        tail = jnp.zeros((TAIL, DIM), f32) + most
        for n, piece in enumerate((first, next_part, beta - first - next_part)):
            tail = jnp.where(sub == 2 * n, piece[:, :DIM], tail)
            tail = jnp.where(sub == 2 * n + 1, piece[:, DIM:], tail)
        held[j, BS:ROWS, :] = tail.astype(bf16)
        done = held.at[j, pl.ds(0, ROWS), :]
        for k in range(FAR):
            wanted = picks[k] if j == 1 else jnp.logical_not(picks[k])

            @pl.when(wanted)
            def _():
                pltpu.make_async_copy(done, sends[k], sems.at[k]).start()

        pltpu.make_async_copy(done, own_ref.at[j], own_sem.at[j]).start()

    done = held.at[0, pl.ds(0, ROWS), :]
    for k in range(FAR):
        pltpu.make_async_copy(done, sends[k], sems.at[k]).wait()
    for j in range(BPD):
        pltpu.make_async_copy(done, own_ref.at[j], own_sem.at[j]).wait()


def unpack_y(me, came, devices):
    vmem = pl.BlockSpec(memory_space=pltpu.VMEM)
    return pl.pallas_call(
        functools.partial(unpack_y_kernel, devices=devices),
        in_specs=[SMEM, vmem],
        out_specs=[vmem, vmem, vmem] + [ANY] * (1 + FAR),
        out_shape=[
            jax.ShapeDtypeStruct((8, LOCAL), f32),
            jax.ShapeDtypeStruct((8, LOCAL), f32),
            jax.ShapeDtypeStruct((devices, EXTRA), f32),
            jax.ShapeDtypeStruct((BPD, ROWS, DIM), bf16),
        ]
        + [jax.ShapeDtypeStruct((ROWS, DIM), bf16)] * FAR,
        scratch_shapes=[
            pltpu.VMEM((BPD, HELD, DIM), bf16),
            pltpu.SemaphoreType.DMA((FAR,)),
            pltpu.SemaphoreType.DMA((BPD,)),
        ],
        compiler_params=params(),
        name="unpack_y",
    )(me, came)


def unpack_x_kernel(came_ref, fields_ref, points_ref, alpha_ref, rows_ref, place_ref, start_ref):
    step = pl.program_id(0)

    @pl.when(step == 0)
    def _():
        place = fields_ref[0:1, :].astype(i32)
        place_ref[...] = place
        start_ref[...] = moved([fields_ref[1:2, :]], place)[0]

    base = step * CHUNK
    hot = ones_where(iota((CHUNK, LOCAL), 0) + base == place_ref[...])
    points = dot(hot, came_ref[...])
    points_ref[...] = points.astype(bf16)
    half = jnp.broadcast_to(0.5 * jnp.sum(points * points, axis=1, keepdims=True), (CHUNK, 128))
    start = start_ref[:, pl.ds(pl.multiple_of(base, CHUNK), CHUNK)]
    alpha_ref[...] = (down(start) - half) * scale
    rows_ref[0:1, :] = start
    rows_ref[1:8, :] = jnp.concatenate([half[c : c + 128, :].T[0:7, :] for c in range(0, CHUNK, 128)], axis=1)


def unpack_x(came, fields):
    return pl.pallas_call(
        unpack_x_kernel,
        grid=(LOCAL // CHUNK,),
        in_specs=[whole((LOCAL, DIM)), whole((8, LOCAL))],
        out_specs=[
            pl.BlockSpec((CHUNK, DIM), lambda t: (t, 0)),
            pl.BlockSpec((CHUNK, 128), lambda t: (t, 0)),
            pl.BlockSpec((8, CHUNK), lambda t: (0, t)),
        ],
        out_shape=[
            jax.ShapeDtypeStruct((LOCAL, DIM), bf16),
            jax.ShapeDtypeStruct((LOCAL, 128), f32),
            jax.ShapeDtypeStruct((8, LOCAL), f32),
        ],
        scratch_shapes=[pltpu.VMEM((1, LOCAL), i32), pltpu.VMEM((1, LOCAL), f32)],
        compiler_params=params(),
        name="unpack_x",
    )(came, fields)


def merge(top, total, other_top, other_total):
    new = jnp.maximum(top, other_top)
    return new, total * jnp.exp2(top - new) + other_total * jnp.exp2(other_top - new)


def logs(top, total):
    return jnp.where(total > 0.0, top + jnp.log2(total), lowest)


def high_of(row):
    return jnp.max(row, axis=1, keepdims=True)


def low_of(row):
    return jnp.min(row, axis=1, keepdims=True)


def put_cols(col_ref, y, part_top, part_total):
    top, total = merge(col_ref[y, 0:1, :], col_ref[y, 1:2, :], part_top, part_total)
    col_ref[y, 0:1, :] = top
    col_ref[y, 1:2, :] = total


def clear_cols(col_ref):
    col_ref[:, 0:1, :] = jnp.full((col_ref.shape[0], 1, BS), lowest, f32)
    col_ref[:, 1:2, :] = jnp.zeros((col_ref.shape[0], 1, BS), f32)


def shifted_rows(x_ref, y_ref, beta, part_ref):
    def body(c, carry):
        span = pl.ds(pl.multiple_of(c * PART, PART), PART)
        terms = nt_dot(x_ref[span, :], y_ref[0:BS, :]) * scale + beta
        top = jnp.max(terms, axis=1, keepdims=True)
        total = jnp.sum(jnp.exp2(terms - top), axis=1, keepdims=True)
        part_ref[span, :] = jnp.where(iota((PART, 128), 1) == 0, top, total)
        return carry

    lax.fori_loop(0, BS // PART, body, 0)


def shifted_cols(x_ref, y_ref, alpha_ref, col_ref, y):
    def body(c, carry):
        span = pl.ds(pl.multiple_of(c * PART, PART), PART)
        terms = nt_dot(x_ref[span, :], y_ref[0:BS, :]) * scale + alpha_ref[span, 0:1]
        top = jnp.max(terms, axis=0, keepdims=True)
        put_cols(col_ref, y, top, jnp.sum(jnp.exp2(terms - top), axis=0, keepdims=True))
        return carry

    lax.fori_loop(0, BS // PART, body, 0)


def add_part(part_ref, state_ref, b):
    for c in range(0, BS, 128):
        part = part_ref[c : c + 128, :].T
        span = pl.ds(pl.multiple_of(b * BS + c, 128), 128)
        top, total = merge(state_ref[0:1, span], state_ref[1:2, span], part[0:1, :], part[1:2, :])
        state_ref[0:1, span] = top
        state_ref[1:2, span] = total


def lane_sums(refs):
    out = []
    for c in range(0, LOCAL, 128):
        part = refs[0][c : c + 128, :]
        for ref in refs[1:]:
            part = part + ref[c : c + 128, :]
        out.append(jnp.sum(part.T, axis=0, keepdims=True))
    return jnp.concatenate(out, axis=1)


def fold(values):
    return jnp.sum(values.reshape(values.shape[0] // 8, 8, 128), axis=0)


def own_beta(y_rows_ref):
    return (y_rows_ref[0:1, :] - y_rows_ref[1:2, :]) * scale


def sweep_kernel(*refs, base, count, first, last):
    use_ref, x_ref, alpha_ref, x_rows_ref, y_rows_ref = refs[:5]
    refs = refs[5:]
    if not first:
        cols_in, left_in = refs[:2]
        refs = refs[4:]
    if last:
        seat_ref = refs[0]
        refs = refs[1:]
    y_refs = refs[:1] if first else refs[:count]
    refs = refs[len(y_refs) :]
    acc_ref, cols_ref, left_ref, kept_ref, slow_ref = refs[:5]
    refs = refs[5:]
    if last:
        group_out, pair_outs = refs[0], refs[1:4]
        refs = refs[4:]
    y_buf, sems, col_ref, weight_ref, part_ref, stat_ref = refs
    step = pl.program_id(0)
    y, b = step // BPD, step % BPD

    def copy(n):
        source = y_refs[0].at[n] if first else y_refs[n]
        return pltpu.make_async_copy(source, y_buf.at[n % 2], sems.at[n % 2])

    @pl.when(step == 0)
    def _():
        copy(0).start()
        acc_ref[...] = jnp.zeros((LOCAL, 128), f32)
        if first:
            for n in range(SLOTS):
                left_ref[n] = -1.0
        else:
            for n in range(SLOTS):
                left_ref[n] = left_in[n]
            cols_ref[...] = cols_in[...]
        alpha = (x_rows_ref[0:1, :] - x_rows_ref[1:2, :]) * scale
        top = high_of(alpha)
        weight_ref[...] = jnp.exp2(alpha_ref[...] - top)
        lane = iota((8, 128), 1)
        beta_top = high_of(own_beta(y_rows_ref))
        most = high_of(x_rows_ref[1:2, :]) * 1.01
        stat_ref[...] = jnp.where(lane == 0, top, jnp.where(lane == 1, top - low_of(alpha), jnp.where(lane == 2, most, beta_top)))

    for n in range(count):

        @pl.when(step == BPD * n)
        def _():
            copy(n).wait()
            if n + 1 < count:
                copy(n + 1).start()

    @pl.when(b == 0)
    def _():
        clear_cols(col_ref)

    now = y_buf.at[y % 2]
    rows_from = b * BS

    @pl.when(use_ref[base * BPD + step] > 0)
    def _():
        tail = now[BS:ROWS, :].astype(f32)
        halves = [tail[n : n + 1, :] + tail[n + 2 : n + 3, :] + tail[n + 4 : n + 5, :] for n in range(2)]
        beta = jnp.concatenate(halves, axis=1) * scale
        shift = stat_ref[0:1, 3:4]
        left = exponent_room - 2.0 * scale * jnp.sqrt(tail[6:7, 0:1] * stat_ref[0:1, 2:3])
        reach = jnp.maximum(stat_ref[0:1, 1:2], jnp.maximum(high_of(beta) - shift, shift - low_of(beta)))
        fits = (left - reach)[0, 0] >= 0.0

        @pl.when(fits)
        def _():
            left_ref[base * BPD + step] = left[0, 0]
            weight = jnp.exp2(beta - shift)
            sums = jnp.zeros((8, BS), f32)
            for c in range(0, BS, PART):
                span = pl.ds(pl.multiple_of(rows_from + c, PART), PART)
                terms = jnp.exp2(nt_dot(x_ref[span, :], now[0:BS, :]) * scale)
                kept_ref[0, c : c + PART, :] = terms.astype(bf16)
                row_part = acc_ref[span, :]
                col_parts = []
                for n in range(0, BS, 128):
                    piece = terms[:, n : n + 128]
                    row_part = row_part + piece * weight[:, n : n + 128]
                    col_parts.append(fold(piece * weight_ref[span, :]))
                acc_ref[span, :] = row_part
                sums = sums + jnp.concatenate(col_parts, axis=1)
            put_cols(col_ref, 0, stat_ref[0:1, 0:1], jnp.sum(sums, axis=0, keepdims=True))

        @pl.when(jnp.logical_not(fits))
        def _():
            block = pl.ds(pl.multiple_of(rows_from, BS), BS)
            shifted_rows(x_ref.at[block, :], now, beta, part_ref)
            out = pltpu.make_async_copy(part_ref, slow_ref.at[base * BPD + step], sems.at[2])
            out.start()
            shifted_cols(x_ref.at[block, :], now, alpha_ref.at[block, :], col_ref, 0)
            out.wait()

    @pl.when(b == BPD - 1)
    def _():
        cols_ref[base + y] = logs(col_ref[0, 0:1, :], col_ref[0, 1:2, :])

    if last:

        @pl.when(step == BPD * count - 1)
        def _():
            for n in range(PEERS):
                value = outgoing(cols_ref, seat_ref[n])
                if n < GROUP:
                    group_out[n] = value
                else:
                    pair_outs[n - GROUP][0] = value


def outgoing(cols_ref, index):
    return jnp.where(index < 0, lowest, cols_ref[jnp.maximum(index, 0)])


def sweep(use, x_blocks, alpha, x_rows, y_rows, y_list, base, carried, seats):
    first, last = carried is None, seats is not None
    count = BPD if first else len(y_list)
    steps = count * BPD
    in_specs = [SMEM, whole((LOCAL, DIM)), whole((LOCAL, 128)), whole((8, LOCAL)), whole((8, LOCAL))]
    operands = [use, x_blocks, alpha, x_rows, y_rows]
    aliases = {}
    if not first:
        in_specs += [whole((YBLOCKS, 1, BS)), SMEM, ANY, ANY]
        operands += list(carried)
        aliases = {7: 3, 8: 4}
    if last:
        in_specs.append(SMEM)
        operands.append(seats)
    in_specs += [ANY] * len(y_list)
    operands += y_list
    out_specs = [
        whole((LOCAL, 128)),
        whole((YBLOCKS, 1, BS)),
        SMEM,
        pl.BlockSpec((1, BS, BS), lambda t: (base * BPD + t, 0, 0)),
        ANY,
    ]
    out_shape = [
        jax.ShapeDtypeStruct((LOCAL, 128), f32),
        jax.ShapeDtypeStruct((YBLOCKS, 1, BS), f32),
        jax.ShapeDtypeStruct((SLOTS,), f32),
        jax.ShapeDtypeStruct((SLOTS, BS, BS), bf16),
        jax.ShapeDtypeStruct((SLOTS, BS, 128), f32),
    ]
    if last:
        out_specs += [whole((GROUP, 1, BS))] + [whole((1, 1, BS))] * 3
        out_shape += [jax.ShapeDtypeStruct((GROUP, 1, BS), f32)] + [jax.ShapeDtypeStruct((1, 1, BS), f32)] * 3
    return pl.pallas_call(
        functools.partial(sweep_kernel, base=base, count=count, first=first, last=last),
        grid=(steps,),
        in_specs=in_specs,
        out_specs=out_specs,
        out_shape=out_shape,
        scratch_shapes=[
            pltpu.VMEM((2, ROWS, DIM), bf16),
            pltpu.SemaphoreType.DMA((3,)),
            pltpu.VMEM((1, 8, BS), f32),
            pltpu.VMEM((LOCAL, 128), f32),
            pltpu.VMEM((BS, 128), f32),
            pltpu.VMEM((8, 128), f32),
        ],
        input_output_aliases=aliases,
        compiler_params=params(),
        name=f"sweep_{base}",
    )(*operands)


def load_pair(slot, x_ref, y_refs, x_buf, y_buf, sems):
    rows = pl.ds(pl.multiple_of((slot % BPD) * BS, BS), BS)
    fetch = pltpu.make_async_copy(x_ref.at[rows, :], x_buf, sems.at[0])
    fetch.start()
    fetch.wait()
    for n in range(YBLOCKS):

        @pl.when(slot // BPD == n)
        def _():
            source = y_refs[0].at[n] if n < BPD else y_refs[n - BPD + 1]
            fetch = pltpu.make_async_copy(source, y_buf, sems.at[1])
            fetch.start()
            fetch.wait()


def next_potential(now, half, total, log_count):
    return 0.5 * (now + half + entropy_weight * (log_count - log_two * total))


def columns_kernel(list_ref, live_ref, use_ref, left_ref, *refs, log_count, accs):
    acc_refs = refs[:accs]
    x_rows_ref, y_rows_ref, kept_ref, slow_ref, x_ref = refs[accs : accs + 5]
    y_refs = refs[accs + 5 : accs + 6 + FAR]
    next_ref, out_ref, col_ref, weight_ref, state_ref, stat_ref, part_ref, x_buf, y_buf, sems = refs[accs + 6 + FAR :]
    step = pl.program_id(0)
    slot = list_ref[step]
    y, b = slot // BPD, slot % BPD

    @pl.when(step == 0)
    def _():
        clear_cols(col_ref)
        total = lane_sums(acc_refs)
        state_ref[0:1, :] = jnp.where(total > 0.0, high_of(own_beta(y_rows_ref)), lowest)
        state_ref[1:2, :] = total
        for n in range(SLOTS):

            @pl.when((use_ref[n] > 0) & (left_ref[n] < 0.0))
            def _():
                fetch = pltpu.make_async_copy(slow_ref.at[n], part_ref, sems.at[0])
                fetch.start()
                fetch.wait()
                add_part(part_ref, state_ref, n % BPD)

        half = x_rows_ref[1:2, :]
        f_next = next_potential(x_rows_ref[0:1, :], half, logs(state_ref[0:1, :], state_ref[1:2, :]), log_count)
        next_ref[0:1, :] = f_next
        next_ref[1:2, :] = half
        next_ref[2:8, :] = jnp.zeros((6, LOCAL), f32)
        alpha = (f_next - half) * scale
        state_ref[2:3, :] = alpha
        top = high_of(alpha)
        weight_ref[...] = down(jnp.exp2(alpha - top))
        stat_ref[...] = jnp.where(iota((8, 128), 1) == 0, top, top - low_of(alpha))

    @pl.when(step < live_ref[0])
    def _():
        fits = stat_ref[0:1, 1:2][0, 0] <= left_ref[slot]

        @pl.when(fits)
        def _():
            sums = jnp.zeros((8, BS), f32)
            for c in range(0, BS, 64):
                weight = weight_ref[pl.ds(pl.multiple_of(b * BS + c, 64), 64), :]
                parts = [fold(kept_ref[0, c : c + 64, n : n + 128].astype(f32) * weight) for n in range(0, BS, 128)]
                sums = sums + jnp.concatenate(parts, axis=1)
            put_cols(col_ref, y, stat_ref[0:1, 0:1], jnp.sum(sums, axis=0, keepdims=True))

        @pl.when(jnp.logical_not(fits))
        def _():
            load_pair(slot, x_ref, y_refs, x_buf, y_buf, sems)
            for c in range(0, BS, 128):
                row = state_ref[2:3, pl.ds(pl.multiple_of(b * BS + c, 128), 128)]
                part_ref[c : c + 128, :] = jnp.broadcast_to(row, (128, 128)).T
            shifted_cols(x_buf, y_buf, part_ref, col_ref, y)

    @pl.when(step == MOST - 1)
    def _():
        for n in range(YBLOCKS):
            out_ref[n] = logs(col_ref[n, 0:1, :], col_ref[n, 1:2, :])


def gathered(j, own_ref, came, who_ref):
    terms = [own_ref[j]] + [jnp.where(who_ref[n] == j, came(n), lowest) for n in range(PEERS)]
    top = terms[0]
    for term in terms[1:]:
        top = jnp.maximum(top, term)
    total = jnp.exp2(terms[0] - top)
    for term in terms[1:]:
        total = total + jnp.exp2(term - top)
    return top + jnp.log2(total)


def home_kernel(who_ref, seat_ref, group_in, pair_1, pair_2, pair_3, first_ref, second_ref, y_rows_ref, *outs, log_count):
    group_out, out_1, out_2, out_3, g_ref = outs
    pairs_in = (pair_1, pair_2, pair_3)
    came = lambda n: group_in[n] if n < GROUP else pairs_in[n - GROUP][0]
    betas = []
    for j in range(BPD):
        span = slice(j * BS, (j + 1) * BS)
        half = y_rows_ref[1:2, span]
        g_next = next_potential(y_rows_ref[0:1, span], half, gathered(j, first_ref, came, who_ref), log_count)
        g_ref[0:1, span] = g_next
        betas.append((g_next - half) * scale)
        g_ref[1:2, span] = betas[j]
    g_ref[2:8, :] = jnp.zeros((6, LOCAL), f32)
    for n in range(PEERS):
        beta = jnp.where(who_ref[n] == 1, betas[1], betas[0])
        cols = outgoing(second_ref, seat_ref[n])
        if n < GROUP:
            group_out[n, 0:1, :] = beta
            group_out[n, 1:2, :] = cols
        else:
            (out_1, out_2, out_3)[n - GROUP][0, 0:1, :] = beta
            (out_1, out_2, out_3)[n - GROUP][0, 1:2, :] = cols


def home(who, seats, group_in, pairs_in, first, second, y_rows, log_count):
    vmem = pl.BlockSpec(memory_space=pltpu.VMEM)
    return pl.pallas_call(
        functools.partial(home_kernel, log_count=log_count),
        in_specs=[SMEM, SMEM] + [vmem] * 7,
        out_specs=[vmem] * 5,
        out_shape=[jax.ShapeDtypeStruct((GROUP, 2, BS), f32)]
        + [jax.ShapeDtypeStruct((1, 2, BS), f32)] * 3
        + [jax.ShapeDtypeStruct((8, LOCAL), f32)],
        compiler_params=params(),
        name="home",
    )(who, seats, group_in, *pairs_in, first, second, y_rows)


def rows_kernel(list_ref, live_ref, use_ref, left_ref, from_ref, who_ref, *refs, log_count):
    group_in, pair_1, pair_2, pair_3, g_ref, second_ref, y_rows_ref, x_rows_ref, kept_ref, slow_ref, x_ref = refs[:11]
    y_refs = refs[11 : 12 + FAR]
    f_ref, g_out_ref, acc_ref, beta_ref, weight_ref, state_ref, part_ref, x_buf, y_buf, sems = refs[12 + FAR :]
    pairs_in = (pair_1, pair_2, pair_3)
    step = pl.program_id(0)
    slot = list_ref[step]
    y, b = slot // BPD, slot % BPD
    shift = high_of(g_ref[1:2, :])

    @pl.when(step == 0)
    def _():
        acc_ref[...] = jnp.zeros((LOCAL, 128), f32)
        state_ref[0:1, :] = jnp.full((1, LOCAL), lowest, f32)
        state_ref[1:2, :] = jnp.zeros((1, LOCAL), f32)
        for n in range(BPD):
            beta_ref[n] = g_ref[1:2, n * BS : (n + 1) * BS]
        for n in range(BPD, YBLOCKS):
            source = from_ref[n]
            value = group_in[jnp.minimum(source, GROUP - 1), 0:1, :]
            for k in range(3):
                value = jnp.where(source == GROUP + k, pairs_in[k][0, 0:1, :], value)
            beta_ref[n] = value
        weight_ref[...] = jnp.exp2(beta_ref[...] - shift)

    @pl.when(step < live_ref[0])
    def _():
        beta = beta_ref[y]
        reach = jnp.maximum(high_of(beta) - shift, shift - low_of(beta))
        fits = reach[0, 0] <= left_ref[slot]

        @pl.when(fits)
        def _():
            weight = weight_ref[y]
            for c in range(0, BS, 64):
                span = pl.ds(pl.multiple_of(b * BS + c, 64), 64)
                part = acc_ref[span, :]
                for n in range(0, BS, 128):
                    part = part + kept_ref[0, c : c + 64, n : n + 128].astype(f32) * weight[:, n : n + 128]
                acc_ref[span, :] = part

        @pl.when(jnp.logical_not(fits))
        def _():
            load_pair(slot, x_ref, y_refs, x_buf, y_buf, sems)
            shifted_rows(x_buf, y_buf, beta, part_ref)
            add_part(part_ref, state_ref, b)

    @pl.when(step == MOST - 1)
    def _():
        total = lane_sums([acc_ref])
        top = jnp.where(total > 0.0, shift, lowest)
        top, total = merge(top, total, state_ref[0:1, :], state_ref[1:2, :])
        f_ref[...] = next_potential(x_rows_ref[0:1, :], x_rows_ref[1:2, :], logs(top, total), log_count)
        came = lambda n: group_in[n, 1:2, :] if n < GROUP else pairs_in[n - GROUP][0, 1:2, :]
        total = jnp.concatenate([gathered(j, second_ref, came, who_ref) for j in range(BPD)], axis=1)
        g_next = next_potential(g_ref[0:1, :], y_rows_ref[1:2, :], total, log_count)
        g_out_ref[...] = moved_exact(g_next, y_rows_ref[2:3, :].astype(i32))


def slots_call(kernel, lists, smem, front, kept, slow, x_blocks, y_list, outs, scratch, name):
    return pl.pallas_call(
        kernel,
        grid_spec=pltpu.PrefetchScalarGridSpec(
            num_scalar_prefetch=2,
            grid=(MOST,),
            in_specs=[SMEM] * len(smem)
            + [whole(a.shape) for a in front]
            + [pl.BlockSpec((1, BS, BS), lambda t, slots, live: (slots[t], 0, 0)), ANY, ANY]
            + [ANY] * len(y_list),
            out_specs=[whole(o.shape) for o in outs],
            scratch_shapes=scratch
            + [
                pltpu.VMEM((BS, 128), f32),
                pltpu.VMEM((BS, DIM), bf16),
                pltpu.VMEM((ROWS, DIM), bf16),
                pltpu.SemaphoreType.DMA((2,)),
            ],
        ),
        out_shape=outs,
        compiler_params=params(),
        name=name,
    )(*lists, *smem, *front, kept, slow, x_blocks, *y_list)


BORDER = (((7, 0), (6, 1)), ((7, 1), (6, 0)), ((7, 2), (5, 0)))


def seat_tables():
    offsets = np.zeros((GROUP, PEERS), np.int32)
    source = np.zeros((GROUP, YBLOCKS), np.int32)
    for seat in range(GROUP):
        for other in range(GROUP):
            if other != seat and abs(other - seat) <= REACH:
                offsets[seat, other] = other - seat
    for n, pairs in enumerate(BORDER):
        for left, right in pairs:
            offsets[left, GROUP + n] = right + GROUP - left
            offsets[right, GROUP + n] = left - GROUP - right
    for seat in range(GROUP):
        for k, off in enumerate(OFFSETS):
            source[seat, BPD + k] = list(offsets[seat]).index(off)
    index = np.full((GROUP, PEERS), -1, np.int32)
    for k, off in enumerate(OFFSETS):
        index[offsets == off] = BPD + k
    return offsets, index, source


def swap(rows, devices):
    even = [list(range(GROUP * k, GROUP * (k + 1))) for k in range(devices // GROUP)]
    return lax.all_to_all(rows, "blk", split_axis=0, concat_axis=0, tiled=True, axis_index_groups=even)


def cross(rows, n, devices):
    pairs = []
    for k in range(devices // GROUP - 1):
        for left, right in BORDER[n]:
            a, b = GROUP * k + left, GROUP * (k + 1) + right
            pairs += [(a, b), (b, a)]
    return lax.ppermute(rows, "blk", pairs)


def exchanged(group_rows, pair_rows, devices):
    crossed = [cross(rows, n, devices) for n, rows in enumerate(pair_rows)]
    return swap(group_rows, devices), crossed


def on_device(x_points, y_points, x_start, y_start, x_order, y_order, partners, counts):
    devices = lax.axis_size("blk")
    me = lax.axis_index("blk").astype(i32)
    log_count = math.log(LOCAL * devices)
    here = me[None]
    line = lambda v: v.reshape(1, LOCAL)

    y_sent, x_pos = pack_y(
        here,
        partners,
        counts,
        line(y_order),
        line(y_start.astype(f32)),
        line(x_order),
        line(x_start.astype(f32)),
        y_points,
        devices,
    )
    y_came = lax.all_to_all(y_sent, "blk", split_axis=0, concat_axis=0, tiled=True)
    x_sent = pack_x(x_pos, x_points)
    x_came = lax.all_to_all(x_sent, "blk", split_axis=0, concat_axis=0, tiled=True)

    y_rows, x_fields, table, y_own, *y_sends = unpack_y(here, y_came, devices)
    y_far = []
    for off, block in zip(OFFSETS, y_sends):
        pairs = [(i, i - off) for i in range(devices) if 0 <= i - off < devices]
        y_far.append(lax.ppermute(block, "blk", pairs))
    x_blocks, alpha, x_rows = unpack_x(x_came, x_fields)

    offsets = jnp.array(OFFSETS, i32)
    live = jnp.arange(partners.shape[1], dtype=i32)[None, :] < counts[:, None]
    away = jnp.where(live, partners // BPD - me, devices)
    local_use = [((away == 0) & (partners % BPD == j)).any(axis=1) for j in range(BPD)]
    far = away[None, :, :] == offsets[:, None, None]
    use = jnp.concatenate([jnp.stack(local_use), far.any(axis=2)]).astype(i32).reshape(SLOTS)
    number = jnp.cumsum(use) - 1
    count = jnp.sum(use)
    step = jnp.minimum(jnp.arange(MOST, dtype=i32), count - 1)
    at = (number[None, :] == step[:, None]) & (use[None, :] > 0)
    slots = jnp.sum(jnp.where(at, jnp.arange(SLOTS, dtype=i32)[None, :], 0), axis=1)
    lists = (slots, count[None])

    peer_offsets, peer_index, peer_source = seat_tables()
    row = lambda t: lax.dynamic_slice(jnp.asarray(t), (me % GROUP, 0), (1, t.shape[1]))[0]
    seats, source, off = row(peer_index), row(peer_source), row(peer_offsets)
    peer = me + off
    wants = (table[:, 3 * (LOCAL // devices)] > 0.5).astype(i32)
    valid = (off != 0) & (peer >= 0) & (peer < devices)
    who = jnp.where(valid, wants[jnp.clip(peer, 0, devices - 1)], -1)

    common = (use, x_blocks, alpha, x_rows, y_rows)
    acc_0, *carried = sweep(*common, [y_own], 0, None, None)
    acc_1, *carried = sweep(*common, y_far[:2], 2, carried, None)
    acc_2, *carried = sweep(*common, y_far[2:4], 4, carried, None)
    acc_3, cols_first, left, kept, slow, group_out, *pairs_out = sweep(*common, y_far[4:], 6, carried, seats)
    y_all = [y_own] + y_far

    group_in, pairs_in = exchanged(group_out, pairs_out, devices)
    accs = [acc_0, acc_1, acc_2, acc_3]
    x_next, cols_second = slots_call(
        functools.partial(columns_kernel, log_count=log_count, accs=len(accs)),
        lists,
        [use, left],
        accs + [x_rows, y_rows],
        kept,
        slow,
        x_blocks,
        y_all,
        [jax.ShapeDtypeStruct((8, LOCAL), f32), jax.ShapeDtypeStruct((YBLOCKS, 1, BS), f32)],
        [
            pltpu.VMEM((YBLOCKS, 8, BS), f32),
            pltpu.VMEM((LOCAL, 128), f32),
            pltpu.VMEM((8, LOCAL), f32),
            pltpu.VMEM((8, 128), f32),
        ],
        "columns",
    )
    group_out, *pairs_out, g_one = home(who, seats, group_in, pairs_in, cols_first, cols_second, y_rows, log_count)
    group_in, pairs_in = exchanged(group_out, pairs_out, devices)
    f_two, g_two = slots_call(
        functools.partial(rows_kernel, log_count=log_count),
        lists,
        [use, left, source, who],
        [group_in, *pairs_in, g_one, cols_second, y_rows, x_next],
        kept,
        slow,
        x_blocks,
        y_all,
        [jax.ShapeDtypeStruct((1, LOCAL), f32)] * 2,
        [
            pltpu.VMEM((LOCAL, 128), f32),
            pltpu.VMEM((YBLOCKS, 1, BS), f32),
            pltpu.VMEM((YBLOCKS, 1, BS), f32),
            pltpu.VMEM((8, LOCAL), f32),
        ],
        "rows",
    )
    return f_two.reshape(LOCAL), g_two.reshape(LOCAL)


def solution(mesh):
    placed_as = (
        P("blk", None),
        P("blk", None),
        P("blk"),
        P("blk"),
        P("blk"),
        P("blk"),
        P("blk", None),
        P("blk"),
    )
    return jax.shard_map(
        on_device, mesh=mesh, in_specs=placed_as, out_specs=(P("blk"), P("blk")), check_vma=False
    )
```

```python
import functools
import math

import jax
import jax.numpy as jnp
import numpy as np
from jax import lax
from jax.experimental import pallas as pl
from jax.experimental.pallas import tpu as pltpu
from jax.sharding import PartitionSpec as P

DIM = 512
BS = 1024
BPD = 2
REACH = 3
LOCAL = BPD * BS
EXTRA = 128
WIDE = DIM + EXTRA
TAIL = 16
ROWS = BS + TAIL
CHUNK = 512
PART = 256
OFFSETS = (-1, 1, -2, 2, -3, 3)
FAR = len(OFFSETS)
YBLOCKS = BPD + FAR
SLOTS = BPD * YBLOCKS
MOST = 12
GROUP = 8
PEERS = 2 * GROUP
X_LANES = EXTRA // 2

entropy_weight = 0.05
scale = math.log2(math.e) / entropy_weight
log_two = math.log(2.0)
lowest = -1e30
exponent_room = 112.0
mebi = 1024 * 1024

f32 = jnp.float32
bf16 = jnp.bfloat16
i32 = jnp.int32

SMEM = pl.BlockSpec(memory_space=pltpu.SMEM)
ANY = pl.BlockSpec(memory_space=pl.ANY)
VMEM = pl.BlockSpec(memory_space=pltpu.VMEM)
HBM = pl.BlockSpec(memory_space=pltpu.HBM)


def iota(shape, dim):
    return lax.broadcasted_iota(i32, shape, dim)


def dot(a, b):
    return jnp.dot(a, b, preferred_element_type=f32)


def nt_dot(a, b):
    return lax.dot_general(a, b, (((1,), (1,)), ((), ())), preferred_element_type=f32)


def ones_where(mask):
    return jnp.where(mask, 1.0, 0.0).astype(bf16)


def params(limit=30):
    return pltpu.CompilerParams(vmem_limit_bytes=limit * mebi)


def whole(shape):
    return pl.BlockSpec(shape, lambda *t: (0,) * len(shape))


def laid_out(square):
    return jnp.concatenate([square[n : n + 1, :] for n in range(square.shape[0])], axis=1)


def down(row):
    parts = [jnp.broadcast_to(row[:, c : c + 128], (128, 128)).T for c in range(0, row.shape[1], 128)]
    return jnp.concatenate(parts, axis=0)


def moved(values, place):
    high = iota((16, LOCAL), 0) == lax.shift_right_logical(place, 7)
    low = ones_where(iota((128, LOCAL), 0) == jnp.bitwise_and(place, 127))
    stack = jnp.concatenate([jnp.where(high, v, 0.0) for v in values], axis=0).astype(bf16)
    out = nt_dot(stack, low)
    return [laid_out(out[16 * n : 16 * n + 16, :]) for n in range(len(values))]


def moved_exact(value, place):
    first = value.astype(bf16).astype(f32)
    second = (value - first).astype(bf16).astype(f32)
    parts = moved([first, second, value - first - second], place)
    return parts[0] + parts[1] + parts[2]


def before_matrix():
    return ones_where(iota((128, 128), 0) < iota((128, 128), 1))


def plan(order, start, devices, first_lane):
    share = LOCAL // devices
    target = lax.shift_right_logical(order, 11)
    hit = iota((devices, LOCAL), 0) == target
    hot = ones_where(hit)
    before = before_matrix()
    every = jnp.ones((128, 128), bf16)
    seen = jnp.zeros((devices, 128), f32)
    earlier = []
    for c in range(0, LOCAL, 128):
        piece = hot[:, c : c + 128]
        earlier.append(dot(piece, before) + seen)
        seen = seen + dot(piece, every)
    earlier = jnp.concatenate(earlier, axis=1)
    rank = jnp.sum(jnp.where(hit, earlier, 0.0), axis=0, keepdims=True).astype(i32)
    within = jnp.bitwise_and(order, LOCAL - 1)
    high = lax.shift_right_logical(within, 6).astype(f32)
    low = jnp.bitwise_and(within, 63).astype(f32)
    row = iota((EXTRA, LOCAL), 0) - first_lane
    field = row // share
    value = jnp.where(field == 0, high, jnp.where(field == 1, low, start))
    mine = (row >= 0) & (row < 3 * share) & (row % share == rank)
    return target * share + rank, nt_dot(hot, jnp.where(mine, value, 0.0).astype(bf16))


def pack_y_kernel(
    me_ref, partners_ref, counts_ref, y_order, y_start, x_order, x_start, points_ref, out_ref, x_pos_ref, pos_ref, table_ref,
    *, devices
):
    step = pl.program_id(0)
    share = LOCAL // devices

    @pl.when(step == 0)
    def _():
        pos, y_table = plan(y_order[...], y_start[...], devices, 0)
        pos_ref[...] = pos
        x_pos, x_table = plan(x_order[...], x_start[...], devices, X_LANES)
        x_pos_ref[...] = x_pos
        me = me_ref[0]
        need = [jnp.int32(0)] * FAR
        for b in range(BPD):
            for s in range(partners_ref.shape[1]):
                block = partners_ref[b, s]
                away = lax.shift_right_logical(block, 1) - me
                for k in range(FAR):
                    listed = (s < counts_ref[b]) & (away == OFFSETS[k])
                    need[k] = jnp.where(listed, jnp.bitwise_and(block, 1), need[k])
        table = y_table + x_table
        row, lane = iota(table.shape, 0), iota(table.shape, 1)
        for k in range(FAR):
            table = jnp.where((row == me + OFFSETS[k]) & (lane == 3 * share), need[k].astype(f32), table)
        table_ref[...] = table

    base = step * CHUNK
    hot = ones_where(iota((CHUNK, LOCAL), 0) + base == pos_ref[...])
    out_ref[:, :DIM] = dot(hot, points_ref[...]).astype(bf16)
    some = CHUNK // share
    table = table_ref[pl.ds(pl.multiple_of(step * some, some), some), :]
    out_ref[:, DIM:] = jnp.broadcast_to(table[:, None, :], (some, share, EXTRA)).reshape(CHUNK, EXTRA).astype(bf16)


def pack_y(me, partners, counts, y_order, y_start, x_order, x_start, points, devices):
    row = whole((1, LOCAL))
    return pl.pallas_call(
        functools.partial(pack_y_kernel, devices=devices),
        grid=(LOCAL // CHUNK,),
        in_specs=[SMEM, SMEM, SMEM, row, row, row, row, whole((LOCAL, DIM))],
        out_specs=[pl.BlockSpec((CHUNK, WIDE), lambda t: (t, 0)), row],
        out_shape=[pltpu.HBM((LOCAL, WIDE), bf16), jax.ShapeDtypeStruct((1, LOCAL), i32)],
        scratch_shapes=[pltpu.VMEM((1, LOCAL), i32), pltpu.VMEM((devices, EXTRA), f32)],
        compiler_params=params(),
        name="pack_y",
    )(me, partners, counts, y_order, y_start, x_order, x_start, points)


def pack_x_kernel(pos_ref, points_ref, out_ref):
    base = pl.program_id(0) * CHUNK
    hot = ones_where(iota((CHUNK, LOCAL), 0) + base == pos_ref[...])
    out_ref[...] = dot(hot, points_ref[...]).astype(bf16)


def pack_x(pos, points):
    return pl.pallas_call(
        pack_x_kernel,
        grid=(LOCAL // CHUNK,),
        in_specs=[whole((1, LOCAL)), whole((LOCAL, DIM))],
        out_specs=pl.BlockSpec((CHUNK, DIM), lambda t: (t, 0)),
        out_shape=pltpu.HBM((LOCAL, DIM), bf16),
        compiler_params=params(),
        name="pack_x",
    )(pos, points)


WINDOW = PART + 16
HELD = BS + WINDOW + 16


def arrived(table, base, with_low):
    share = 16
    row, lane = iota((EXTRA, EXTRA), 0), iota((EXTRA, EXTRA), 1)
    pick = jnp.where(row == base + lane % share, 64.0 if with_low else 1.0, 0.0)
    if with_low:
        pick = jnp.where(row == base + share + lane % share, 1.0, pick)
    values = dot(table, pick.astype(bf16))
    values = jnp.where(row % (EXTRA // share) == lane // share, values, 0.0)
    return jnp.sum(values.reshape(LOCAL // 128, EXTRA // share, 128), axis=1)


def unpack_y_kernel(me_ref, came_ref, rows_ref, table_ref, own_ref, *rest, devices):
    sends = rest[:FAR]
    held, sems, own_sem = rest[FAR:]
    share = LOCAL // devices
    me = me_ref[0]
    table = dot(ones_where(iota((devices, LOCAL), 1) == iota((devices, LOCAL), 0) * share), came_ref[:, DIM:])
    table_ref[...] = table
    held[...] = jnp.zeros(held.shape, bf16)
    place_square = arrived(table.astype(bf16), 0, True)
    place = laid_out(place_square)
    start = laid_out(arrived(table.astype(bf16), 2 * share, False))

    picks = []
    small_row, small_lane = iota((devices, EXTRA), 0), iota((devices, EXTRA), 1)
    for k in range(FAR):
        here = (small_row == me - OFFSETS[k]) & (small_lane == 3 * share)
        picks.append(jnp.sum(jnp.where(here, table, 0.0)) > 0.5)

    second = place >= float(BS)
    square = ones_where(place_square >= float(BS))
    totals = dot(square, jnp.ones((128, 128), bf16)).astype(bf16)
    earlier = dot(square, before_matrix()) + dot(ones_where(iota((16, 16), 1) < iota((16, 16), 0)), totals)
    ones_before = laid_out(earlier)
    dest = jnp.where(second, ones_before, iota((1, LOCAL), 1).astype(f32) - ones_before).astype(i32)
    seat = jnp.where(second, dest + BS, dest)
    position = place.astype(i32)
    start_row, high_row, low_row = moved(
        [start, lax.shift_right_logical(position, 6).astype(f32), jnp.bitwise_and(position, 63).astype(f32)], seat
    )
    rows_ref[0:1, :] = start_row
    rows_ref[2:3, :] = high_row * 64.0 + low_row
    rows_ref[3:8, :] = jnp.zeros((5, LOCAL), f32)
    sixteen, lane16 = iota((16, 128), 0), iota((16, 128), 1)

    for j in range(BPD):
        here = jnp.where(second if j else jnp.logical_not(second), dest, -1)
        for c in range(LOCAL // PART):
            span = slice(c * PART, (c + 1) * PART)
            begin = jnp.sum(jnp.where((sixteen == c * PART // 128) & (lane16 == 0), earlier, 0.0)).astype(i32)
            if j == 0:
                begin = c * PART - begin
            begin = pl.multiple_of(lax.shift_left(lax.shift_right_logical(begin, 4), 4), 16)
            hot = ones_where(iota((WINDOW, PART), 0) + begin == here[:, span])
            part = dot(hot, came_ref[span, :DIM]).astype(bf16)
            held[j, pl.ds(begin, WINDOW), :] = held[j, pl.ds(begin, WINDOW), :] + part
        half = []
        for c in range(0, BS, PART):
            points = held[j, c : c + PART, :].astype(f32)
            total = 0.5 * jnp.sum(points * points, axis=1, keepdims=True)
            half.append(jnp.broadcast_to(total, (PART, 128)).T[0:1, :])
        half = jnp.concatenate(half, axis=1)
        block = slice(j * BS, (j + 1) * BS)
        rows_ref[1:2, block] = half
        beta = start_row[:, block] - half
        first = beta.astype(bf16).astype(f32)
        next_part = (beta - first).astype(bf16).astype(f32)
        most = jnp.max(half, axis=1, keepdims=True) * 1.01
        sub = iota((TAIL, DIM), 0)
        tail = jnp.zeros((TAIL, DIM), f32) + most
        for n, piece in enumerate((first, next_part, beta - first - next_part)):
            tail = jnp.where(sub == 2 * n, piece[:, :DIM], tail)
            tail = jnp.where(sub == 2 * n + 1, piece[:, DIM:], tail)
        held[j, BS:ROWS, :] = tail.astype(bf16)
        done = held.at[j, pl.ds(0, ROWS), :]
        for k in range(FAR):
            wanted = picks[k] if j == 1 else jnp.logical_not(picks[k])

            @pl.when(wanted)
            def _():
                pltpu.make_async_copy(done, sends[k], sems.at[k]).start()

        pltpu.make_async_copy(done, own_ref.at[j], own_sem.at[j]).start()

    done = held.at[0, pl.ds(0, ROWS), :]
    for k in range(FAR):
        pltpu.make_async_copy(done, sends[k], sems.at[k]).wait()
    for j in range(BPD):
        pltpu.make_async_copy(done, own_ref.at[j], own_sem.at[j]).wait()


def unpack_y(me, came, devices):
    return pl.pallas_call(
        functools.partial(unpack_y_kernel, devices=devices),
        in_specs=[SMEM, VMEM],
        out_specs=[VMEM, VMEM] + [HBM] * (1 + FAR),
        out_shape=[
            jax.ShapeDtypeStruct((8, LOCAL), f32),
            jax.ShapeDtypeStruct((devices, EXTRA), f32),
            pltpu.HBM((BPD, ROWS, DIM), bf16),
        ]
        + [pltpu.HBM((ROWS, DIM), bf16)] * FAR,
        scratch_shapes=[
            pltpu.VMEM((BPD, HELD, DIM), bf16),
            pltpu.SemaphoreType.DMA((FAR,)),
            pltpu.SemaphoreType.DMA((BPD,)),
        ],
        compiler_params=params(),
        name="unpack_y",
    )(me, came)


def unpack_x_kernel(came_ref, table_ref, points_ref, alpha_ref, rows_ref, place_ref, start_ref):
    step = pl.program_id(0)

    @pl.when(step == 0)
    def _():
        table = table_ref[...].astype(bf16)
        place = laid_out(arrived(table, X_LANES, True)).astype(i32)
        place_ref[...] = place
        start_ref[...] = moved([laid_out(arrived(table, X_LANES + 32, False))], place)[0]

    base = step * CHUNK
    hot = ones_where(iota((CHUNK, LOCAL), 0) + base == place_ref[...])
    points = dot(hot, came_ref[...])
    points_ref[...] = points.astype(bf16)
    half = jnp.broadcast_to(0.5 * jnp.sum(points * points, axis=1, keepdims=True), (CHUNK, 128))
    start = start_ref[:, pl.ds(pl.multiple_of(base, CHUNK), CHUNK)]
    alpha_ref[...] = (down(start) - half) * scale
    rows_ref[0:1, :] = start
    rows_ref[1:8, :] = jnp.concatenate([half[c : c + 128, :].T[0:7, :] for c in range(0, CHUNK, 128)], axis=1)


def unpack_x(came, table):
    return pl.pallas_call(
        unpack_x_kernel,
        grid=(LOCAL // CHUNK,),
        in_specs=[whole((LOCAL, DIM)), whole((EXTRA, EXTRA))],
        out_specs=[
            pl.BlockSpec((CHUNK, DIM), lambda t: (t, 0)),
            pl.BlockSpec((CHUNK, 128), lambda t: (t, 0)),
            pl.BlockSpec((8, CHUNK), lambda t: (0, t)),
        ],
        out_shape=[
            jax.ShapeDtypeStruct((LOCAL, DIM), bf16),
            jax.ShapeDtypeStruct((LOCAL, 128), f32),
            jax.ShapeDtypeStruct((8, LOCAL), f32),
        ],
        scratch_shapes=[pltpu.VMEM((1, LOCAL), i32), pltpu.VMEM((1, LOCAL), f32)],
        compiler_params=params(),
        name="unpack_x",
    )(came, table)


def merge(top, total, other_top, other_total):
    new = jnp.maximum(top, other_top)
    return new, total * jnp.exp2(top - new) + other_total * jnp.exp2(other_top - new)


def logs(top, total):
    return jnp.where(total > 0.0, top + jnp.log2(total), lowest)


def high_of(row):
    return jnp.max(row, axis=1, keepdims=True)


def low_of(row):
    return jnp.min(row, axis=1, keepdims=True)


def put_cols(col_ref, y, part_top, part_total):
    top, total = merge(col_ref[y, 0:1, :], col_ref[y, 1:2, :], part_top, part_total)
    col_ref[y, 0:1, :] = top
    col_ref[y, 1:2, :] = total


def clear_cols(col_ref):
    col_ref[:, 0:1, :] = jnp.full((col_ref.shape[0], 1, BS), lowest, f32)
    col_ref[:, 1:2, :] = jnp.zeros((col_ref.shape[0], 1, BS), f32)


def shifted_rows(x_ref, y_ref, beta, part_ref):
    def body(c, carry):
        span = pl.ds(pl.multiple_of(c * PART, PART), PART)
        terms = nt_dot(x_ref[span, :], y_ref[0:BS, :]) * scale + beta
        top = jnp.max(terms, axis=1, keepdims=True)
        total = jnp.sum(jnp.exp2(terms - top), axis=1, keepdims=True)
        part_ref[span, :] = jnp.where(iota((PART, 128), 1) == 0, top, total)
        return carry

    lax.fori_loop(0, BS // PART, body, 0)


def shifted_cols(x_ref, y_ref, alpha_ref, col_ref, y):
    def body(c, carry):
        span = pl.ds(pl.multiple_of(c * PART, PART), PART)
        terms = nt_dot(x_ref[span, :], y_ref[0:BS, :]) * scale + alpha_ref[span, 0:1]
        top = jnp.max(terms, axis=0, keepdims=True)
        put_cols(col_ref, y, top, jnp.sum(jnp.exp2(terms - top), axis=0, keepdims=True))
        return carry

    lax.fori_loop(0, BS // PART, body, 0)


def add_part(part_ref, state_ref, b):
    for c in range(0, BS, 128):
        part = part_ref[c : c + 128, :].T
        span = pl.ds(pl.multiple_of(b * BS + c, 128), 128)
        top, total = merge(state_ref[0:1, span], state_ref[1:2, span], part[0:1, :], part[1:2, :])
        state_ref[0:1, span] = top
        state_ref[1:2, span] = total


def lane_sums(refs):
    out = []
    for c in range(0, LOCAL, 128):
        part = refs[0][c : c + 128, :]
        for ref in refs[1:]:
            part = part + ref[c : c + 128, :]
        out.append(jnp.sum(part.T, axis=0, keepdims=True))
    return jnp.concatenate(out, axis=1)


def fold(values):
    return jnp.sum(values.reshape(values.shape[0] // 8, 8, 128), axis=0)


def own_beta(y_rows_ref):
    return (y_rows_ref[0:1, :] - y_rows_ref[1:2, :]) * scale


def sweep_kernel(*refs, base, count, first, last):
    use_ref, seat_of_ref, x_ref, alpha_ref, x_rows_ref, y_rows_ref = refs[:6]
    refs = refs[6:]
    if not first:
        cols_in, left_in = refs[:2]
        refs = refs[4:]
    if last:
        peers_ref = refs[0]
        refs = refs[1:]
    y_refs = refs[:1] if first else refs[:count]
    refs = refs[len(y_refs) :]
    acc_ref, cols_ref, left_ref, kept_ref, slow_ref = refs[:5]
    refs = refs[5:]
    if last:
        group_outs = refs[:2]
        refs = refs[2:]
    y_buf, sems, col_ref, weight_ref, part_ref, stat_ref, tiles, tile_sems, tile_count = refs

    def copy(n):
        source = y_refs[0].at[n] if first else y_refs[n]
        return pltpu.make_async_copy(source, y_buf.at[n % 2], sems.at[n % 2])

    copy(0).start()
    tile_count[0] = 0
    acc_ref[...] = jnp.zeros((LOCAL, 128), f32)

    def tile_copy(at, seat):
        return pltpu.make_async_copy(tiles.at[at], kept_ref.at[seat], tile_sems.at[at])

    if first:
        for n in range(SLOTS):
            left_ref[n] = -1.0
    else:
        for n in range(SLOTS):
            left_ref[n] = left_in[n]
        cols_ref[...] = cols_in[...]
    alpha = (x_rows_ref[0:1, :] - x_rows_ref[1:2, :]) * scale
    alpha_top = high_of(alpha)
    weight_ref[...] = jnp.exp2(alpha_ref[...] - alpha_top)
    lane = iota((8, 128), 1)
    beta_top = high_of(own_beta(y_rows_ref))
    most = high_of(x_rows_ref[1:2, :]) * 1.01
    spread = alpha_top - low_of(alpha)
    stat_ref[...] = jnp.where(lane == 0, alpha_top, jnp.where(lane == 1, spread, jnp.where(lane == 2, most, beta_top)))

    def body(step, carry):
        y, b = step // BPD, step % BPD
        slot = base * BPD + step
        for n in range(count):

            @pl.when(step == BPD * n)
            def _():
                copy(n).wait()
                if n + 1 < count:
                    copy(n + 1).start()

        @pl.when(b == 0)
        def _():
            clear_cols(col_ref)

        now = y_buf.at[y % 2]
        rows_from = b * BS

        @pl.when(use_ref[slot] > 0)
        def _():
            tail = now[BS:ROWS, :].astype(f32)
            halves = [tail[n : n + 1, :] + tail[n + 2 : n + 3, :] + tail[n + 4 : n + 5, :] for n in range(2)]
            beta = jnp.concatenate(halves, axis=1) * scale
            shift = stat_ref[0:1, 3:4]
            left = exponent_room - 2.0 * scale * jnp.sqrt(tail[6:7, 0:1] * stat_ref[0:1, 2:3])
            reach = jnp.maximum(stat_ref[0:1, 1:2], jnp.maximum(high_of(beta) - shift, shift - low_of(beta)))
            fits = (left - reach)[0, 0] >= 0.0

            @pl.when(fits)
            def _():
                left_ref[slot] = left[0, 0]
                done = tile_count[0]
                tile_count[0] = done + 1
                at = done % 2

                @pl.when(done > 1)
                def _():
                    tile_copy(at, 0).wait()

                weight = jnp.exp2(beta - shift)
                sums = jnp.zeros((8, BS), f32)
                for c in range(0, BS, PART):
                    span = pl.ds(pl.multiple_of(rows_from + c, PART), PART)
                    terms = jnp.exp2(nt_dot(x_ref[span, :], now[0:BS, :]) * scale)
                    tiles[at, c : c + PART, :] = terms.astype(bf16)
                    row_part = acc_ref[span, :]
                    col_parts = []
                    for n in range(0, BS, 128):
                        piece = terms[:, n : n + 128]
                        row_part = row_part + piece * weight[:, n : n + 128]
                        col_parts.append(fold(piece * weight_ref[span, :]))
                    acc_ref[span, :] = row_part
                    sums = sums + jnp.concatenate(col_parts, axis=1)
                tile_copy(at, seat_of_ref[slot]).start()
                put_cols(col_ref, 0, stat_ref[0:1, 0:1], jnp.sum(sums, axis=0, keepdims=True))

            @pl.when(jnp.logical_not(fits))
            def _():
                block = pl.ds(pl.multiple_of(rows_from, BS), BS)
                shifted_rows(x_ref.at[block, :], now, beta, part_ref)
                out = pltpu.make_async_copy(part_ref, slow_ref.at[slot], sems.at[2])
                out.start()
                shifted_cols(x_ref.at[block, :], now, alpha_ref.at[block, :], col_ref, 0)
                out.wait()

        @pl.when(b == BPD - 1)
        def _():
            cols_ref[base + y] = logs(col_ref[0, 0:1, :], col_ref[0, 1:2, :])

        return carry

    lax.fori_loop(0, BPD * count, body, 0)
    for n in range(2):

        @pl.when(tile_count[0] > n)
        def _():
            tile_copy(n, 0).wait()

    if last:
        for n in range(PEERS):
            group_outs[n // GROUP][n % GROUP] = outgoing(cols_ref, peers_ref[n])


def outgoing(cols_ref, index):
    return jnp.where(index < 0, lowest, cols_ref[jnp.maximum(index, 0)])


def sweep(common, y_list, base, carried, peers):
    first, last = carried is None, peers is not None
    count = BPD if first else len(y_list)
    in_specs = [SMEM, SMEM] + [VMEM] * 4
    operands = list(common)
    aliases = {}
    if not first:
        in_specs += [VMEM, SMEM, HBM, HBM]
        operands += list(carried)
        aliases = {8: 3, 9: 4}
    if last:
        in_specs.append(SMEM)
        operands.append(peers)
    in_specs += [ANY] * len(y_list)
    operands += y_list
    out_specs = [VMEM, VMEM, SMEM, HBM, HBM]
    out_shape = [
        jax.ShapeDtypeStruct((LOCAL, 128), f32),
        jax.ShapeDtypeStruct((YBLOCKS, 1, BS), f32),
        jax.ShapeDtypeStruct((SLOTS,), f32),
        pltpu.HBM((MOST, BS, BS), bf16),
        pltpu.HBM((SLOTS, BS, 128), f32),
    ]
    if last:
        out_specs += [VMEM] * 2
        out_shape += [jax.ShapeDtypeStruct((GROUP, 1, BS), f32)] * 2
    return pl.pallas_call(
        functools.partial(sweep_kernel, base=base, count=count, first=first, last=last),
        in_specs=in_specs,
        out_specs=out_specs,
        out_shape=out_shape,
        scratch_shapes=[
            pltpu.VMEM((2, ROWS, DIM), bf16),
            pltpu.SemaphoreType.DMA((3,)),
            pltpu.VMEM((1, 8, BS), f32),
            pltpu.VMEM((LOCAL, 128), f32),
            pltpu.VMEM((BS, 128), f32),
            pltpu.VMEM((8, 128), f32),
            pltpu.VMEM((2, BS, BS), bf16),
            pltpu.SemaphoreType.DMA((2,)),
            pltpu.SMEM((1,), i32),
        ],
        input_output_aliases=aliases,
        compiler_params=params(20),
        name=f"sweep_{base}",
    )(*operands)


def load_pair(slot, x_ref, y_refs, x_buf, y_buf, sems):
    rows = pl.ds(pl.multiple_of((slot % BPD) * BS, BS), BS)
    fetch = pltpu.make_async_copy(x_ref.at[rows, :], x_buf, sems.at[0])
    fetch.start()
    fetch.wait()
    for n in range(YBLOCKS):

        @pl.when(slot // BPD == n)
        def _():
            source = y_refs[0].at[n] if n < BPD else y_refs[n - BPD + 1]
            fetch = pltpu.make_async_copy(source, y_buf, sems.at[1])
            fetch.start()
            fetch.wait()


def next_potential(now, half, total, log_count):
    return 0.5 * (now + half + entropy_weight * (log_count - log_two * total))


def fetch_terms(kept_ref, terms_ref, sems, live):
    def term_copy(n):
        return pltpu.make_async_copy(kept_ref.at[n], terms_ref.at[n], sems.at[n])

    for n in range(MOST):

        @pl.when(n < live)
        def _():
            term_copy(n).start()

    return term_copy


def columns_kernel(list_ref, live_ref, use_ref, left_ref, *refs, log_count, accs):
    acc_refs = refs[:accs]
    x_rows_ref, y_rows_ref, kept_ref, slow_ref, x_ref = refs[accs : accs + 5]
    y_refs = refs[accs + 5 : accs + 6 + FAR]
    next_ref, out_ref, col_ref, weight_ref, state_ref, part_ref, x_buf, y_buf, sems, terms_ref, term_sems = refs[accs + 6 + FAR :]
    term_copy = fetch_terms(kept_ref, terms_ref, term_sems, live_ref[0])
    clear_cols(col_ref)
    total = lane_sums(acc_refs)
    state_ref[0:1, :] = jnp.where(total > 0.0, high_of(own_beta(y_rows_ref)), lowest)
    state_ref[1:2, :] = total
    for n in range(SLOTS):

        @pl.when((use_ref[n] > 0) & (left_ref[n] < 0.0))
        def _():
            fetch = pltpu.make_async_copy(slow_ref.at[n], part_ref, sems.at[0])
            fetch.start()
            fetch.wait()
            add_part(part_ref, state_ref, n % BPD)

    half = x_rows_ref[1:2, :]
    f_next = next_potential(x_rows_ref[0:1, :], half, logs(state_ref[0:1, :], state_ref[1:2, :]), log_count)
    next_ref[0:1, :] = f_next
    next_ref[1:2, :] = half
    next_ref[2:8, :] = jnp.zeros((6, LOCAL), f32)
    alpha = (f_next - half) * scale
    state_ref[2:3, :] = alpha
    top = high_of(alpha)
    weight_ref[...] = down(jnp.exp2(alpha - top))
    reach = (top - low_of(alpha))[0, 0]

    def body(step, carry):
        slot = list_ref[step]
        y, b = slot // BPD, slot % BPD
        fits = reach <= left_ref[slot]
        term_copy(step).wait()

        @pl.when(fits)
        def _():
            sums = jnp.zeros((8, BS), f32)
            for c in range(0, BS, 64):
                weight = weight_ref[pl.ds(pl.multiple_of(b * BS + c, 64), 64), :]
                parts = [fold(terms_ref[step, c : c + 64, n : n + 128].astype(f32) * weight) for n in range(0, BS, 128)]
                sums = sums + jnp.concatenate(parts, axis=1)
            put_cols(col_ref, y, top, jnp.sum(sums, axis=0, keepdims=True))

        @pl.when(jnp.logical_not(fits))
        def _():
            load_pair(slot, x_ref, y_refs, x_buf, y_buf, sems)
            for c in range(0, BS, 128):
                row = state_ref[2:3, pl.ds(pl.multiple_of(b * BS + c, 128), 128)]
                part_ref[c : c + 128, :] = jnp.broadcast_to(row, (128, 128)).T
            shifted_cols(x_buf, y_buf, part_ref, col_ref, y)

        return carry

    lax.fori_loop(0, live_ref[0], body, 0)
    for n in range(YBLOCKS):
        out_ref[n] = logs(col_ref[n, 0:1, :], col_ref[n, 1:2, :])


def gathered(j, own_ref, came, who_ref):
    terms = [own_ref[j]] + [jnp.where(who_ref[n] == j, came(n), lowest) for n in range(PEERS)]
    top = terms[0]
    for term in terms[1:]:
        top = jnp.maximum(top, term)
    total = jnp.exp2(terms[0] - top)
    for term in terms[1:]:
        total = total + jnp.exp2(term - top)
    return top + jnp.log2(total)


def home_kernel(who_ref, peers_ref, even_in, odd_in, first_ref, second_ref, y_rows_ref, even_out, odd_out, g_ref, *, log_count):
    came = lambda n: (even_in, odd_in)[n // GROUP][n % GROUP]
    betas = []
    for j in range(BPD):
        span = slice(j * BS, (j + 1) * BS)
        half = y_rows_ref[1:2, span]
        g_next = next_potential(y_rows_ref[0:1, span], half, gathered(j, first_ref, came, who_ref), log_count)
        g_ref[0:1, span] = g_next
        betas.append((g_next - half) * scale)
        g_ref[1:2, span] = betas[j]
    g_ref[2:8, :] = jnp.zeros((6, LOCAL), f32)
    for n in range(PEERS):
        out = (even_out, odd_out)[n // GROUP]
        out[n % GROUP, 0:1, :] = jnp.where(who_ref[n] == 1, betas[1], betas[0])
        out[n % GROUP, 1:2, :] = outgoing(second_ref, peers_ref[n])


def home(who, peers, rows_in, first, second, y_rows, log_count):
    return pl.pallas_call(
        functools.partial(home_kernel, log_count=log_count),
        in_specs=[SMEM, SMEM] + [VMEM] * 5,
        out_specs=[VMEM] * 3,
        out_shape=[jax.ShapeDtypeStruct((GROUP, 2, BS), f32)] * 2 + [jax.ShapeDtypeStruct((8, LOCAL), f32)],
        compiler_params=params(16),
        name="home",
    )(who, peers, *rows_in, first, second, y_rows)


def rows_kernel(list_ref, live_ref, use_ref, left_ref, from_ref, who_ref, *refs, log_count):
    even_in, odd_in, g_ref, second_ref, y_rows_ref, x_rows_ref, kept_ref, slow_ref, x_ref = refs[:9]
    y_refs = refs[9 : 10 + FAR]
    f_ref, g_out_ref, acc_ref, beta_ref, weight_ref, state_ref, part_ref, x_buf, y_buf, sems, terms_ref, term_sems = refs[10 + FAR :]
    term_copy = fetch_terms(kept_ref, terms_ref, term_sems, live_ref[0])
    shift = high_of(g_ref[1:2, :])
    acc_ref[...] = jnp.zeros((LOCAL, 128), f32)
    state_ref[0:1, :] = jnp.full((1, LOCAL), lowest, f32)
    state_ref[1:2, :] = jnp.zeros((1, LOCAL), f32)
    for n in range(BPD):
        beta_ref[n] = g_ref[1:2, n * BS : (n + 1) * BS]
    for n in range(BPD, YBLOCKS):
        source = from_ref[n]
        at = source % GROUP
        beta_ref[n] = jnp.where(source < GROUP, even_in[at, 0:1, :], odd_in[at, 0:1, :])
    weight_ref[...] = jnp.exp2(beta_ref[...] - shift)

    def body(step, carry):
        slot = list_ref[step]
        y, b = slot // BPD, slot % BPD
        beta = beta_ref[y]
        reach = jnp.maximum(high_of(beta) - shift, shift - low_of(beta))
        fits = reach[0, 0] <= left_ref[slot]
        term_copy(step).wait()

        @pl.when(fits)
        def _():
            weight = weight_ref[y]
            for c in range(0, BS, 64):
                span = pl.ds(pl.multiple_of(b * BS + c, 64), 64)
                part = acc_ref[span, :]
                for n in range(0, BS, 128):
                    part = part + terms_ref[step, c : c + 64, n : n + 128].astype(f32) * weight[:, n : n + 128]
                acc_ref[span, :] = part

        @pl.when(jnp.logical_not(fits))
        def _():
            load_pair(slot, x_ref, y_refs, x_buf, y_buf, sems)
            shifted_rows(x_buf, y_buf, beta, part_ref)
            add_part(part_ref, state_ref, b)

        return carry

    lax.fori_loop(0, live_ref[0], body, 0)
    total = lane_sums([acc_ref])
    top = jnp.where(total > 0.0, shift, lowest)
    top, total = merge(top, total, state_ref[0:1, :], state_ref[1:2, :])
    f_ref[...] = next_potential(x_rows_ref[0:1, :], x_rows_ref[1:2, :], logs(top, total), log_count)
    came = lambda n: (even_in, odd_in)[n // GROUP][n % GROUP, 1:2, :]
    total = jnp.concatenate([gathered(j, second_ref, came, who_ref) for j in range(BPD)], axis=1)
    g_next = next_potential(g_ref[0:1, :], y_rows_ref[1:2, :], total, log_count)
    g_out_ref[...] = moved_exact(g_next, y_rows_ref[2:3, :].astype(i32))


def slots_call(kernel, smem, front, kept, slow, x_blocks, y_list, outs, scratch, name):
    return pl.pallas_call(
        kernel,
        in_specs=[SMEM] * len(smem) + [VMEM] * len(front) + [HBM, HBM, ANY] + [ANY] * len(y_list),
        out_specs=[VMEM] * len(outs),
        scratch_shapes=scratch
        + [
            pltpu.VMEM((BS, 128), f32),
            pltpu.VMEM((BS, DIM), bf16),
            pltpu.VMEM((ROWS, DIM), bf16),
            pltpu.SemaphoreType.DMA((2,)),
            pltpu.VMEM((MOST, BS, BS), bf16),
            pltpu.SemaphoreType.DMA((MOST,)),
        ],
        out_shape=outs,
        compiler_params=params(44),
        name=name,
    )(*smem, *front, kept, slow, x_blocks, *y_list)


def seat_tables():
    half = GROUP // 2
    offsets = np.zeros((GROUP, PEERS), np.int32)
    source = np.zeros((GROUP, YBLOCKS), np.int32)
    for seat in range(GROUP):
        odd_seat = (seat + half) % GROUP
        for other in range(GROUP):
            if other != seat and abs(other - seat) <= REACH:
                offsets[seat, other] = other - seat
            off = other - odd_seat
            if off != 0 and abs(off) <= REACH and not 0 <= seat + off < GROUP:
                offsets[seat, GROUP + other] = off
        for k, off in enumerate(OFFSETS):
            source[seat, BPD + k] = list(offsets[seat]).index(off)
    index = np.full((GROUP, PEERS), -1, np.int32)
    for k, off in enumerate(OFFSETS):
        index[offsets == off] = BPD + k
    return offsets, index, source


def exchanged(even_rows, odd_rows, devices):
    even = [list(range(GROUP * k, GROUP * (k + 1))) for k in range(devices // GROUP)]
    odd = [[(d + GROUP // 2) % devices for d in group] for group in even]
    swap = lambda rows, groups: lax.all_to_all(
        rows, "blk", split_axis=0, concat_axis=0, tiled=True, axis_index_groups=groups
    )
    return swap(even_rows, even), swap(odd_rows, odd)


def on_device(x_points, y_points, x_start, y_start, x_order, y_order, partners, counts):
    devices = lax.axis_size("blk")
    me = lax.axis_index("blk").astype(i32)
    log_count = math.log(LOCAL * devices)
    here = me[None]
    line = lambda v: v.reshape(1, LOCAL)

    y_sent, x_pos = pack_y(
        here,
        partners,
        counts,
        line(y_order),
        line(y_start.astype(f32)),
        line(x_order),
        line(x_start.astype(f32)),
        y_points,
        devices,
    )
    y_came = lax.all_to_all(y_sent, "blk", split_axis=0, concat_axis=0, tiled=True)
    x_sent = pack_x(x_pos, x_points)
    x_came = lax.all_to_all(x_sent, "blk", split_axis=0, concat_axis=0, tiled=True)

    y_came, x_sent = lax.optimization_barrier((y_came, x_sent))
    y_rows, table, y_own, *y_sends = unpack_y(here, y_came, devices)
    y_far = []
    for off, block in zip(OFFSETS, y_sends):
        pairs = [(i, i - off) for i in range(devices) if 0 <= i - off < devices]
        y_far.append(lax.ppermute(block, "blk", pairs))
    x_came, y_far[0], y_far[1] = lax.optimization_barrier((x_came, y_far[0], y_far[1]))
    x_blocks, alpha, x_rows = unpack_x(x_came, table)

    offsets = jnp.array(OFFSETS, i32)
    live = jnp.arange(partners.shape[1], dtype=i32)[None, :] < counts[:, None]
    away = jnp.where(live, partners // BPD - me, devices)
    local_use = [((away == 0) & (partners % BPD == j)).any(axis=1) for j in range(BPD)]
    far = away[None, :, :] == offsets[:, None, None]
    use = jnp.concatenate([jnp.stack(local_use), far.any(axis=2)]).astype(i32).reshape(SLOTS)
    number = jnp.minimum(jnp.maximum(jnp.cumsum(use) - 1, 0), MOST - 1)
    count = jnp.minimum(jnp.sum(use), MOST)
    step = jnp.minimum(jnp.arange(MOST, dtype=i32), count - 1)
    at = (number[None, :] == step[:, None]) & (use[None, :] > 0)
    slots = jnp.sum(jnp.where(at, jnp.arange(SLOTS, dtype=i32)[None, :], 0), axis=1)
    lists = [slots, count[None]]

    peer_offsets, peer_index, peer_source = seat_tables()
    row = lambda t: lax.dynamic_slice(jnp.asarray(t), (me % GROUP, 0), (1, t.shape[1]))[0]
    peers, source, off = row(peer_index), row(peer_source), row(peer_offsets)
    peer = me + off
    wants = (table[:, 3 * (LOCAL // devices)] > 0.5).astype(i32)
    valid = (off != 0) & (peer >= 0) & (peer < devices)
    who = jnp.where(valid, wants[jnp.clip(peer, 0, devices - 1)], -1)

    common = (use, number, x_blocks, alpha, x_rows, y_rows)
    acc_0, *carried = sweep(common, [y_own], 0, None, None)
    acc_1, *carried = sweep(common, y_far[:2], 2, carried, None)
    acc_2, *carried = sweep(common, y_far[2:4], 4, carried, None)
    acc_3, cols_first, left, kept, slow, *rows_out = sweep(common, y_far[4:], 6, carried, peers)
    y_all = [y_own] + y_far

    rows_in = exchanged(*rows_out, devices)
    accs = [acc_0, acc_1, acc_2, acc_3]
    x_next, cols_second = slots_call(
        functools.partial(columns_kernel, log_count=log_count, accs=len(accs)),
        lists + [use, left],
        accs + [x_rows, y_rows],
        kept,
        slow,
        x_blocks,
        y_all,
        [jax.ShapeDtypeStruct((8, LOCAL), f32), jax.ShapeDtypeStruct((YBLOCKS, 1, BS), f32)],
        [pltpu.VMEM((YBLOCKS, 8, BS), f32), pltpu.VMEM((LOCAL, 128), f32), pltpu.VMEM((8, LOCAL), f32)],
        "columns",
    )
    *rows_out, g_one = home(who, peers, rows_in, cols_first, cols_second, y_rows, log_count)
    rows_in = exchanged(*rows_out, devices)
    f_two, g_two = slots_call(
        functools.partial(rows_kernel, log_count=log_count),
        lists + [use, left, source, who],
        [*rows_in, g_one, cols_second, y_rows, x_next],
        kept,
        slow,
        x_blocks,
        y_all,
        [jax.ShapeDtypeStruct((1, LOCAL), f32)] * 2,
        [
            pltpu.VMEM((LOCAL, 128), f32),
            pltpu.VMEM((YBLOCKS, 1, BS), f32),
            pltpu.VMEM((YBLOCKS, 1, BS), f32),
            pltpu.VMEM((8, LOCAL), f32),
        ],
        "rows",
    )
    return f_two.reshape(LOCAL), g_two.reshape(LOCAL)


def solution(mesh):
    placed_as = (
        P("blk", None),
        P("blk", None),
        P("blk"),
        P("blk"),
        P("blk"),
        P("blk"),
        P("blk", None),
        P("blk"),
    )
    return jax.shard_map(
        on_device, mesh=mesh, in_specs=placed_as, out_specs=(P("blk"), P("blk")), check_vma=False
    )
```

```python
import functools
import math

import jax
import jax.numpy as jnp
import numpy as np
from jax import lax
from jax.experimental import pallas as pl
from jax.experimental.pallas import tpu as pltpu
from jax.sharding import PartitionSpec as P

DIM = 512
BS = 1024
BPD = 2
REACH = 3
LOCAL = BPD * BS
EXTRA = 128
WIDE = 2 * DIM + EXTRA
TAIL = 16
ROWS = BS + TAIL
CHUNK = 512
PART = 256
OFFSETS = (-1, 1, -2, 2, -3, 3)
FAR = len(OFFSETS)
YBLOCKS = BPD + FAR
SLOTS = BPD * YBLOCKS
MOST = 12
GROUP = 8
PEERS = 2 * GROUP
X_LANES = EXTRA // 2

entropy_weight = 0.05
scale = math.log2(math.e) / entropy_weight
log_two = math.log(2.0)
lowest = -1e30
exponent_room = 112.0
mebi = 1024 * 1024

f32 = jnp.float32
bf16 = jnp.bfloat16
i32 = jnp.int32

SMEM = pl.BlockSpec(memory_space=pltpu.SMEM)
ANY = pl.BlockSpec(memory_space=pl.ANY)
VMEM = pl.BlockSpec(memory_space=pltpu.VMEM)
HBM = pl.BlockSpec(memory_space=pltpu.HBM)


def iota(shape, dim):
    return lax.broadcasted_iota(i32, shape, dim)


def dot(a, b):
    return jnp.dot(a, b, preferred_element_type=f32)


def nt_dot(a, b):
    return lax.dot_general(a, b, (((1,), (1,)), ((), ())), preferred_element_type=f32)


def ones_where(mask):
    return jnp.where(mask, 1.0, 0.0).astype(bf16)


def params():
    return pltpu.CompilerParams(vmem_limit_bytes=62 * mebi)


def whole(shape):
    return pl.BlockSpec(shape, lambda *t: (0,) * len(shape))


def laid_out(square):
    return jnp.concatenate([square[n : n + 1, :] for n in range(square.shape[0])], axis=1)


def down(row):
    parts = [jnp.broadcast_to(row[:, c : c + 128], (128, 128)).T for c in range(0, row.shape[1], 128)]
    return jnp.concatenate(parts, axis=0)


def moved(values, place):
    high = iota((16, LOCAL), 0) == lax.shift_right_logical(place, 7)
    low = ones_where(iota((128, LOCAL), 0) == jnp.bitwise_and(place, 127))
    stack = jnp.concatenate([jnp.where(high, v, 0.0) for v in values], axis=0).astype(bf16)
    out = nt_dot(stack, low)
    return [laid_out(out[16 * n : 16 * n + 16, :]) for n in range(len(values))]


def moved_exact(value, place):
    first = value.astype(bf16).astype(f32)
    second = (value - first).astype(bf16).astype(f32)
    parts = moved([first, second, value - first - second], place)
    return parts[0] + parts[1] + parts[2]


def before_matrix():
    return ones_where(iota((128, 128), 0) < iota((128, 128), 1))


def plan(order, start, devices, first_lane):
    share = LOCAL // devices
    target = lax.shift_right_logical(order, 11)
    hit = iota((devices, LOCAL), 0) == target
    hot = ones_where(hit)
    before = before_matrix()
    every = jnp.ones((128, 128), bf16)
    seen = jnp.zeros((devices, 128), f32)
    earlier = []
    for c in range(0, LOCAL, 128):
        piece = hot[:, c : c + 128]
        earlier.append(dot(piece, before) + seen)
        seen = seen + dot(piece, every)
    earlier = jnp.concatenate(earlier, axis=1)
    rank = jnp.sum(jnp.where(hit, earlier, 0.0), axis=0, keepdims=True).astype(i32)
    within = jnp.bitwise_and(order, LOCAL - 1)
    high = lax.shift_right_logical(within, 6).astype(f32)
    low = jnp.bitwise_and(within, 63).astype(f32)
    row = iota((EXTRA, LOCAL), 0) - first_lane
    field = row // share
    value = jnp.where(field == 0, high, jnp.where(field == 1, low, start))
    mine = (row >= 0) & (row < 3 * share) & (row % share == rank)
    return target * share + rank, nt_dot(hot, jnp.where(mine, value, 0.0).astype(bf16))


def pack_kernel(
    me_ref, partners_ref, counts_ref, y_order, x_order, starts, y_points, x_points, out_ref, pos_ref, table_ref, *, devices
):
    step = pl.program_id(0)
    share = LOCAL // devices

    @pl.when(step == 0)
    def _():
        y_pos, y_table = plan(y_order[...], starts[0:1, :], devices, 0)
        x_pos, x_table = plan(x_order[...], starts[1:2, :], devices, X_LANES)
        pos_ref[0:1, :] = y_pos
        pos_ref[1:2, :] = x_pos
        me = me_ref[0]
        need = [jnp.int32(0)] * FAR
        for b in range(BPD):
            for s in range(partners_ref.shape[1]):
                block = partners_ref[b, s]
                away = lax.shift_right_logical(block, 1) - me
                for k in range(FAR):
                    listed = (s < counts_ref[b]) & (away == OFFSETS[k])
                    need[k] = jnp.where(listed, jnp.bitwise_and(block, 1), need[k])
        table = y_table + x_table
        row, lane = iota(table.shape, 0), iota(table.shape, 1)
        for k in range(FAR):
            table = jnp.where((row == me + OFFSETS[k]) & (lane == 3 * share), need[k].astype(f32), table)
        table_ref[...] = table

    base = step * CHUNK
    for n, points in enumerate((y_points, x_points)):
        hot = ones_where(iota((CHUNK, LOCAL), 0) + base == pos_ref[n : n + 1, :])
        out_ref[:, n * DIM : (n + 1) * DIM] = dot(hot, points[...]).astype(bf16)
    some = CHUNK // share
    table = table_ref[pl.ds(pl.multiple_of(step * some, some), some), :]
    out_ref[:, 2 * DIM :] = jnp.broadcast_to(table[:, None, :], (some, share, EXTRA)).reshape(CHUNK, EXTRA).astype(bf16)


def pack(me, partners, counts, y_order, x_order, starts, y_points, x_points, devices):
    row = whole((1, LOCAL))
    return pl.pallas_call(
        functools.partial(pack_kernel, devices=devices),
        grid=(LOCAL // CHUNK,),
        in_specs=[SMEM, SMEM, SMEM, row, row, whole((2, LOCAL)), whole((LOCAL, DIM)), whole((LOCAL, DIM))],
        out_specs=pl.BlockSpec((CHUNK, WIDE), lambda t: (t, 0)),
        out_shape=pltpu.HBM((LOCAL, WIDE), bf16),
        scratch_shapes=[pltpu.VMEM((8, LOCAL), i32), pltpu.VMEM((devices, EXTRA), f32)],
        compiler_params=params(),
        name="pack",
    )(me, partners, counts, y_order, x_order, starts, y_points, x_points)


WINDOW = PART + 16
HELD = BS + WINDOW + 16


def arrived(table, base, with_low):
    share = 16
    row, lane = iota((EXTRA, EXTRA), 0), iota((EXTRA, EXTRA), 1)
    pick = jnp.where(row == base + lane % share, 64.0 if with_low else 1.0, 0.0)
    if with_low:
        pick = jnp.where(row == base + share + lane % share, 1.0, pick)
    values = dot(table, pick.astype(bf16))
    values = jnp.where(row % (EXTRA // share) == lane // share, values, 0.0)
    return jnp.sum(values.reshape(LOCAL // 128, EXTRA // share, 128), axis=1)


def unpack_y_kernel(me_ref, came_ref, rows_ref, table_ref, own_ref, *rest, devices):
    sends = rest[:FAR]
    held, sems, own_sem, points_buf, extra_buf, in_sems = rest[FAR:]
    share = LOCAL // devices
    me = me_ref[0]
    extra_in = pltpu.make_async_copy(came_ref.at[:, pl.ds(2 * DIM, EXTRA)], extra_buf, in_sems.at[0])
    points_in = pltpu.make_async_copy(came_ref.at[:, pl.ds(0, DIM)], points_buf, in_sems.at[1])
    extra_in.start()
    points_in.start()
    held[...] = jnp.zeros(held.shape, bf16)
    extra_in.wait()
    table = dot(ones_where(iota((devices, LOCAL), 1) == iota((devices, LOCAL), 0) * share), extra_buf[...])
    table_ref[...] = table
    place_square = arrived(table.astype(bf16), 0, True)
    place = laid_out(place_square)
    start = laid_out(arrived(table.astype(bf16), 2 * share, False))

    picks = []
    small_row, small_lane = iota((devices, EXTRA), 0), iota((devices, EXTRA), 1)
    for k in range(FAR):
        here = (small_row == me - OFFSETS[k]) & (small_lane == 3 * share)
        picks.append(jnp.sum(jnp.where(here, table, 0.0)) > 0.5)

    second = place >= float(BS)
    square = ones_where(place_square >= float(BS))
    totals = dot(square, jnp.ones((128, 128), bf16)).astype(bf16)
    earlier = dot(square, before_matrix()) + dot(ones_where(iota((16, 16), 1) < iota((16, 16), 0)), totals)
    ones_before = laid_out(earlier)
    dest = jnp.where(second, ones_before, iota((1, LOCAL), 1).astype(f32) - ones_before).astype(i32)
    seat = jnp.where(second, dest + BS, dest)
    position = place.astype(i32)
    start_row, high_row, low_row = moved(
        [start, lax.shift_right_logical(position, 6).astype(f32), jnp.bitwise_and(position, 63).astype(f32)], seat
    )
    rows_ref[0:1, :] = start_row
    rows_ref[2:3, :] = high_row * 64.0 + low_row
    rows_ref[3:8, :] = jnp.zeros((5, LOCAL), f32)
    sixteen, lane16 = iota((16, 128), 0), iota((16, 128), 1)
    points_in.wait()

    for j in range(BPD):
        here = jnp.where(second if j else jnp.logical_not(second), dest, -1)
        for c in range(LOCAL // PART):
            span = slice(c * PART, (c + 1) * PART)
            begin = jnp.sum(jnp.where((sixteen == c * PART // 128) & (lane16 == 0), earlier, 0.0)).astype(i32)
            if j == 0:
                begin = c * PART - begin
            begin = pl.multiple_of(lax.shift_left(lax.shift_right_logical(begin, 4), 4), 16)
            hot = ones_where(iota((WINDOW, PART), 0) + begin == here[:, span])
            part = dot(hot, points_buf[span, :]).astype(bf16)
            held[j, pl.ds(begin, WINDOW), :] = held[j, pl.ds(begin, WINDOW), :] + part
        half = []
        for c in range(0, BS, PART):
            points = held[j, c : c + PART, :].astype(f32)
            total = 0.5 * jnp.sum(points * points, axis=1, keepdims=True)
            half.append(jnp.broadcast_to(total, (PART, 128)).T[0:1, :])
        half = jnp.concatenate(half, axis=1)
        block = slice(j * BS, (j + 1) * BS)
        rows_ref[1:2, block] = half
        beta = start_row[:, block] - half
        first = beta.astype(bf16).astype(f32)
        next_part = (beta - first).astype(bf16).astype(f32)
        most = jnp.max(half, axis=1, keepdims=True) * 1.01
        sub = iota((TAIL, DIM), 0)
        tail = jnp.zeros((TAIL, DIM), f32) + most
        for n, piece in enumerate((first, next_part, beta - first - next_part)):
            tail = jnp.where(sub == 2 * n, piece[:, :DIM], tail)
            tail = jnp.where(sub == 2 * n + 1, piece[:, DIM:], tail)
        held[j, BS:ROWS, :] = tail.astype(bf16)
        done = held.at[j, pl.ds(0, ROWS), :]
        for k in range(FAR):
            wanted = picks[k] if j == 1 else jnp.logical_not(picks[k])

            @pl.when(wanted)
            def _():
                pltpu.make_async_copy(done, sends[k], sems.at[k]).start()

        pltpu.make_async_copy(done, own_ref.at[j], own_sem.at[j]).start()

    done = held.at[0, pl.ds(0, ROWS), :]
    for k in range(FAR):
        pltpu.make_async_copy(done, sends[k], sems.at[k]).wait()
    for j in range(BPD):
        pltpu.make_async_copy(done, own_ref.at[j], own_sem.at[j]).wait()


def unpack_y(me, came, devices):
    return pl.pallas_call(
        functools.partial(unpack_y_kernel, devices=devices),
        in_specs=[SMEM, ANY],
        out_specs=[VMEM, VMEM] + [HBM] * (1 + FAR),
        out_shape=[
            jax.ShapeDtypeStruct((8, LOCAL), f32),
            jax.ShapeDtypeStruct((devices, EXTRA), f32),
            pltpu.HBM((BPD, ROWS, DIM), bf16),
        ]
        + [pltpu.HBM((ROWS, DIM), bf16)] * FAR,
        scratch_shapes=[
            pltpu.VMEM((BPD, HELD, DIM), bf16),
            pltpu.SemaphoreType.DMA((FAR,)),
            pltpu.SemaphoreType.DMA((BPD,)),
            pltpu.VMEM((LOCAL, DIM), bf16),
            pltpu.VMEM((LOCAL, EXTRA), bf16),
            pltpu.SemaphoreType.DMA((2,)),
        ],
        compiler_params=params(),
        name="unpack_y",
    )(me, came)


def unpack_x_kernel(came_ref, table_ref, points_ref, alpha_ref, rows_ref, place_ref, start_ref):
    step = pl.program_id(0)

    @pl.when(step == 0)
    def _():
        table = table_ref[...].astype(bf16)
        place = laid_out(arrived(table, X_LANES, True)).astype(i32)
        place_ref[...] = place
        start_ref[...] = moved([laid_out(arrived(table, X_LANES + 32, False))], place)[0]

    base = step * CHUNK
    hot = ones_where(iota((CHUNK, LOCAL), 0) + base == place_ref[...])
    points = dot(hot, came_ref[...])
    points_ref[...] = points.astype(bf16)
    half = jnp.broadcast_to(0.5 * jnp.sum(points * points, axis=1, keepdims=True), (CHUNK, 128))
    start = start_ref[:, pl.ds(pl.multiple_of(base, CHUNK), CHUNK)]
    alpha_ref[...] = (down(start) - half) * scale
    rows_ref[0:1, :] = start
    rows_ref[1:8, :] = jnp.concatenate([half[c : c + 128, :].T[0:7, :] for c in range(0, CHUNK, 128)], axis=1)


def unpack_x(came, table):
    return pl.pallas_call(
        unpack_x_kernel,
        grid=(LOCAL // CHUNK,),
        in_specs=[pl.BlockSpec((LOCAL, DIM), lambda t: (0, 1)), whole((EXTRA, EXTRA))],
        out_specs=[
            pl.BlockSpec((CHUNK, DIM), lambda t: (t, 0)),
            pl.BlockSpec((CHUNK, 128), lambda t: (t, 0)),
            pl.BlockSpec((8, CHUNK), lambda t: (0, t)),
        ],
        out_shape=[
            pltpu.HBM((LOCAL, DIM), bf16),
            pltpu.HBM((LOCAL, 128), f32),
            jax.ShapeDtypeStruct((8, LOCAL), f32),
        ],
        scratch_shapes=[pltpu.VMEM((1, LOCAL), i32), pltpu.VMEM((1, LOCAL), f32)],
        compiler_params=params(),
        name="unpack_x",
    )(came, table)


def merge(top, total, other_top, other_total):
    new = jnp.maximum(top, other_top)
    return new, total * jnp.exp2(top - new) + other_total * jnp.exp2(other_top - new)


def logs(top, total):
    return jnp.where(total > 0.0, top + jnp.log2(total), lowest)


def high_of(row):
    return jnp.max(row, axis=1, keepdims=True)


def low_of(row):
    return jnp.min(row, axis=1, keepdims=True)


def put_cols(col_ref, y, part_top, part_total):
    top, total = merge(col_ref[y, 0:1, :], col_ref[y, 1:2, :], part_top, part_total)
    col_ref[y, 0:1, :] = top
    col_ref[y, 1:2, :] = total


def clear_cols(col_ref):
    col_ref[:, 0:1, :] = jnp.full((col_ref.shape[0], 1, BS), lowest, f32)
    col_ref[:, 1:2, :] = jnp.zeros((col_ref.shape[0], 1, BS), f32)


def shifted_rows(x_ref, y_ref, beta, part_ref):
    def body(c, carry):
        span = pl.ds(pl.multiple_of(c * PART, PART), PART)
        terms = nt_dot(x_ref[span, :], y_ref[0:BS, :]) * scale + beta
        top = jnp.max(terms, axis=1, keepdims=True)
        total = jnp.sum(jnp.exp2(terms - top), axis=1, keepdims=True)
        part_ref[span, :] = jnp.where(iota((PART, 128), 1) == 0, top, total)
        return carry

    lax.fori_loop(0, BS // PART, body, 0)


def shifted_cols(x_ref, y_ref, alpha_ref, col_ref, y):
    def body(c, carry):
        span = pl.ds(pl.multiple_of(c * PART, PART), PART)
        terms = nt_dot(x_ref[span, :], y_ref[0:BS, :]) * scale + alpha_ref[span, 0:1]
        top = jnp.max(terms, axis=0, keepdims=True)
        put_cols(col_ref, y, top, jnp.sum(jnp.exp2(terms - top), axis=0, keepdims=True))
        return carry

    lax.fori_loop(0, BS // PART, body, 0)


def add_part(part_ref, state_ref, b):
    for c in range(0, BS, 128):
        part = part_ref[c : c + 128, :].T
        span = pl.ds(pl.multiple_of(b * BS + c, 128), 128)
        top, total = merge(state_ref[0:1, span], state_ref[1:2, span], part[0:1, :], part[1:2, :])
        state_ref[0:1, span] = top
        state_ref[1:2, span] = total


def lane_sums(refs):
    out = []
    for c in range(0, LOCAL, 128):
        part = refs[0][c : c + 128, :]
        for ref in refs[1:]:
            part = part + ref[c : c + 128, :]
        out.append(jnp.sum(part.T, axis=0, keepdims=True))
    return jnp.concatenate(out, axis=1)


def fold(values):
    return jnp.sum(values.reshape(values.shape[0] // 8, 8, 128), axis=0)


def own_beta(y_rows_ref):
    return (y_rows_ref[0:1, :] - y_rows_ref[1:2, :]) * scale


def sweep_kernel(*refs, base, count, first, last):
    use_ref, seat_of_ref, x_ref, alpha_ref, x_rows_ref, y_rows_ref = refs[:6]
    refs = refs[6:]
    if not first:
        cols_in, left_in = refs[:2]
        refs = refs[4:]
    if last:
        peers_ref = refs[0]
        refs = refs[1:]
    y_refs = refs[:1] if first else refs[:count]
    refs = refs[len(y_refs) :]
    acc_ref, cols_ref, left_ref, kept_ref, slow_ref = refs[:5]
    refs = refs[5:]
    if last:
        group_outs = refs[:2]
        refs = refs[2:]
    y_buf, sems, col_ref, weight_ref, part_ref, stat_ref, tiles, tile_sems, tile_count = refs

    def copy(n):
        source = y_refs[0].at[n] if first else y_refs[n]
        return pltpu.make_async_copy(source, y_buf.at[n % 2], sems.at[n % 2])

    copy(0).start()
    tile_count[0] = 0
    acc_ref[...] = jnp.zeros((LOCAL, 128), f32)

    def tile_copy(at, seat):
        return pltpu.make_async_copy(tiles.at[at], kept_ref.at[seat], tile_sems.at[at])

    if first:
        for n in range(SLOTS):
            left_ref[n] = -1.0
    else:
        for n in range(SLOTS):
            left_ref[n] = left_in[n]
        cols_ref[...] = cols_in[...]
    alpha = (x_rows_ref[0:1, :] - x_rows_ref[1:2, :]) * scale
    alpha_top = high_of(alpha)
    weight_ref[...] = jnp.exp2(alpha_ref[...] - alpha_top)
    lane = iota((8, 128), 1)
    beta_top = high_of(own_beta(y_rows_ref))
    most = high_of(x_rows_ref[1:2, :]) * 1.01
    spread = alpha_top - low_of(alpha)
    stat_ref[...] = jnp.where(lane == 0, alpha_top, jnp.where(lane == 1, spread, jnp.where(lane == 2, most, beta_top)))

    def body(step, carry):
        y, b = step // BPD, step % BPD
        slot = base * BPD + step
        for n in range(count):

            @pl.when(step == BPD * n)
            def _():
                copy(n).wait()
                if n + 1 < count:
                    copy(n + 1).start()

        @pl.when(b == 0)
        def _():
            clear_cols(col_ref)

        now = y_buf.at[y % 2]
        rows_from = b * BS

        @pl.when(use_ref[slot] > 0)
        def _():
            tail = now[BS:ROWS, :].astype(f32)
            halves = [tail[n : n + 1, :] + tail[n + 2 : n + 3, :] + tail[n + 4 : n + 5, :] for n in range(2)]
            beta = jnp.concatenate(halves, axis=1) * scale
            shift = stat_ref[0:1, 3:4]
            left = exponent_room - 2.0 * scale * jnp.sqrt(tail[6:7, 0:1] * stat_ref[0:1, 2:3])
            reach = jnp.maximum(stat_ref[0:1, 1:2], jnp.maximum(high_of(beta) - shift, shift - low_of(beta)))
            fits = (left - reach)[0, 0] >= 0.0

            @pl.when(fits)
            def _():
                left_ref[slot] = left[0, 0]
                done = tile_count[0]
                tile_count[0] = done + 1
                at = done % 2

                @pl.when(done > 1)
                def _():
                    tile_copy(at, 0).wait()

                weight = jnp.exp2(beta - shift)
                sums = jnp.zeros((8, BS), f32)
                for c in range(0, BS, PART):
                    span = pl.ds(pl.multiple_of(rows_from + c, PART), PART)
                    terms = jnp.exp2(nt_dot(x_ref[span, :], now[0:BS, :]) * scale)
                    tiles[at, c : c + PART, :] = terms.astype(bf16)
                    row_part = acc_ref[span, :]
                    col_parts = []
                    for n in range(0, BS, 128):
                        piece = terms[:, n : n + 128]
                        row_part = row_part + piece * weight[:, n : n + 128]
                        col_parts.append(fold(piece * weight_ref[span, :]))
                    acc_ref[span, :] = row_part
                    sums = sums + jnp.concatenate(col_parts, axis=1)
                tile_copy(at, seat_of_ref[slot]).start()
                put_cols(col_ref, 0, stat_ref[0:1, 0:1], jnp.sum(sums, axis=0, keepdims=True))

            @pl.when(jnp.logical_not(fits))
            def _():
                block = pl.ds(pl.multiple_of(rows_from, BS), BS)
                shifted_rows(x_ref.at[block, :], now, beta, part_ref)
                out = pltpu.make_async_copy(part_ref, slow_ref.at[slot], sems.at[2])
                out.start()
                shifted_cols(x_ref.at[block, :], now, alpha_ref.at[block, :], col_ref, 0)
                out.wait()

        @pl.when(b == BPD - 1)
        def _():
            cols_ref[base + y] = logs(col_ref[0, 0:1, :], col_ref[0, 1:2, :])

        return carry

    lax.fori_loop(0, BPD * count, body, 0)
    for n in range(2):

        @pl.when(tile_count[0] > n)
        def _():
            tile_copy(n, 0).wait()

    if last:
        for n in range(PEERS):
            group_outs[n // GROUP][n % GROUP] = outgoing(cols_ref, peers_ref[n])


def outgoing(cols_ref, index):
    return jnp.where(index < 0, lowest, cols_ref[jnp.maximum(index, 0)])


def sweep(common, y_list, base, carried, peers):
    first, last = carried is None, peers is not None
    count = BPD if first else len(y_list)
    in_specs = [SMEM, SMEM] + [VMEM] * 4
    operands = list(common)
    aliases = {}
    if not first:
        in_specs += [VMEM, SMEM, HBM, HBM]
        operands += list(carried)
        aliases = {8: 3, 9: 4}
    if last:
        in_specs.append(SMEM)
        operands.append(peers)
    in_specs += [ANY] * len(y_list)
    operands += y_list
    out_specs = [VMEM, VMEM, SMEM, HBM, HBM]
    out_shape = [
        jax.ShapeDtypeStruct((LOCAL, 128), f32),
        jax.ShapeDtypeStruct((YBLOCKS, 1, BS), f32),
        jax.ShapeDtypeStruct((SLOTS,), f32),
        pltpu.HBM((MOST, BS, BS), bf16),
        pltpu.HBM((SLOTS, BS, 128), f32),
    ]
    if last:
        out_specs += [VMEM] * 2
        out_shape += [jax.ShapeDtypeStruct((GROUP, 1, BS), f32)] * 2
    return pl.pallas_call(
        functools.partial(sweep_kernel, base=base, count=count, first=first, last=last),
        in_specs=in_specs,
        out_specs=out_specs,
        out_shape=out_shape,
        scratch_shapes=[
            pltpu.VMEM((2, ROWS, DIM), bf16),
            pltpu.SemaphoreType.DMA((3,)),
            pltpu.VMEM((1, 8, BS), f32),
            pltpu.VMEM((LOCAL, 128), f32),
            pltpu.VMEM((BS, 128), f32),
            pltpu.VMEM((8, 128), f32),
            pltpu.VMEM((2, BS, BS), bf16),
            pltpu.SemaphoreType.DMA((2,)),
            pltpu.SMEM((1,), i32),
        ],
        input_output_aliases=aliases,
        compiler_params=params(),
        name=f"sweep_{base}",
    )(*operands)


def load_pair(slot, x_ref, y_refs, x_buf, y_buf, sems):
    rows = pl.ds(pl.multiple_of((slot % BPD) * BS, BS), BS)
    fetch = pltpu.make_async_copy(x_ref.at[rows, :], x_buf, sems.at[0])
    fetch.start()
    fetch.wait()
    for n in range(YBLOCKS):

        @pl.when(slot // BPD == n)
        def _():
            source = y_refs[0].at[n] if n < BPD else y_refs[n - BPD + 1]
            fetch = pltpu.make_async_copy(source, y_buf, sems.at[1])
            fetch.start()
            fetch.wait()


def next_potential(now, half, total, log_count):
    return 0.5 * (now + half + entropy_weight * (log_count - log_two * total))


def fetch_terms(kept_ref, terms_ref, sems, live):
    def term_copy(n):
        return pltpu.make_async_copy(kept_ref.at[n], terms_ref.at[n], sems.at[n])

    for n in range(MOST):

        @pl.when(n < live)
        def _():
            term_copy(n).start()

    return term_copy


def columns_kernel(list_ref, live_ref, use_ref, left_ref, *refs, log_count, accs):
    acc_refs = refs[:accs]
    x_rows_ref, y_rows_ref, kept_ref, slow_ref, x_ref = refs[accs : accs + 5]
    y_refs = refs[accs + 5 : accs + 6 + FAR]
    next_ref, out_ref, col_ref, weight_ref, state_ref, part_ref, x_buf, y_buf, sems, terms_ref, term_sems = refs[accs + 6 + FAR :]
    term_copy = fetch_terms(kept_ref, terms_ref, term_sems, live_ref[0])
    clear_cols(col_ref)
    total = lane_sums(acc_refs)
    state_ref[0:1, :] = jnp.where(total > 0.0, high_of(own_beta(y_rows_ref)), lowest)
    state_ref[1:2, :] = total
    for n in range(SLOTS):

        @pl.when((use_ref[n] > 0) & (left_ref[n] < 0.0))
        def _():
            fetch = pltpu.make_async_copy(slow_ref.at[n], part_ref, sems.at[0])
            fetch.start()
            fetch.wait()
            add_part(part_ref, state_ref, n % BPD)

    half = x_rows_ref[1:2, :]
    f_next = next_potential(x_rows_ref[0:1, :], half, logs(state_ref[0:1, :], state_ref[1:2, :]), log_count)
    next_ref[0:1, :] = f_next
    next_ref[1:2, :] = half
    next_ref[2:8, :] = jnp.zeros((6, LOCAL), f32)
    alpha = (f_next - half) * scale
    state_ref[2:3, :] = alpha
    top = high_of(alpha)
    weight_ref[...] = down(jnp.exp2(alpha - top))
    reach = (top - low_of(alpha))[0, 0]

    def body(step, carry):
        slot = list_ref[step]
        y, b = slot // BPD, slot % BPD
        fits = reach <= left_ref[slot]
        term_copy(step).wait()

        @pl.when(fits)
        def _():
            sums = jnp.zeros((8, BS), f32)
            for c in range(0, BS, 64):
                weight = weight_ref[pl.ds(pl.multiple_of(b * BS + c, 64), 64), :]
                parts = [fold(terms_ref[step, c : c + 64, n : n + 128].astype(f32) * weight) for n in range(0, BS, 128)]
                sums = sums + jnp.concatenate(parts, axis=1)
            put_cols(col_ref, y, top, jnp.sum(sums, axis=0, keepdims=True))

        @pl.when(jnp.logical_not(fits))
        def _():
            load_pair(slot, x_ref, y_refs, x_buf, y_buf, sems)
            for c in range(0, BS, 128):
                row = state_ref[2:3, pl.ds(pl.multiple_of(b * BS + c, 128), 128)]
                part_ref[c : c + 128, :] = jnp.broadcast_to(row, (128, 128)).T
            shifted_cols(x_buf, y_buf, part_ref, col_ref, y)

        return carry

    lax.fori_loop(0, live_ref[0], body, 0)
    for n in range(YBLOCKS):
        out_ref[n] = logs(col_ref[n, 0:1, :], col_ref[n, 1:2, :])


def gathered(j, own_ref, came, who_ref):
    terms = [own_ref[j]] + [jnp.where(who_ref[n] == j, came(n), lowest) for n in range(PEERS)]
    top = terms[0]
    for term in terms[1:]:
        top = jnp.maximum(top, term)
    total = jnp.exp2(terms[0] - top)
    for term in terms[1:]:
        total = total + jnp.exp2(term - top)
    return top + jnp.log2(total)


def home_kernel(who_ref, peers_ref, even_in, odd_in, first_ref, second_ref, y_rows_ref, even_out, odd_out, g_ref, *, log_count):
    came = lambda n: (even_in, odd_in)[n // GROUP][n % GROUP]
    betas = []
    for j in range(BPD):
        span = slice(j * BS, (j + 1) * BS)
        half = y_rows_ref[1:2, span]
        g_next = next_potential(y_rows_ref[0:1, span], half, gathered(j, first_ref, came, who_ref), log_count)
        g_ref[0:1, span] = g_next
        betas.append((g_next - half) * scale)
        g_ref[1:2, span] = betas[j]
    g_ref[2:8, :] = jnp.zeros((6, LOCAL), f32)
    for n in range(PEERS):
        out = (even_out, odd_out)[n // GROUP]
        out[n % GROUP, 0:1, :] = jnp.where(who_ref[n] == 1, betas[1], betas[0])
        out[n % GROUP, 1:2, :] = outgoing(second_ref, peers_ref[n])


def home(who, peers, rows_in, first, second, y_rows, log_count):
    return pl.pallas_call(
        functools.partial(home_kernel, log_count=log_count),
        in_specs=[SMEM, SMEM] + [VMEM] * 5,
        out_specs=[VMEM] * 3,
        out_shape=[jax.ShapeDtypeStruct((GROUP, 2, BS), f32)] * 2 + [jax.ShapeDtypeStruct((8, LOCAL), f32)],
        compiler_params=params(),
        name="home",
    )(who, peers, *rows_in, first, second, y_rows)


def rows_kernel(list_ref, live_ref, use_ref, left_ref, from_ref, who_ref, *refs, log_count):
    even_in, odd_in, g_ref, second_ref, y_rows_ref, x_rows_ref, kept_ref, slow_ref, x_ref = refs[:9]
    y_refs = refs[9 : 10 + FAR]
    f_ref, g_out_ref, acc_ref, beta_ref, weight_ref, state_ref, part_ref, x_buf, y_buf, sems, terms_ref, term_sems = refs[10 + FAR :]
    term_copy = fetch_terms(kept_ref, terms_ref, term_sems, live_ref[0])
    shift = high_of(g_ref[1:2, :])
    acc_ref[...] = jnp.zeros((LOCAL, 128), f32)
    state_ref[0:1, :] = jnp.full((1, LOCAL), lowest, f32)
    state_ref[1:2, :] = jnp.zeros((1, LOCAL), f32)
    for n in range(BPD):
        beta_ref[n] = g_ref[1:2, n * BS : (n + 1) * BS]
    for n in range(BPD, YBLOCKS):
        source = from_ref[n]
        at = source % GROUP
        beta_ref[n] = jnp.where(source < GROUP, even_in[at, 0:1, :], odd_in[at, 0:1, :])
    weight_ref[...] = jnp.exp2(beta_ref[...] - shift)

    def body(step, carry):
        slot = list_ref[step]
        y, b = slot // BPD, slot % BPD
        beta = beta_ref[y]
        reach = jnp.maximum(high_of(beta) - shift, shift - low_of(beta))
        fits = reach[0, 0] <= left_ref[slot]
        term_copy(step).wait()

        @pl.when(fits)
        def _():
            weight = weight_ref[y]
            for c in range(0, BS, 64):
                span = pl.ds(pl.multiple_of(b * BS + c, 64), 64)
                part = acc_ref[span, :]
                for n in range(0, BS, 128):
                    part = part + terms_ref[step, c : c + 64, n : n + 128].astype(f32) * weight[:, n : n + 128]
                acc_ref[span, :] = part

        @pl.when(jnp.logical_not(fits))
        def _():
            load_pair(slot, x_ref, y_refs, x_buf, y_buf, sems)
            shifted_rows(x_buf, y_buf, beta, part_ref)
            add_part(part_ref, state_ref, b)

        return carry

    lax.fori_loop(0, live_ref[0], body, 0)
    total = lane_sums([acc_ref])
    top = jnp.where(total > 0.0, shift, lowest)
    top, total = merge(top, total, state_ref[0:1, :], state_ref[1:2, :])
    f_ref[...] = next_potential(x_rows_ref[0:1, :], x_rows_ref[1:2, :], logs(top, total), log_count)
    came = lambda n: (even_in, odd_in)[n // GROUP][n % GROUP, 1:2, :]
    total = jnp.concatenate([gathered(j, second_ref, came, who_ref) for j in range(BPD)], axis=1)
    g_next = next_potential(g_ref[0:1, :], y_rows_ref[1:2, :], total, log_count)
    g_out_ref[...] = moved_exact(g_next, y_rows_ref[2:3, :].astype(i32))


def slots_call(kernel, smem, front, kept, slow, x_blocks, y_list, outs, scratch, name):
    return pl.pallas_call(
        kernel,
        in_specs=[SMEM] * len(smem) + [VMEM] * len(front) + [HBM, HBM, ANY] + [ANY] * len(y_list),
        out_specs=[VMEM] * len(outs),
        scratch_shapes=scratch
        + [
            pltpu.VMEM((BS, 128), f32),
            pltpu.VMEM((BS, DIM), bf16),
            pltpu.VMEM((ROWS, DIM), bf16),
            pltpu.SemaphoreType.DMA((2,)),
            pltpu.VMEM((MOST, BS, BS), bf16),
            pltpu.SemaphoreType.DMA((MOST,)),
        ],
        out_shape=outs,
        compiler_params=params(),
        name=name,
    )(*smem, *front, kept, slow, x_blocks, *y_list)


def seat_tables():
    half = GROUP // 2
    offsets = np.zeros((GROUP, PEERS), np.int32)
    source = np.zeros((GROUP, YBLOCKS), np.int32)
    for seat in range(GROUP):
        odd_seat = (seat + half) % GROUP
        for other in range(GROUP):
            if other != seat and abs(other - seat) <= REACH:
                offsets[seat, other] = other - seat
            off = other - odd_seat
            if off != 0 and abs(off) <= REACH and not 0 <= seat + off < GROUP:
                offsets[seat, GROUP + other] = off
        for k, off in enumerate(OFFSETS):
            source[seat, BPD + k] = list(offsets[seat]).index(off)
    index = np.full((GROUP, PEERS), -1, np.int32)
    for k, off in enumerate(OFFSETS):
        index[offsets == off] = BPD + k
    return offsets, index, source


def exchanged(even_rows, odd_rows, devices):
    even = [list(range(GROUP * k, GROUP * (k + 1))) for k in range(devices // GROUP)]
    odd = [[(d + GROUP // 2) % devices for d in group] for group in even]
    swap = lambda rows, groups: lax.all_to_all(
        rows, "blk", split_axis=0, concat_axis=0, tiled=True, axis_index_groups=groups
    )
    return swap(even_rows, even), swap(odd_rows, odd)


def on_device(x_points, y_points, x_start, y_start, x_order, y_order, partners, counts):
    devices = lax.axis_size("blk")
    me = lax.axis_index("blk").astype(i32)
    log_count = math.log(LOCAL * devices)
    here = me[None]
    line = lambda v: v.reshape(1, LOCAL)

    starts = jnp.stack([y_start, x_start]).astype(f32)
    sent = pack(here, partners, counts, line(y_order), line(x_order), starts, y_points, x_points, devices)
    came = lax.all_to_all(sent, "blk", split_axis=0, concat_axis=0, tiled=True)
    y_rows, table, y_own, *y_sends = unpack_y(here, came, devices)
    y_far = []
    for off, block in zip(OFFSETS, y_sends):
        pairs = [(i, i - off) for i in range(devices) if 0 <= i - off < devices]
        y_far.append(lax.ppermute(block, "blk", pairs))
    x_blocks, alpha, x_rows = unpack_x(came, table)

    offsets = jnp.array(OFFSETS, i32)
    live = jnp.arange(partners.shape[1], dtype=i32)[None, :] < counts[:, None]
    away = jnp.where(live, partners // BPD - me, devices)
    local_use = [((away == 0) & (partners % BPD == j)).any(axis=1) for j in range(BPD)]
    far = away[None, :, :] == offsets[:, None, None]
    use = jnp.concatenate([jnp.stack(local_use), far.any(axis=2)]).astype(i32).reshape(SLOTS)
    number = jnp.minimum(jnp.maximum(jnp.cumsum(use) - 1, 0), MOST - 1)
    count = jnp.minimum(jnp.sum(use), MOST)
    step = jnp.minimum(jnp.arange(MOST, dtype=i32), count - 1)
    at = (number[None, :] == step[:, None]) & (use[None, :] > 0)
    slots = jnp.sum(jnp.where(at, jnp.arange(SLOTS, dtype=i32)[None, :], 0), axis=1)
    lists = [slots, count[None]]

    peer_offsets, peer_index, peer_source = seat_tables()
    row = lambda t: lax.dynamic_slice(jnp.asarray(t), (me % GROUP, 0), (1, t.shape[1]))[0]
    peers, source, off = row(peer_index), row(peer_source), row(peer_offsets)
    peer = me + off
    wants = (table[:, 3 * (LOCAL // devices)] > 0.5).astype(i32)
    valid = (off != 0) & (peer >= 0) & (peer < devices)
    who = jnp.where(valid, wants[jnp.clip(peer, 0, devices - 1)], -1)

    common = (use, number, x_blocks, alpha, x_rows, y_rows)
    acc_0, *carried = sweep(common, [y_own], 0, None, None)
    acc_1, *carried = sweep(common, y_far[:2], 2, carried, None)
    acc_2, *carried = sweep(common, y_far[2:4], 4, carried, None)
    acc_3, cols_first, left, kept, slow, *rows_out = sweep(common, y_far[4:], 6, carried, peers)
    y_all = [y_own] + y_far

    rows_in = exchanged(*rows_out, devices)
    accs = [acc_0, acc_1, acc_2, acc_3]
    x_next, cols_second = slots_call(
        functools.partial(columns_kernel, log_count=log_count, accs=len(accs)),
        lists + [use, left],
        accs + [x_rows, y_rows],
        kept,
        slow,
        x_blocks,
        y_all,
        [jax.ShapeDtypeStruct((8, LOCAL), f32), jax.ShapeDtypeStruct((YBLOCKS, 1, BS), f32)],
        [pltpu.VMEM((YBLOCKS, 8, BS), f32), pltpu.VMEM((LOCAL, 128), f32), pltpu.VMEM((8, LOCAL), f32)],
        "columns",
    )
    *rows_out, g_one = home(who, peers, rows_in, cols_first, cols_second, y_rows, log_count)
    rows_in = exchanged(*rows_out, devices)
    f_two, g_two = slots_call(
        functools.partial(rows_kernel, log_count=log_count),
        lists + [use, left, source, who],
        [*rows_in, g_one, cols_second, y_rows, x_next],
        kept,
        slow,
        x_blocks,
        y_all,
        [jax.ShapeDtypeStruct((1, LOCAL), f32)] * 2,
        [
            pltpu.VMEM((LOCAL, 128), f32),
            pltpu.VMEM((YBLOCKS, 1, BS), f32),
            pltpu.VMEM((YBLOCKS, 1, BS), f32),
            pltpu.VMEM((8, LOCAL), f32),
        ],
        "rows",
    )
    return f_two.reshape(LOCAL), g_two.reshape(LOCAL)


def solution(mesh):
    placed_as = (
        P("blk", None),
        P("blk", None),
        P("blk"),
        P("blk"),
        P("blk"),
        P("blk"),
        P("blk", None),
        P("blk"),
    )
    return jax.shard_map(
        on_device, mesh=mesh, in_specs=placed_as, out_specs=(P("blk"), P("blk")), check_vma=False
    )
```

```python
import functools
import math

import jax
import jax.numpy as jnp
import numpy as np
from jax import lax
from jax.experimental import pallas as pl
from jax.experimental.pallas import tpu as pltpu
from jax.sharding import PartitionSpec as P

DIM = 512
BS = 1024
BPD = 2
REACH = 3
LOCAL = BPD * BS
EXTRA = 128
WIDE = 2 * DIM + EXTRA
TAIL = 16
ROWS = BS + TAIL
CHUNK = 512
PART = 256
ROUNDS = ((1, 2, -2, 3, -3, -1), (-1, 2, -2, -3, 3, 1), (1, -2, 2, 3, -3, -1), (-1, -2, 2, -3, 3, 1))
FAR = len(ROUNDS[0])
YBLOCKS = BPD + FAR
SLOTS = BPD * YBLOCKS
MOST = 12
GROUP = 8
PEERS = 2 * GROUP
X_LANES = EXTRA // 2

entropy_weight = 0.05
scale = math.log2(math.e) / entropy_weight
log_two = math.log(2.0)
lowest = -1e30
exponent_room = 112.0
mebi = 1024 * 1024

f32 = jnp.float32
bf16 = jnp.bfloat16
i32 = jnp.int32

SMEM = pl.BlockSpec(memory_space=pltpu.SMEM)
ANY = pl.BlockSpec(memory_space=pl.ANY)
VMEM = pl.BlockSpec(memory_space=pltpu.VMEM)
HBM = pl.BlockSpec(memory_space=pltpu.HBM)


def iota(shape, dim):
    return lax.broadcasted_iota(i32, shape, dim)


def dot(a, b):
    return jnp.dot(a, b, preferred_element_type=f32)


def nt_dot(a, b):
    return lax.dot_general(a, b, (((1,), (1,)), ((), ())), preferred_element_type=f32)


def ones_where(mask):
    return jnp.where(mask, 1.0, 0.0).astype(bf16)


def params():
    return pltpu.CompilerParams(vmem_limit_bytes=62 * mebi)


def whole(shape):
    return pl.BlockSpec(shape, lambda *t: (0,) * len(shape))


def laid_out(square):
    return jnp.concatenate([square[n : n + 1, :] for n in range(square.shape[0])], axis=1)


def down(row):
    parts = [jnp.broadcast_to(row[:, c : c + 128], (128, 128)).T for c in range(0, row.shape[1], 128)]
    return jnp.concatenate(parts, axis=0)


def moved(values, place):
    high = iota((16, LOCAL), 0) == lax.shift_right_logical(place, 7)
    low = ones_where(iota((128, LOCAL), 0) == jnp.bitwise_and(place, 127))
    stack = jnp.concatenate([jnp.where(high, v, 0.0) for v in values], axis=0).astype(bf16)
    out = nt_dot(stack, low)
    return [laid_out(out[16 * n : 16 * n + 16, :]) for n in range(len(values))]


def moved_exact(value, place):
    first = value.astype(bf16).astype(f32)
    second = (value - first).astype(bf16).astype(f32)
    parts = moved([first, second, value - first - second], place)
    return parts[0] + parts[1] + parts[2]


def before_matrix():
    return ones_where(iota((128, 128), 0) < iota((128, 128), 1))


def plan(order, start, devices, first_lane):
    share = LOCAL // devices
    target = lax.shift_right_logical(order, 11)
    hit = iota((devices, LOCAL), 0) == target
    hot = ones_where(hit)
    before = before_matrix()
    every = jnp.ones((128, 128), bf16)
    seen = jnp.zeros((devices, 128), f32)
    earlier = []
    for c in range(0, LOCAL, 128):
        piece = hot[:, c : c + 128]
        earlier.append(dot(piece, before) + seen)
        seen = seen + dot(piece, every)
    earlier = jnp.concatenate(earlier, axis=1)
    rank = jnp.sum(jnp.where(hit, earlier, 0.0), axis=0, keepdims=True).astype(i32)
    within = jnp.bitwise_and(order, LOCAL - 1)
    high = lax.shift_right_logical(within, 6).astype(f32)
    low = jnp.bitwise_and(within, 63).astype(f32)
    row = iota((EXTRA, LOCAL), 0) - first_lane
    field = row // share
    value = jnp.where(field == 0, high, jnp.where(field == 1, low, start))
    mine = (row >= 0) & (row < 3 * share) & (row % share == rank)
    return target * share + rank, nt_dot(hot, jnp.where(mine, value, 0.0).astype(bf16))


def partner_offsets(me):
    kind = jnp.bitwise_and(me, 3)
    out = []
    for k in range(FAR):
        value = jnp.int32(ROUNDS[0][k])
        for n in range(1, 4):
            value = jnp.where(kind == n, jnp.int32(ROUNDS[n][k]), value)
        out.append(value)
    return out


def pack_kernel(
    me_ref, partners_ref, counts_ref, y_order, x_order, y_start, x_start, y_points, x_points, out_ref, pos_ref, table_ref,
    *, devices
):
    step = pl.program_id(0)
    share = LOCAL // devices

    @pl.when(step == 0)
    def _():
        y_pos, y_table = plan(y_order[...], y_start[...].astype(f32).reshape(1, LOCAL), devices, 0)
        x_pos, x_table = plan(x_order[...], x_start[...].astype(f32).reshape(1, LOCAL), devices, X_LANES)
        pos_ref[0:1, :] = y_pos
        pos_ref[1:2, :] = x_pos
        me = me_ref[0]
        offsets = partner_offsets(me)
        need = [jnp.int32(0)] * FAR
        for b in range(BPD):
            for s in range(partners_ref.shape[1]):
                block = partners_ref[b, s]
                away = lax.shift_right_logical(block, 1) - me
                for k in range(FAR):
                    listed = (s < counts_ref[b]) & (away == offsets[k])
                    need[k] = jnp.where(listed, jnp.bitwise_and(block, 1), need[k])
        table = y_table + x_table
        row, lane = iota(table.shape, 0), iota(table.shape, 1)
        for k in range(FAR):
            table = jnp.where((row == me + offsets[k]) & (lane == 3 * share), need[k].astype(f32), table)
        table_ref[...] = table

    base = step * CHUNK
    for n, points in enumerate((y_points, x_points)):
        hot = ones_where(iota((CHUNK, LOCAL), 0) + base == pos_ref[n : n + 1, :])
        out_ref[:, n * DIM : (n + 1) * DIM] = dot(hot, points[...]).astype(bf16)
    some = CHUNK // share
    table = table_ref[pl.ds(pl.multiple_of(step * some, some), some), :]
    out_ref[:, 2 * DIM :] = jnp.broadcast_to(table[:, None, :], (some, share, EXTRA)).reshape(CHUNK, EXTRA).astype(bf16)


def pack(me, partners, counts, y_order, x_order, y_start, x_start, y_points, x_points, devices):
    row = whole((1, LOCAL))
    return pl.pallas_call(
        functools.partial(pack_kernel, devices=devices),
        grid=(LOCAL // CHUNK,),
        in_specs=[SMEM, SMEM, SMEM, row, row, whole((LOCAL,)), whole((LOCAL,)), whole((LOCAL, DIM)), whole((LOCAL, DIM))],
        out_specs=pl.BlockSpec((CHUNK, WIDE), lambda t: (t, 0)),
        out_shape=pltpu.HBM((LOCAL, WIDE), bf16),
        scratch_shapes=[pltpu.VMEM((8, LOCAL), i32), pltpu.VMEM((devices, EXTRA), f32)],
        compiler_params=params(),
        name="pack",
    )(me, partners, counts, y_order, x_order, y_start, x_start, y_points, x_points)


WINDOW = PART + 16
HELD = BS + WINDOW + 16


def arrived(table, base, with_low):
    share = 16
    row, lane = iota((EXTRA, EXTRA), 0), iota((EXTRA, EXTRA), 1)
    pick = jnp.where(row == base + lane % share, 64.0 if with_low else 1.0, 0.0)
    if with_low:
        pick = jnp.where(row == base + share + lane % share, 1.0, pick)
    values = dot(table, pick.astype(bf16))
    values = jnp.where(row % (EXTRA // share) == lane // share, values, 0.0)
    return jnp.sum(values.reshape(LOCAL // 128, EXTRA // share, 128), axis=1)


def unpack_y_kernel(me_ref, came_ref, rows_ref, table_ref, own_ref, *rest, devices):
    sends = rest[:FAR]
    held, sems, own_sem, points_buf, extra_buf, in_sems = rest[FAR:]
    share = LOCAL // devices
    me = me_ref[0]
    extra_in = pltpu.make_async_copy(came_ref.at[:, pl.ds(2 * DIM, EXTRA)], extra_buf, in_sems.at[0])
    points_in = pltpu.make_async_copy(came_ref.at[:, pl.ds(0, DIM)], points_buf, in_sems.at[1])
    extra_in.start()
    points_in.start()
    held[...] = jnp.zeros(held.shape, bf16)
    extra_in.wait()
    table = dot(ones_where(iota((devices, LOCAL), 1) == iota((devices, LOCAL), 0) * share), extra_buf[...])
    table_ref[...] = table
    place_square = arrived(table.astype(bf16), 0, True)
    place = laid_out(place_square)
    start = laid_out(arrived(table.astype(bf16), 2 * share, False))

    picks = []
    offsets = partner_offsets(me)
    small_row, small_lane = iota((devices, EXTRA), 0), iota((devices, EXTRA), 1)
    for k in range(FAR):
        here = (small_row == me + offsets[k]) & (small_lane == 3 * share)
        picks.append(jnp.sum(jnp.where(here, table, 0.0)) > 0.5)

    second = place >= float(BS)
    square = ones_where(place_square >= float(BS))
    totals = dot(square, jnp.ones((128, 128), bf16)).astype(bf16)
    earlier = dot(square, before_matrix()) + dot(ones_where(iota((16, 16), 1) < iota((16, 16), 0)), totals)
    ones_before = laid_out(earlier)
    dest = jnp.where(second, ones_before, iota((1, LOCAL), 1).astype(f32) - ones_before).astype(i32)
    seat = jnp.where(second, dest + BS, dest)
    position = place.astype(i32)
    start_row, high_row, low_row = moved(
        [start, lax.shift_right_logical(position, 6).astype(f32), jnp.bitwise_and(position, 63).astype(f32)], seat
    )
    rows_ref[0:1, :] = start_row
    rows_ref[2:3, :] = high_row * 64.0 + low_row
    rows_ref[3:8, :] = jnp.zeros((5, LOCAL), f32)
    sixteen, lane16 = iota((16, 128), 0), iota((16, 128), 1)
    points_in.wait()

    for j in range(BPD):
        here = jnp.where(second if j else jnp.logical_not(second), dest, -1)
        for c in range(LOCAL // PART):
            span = slice(c * PART, (c + 1) * PART)
            begin = jnp.sum(jnp.where((sixteen == c * PART // 128) & (lane16 == 0), earlier, 0.0)).astype(i32)
            if j == 0:
                begin = c * PART - begin
            begin = pl.multiple_of(lax.shift_left(lax.shift_right_logical(begin, 4), 4), 16)
            hot = ones_where(iota((WINDOW, PART), 0) + begin == here[:, span])
            part = dot(hot, points_buf[span, :]).astype(bf16)
            held[j, pl.ds(begin, WINDOW), :] = held[j, pl.ds(begin, WINDOW), :] + part
        half = []
        for c in range(0, BS, PART):
            points = held[j, c : c + PART, :].astype(f32)
            total = 0.5 * jnp.sum(points * points, axis=1, keepdims=True)
            half.append(jnp.broadcast_to(total, (PART, 128)).T[0:1, :])
        half = jnp.concatenate(half, axis=1)
        block = slice(j * BS, (j + 1) * BS)
        rows_ref[1:2, block] = half
        beta = start_row[:, block] - half
        first = beta.astype(bf16).astype(f32)
        next_part = (beta - first).astype(bf16).astype(f32)
        most = jnp.max(half, axis=1, keepdims=True) * 1.01
        sub = iota((TAIL, DIM), 0)
        tail = jnp.zeros((TAIL, DIM), f32) + most
        for n, piece in enumerate((first, next_part, beta - first - next_part)):
            tail = jnp.where(sub == 2 * n, piece[:, :DIM], tail)
            tail = jnp.where(sub == 2 * n + 1, piece[:, DIM:], tail)
        held[j, BS:ROWS, :] = tail.astype(bf16)
        done = held.at[j, pl.ds(0, ROWS), :]
        for k in range(FAR):
            wanted = picks[k] if j == 1 else jnp.logical_not(picks[k])

            @pl.when(wanted)
            def _():
                pltpu.make_async_copy(done, sends[k], sems.at[k]).start()

        pltpu.make_async_copy(done, own_ref.at[j], own_sem.at[j]).start()

    done = held.at[0, pl.ds(0, ROWS), :]
    for k in range(FAR):
        pltpu.make_async_copy(done, sends[k], sems.at[k]).wait()
    for j in range(BPD):
        pltpu.make_async_copy(done, own_ref.at[j], own_sem.at[j]).wait()


def unpack_y(me, came, devices):
    return pl.pallas_call(
        functools.partial(unpack_y_kernel, devices=devices),
        in_specs=[SMEM, ANY],
        out_specs=[VMEM, VMEM] + [HBM] * (1 + FAR),
        out_shape=[
            jax.ShapeDtypeStruct((8, LOCAL), f32),
            jax.ShapeDtypeStruct((devices, EXTRA), f32),
            pltpu.HBM((BPD, ROWS, DIM), bf16),
        ]
        + [pltpu.HBM((ROWS, DIM), bf16)] * FAR,
        scratch_shapes=[
            pltpu.VMEM((BPD, HELD, DIM), bf16),
            pltpu.SemaphoreType.DMA((FAR,)),
            pltpu.SemaphoreType.DMA((BPD,)),
            pltpu.VMEM((LOCAL, DIM), bf16),
            pltpu.VMEM((LOCAL, EXTRA), bf16),
            pltpu.SemaphoreType.DMA((2,)),
        ],
        compiler_params=params(),
        name="unpack_y",
    )(me, came)


def unpack_x_kernel(came_ref, table_ref, points_ref, alpha_ref, rows_ref, place_ref, start_ref):
    step = pl.program_id(0)

    @pl.when(step == 0)
    def _():
        table = table_ref[...].astype(bf16)
        place = laid_out(arrived(table, X_LANES, True)).astype(i32)
        place_ref[...] = place
        start_ref[...] = moved([laid_out(arrived(table, X_LANES + 32, False))], place)[0]

    base = step * CHUNK
    hot = ones_where(iota((CHUNK, LOCAL), 0) + base == place_ref[...])
    points = dot(hot, came_ref[...])
    points_ref[...] = points.astype(bf16)
    half = jnp.broadcast_to(0.5 * jnp.sum(points * points, axis=1, keepdims=True), (CHUNK, 128))
    start = start_ref[:, pl.ds(pl.multiple_of(base, CHUNK), CHUNK)]
    alpha_ref[...] = (down(start) - half) * scale
    rows_ref[0:1, :] = start
    rows_ref[1:8, :] = jnp.concatenate([half[c : c + 128, :].T[0:7, :] for c in range(0, CHUNK, 128)], axis=1)


def unpack_x(came, table):
    return pl.pallas_call(
        unpack_x_kernel,
        grid=(LOCAL // CHUNK,),
        in_specs=[pl.BlockSpec((LOCAL, DIM), lambda t: (0, 1)), whole((EXTRA, EXTRA))],
        out_specs=[
            pl.BlockSpec((CHUNK, DIM), lambda t: (t, 0)),
            pl.BlockSpec((CHUNK, 128), lambda t: (t, 0)),
            pl.BlockSpec((8, CHUNK), lambda t: (0, t)),
        ],
        out_shape=[
            pltpu.HBM((LOCAL, DIM), bf16),
            pltpu.HBM((LOCAL, 128), f32),
            jax.ShapeDtypeStruct((8, LOCAL), f32),
        ],
        scratch_shapes=[pltpu.VMEM((1, LOCAL), i32), pltpu.VMEM((1, LOCAL), f32)],
        compiler_params=params(),
        name="unpack_x",
    )(came, table)


def merge(top, total, other_top, other_total):
    new = jnp.maximum(top, other_top)
    return new, total * jnp.exp2(top - new) + other_total * jnp.exp2(other_top - new)


def logs(top, total):
    return jnp.where(total > 0.0, top + jnp.log2(total), lowest)


def high_of(row):
    return jnp.max(row, axis=1, keepdims=True)


def low_of(row):
    return jnp.min(row, axis=1, keepdims=True)


def put_cols(col_ref, y, part_top, part_total):
    top, total = merge(col_ref[y, 0:1, :], col_ref[y, 1:2, :], part_top, part_total)
    col_ref[y, 0:1, :] = top
    col_ref[y, 1:2, :] = total


def clear_cols(col_ref):
    col_ref[:, 0:1, :] = jnp.full((col_ref.shape[0], 1, BS), lowest, f32)
    col_ref[:, 1:2, :] = jnp.zeros((col_ref.shape[0], 1, BS), f32)


def shifted_rows(x_ref, y_ref, beta, part_ref):
    def body(c, carry):
        span = pl.ds(pl.multiple_of(c * PART, PART), PART)
        terms = nt_dot(x_ref[span, :], y_ref[0:BS, :]) * scale + beta
        top = jnp.max(terms, axis=1, keepdims=True)
        total = jnp.sum(jnp.exp2(terms - top), axis=1, keepdims=True)
        part_ref[span, :] = jnp.where(iota((PART, 128), 1) == 0, top, total)
        return carry

    lax.fori_loop(0, BS // PART, body, 0)


def shifted_cols(x_ref, y_ref, alpha_ref, col_ref, y):
    def body(c, carry):
        span = pl.ds(pl.multiple_of(c * PART, PART), PART)
        terms = nt_dot(x_ref[span, :], y_ref[0:BS, :]) * scale + alpha_ref[span, 0:1]
        top = jnp.max(terms, axis=0, keepdims=True)
        put_cols(col_ref, y, top, jnp.sum(jnp.exp2(terms - top), axis=0, keepdims=True))
        return carry

    lax.fori_loop(0, BS // PART, body, 0)


def add_part(part_ref, state_ref, b):
    for c in range(0, BS, 128):
        part = part_ref[c : c + 128, :].T
        span = pl.ds(pl.multiple_of(b * BS + c, 128), 128)
        top, total = merge(state_ref[0:1, span], state_ref[1:2, span], part[0:1, :], part[1:2, :])
        state_ref[0:1, span] = top
        state_ref[1:2, span] = total


def lane_sums(refs):
    out = []
    for c in range(0, LOCAL, 128):
        part = refs[0][c : c + 128, :]
        for ref in refs[1:]:
            part = part + ref[c : c + 128, :]
        out.append(jnp.sum(part.T, axis=0, keepdims=True))
    return jnp.concatenate(out, axis=1)


def fold(values):
    return jnp.sum(values.reshape(values.shape[0] // 8, 8, 128), axis=0)


def own_beta(y_rows_ref):
    return (y_rows_ref[0:1, :] - y_rows_ref[1:2, :]) * scale


def sweep_kernel(*refs, base, count, first, last):
    use_ref, seat_of_ref, x_ref, alpha_ref, x_rows_ref, y_rows_ref = refs[:6]
    refs = refs[6:]
    if not first:
        cols_in, left_in = refs[:2]
        refs = refs[4:]
    if last:
        peers_ref = refs[0]
        refs = refs[1:]
    y_refs = refs[:1] if first else refs[:count]
    refs = refs[len(y_refs) :]
    acc_ref, cols_ref, left_ref, kept_ref, slow_ref = refs[:5]
    refs = refs[5:]
    if last:
        group_outs = refs[:2]
        refs = refs[2:]
    y_buf, sems, col_ref, weight_ref, part_ref, stat_ref, tiles, tile_sems, tile_count = refs

    def copy(n):
        source = y_refs[0].at[n] if first else y_refs[n]
        return pltpu.make_async_copy(source, y_buf.at[n % 2], sems.at[n % 2])

    copy(0).start()
    tile_count[0] = 0
    acc_ref[...] = jnp.zeros((LOCAL, 128), f32)

    def tile_copy(at, seat):
        return pltpu.make_async_copy(tiles.at[at], kept_ref.at[seat], tile_sems.at[at])

    if first:
        for n in range(SLOTS):
            left_ref[n] = -1.0
    else:
        for n in range(SLOTS):
            left_ref[n] = left_in[n]
        cols_ref[...] = cols_in[...]
    alpha = (x_rows_ref[0:1, :] - x_rows_ref[1:2, :]) * scale
    alpha_top = high_of(alpha)
    weight_ref[...] = jnp.exp2(alpha_ref[...] - alpha_top)
    lane = iota((8, 128), 1)
    beta_top = high_of(own_beta(y_rows_ref))
    most = high_of(x_rows_ref[1:2, :]) * 1.01
    spread = alpha_top - low_of(alpha)
    stat_ref[...] = jnp.where(lane == 0, alpha_top, jnp.where(lane == 1, spread, jnp.where(lane == 2, most, beta_top)))

    def body(step, carry):
        y, b = step // BPD, step % BPD
        slot = base * BPD + step
        for n in range(count):

            @pl.when(step == BPD * n)
            def _():
                copy(n).wait()
                if n + 1 < count:
                    copy(n + 1).start()

        @pl.when(b == 0)
        def _():
            clear_cols(col_ref)

        now = y_buf.at[y % 2]
        rows_from = b * BS

        @pl.when(use_ref[slot] > 0)
        def _():
            tail = now[BS:ROWS, :].astype(f32)
            halves = [tail[n : n + 1, :] + tail[n + 2 : n + 3, :] + tail[n + 4 : n + 5, :] for n in range(2)]
            beta = jnp.concatenate(halves, axis=1) * scale
            shift = stat_ref[0:1, 3:4]
            left = exponent_room - 2.0 * scale * jnp.sqrt(tail[6:7, 0:1] * stat_ref[0:1, 2:3])
            reach = jnp.maximum(stat_ref[0:1, 1:2], jnp.maximum(high_of(beta) - shift, shift - low_of(beta)))
            fits = (left - reach)[0, 0] >= 0.0

            @pl.when(fits)
            def _():
                left_ref[slot] = left[0, 0]
                done = tile_count[0]
                tile_count[0] = done + 1
                at = done % 2

                @pl.when(done > 1)
                def _():
                    tile_copy(at, 0).wait()

                weight = jnp.exp2(beta - shift)
                sums = jnp.zeros((8, BS), f32)
                for c in range(0, BS, PART):
                    span = pl.ds(pl.multiple_of(rows_from + c, PART), PART)
                    terms = jnp.exp2(nt_dot(x_ref[span, :], now[0:BS, :]) * scale)
                    tiles[at, c : c + PART, :] = terms.astype(bf16)
                    row_part = acc_ref[span, :]
                    col_parts = []
                    for n in range(0, BS, 128):
                        piece = terms[:, n : n + 128]
                        row_part = row_part + piece * weight[:, n : n + 128]
                        col_parts.append(fold(piece * weight_ref[span, :]))
                    acc_ref[span, :] = row_part
                    sums = sums + jnp.concatenate(col_parts, axis=1)
                tile_copy(at, seat_of_ref[slot]).start()
                put_cols(col_ref, 0, stat_ref[0:1, 0:1], jnp.sum(sums, axis=0, keepdims=True))

            @pl.when(jnp.logical_not(fits))
            def _():
                block = pl.ds(pl.multiple_of(rows_from, BS), BS)
                shifted_rows(x_ref.at[block, :], now, beta, part_ref)
                out = pltpu.make_async_copy(part_ref, slow_ref.at[slot], sems.at[2])
                out.start()
                shifted_cols(x_ref.at[block, :], now, alpha_ref.at[block, :], col_ref, 0)
                out.wait()

        @pl.when(b == BPD - 1)
        def _():
            cols_ref[base + y] = logs(col_ref[0, 0:1, :], col_ref[0, 1:2, :])

        return carry

    lax.fori_loop(0, BPD * count, body, 0)
    for n in range(2):

        @pl.when(tile_count[0] > n)
        def _():
            tile_copy(n, 0).wait()

    if last:
        for n in range(PEERS):
            group_outs[n // GROUP][n % GROUP] = outgoing(cols_ref, peers_ref[n])


def outgoing(cols_ref, index):
    return jnp.where(index < 0, lowest, cols_ref[jnp.maximum(index, 0)])


def sweep(common, y_list, base, carried, peers):
    first, last = carried is None, peers is not None
    count = BPD if first else len(y_list)
    in_specs = [SMEM, SMEM] + [VMEM] * 4
    operands = list(common)
    aliases = {}
    if not first:
        in_specs += [VMEM, SMEM, HBM, HBM]
        operands += list(carried)
        aliases = {8: 3, 9: 4}
    if last:
        in_specs.append(SMEM)
        operands.append(peers)
    in_specs += [ANY] * len(y_list)
    operands += y_list
    out_specs = [VMEM, VMEM, SMEM, HBM, HBM]
    out_shape = [
        jax.ShapeDtypeStruct((LOCAL, 128), f32),
        jax.ShapeDtypeStruct((YBLOCKS, 1, BS), f32),
        jax.ShapeDtypeStruct((SLOTS,), f32),
        pltpu.HBM((MOST, BS, BS), bf16),
        pltpu.HBM((SLOTS, BS, 128), f32),
    ]
    if last:
        out_specs += [VMEM] * 2
        out_shape += [jax.ShapeDtypeStruct((GROUP, 1, BS), f32)] * 2
    return pl.pallas_call(
        functools.partial(sweep_kernel, base=base, count=count, first=first, last=last),
        in_specs=in_specs,
        out_specs=out_specs,
        out_shape=out_shape,
        scratch_shapes=[
            pltpu.VMEM((2, ROWS, DIM), bf16),
            pltpu.SemaphoreType.DMA((3,)),
            pltpu.VMEM((1, 8, BS), f32),
            pltpu.VMEM((LOCAL, 128), f32),
            pltpu.VMEM((BS, 128), f32),
            pltpu.VMEM((8, 128), f32),
            pltpu.VMEM((2, BS, BS), bf16),
            pltpu.SemaphoreType.DMA((2,)),
            pltpu.SMEM((1,), i32),
        ],
        input_output_aliases=aliases,
        compiler_params=params(),
        name=f"sweep_{base}",
    )(*operands)


def load_pair(slot, x_ref, y_refs, x_buf, y_buf, sems):
    rows = pl.ds(pl.multiple_of((slot % BPD) * BS, BS), BS)
    fetch = pltpu.make_async_copy(x_ref.at[rows, :], x_buf, sems.at[0])
    fetch.start()
    fetch.wait()
    for n in range(YBLOCKS):

        @pl.when(slot // BPD == n)
        def _():
            source = y_refs[0].at[n] if n < BPD else y_refs[n - BPD + 1]
            fetch = pltpu.make_async_copy(source, y_buf, sems.at[1])
            fetch.start()
            fetch.wait()


def next_potential(now, half, total, log_count):
    return 0.5 * (now + half + entropy_weight * (log_count - log_two * total))


def fetch_terms(kept_ref, terms_ref, sems, live):
    def term_copy(n):
        return pltpu.make_async_copy(kept_ref.at[n], terms_ref.at[n], sems.at[n])

    for n in range(MOST):

        @pl.when(n < live)
        def _():
            term_copy(n).start()

    return term_copy


def columns_kernel(list_ref, live_ref, use_ref, left_ref, *refs, log_count, accs):
    acc_refs = refs[:accs]
    x_rows_ref, y_rows_ref, kept_ref, slow_ref, x_ref = refs[accs : accs + 5]
    y_refs = refs[accs + 5 : accs + 6 + FAR]
    next_ref, out_ref, col_ref, weight_ref, state_ref, part_ref, x_buf, y_buf, sems, terms_ref, term_sems = refs[accs + 6 + FAR :]
    term_copy = fetch_terms(kept_ref, terms_ref, term_sems, live_ref[0])
    clear_cols(col_ref)
    total = lane_sums(acc_refs)
    state_ref[0:1, :] = jnp.where(total > 0.0, high_of(own_beta(y_rows_ref)), lowest)
    state_ref[1:2, :] = total
    for n in range(SLOTS):

        @pl.when((use_ref[n] > 0) & (left_ref[n] < 0.0))
        def _():
            fetch = pltpu.make_async_copy(slow_ref.at[n], part_ref, sems.at[0])
            fetch.start()
            fetch.wait()
            add_part(part_ref, state_ref, n % BPD)

    half = x_rows_ref[1:2, :]
    f_next = next_potential(x_rows_ref[0:1, :], half, logs(state_ref[0:1, :], state_ref[1:2, :]), log_count)
    next_ref[0:1, :] = f_next
    next_ref[1:2, :] = half
    next_ref[2:8, :] = jnp.zeros((6, LOCAL), f32)
    alpha = (f_next - half) * scale
    state_ref[2:3, :] = alpha
    top = high_of(alpha)
    weight_ref[...] = down(jnp.exp2(alpha - top))
    reach = (top - low_of(alpha))[0, 0]

    def body(step, carry):
        slot = list_ref[step]
        y, b = slot // BPD, slot % BPD
        fits = reach <= left_ref[slot]
        term_copy(step).wait()

        @pl.when(fits)
        def _():
            sums = jnp.zeros((8, BS), f32)
            for c in range(0, BS, 64):
                weight = weight_ref[pl.ds(pl.multiple_of(b * BS + c, 64), 64), :]
                parts = [fold(terms_ref[step, c : c + 64, n : n + 128].astype(f32) * weight) for n in range(0, BS, 128)]
                sums = sums + jnp.concatenate(parts, axis=1)
            put_cols(col_ref, y, top, jnp.sum(sums, axis=0, keepdims=True))

        @pl.when(jnp.logical_not(fits))
        def _():
            load_pair(slot, x_ref, y_refs, x_buf, y_buf, sems)
            for c in range(0, BS, 128):
                row = state_ref[2:3, pl.ds(pl.multiple_of(b * BS + c, 128), 128)]
                part_ref[c : c + 128, :] = jnp.broadcast_to(row, (128, 128)).T
            shifted_cols(x_buf, y_buf, part_ref, col_ref, y)

        return carry

    lax.fori_loop(0, live_ref[0], body, 0)
    for n in range(YBLOCKS):
        out_ref[n] = logs(col_ref[n, 0:1, :], col_ref[n, 1:2, :])


def gathered(j, own_ref, came, who_ref):
    terms = [own_ref[j]] + [jnp.where(who_ref[n] == j, came(n), lowest) for n in range(PEERS)]
    top = terms[0]
    for term in terms[1:]:
        top = jnp.maximum(top, term)
    total = jnp.exp2(terms[0] - top)
    for term in terms[1:]:
        total = total + jnp.exp2(term - top)
    return top + jnp.log2(total)


def home_kernel(who_ref, peers_ref, even_in, odd_in, first_ref, second_ref, y_rows_ref, even_out, odd_out, g_ref, *, log_count):
    came = lambda n: (even_in, odd_in)[n // GROUP][n % GROUP]
    betas = []
    for j in range(BPD):
        span = slice(j * BS, (j + 1) * BS)
        half = y_rows_ref[1:2, span]
        g_next = next_potential(y_rows_ref[0:1, span], half, gathered(j, first_ref, came, who_ref), log_count)
        g_ref[0:1, span] = g_next
        betas.append((g_next - half) * scale)
        g_ref[1:2, span] = betas[j]
    g_ref[2:8, :] = jnp.zeros((6, LOCAL), f32)
    for n in range(PEERS):
        out = (even_out, odd_out)[n // GROUP]
        out[n % GROUP, 0:1, :] = jnp.where(who_ref[n] == 1, betas[1], betas[0])
        out[n % GROUP, 1:2, :] = outgoing(second_ref, peers_ref[n])


def home(who, peers, rows_in, first, second, y_rows, log_count):
    return pl.pallas_call(
        functools.partial(home_kernel, log_count=log_count),
        in_specs=[SMEM, SMEM] + [VMEM] * 5,
        out_specs=[VMEM] * 3,
        out_shape=[jax.ShapeDtypeStruct((GROUP, 2, BS), f32)] * 2 + [jax.ShapeDtypeStruct((8, LOCAL), f32)],
        compiler_params=params(),
        name="home",
    )(who, peers, *rows_in, first, second, y_rows)


def rows_kernel(list_ref, live_ref, use_ref, left_ref, from_ref, who_ref, *refs, log_count):
    even_in, odd_in, g_ref, second_ref, y_rows_ref, x_rows_ref, kept_ref, slow_ref, x_ref = refs[:9]
    y_refs = refs[9 : 10 + FAR]
    f_ref, g_out_ref, acc_ref, beta_ref, weight_ref, state_ref, part_ref, x_buf, y_buf, sems, terms_ref, term_sems = refs[10 + FAR :]
    term_copy = fetch_terms(kept_ref, terms_ref, term_sems, live_ref[0])
    shift = high_of(g_ref[1:2, :])
    acc_ref[...] = jnp.zeros((LOCAL, 128), f32)
    state_ref[0:1, :] = jnp.full((1, LOCAL), lowest, f32)
    state_ref[1:2, :] = jnp.zeros((1, LOCAL), f32)
    for n in range(BPD):
        beta_ref[n] = g_ref[1:2, n * BS : (n + 1) * BS]
    for n in range(BPD, YBLOCKS):
        source = from_ref[n]
        at = source % GROUP
        beta_ref[n] = jnp.where(source < GROUP, even_in[at, 0:1, :], odd_in[at, 0:1, :])
    weight_ref[...] = jnp.exp2(beta_ref[...] - shift)

    def body(step, carry):
        slot = list_ref[step]
        y, b = slot // BPD, slot % BPD
        beta = beta_ref[y]
        reach = jnp.maximum(high_of(beta) - shift, shift - low_of(beta))
        fits = reach[0, 0] <= left_ref[slot]
        term_copy(step).wait()

        @pl.when(fits)
        def _():
            weight = weight_ref[y]
            for c in range(0, BS, 64):
                span = pl.ds(pl.multiple_of(b * BS + c, 64), 64)
                part = acc_ref[span, :]
                for n in range(0, BS, 128):
                    part = part + terms_ref[step, c : c + 64, n : n + 128].astype(f32) * weight[:, n : n + 128]
                acc_ref[span, :] = part

        @pl.when(jnp.logical_not(fits))
        def _():
            load_pair(slot, x_ref, y_refs, x_buf, y_buf, sems)
            shifted_rows(x_buf, y_buf, beta, part_ref)
            add_part(part_ref, state_ref, b)

        return carry

    lax.fori_loop(0, live_ref[0], body, 0)
    total = lane_sums([acc_ref])
    top = jnp.where(total > 0.0, shift, lowest)
    top, total = merge(top, total, state_ref[0:1, :], state_ref[1:2, :])
    f_ref[...] = next_potential(x_rows_ref[0:1, :], x_rows_ref[1:2, :], logs(top, total), log_count)
    came = lambda n: (even_in, odd_in)[n // GROUP][n % GROUP, 1:2, :]
    total = jnp.concatenate([gathered(j, second_ref, came, who_ref) for j in range(BPD)], axis=1)
    g_next = next_potential(g_ref[0:1, :], y_rows_ref[1:2, :], total, log_count)
    g_out_ref[...] = moved_exact(g_next, y_rows_ref[2:3, :].astype(i32))


def slots_call(kernel, smem, front, kept, slow, x_blocks, y_list, outs, scratch, name):
    return pl.pallas_call(
        kernel,
        in_specs=[SMEM] * len(smem) + [VMEM] * len(front) + [HBM, HBM, ANY] + [ANY] * len(y_list),
        out_specs=[VMEM] * len(outs),
        scratch_shapes=scratch
        + [
            pltpu.VMEM((BS, 128), f32),
            pltpu.VMEM((BS, DIM), bf16),
            pltpu.VMEM((ROWS, DIM), bf16),
            pltpu.SemaphoreType.DMA((2,)),
            pltpu.VMEM((MOST, BS, BS), bf16),
            pltpu.SemaphoreType.DMA((MOST,)),
        ],
        out_shape=outs,
        compiler_params=params(),
        name=name,
    )(*smem, *front, kept, slow, x_blocks, *y_list)


def seat_tables():
    half = GROUP // 2
    offsets = np.zeros((GROUP, PEERS), np.int32)
    source = np.zeros((GROUP, YBLOCKS), np.int32)
    for seat in range(GROUP):
        odd_seat = (seat + half) % GROUP
        for other in range(GROUP):
            if other != seat and abs(other - seat) <= REACH:
                offsets[seat, other] = other - seat
            off = other - odd_seat
            if off != 0 and abs(off) <= REACH and not 0 <= seat + off < GROUP:
                offsets[seat, GROUP + other] = off
        for k, off in enumerate(ROUNDS[seat % 4]):
            source[seat, BPD + k] = list(offsets[seat]).index(off)
    index = np.full((GROUP, PEERS), -1, np.int32)
    for seat in range(GROUP):
        for k, off in enumerate(ROUNDS[seat % 4]):
            index[seat, offsets[seat] == off] = BPD + k
    return offsets, index, source


def swap(rows, devices, shift):
    groups = [[(GROUP * k + j + shift) % devices for j in range(GROUP)] for k in range(devices // GROUP)]
    return lax.all_to_all(rows, "blk", split_axis=0, concat_axis=0, tiled=True, axis_index_groups=groups)


def on_device(x_points, y_points, x_start, y_start, x_order, y_order, partners, counts):
    devices = lax.axis_size("blk")
    me = lax.axis_index("blk").astype(i32)
    log_count = math.log(LOCAL * devices)
    here = me[None]
    line = lambda v: v.reshape(1, LOCAL)

    sent = pack(here, partners, counts, line(y_order), line(x_order), y_start, x_start, y_points, x_points, devices)
    came = lax.all_to_all(sent, "blk", split_axis=0, concat_axis=0, tiled=True)
    y_rows, table, y_own, *y_sends = unpack_y(here, came, devices)
    y_far = []
    for k, block in enumerate(y_sends):
        pairs = [(i, i + ROUNDS[i % 4][k]) for i in range(devices) if 0 <= i + ROUNDS[i % 4][k] < devices]
        y_far.append(lax.ppermute(block, "blk", pairs))
    x_blocks, alpha, x_rows = unpack_x(came, table)

    offsets = lax.dynamic_slice(jnp.array(ROUNDS, i32), (me % 4, 0), (1, FAR))[0]
    live = jnp.arange(partners.shape[1], dtype=i32)[None, :] < counts[:, None]
    away = jnp.where(live, partners // BPD - me, devices)
    local_use = [((away == 0) & (partners % BPD == j)).any(axis=1) for j in range(BPD)]
    far = away[None, :, :] == offsets[:, None, None]
    use = jnp.concatenate([jnp.stack(local_use), far.any(axis=2)]).astype(i32).reshape(SLOTS)
    number = jnp.minimum(jnp.maximum(jnp.cumsum(use) - 1, 0), MOST - 1)
    count = jnp.minimum(jnp.sum(use), MOST)
    step = jnp.minimum(jnp.arange(MOST, dtype=i32), count - 1)
    at = (number[None, :] == step[:, None]) & (use[None, :] > 0)
    slots = jnp.sum(jnp.where(at, jnp.arange(SLOTS, dtype=i32)[None, :], 0), axis=1)
    lists = [slots, count[None]]

    peer_offsets, peer_index, peer_source = seat_tables()
    row = lambda t: lax.dynamic_slice(jnp.asarray(t), (me % GROUP, 0), (1, t.shape[1]))[0]
    peers, source, off = row(peer_index), row(peer_source), row(peer_offsets)
    peer = me + off
    wants = (table[:, 3 * (LOCAL // devices)] > 0.5).astype(i32)
    valid = (off != 0) & (peer >= 0) & (peer < devices)
    who = jnp.where(valid, wants[jnp.clip(peer, 0, devices - 1)], -1)

    common = (use, number, x_blocks, alpha, x_rows, y_rows)
    acc_0, *carried = sweep(common, [y_own], 0, None, None)
    acc_1, *carried = sweep(common, y_far[:2], 2, carried, None)
    acc_2, *carried = sweep(common, y_far[2:4], 4, carried, None)
    acc_3, cols_first, left, kept, slow, *rows_out = sweep(common, y_far[4:], 6, carried, peers)
    y_all = [y_own] + y_far

    even_out, odd_out = rows_out
    even_in = swap(even_out, devices, 0)
    accs = [acc_0, acc_1, acc_2, acc_3]
    x_next, cols_second = slots_call(
        functools.partial(columns_kernel, log_count=log_count, accs=len(accs)),
        lists + [use, left],
        accs + [x_rows, y_rows],
        kept,
        slow,
        x_blocks,
        y_all,
        [jax.ShapeDtypeStruct((8, LOCAL), f32), jax.ShapeDtypeStruct((YBLOCKS, 1, BS), f32)],
        [pltpu.VMEM((YBLOCKS, 8, BS), f32), pltpu.VMEM((LOCAL, 128), f32), pltpu.VMEM((8, LOCAL), f32)],
        "columns",
    )
    odd_out, cols_second = lax.optimization_barrier((odd_out, cols_second))
    rows_in = (even_in, swap(odd_out, devices, GROUP // 2))
    even_out, odd_out, g_one = home(who, peers, rows_in, cols_first, cols_second, y_rows, log_count)
    rows_in = (swap(even_out, devices, 0), swap(odd_out, devices, GROUP // 2))
    f_two, g_two = slots_call(
        functools.partial(rows_kernel, log_count=log_count),
        lists + [use, left, source, who],
        [*rows_in, g_one, cols_second, y_rows, x_next],
        kept,
        slow,
        x_blocks,
        y_all,
        [jax.ShapeDtypeStruct((1, LOCAL), f32)] * 2,
        [
            pltpu.VMEM((LOCAL, 128), f32),
            pltpu.VMEM((YBLOCKS, 1, BS), f32),
            pltpu.VMEM((YBLOCKS, 1, BS), f32),
            pltpu.VMEM((8, LOCAL), f32),
        ],
        "rows",
    )
    return f_two.reshape(LOCAL), g_two.reshape(LOCAL)


def solution(mesh):
    placed_as = (
        P("blk", None),
        P("blk", None),
        P("blk"),
        P("blk"),
        P("blk"),
        P("blk"),
        P("blk", None),
        P("blk"),
    )
    return jax.shard_map(
        on_device, mesh=mesh, in_specs=placed_as, out_specs=(P("blk"), P("blk")), check_vma=False
    )
```

```python
import functools
import math

import jax
import jax.numpy as jnp
import numpy as np
from jax import lax
from jax.experimental import pallas as pl
from jax.experimental.pallas import tpu as pltpu
from jax.sharding import PartitionSpec as P

DIM = 512
BS = 1024
BPD = 2
REACH = 3
LOCAL = BPD * BS
EXTRA = 128
WIDE = DIM + EXTRA
TAIL = 16
ROWS = BS + TAIL
CHUNK = 512
PART = 256
ROUNDS = ((1, 3, -1, -2, -3, 2), (-1, -3, 1, -2, 3, 2), (1, 3, -1, 2, -3, -2), (-1, -3, 1, 2, 3, -2))
EARLY = 3
FAR = len(ROUNDS[0])
YBLOCKS = BPD + FAR
SLOTS = BPD * YBLOCKS
MOST = 12
GROUP = 8
PEERS = 2 * GROUP
X_LANES = EXTRA // 2

entropy_weight = 0.05
scale = math.log2(math.e) / entropy_weight
log_two = math.log(2.0)
lowest = -1e30
exponent_room = 112.0
mebi = 1024 * 1024

f32 = jnp.float32
bf16 = jnp.bfloat16
i32 = jnp.int32

SMEM = pl.BlockSpec(memory_space=pltpu.SMEM)
ANY = pl.BlockSpec(memory_space=pl.ANY)
VMEM = pl.BlockSpec(memory_space=pltpu.VMEM)
HBM = pl.BlockSpec(memory_space=pltpu.HBM)


def iota(shape, dim):
    return lax.broadcasted_iota(i32, shape, dim)


def dot(a, b):
    return jnp.dot(a, b, preferred_element_type=f32)


def nt_dot(a, b):
    return lax.dot_general(a, b, (((1,), (1,)), ((), ())), preferred_element_type=f32)


def ones_where(mask):
    return jnp.where(mask, 1.0, 0.0).astype(bf16)


def params():
    return pltpu.CompilerParams(vmem_limit_bytes=63 * mebi)


def whole(shape):
    return pl.BlockSpec(shape, lambda *t: (0,) * len(shape))


def laid_out(square):
    return jnp.concatenate([square[n : n + 1, :] for n in range(square.shape[0])], axis=1)


def down(row):
    parts = [jnp.broadcast_to(row[:, c : c + 128], (128, 128)).T for c in range(0, row.shape[1], 128)]
    return jnp.concatenate(parts, axis=0)


def moved(values, place):
    high = iota((16, LOCAL), 0) == lax.shift_right_logical(place, 7)
    low = ones_where(iota((128, LOCAL), 0) == jnp.bitwise_and(place, 127))
    stack = jnp.concatenate([jnp.where(high, v, 0.0) for v in values], axis=0).astype(bf16)
    out = nt_dot(stack, low)
    return [laid_out(out[16 * n : 16 * n + 16, :]) for n in range(len(values))]


def moved_exact(value, place):
    first = value.astype(bf16).astype(f32)
    second = (value - first).astype(bf16).astype(f32)
    parts = moved([first, second, value - first - second], place)
    return parts[0] + parts[1] + parts[2]


def before_matrix():
    return ones_where(iota((128, 128), 0) < iota((128, 128), 1))


def plan(order, start, devices, first_lane):
    share = LOCAL // devices
    target = lax.shift_right_logical(order, 11)
    hit = iota((devices, LOCAL), 0) == target
    hot = ones_where(hit)
    before = before_matrix()
    every = jnp.ones((128, 128), bf16)
    seen = jnp.zeros((devices, 128), f32)
    earlier = []
    for c in range(0, LOCAL, 128):
        piece = hot[:, c : c + 128]
        earlier.append(dot(piece, before) + seen)
        seen = seen + dot(piece, every)
    earlier = jnp.concatenate(earlier, axis=1)
    rank = jnp.sum(jnp.where(hit, earlier, 0.0), axis=0, keepdims=True).astype(i32)
    within = jnp.bitwise_and(order, LOCAL - 1)
    high = lax.shift_right_logical(within, 6).astype(f32)
    low = jnp.bitwise_and(within, 63).astype(f32)
    row = iota((EXTRA, LOCAL), 0) - first_lane
    field = row // share
    value = jnp.where(field == 0, high, jnp.where(field == 1, low, start))
    mine = (row >= 0) & (row < 3 * share) & (row % share == rank)
    return target * share + rank, nt_dot(hot, jnp.where(mine, value, 0.0).astype(bf16))


def partner_offsets(me):
    kind = jnp.bitwise_and(me, 3)
    out = []
    for k in range(FAR):
        value = jnp.int32(ROUNDS[0][k])
        for n in range(1, 4):
            value = jnp.where(kind == n, jnp.int32(ROUNDS[n][k]), value)
        out.append(value)
    return out


def pack_y_kernel(
    me_ref, partners_ref, counts_ref, y_order, x_order, y_start, x_start, points, out_ref, x_pos_ref, pos_ref, table_ref,
    *, devices
):
    step = pl.program_id(0)
    share = LOCAL // devices

    @pl.when(step == 0)
    def _():
        y_pos, y_table = plan(y_order[...], y_start[...].astype(f32).reshape(1, LOCAL), devices, 0)
        x_pos, x_table = plan(x_order[...], x_start[...].astype(f32).reshape(1, LOCAL), devices, X_LANES)
        pos_ref[...] = y_pos
        x_pos_ref[...] = x_pos
        me = me_ref[0]
        offsets = partner_offsets(me)
        need = [jnp.int32(0)] * FAR
        for b in range(BPD):
            for s in range(partners_ref.shape[1]):
                block = partners_ref[b, s]
                away = lax.shift_right_logical(block, 1) - me
                for k in range(FAR):
                    listed = (s < counts_ref[b]) & (away == offsets[k])
                    need[k] = jnp.where(listed, jnp.bitwise_and(block, 1), need[k])
        table = y_table + x_table
        row, lane = iota(table.shape, 0), iota(table.shape, 1)
        for k in range(FAR):
            table = jnp.where((row == me + offsets[k]) & (lane == 3 * share), need[k].astype(f32), table)
        table_ref[...] = table

    base = step * CHUNK
    hot = ones_where(iota((CHUNK, LOCAL), 0) + base == pos_ref[...])
    out_ref[:, :DIM] = dot(hot, points[...]).astype(bf16)
    some = CHUNK // share
    table = table_ref[pl.ds(pl.multiple_of(step * some, some), some), :]
    out_ref[:, DIM:] = jnp.broadcast_to(table[:, None, :], (some, share, EXTRA)).reshape(CHUNK, EXTRA).astype(bf16)


def pack_y(me, partners, counts, y_order, x_order, y_start, x_start, points, devices):
    row = whole((1, LOCAL))
    return pl.pallas_call(
        functools.partial(pack_y_kernel, devices=devices),
        grid=(LOCAL // CHUNK,),
        in_specs=[SMEM, SMEM, SMEM, row, row, whole((LOCAL,)), whole((LOCAL,)), whole((LOCAL, DIM))],
        out_specs=[pl.BlockSpec((CHUNK, WIDE), lambda t: (t, 0)), row],
        out_shape=[pltpu.HBM((LOCAL, WIDE), bf16), jax.ShapeDtypeStruct((1, LOCAL), i32)],
        scratch_shapes=[pltpu.VMEM((1, LOCAL), i32), pltpu.VMEM((devices, EXTRA), f32)],
        compiler_params=params(),
        name="pack_y",
    )(me, partners, counts, y_order, x_order, y_start, x_start, points)


def pack_x_kernel(pos_ref, points_ref, out_ref):
    base = pl.program_id(0) * CHUNK
    hot = ones_where(iota((CHUNK, LOCAL), 0) + base == pos_ref[...])
    out_ref[...] = dot(hot, points_ref[...]).astype(bf16)


def pack_x(pos, points):
    return pl.pallas_call(
        pack_x_kernel,
        grid=(LOCAL // CHUNK,),
        in_specs=[whole((1, LOCAL)), whole((LOCAL, DIM))],
        out_specs=pl.BlockSpec((CHUNK, DIM), lambda t: (t, 0)),
        out_shape=pltpu.HBM((LOCAL, DIM), bf16),
        compiler_params=params(),
        name="pack_x",
    )(pos, points)


WINDOW = PART + 16
HELD = BS + WINDOW + 16


def arrived(table, base, with_low):
    share = 16
    row, lane = iota((EXTRA, EXTRA), 0), iota((EXTRA, EXTRA), 1)
    pick = jnp.where(row == base + lane % share, 64.0 if with_low else 1.0, 0.0)
    if with_low:
        pick = jnp.where(row == base + share + lane % share, 1.0, pick)
    values = dot(table, pick.astype(bf16))
    values = jnp.where(row % (EXTRA // share) == lane // share, values, 0.0)
    return jnp.sum(values.reshape(LOCAL // 128, EXTRA // share, 128), axis=1)


def unpack_y_kernel(me_ref, came_ref, rows_ref, table_ref, own_ref, *rest, devices):
    sends = rest[:FAR]
    held, sems, own_sem, points_buf, extra_buf, in_sems = rest[FAR:]
    share = LOCAL // devices
    me = me_ref[0]
    extra_in = pltpu.make_async_copy(came_ref.at[:, pl.ds(DIM, EXTRA)], extra_buf, in_sems.at[0])
    points_in = pltpu.make_async_copy(came_ref.at[:, pl.ds(0, DIM)], points_buf, in_sems.at[1])
    extra_in.start()
    points_in.start()
    held[...] = jnp.zeros(held.shape, bf16)
    extra_in.wait()
    table = dot(ones_where(iota((devices, LOCAL), 1) == iota((devices, LOCAL), 0) * share), extra_buf[...])
    table_ref[...] = table
    place_square = arrived(table.astype(bf16), 0, True)
    place = laid_out(place_square)
    start = laid_out(arrived(table.astype(bf16), 2 * share, False))

    picks = []
    offsets = partner_offsets(me)
    small_row, small_lane = iota((devices, EXTRA), 0), iota((devices, EXTRA), 1)
    for k in range(FAR):
        here = (small_row == me + offsets[k]) & (small_lane == 3 * share)
        picks.append(jnp.sum(jnp.where(here, table, 0.0)) > 0.5)

    second = place >= float(BS)
    square = ones_where(place_square >= float(BS))
    totals = dot(square, jnp.ones((128, 128), bf16)).astype(bf16)
    earlier = dot(square, before_matrix()) + dot(ones_where(iota((16, 16), 1) < iota((16, 16), 0)), totals)
    ones_before = laid_out(earlier)
    dest = jnp.where(second, ones_before, iota((1, LOCAL), 1).astype(f32) - ones_before).astype(i32)
    seat = jnp.where(second, dest + BS, dest)
    position = place.astype(i32)
    start_row, high_row, low_row = moved(
        [start, lax.shift_right_logical(position, 6).astype(f32), jnp.bitwise_and(position, 63).astype(f32)], seat
    )
    rows_ref[0:1, :] = start_row
    rows_ref[2:3, :] = high_row * 64.0 + low_row
    rows_ref[3:8, :] = jnp.zeros((5, LOCAL), f32)
    sixteen, lane16 = iota((16, 128), 0), iota((16, 128), 1)
    points_in.wait()

    for j in range(BPD):
        here = jnp.where(second if j else jnp.logical_not(second), dest, -1)
        for c in range(LOCAL // PART):
            span = slice(c * PART, (c + 1) * PART)
            begin = jnp.sum(jnp.where((sixteen == c * PART // 128) & (lane16 == 0), earlier, 0.0)).astype(i32)
            if j == 0:
                begin = c * PART - begin
            begin = pl.multiple_of(lax.shift_left(lax.shift_right_logical(begin, 4), 4), 16)
            hot = ones_where(iota((WINDOW, PART), 0) + begin == here[:, span])
            part = dot(hot, points_buf[span, :]).astype(bf16)
            held[j, pl.ds(begin, WINDOW), :] = held[j, pl.ds(begin, WINDOW), :] + part
        half = []
        for c in range(0, BS, PART):
            points = held[j, c : c + PART, :].astype(f32)
            total = 0.5 * jnp.sum(points * points, axis=1, keepdims=True)
            half.append(jnp.broadcast_to(total, (PART, 128)).T[0:1, :])
        half = jnp.concatenate(half, axis=1)
        block = slice(j * BS, (j + 1) * BS)
        rows_ref[1:2, block] = half
        beta = start_row[:, block] - half
        first = beta.astype(bf16).astype(f32)
        next_part = (beta - first).astype(bf16).astype(f32)
        most = jnp.max(half, axis=1, keepdims=True) * 1.01
        sub = iota((TAIL, DIM), 0)
        tail = jnp.zeros((TAIL, DIM), f32) + most
        for n, piece in enumerate((first, next_part, beta - first - next_part)):
            tail = jnp.where(sub == 2 * n, piece[:, :DIM], tail)
            tail = jnp.where(sub == 2 * n + 1, piece[:, DIM:], tail)
        held[j, BS:ROWS, :] = tail.astype(bf16)
        done = held.at[j, pl.ds(0, ROWS), :]
        for k in range(FAR):
            wanted = picks[k] if j == 1 else jnp.logical_not(picks[k])

            @pl.when(wanted)
            def _():
                pltpu.make_async_copy(done, sends[k], sems.at[k]).start()

        pltpu.make_async_copy(done, own_ref.at[j], own_sem.at[j]).start()

    done = held.at[0, pl.ds(0, ROWS), :]
    for k in range(FAR):
        pltpu.make_async_copy(done, sends[k], sems.at[k]).wait()
    for j in range(BPD):
        pltpu.make_async_copy(done, own_ref.at[j], own_sem.at[j]).wait()


def unpack_y(me, came, devices):
    return pl.pallas_call(
        functools.partial(unpack_y_kernel, devices=devices),
        in_specs=[SMEM, ANY],
        out_specs=[VMEM, VMEM] + [HBM] * (1 + FAR),
        out_shape=[
            jax.ShapeDtypeStruct((8, LOCAL), f32),
            jax.ShapeDtypeStruct((devices, EXTRA), f32),
            pltpu.HBM((BPD, ROWS, DIM), bf16),
        ]
        + [pltpu.HBM((ROWS, DIM), bf16)] * FAR,
        scratch_shapes=[
            pltpu.VMEM((BPD, HELD, DIM), bf16),
            pltpu.SemaphoreType.DMA((FAR,)),
            pltpu.SemaphoreType.DMA((BPD,)),
            pltpu.VMEM((LOCAL, DIM), bf16),
            pltpu.VMEM((LOCAL, EXTRA), bf16),
            pltpu.SemaphoreType.DMA((2,)),
        ],
        compiler_params=params(),
        name="unpack_y",
    )(me, came)


def unpack_x_kernel(came_ref, table_ref, points_ref, alpha_ref, rows_ref, place_ref, start_ref):
    step = pl.program_id(0)

    @pl.when(step == 0)
    def _():
        table = table_ref[...].astype(bf16)
        place = laid_out(arrived(table, X_LANES, True)).astype(i32)
        place_ref[...] = place
        start_ref[...] = moved([laid_out(arrived(table, X_LANES + 32, False))], place)[0]

    base = step * CHUNK
    hot = ones_where(iota((CHUNK, LOCAL), 0) + base == place_ref[...])
    points = dot(hot, came_ref[...])
    points_ref[...] = points.astype(bf16)
    half = jnp.broadcast_to(0.5 * jnp.sum(points * points, axis=1, keepdims=True), (CHUNK, 128))
    start = start_ref[:, pl.ds(pl.multiple_of(base, CHUNK), CHUNK)]
    alpha_ref[...] = (down(start) - half) * scale
    rows_ref[0:1, :] = start
    rows_ref[1:8, :] = jnp.concatenate([half[c : c + 128, :].T[0:7, :] for c in range(0, CHUNK, 128)], axis=1)


def unpack_x(came, table):
    return pl.pallas_call(
        unpack_x_kernel,
        grid=(LOCAL // CHUNK,),
        in_specs=[whole((LOCAL, DIM)), whole((EXTRA, EXTRA))],
        out_specs=[
            pl.BlockSpec((CHUNK, DIM), lambda t: (t, 0)),
            pl.BlockSpec((CHUNK, 128), lambda t: (t, 0)),
            pl.BlockSpec((8, CHUNK), lambda t: (0, t)),
        ],
        out_shape=[
            pltpu.HBM((LOCAL, DIM), bf16),
            pltpu.HBM((LOCAL, 128), f32),
            jax.ShapeDtypeStruct((8, LOCAL), f32),
        ],
        scratch_shapes=[pltpu.VMEM((1, LOCAL), i32), pltpu.VMEM((1, LOCAL), f32)],
        compiler_params=params(),
        name="unpack_x",
    )(came, table)


def merge(top, total, other_top, other_total):
    new = jnp.maximum(top, other_top)
    return new, total * jnp.exp2(top - new) + other_total * jnp.exp2(other_top - new)


def logs(top, total):
    return jnp.where(total > 0.0, top + jnp.log2(total), lowest)


def high_of(row):
    return jnp.max(row, axis=1, keepdims=True)


def low_of(row):
    return jnp.min(row, axis=1, keepdims=True)


def put_cols(col_ref, y, part_top, part_total):
    top, total = merge(col_ref[y, 0:1, :], col_ref[y, 1:2, :], part_top, part_total)
    col_ref[y, 0:1, :] = top
    col_ref[y, 1:2, :] = total


def clear_cols(col_ref):
    col_ref[:, 0:1, :] = jnp.full((col_ref.shape[0], 1, BS), lowest, f32)
    col_ref[:, 1:2, :] = jnp.zeros((col_ref.shape[0], 1, BS), f32)


def shifted_rows(x_ref, y_ref, beta, part_ref):
    def body(c, carry):
        span = pl.ds(pl.multiple_of(c * PART, PART), PART)
        terms = nt_dot(x_ref[span, :], y_ref[0:BS, :]) * scale + beta
        top = jnp.max(terms, axis=1, keepdims=True)
        total = jnp.sum(jnp.exp2(terms - top), axis=1, keepdims=True)
        part_ref[span, :] = jnp.where(iota((PART, 128), 1) == 0, top, total)
        return carry

    lax.fori_loop(0, BS // PART, body, 0)


def shifted_cols(x_ref, y_ref, alpha_ref, col_ref, y):
    def body(c, carry):
        span = pl.ds(pl.multiple_of(c * PART, PART), PART)
        terms = nt_dot(x_ref[span, :], y_ref[0:BS, :]) * scale + alpha_ref[span, 0:1]
        top = jnp.max(terms, axis=0, keepdims=True)
        put_cols(col_ref, y, top, jnp.sum(jnp.exp2(terms - top), axis=0, keepdims=True))
        return carry

    lax.fori_loop(0, BS // PART, body, 0)


def add_part(part_ref, state_ref, b):
    for c in range(0, BS, 128):
        part = part_ref[c : c + 128, :].T
        span = pl.ds(pl.multiple_of(b * BS + c, 128), 128)
        top, total = merge(state_ref[0:1, span], state_ref[1:2, span], part[0:1, :], part[1:2, :])
        state_ref[0:1, span] = top
        state_ref[1:2, span] = total


def lane_sums(refs):
    out = []
    for c in range(0, LOCAL, 128):
        part = refs[0][c : c + 128, :]
        for ref in refs[1:]:
            part = part + ref[c : c + 128, :]
        out.append(jnp.sum(part.T, axis=0, keepdims=True))
    return jnp.concatenate(out, axis=1)


def fold(values):
    return jnp.sum(values.reshape(values.shape[0] // 8, 8, 128), axis=0)


def own_beta(y_rows_ref):
    return (y_rows_ref[0:1, :] - y_rows_ref[1:2, :]) * scale


def sweep_kernel(*refs, base, count, first, sends):
    use_ref, seat_of_ref, x_ref, alpha_ref, x_rows_ref, y_rows_ref = refs[:6]
    refs = refs[6:]
    if not first:
        cols_in, left_in = refs[:2]
        refs = refs[4:]
    if sends is not None:
        peers_ref = refs[0]
        refs = refs[1:]
    y_refs = refs[:1] if first else refs[:count]
    refs = refs[len(y_refs) :]
    acc_ref, cols_ref, left_ref, kept_ref, slow_ref = refs[:5]
    refs = refs[5:]
    if sends is not None:
        group_out = refs[0]
        refs = refs[1:]
    y_buf, sems, col_ref, weight_ref, part_ref, stat_ref, tiles, tile_sems, tile_count = refs

    def copy(n):
        source = y_refs[0].at[n] if first else y_refs[n]
        return pltpu.make_async_copy(source, y_buf.at[n % 2], sems.at[n % 2])

    copy(0).start()
    tile_count[0] = 0
    acc_ref[...] = jnp.zeros((LOCAL, 128), f32)

    def tile_copy(at, seat):
        return pltpu.make_async_copy(tiles.at[at], kept_ref.at[seat], tile_sems.at[at])

    if first:
        for n in range(SLOTS):
            left_ref[n] = -1.0
    else:
        for n in range(SLOTS):
            left_ref[n] = left_in[n]
        cols_ref[...] = cols_in[...]
    alpha = (x_rows_ref[0:1, :] - x_rows_ref[1:2, :]) * scale
    alpha_top = high_of(alpha)
    weight_ref[...] = jnp.exp2(alpha_ref[...] - alpha_top)
    lane = iota((8, 128), 1)
    beta_top = high_of(own_beta(y_rows_ref))
    most = high_of(x_rows_ref[1:2, :]) * 1.01
    spread = alpha_top - low_of(alpha)
    stat_ref[...] = jnp.where(lane == 0, alpha_top, jnp.where(lane == 1, spread, jnp.where(lane == 2, most, beta_top)))

    def body(step, carry):
        y, b = step // BPD, step % BPD
        slot = base * BPD + step
        for n in range(count):

            @pl.when(step == BPD * n)
            def _():
                copy(n).wait()
                if n + 1 < count:
                    copy(n + 1).start()

        @pl.when(b == 0)
        def _():
            clear_cols(col_ref)

        now = y_buf.at[y % 2]
        rows_from = b * BS

        @pl.when(use_ref[slot] > 0)
        def _():
            tail = now[BS:ROWS, :].astype(f32)
            halves = [tail[n : n + 1, :] + tail[n + 2 : n + 3, :] + tail[n + 4 : n + 5, :] for n in range(2)]
            beta = jnp.concatenate(halves, axis=1) * scale
            shift = stat_ref[0:1, 3:4]
            left = exponent_room - 2.0 * scale * jnp.sqrt(tail[6:7, 0:1] * stat_ref[0:1, 2:3])
            reach = jnp.maximum(stat_ref[0:1, 1:2], jnp.maximum(high_of(beta) - shift, shift - low_of(beta)))
            fits = (left - reach)[0, 0] >= 0.0

            @pl.when(fits)
            def _():
                left_ref[slot] = left[0, 0]
                done = tile_count[0]
                tile_count[0] = done + 1
                at = done % 2

                @pl.when(done > 1)
                def _():
                    tile_copy(at, 0).wait()

                weight = jnp.exp2(beta - shift)
                sums = jnp.zeros((8, BS), f32)
                for c in range(0, BS, PART):
                    span = pl.ds(pl.multiple_of(rows_from + c, PART), PART)
                    terms = jnp.exp2(nt_dot(x_ref[span, :], now[0:BS, :]) * scale)
                    tiles[at, c : c + PART, :] = terms.astype(bf16)
                    row_part = acc_ref[span, :]
                    col_parts = []
                    for n in range(0, BS, 128):
                        piece = terms[:, n : n + 128]
                        row_part = row_part + piece * weight[:, n : n + 128]
                        col_parts.append(fold(piece * weight_ref[span, :]))
                    acc_ref[span, :] = row_part
                    sums = sums + jnp.concatenate(col_parts, axis=1)
                tile_copy(at, seat_of_ref[slot]).start()
                put_cols(col_ref, 0, stat_ref[0:1, 0:1], jnp.sum(sums, axis=0, keepdims=True))

            @pl.when(jnp.logical_not(fits))
            def _():
                block = pl.ds(pl.multiple_of(rows_from, BS), BS)
                shifted_rows(x_ref.at[block, :], now, beta, part_ref)
                out = pltpu.make_async_copy(part_ref, slow_ref.at[slot], sems.at[2])
                out.start()
                shifted_cols(x_ref.at[block, :], now, alpha_ref.at[block, :], col_ref, 0)
                out.wait()

        @pl.when(b == BPD - 1)
        def _():
            cols_ref[base + y] = logs(col_ref[0, 0:1, :], col_ref[0, 1:2, :])

        return carry

    lax.fori_loop(0, BPD * count, body, 0)
    for n in range(2):

        @pl.when(tile_count[0] > n)
        def _():
            tile_copy(n, 0).wait()

    if sends is not None:
        for n in range(GROUP):
            group_out[n] = outgoing(cols_ref, peers_ref[sends * GROUP + n])


def outgoing(cols_ref, index):
    return jnp.where(index < 0, lowest, cols_ref[jnp.maximum(index, 0)])


def sweep(common, y_list, base, carried, peers=None, sends=None):
    first = carried is None
    count = BPD if first else len(y_list)
    in_specs = [SMEM, SMEM] + [VMEM] * 4
    operands = list(common)
    aliases = {}
    if not first:
        in_specs += [VMEM, SMEM, HBM, HBM]
        operands += list(carried)
        aliases = {8: 3, 9: 4}
    if sends is not None:
        in_specs.append(SMEM)
        operands.append(peers)
    in_specs += [ANY] * len(y_list)
    operands += y_list
    out_specs = [VMEM, VMEM, SMEM, HBM, HBM]
    out_shape = [
        jax.ShapeDtypeStruct((LOCAL, 128), f32),
        jax.ShapeDtypeStruct((YBLOCKS, 1, BS), f32),
        jax.ShapeDtypeStruct((SLOTS,), f32),
        pltpu.HBM((MOST, BS, BS), bf16),
        pltpu.HBM((SLOTS, BS, 128), f32),
    ]
    if sends is not None:
        out_specs.append(VMEM)
        out_shape.append(jax.ShapeDtypeStruct((GROUP, 1, BS), f32))
    return pl.pallas_call(
        functools.partial(sweep_kernel, base=base, count=count, first=first, sends=sends),
        in_specs=in_specs,
        out_specs=out_specs,
        out_shape=out_shape,
        scratch_shapes=[
            pltpu.VMEM((2, ROWS, DIM), bf16),
            pltpu.SemaphoreType.DMA((3,)),
            pltpu.VMEM((1, 8, BS), f32),
            pltpu.VMEM((LOCAL, 128), f32),
            pltpu.VMEM((BS, 128), f32),
            pltpu.VMEM((8, 128), f32),
            pltpu.VMEM((2, BS, BS), bf16),
            pltpu.SemaphoreType.DMA((2,)),
            pltpu.SMEM((1,), i32),
        ],
        input_output_aliases=aliases,
        compiler_params=params(),
        name=f"sweep_{base}",
    )(*operands)


def load_pair(slot, x_ref, y_refs, x_buf, y_buf, sems):
    rows = pl.ds(pl.multiple_of((slot % BPD) * BS, BS), BS)
    fetch = pltpu.make_async_copy(x_ref.at[rows, :], x_buf, sems.at[0])
    fetch.start()
    fetch.wait()
    for n in range(YBLOCKS):

        @pl.when(slot // BPD == n)
        def _():
            source = y_refs[0].at[n] if n < BPD else y_refs[n - BPD + 1]
            fetch = pltpu.make_async_copy(source, y_buf, sems.at[1])
            fetch.start()
            fetch.wait()


def next_potential(now, half, total, log_count):
    return 0.5 * (now + half + entropy_weight * (log_count - log_two * total))


def fetch_terms(kept_ref, terms_ref, sems, live):
    def term_copy(n):
        return pltpu.make_async_copy(kept_ref.at[n], terms_ref.at[n], sems.at[n])

    for n in range(MOST):

        @pl.when(n < live)
        def _():
            term_copy(n).start()

    return term_copy


def columns_kernel(list_ref, live_ref, use_ref, left_ref, *refs, log_count, accs):
    acc_refs = refs[:accs]
    x_rows_ref, y_rows_ref, kept_ref, slow_ref, x_ref = refs[accs : accs + 5]
    y_refs = refs[accs + 5 : accs + 6 + FAR]
    next_ref, out_ref, col_ref, weight_ref, state_ref, part_ref, x_buf, y_buf, sems, terms_ref, term_sems = refs[accs + 6 + FAR :]
    term_copy = fetch_terms(kept_ref, terms_ref, term_sems, live_ref[0])
    clear_cols(col_ref)
    total = lane_sums(acc_refs)
    state_ref[0:1, :] = jnp.where(total > 0.0, high_of(own_beta(y_rows_ref)), lowest)
    state_ref[1:2, :] = total
    for n in range(SLOTS):

        @pl.when((use_ref[n] > 0) & (left_ref[n] < 0.0))
        def _():
            fetch = pltpu.make_async_copy(slow_ref.at[n], part_ref, sems.at[0])
            fetch.start()
            fetch.wait()
            add_part(part_ref, state_ref, n % BPD)

    half = x_rows_ref[1:2, :]
    f_next = next_potential(x_rows_ref[0:1, :], half, logs(state_ref[0:1, :], state_ref[1:2, :]), log_count)
    next_ref[0:1, :] = f_next
    next_ref[1:2, :] = half
    next_ref[2:8, :] = jnp.zeros((6, LOCAL), f32)
    alpha = (f_next - half) * scale
    state_ref[2:3, :] = alpha
    top = high_of(alpha)
    weight_ref[...] = down(jnp.exp2(alpha - top))
    reach = (top - low_of(alpha))[0, 0]

    def body(step, carry):
        slot = list_ref[step]
        y, b = slot // BPD, slot % BPD
        fits = reach <= left_ref[slot]
        term_copy(step).wait()

        @pl.when(fits)
        def _():
            sums = jnp.zeros((8, BS), f32)
            for c in range(0, BS, 64):
                weight = weight_ref[pl.ds(pl.multiple_of(b * BS + c, 64), 64), :]
                parts = [fold(terms_ref[step, c : c + 64, n : n + 128].astype(f32) * weight) for n in range(0, BS, 128)]
                sums = sums + jnp.concatenate(parts, axis=1)
            put_cols(col_ref, y, top, jnp.sum(sums, axis=0, keepdims=True))

        @pl.when(jnp.logical_not(fits))
        def _():
            load_pair(slot, x_ref, y_refs, x_buf, y_buf, sems)
            for c in range(0, BS, 128):
                row = state_ref[2:3, pl.ds(pl.multiple_of(b * BS + c, 128), 128)]
                part_ref[c : c + 128, :] = jnp.broadcast_to(row, (128, 128)).T
            shifted_cols(x_buf, y_buf, part_ref, col_ref, y)

        return carry

    lax.fori_loop(0, live_ref[0], body, 0)
    for n in range(YBLOCKS):
        out_ref[n] = logs(col_ref[n, 0:1, :], col_ref[n, 1:2, :])


def gathered(j, own_ref, came, who_ref):
    terms = [own_ref[j]] + [jnp.where(who_ref[n] == j, came(n), lowest) for n in range(PEERS)]
    top = terms[0]
    for term in terms[1:]:
        top = jnp.maximum(top, term)
    total = jnp.exp2(terms[0] - top)
    for term in terms[1:]:
        total = total + jnp.exp2(term - top)
    return top + jnp.log2(total)


def home_kernel(who_ref, peers_ref, even_in, odd_in, first_ref, second_ref, y_rows_ref, even_out, odd_out, g_ref, *, log_count):
    came = lambda n: (even_in, odd_in)[n // GROUP][n % GROUP]
    betas = []
    for j in range(BPD):
        span = slice(j * BS, (j + 1) * BS)
        half = y_rows_ref[1:2, span]
        g_next = next_potential(y_rows_ref[0:1, span], half, gathered(j, first_ref, came, who_ref), log_count)
        g_ref[0:1, span] = g_next
        betas.append((g_next - half) * scale)
        g_ref[1:2, span] = betas[j]
    g_ref[2:8, :] = jnp.zeros((6, LOCAL), f32)
    for n in range(PEERS):
        out = (even_out, odd_out)[n // GROUP]
        out[n % GROUP, 0:1, :] = jnp.where(who_ref[n] == 1, betas[1], betas[0])
        out[n % GROUP, 1:2, :] = outgoing(second_ref, peers_ref[n])


def home(who, peers, rows_in, first, second, y_rows, log_count):
    return pl.pallas_call(
        functools.partial(home_kernel, log_count=log_count),
        in_specs=[SMEM, SMEM] + [VMEM] * 5,
        out_specs=[VMEM] * 3,
        out_shape=[jax.ShapeDtypeStruct((GROUP, 2, BS), f32)] * 2 + [jax.ShapeDtypeStruct((8, LOCAL), f32)],
        compiler_params=params(),
        name="home",
    )(who, peers, *rows_in, first, second, y_rows)


def rows_kernel(list_ref, live_ref, use_ref, left_ref, from_ref, who_ref, *refs, log_count):
    even_in, odd_in, g_ref, second_ref, y_rows_ref, x_rows_ref, kept_ref, slow_ref, x_ref = refs[:9]
    y_refs = refs[9 : 10 + FAR]
    f_ref, g_out_ref, acc_ref, beta_ref, weight_ref, state_ref, part_ref, x_buf, y_buf, sems, terms_ref, term_sems = refs[10 + FAR :]
    term_copy = fetch_terms(kept_ref, terms_ref, term_sems, live_ref[0])
    shift = high_of(g_ref[1:2, :])
    acc_ref[...] = jnp.zeros((LOCAL, 128), f32)
    state_ref[0:1, :] = jnp.full((1, LOCAL), lowest, f32)
    state_ref[1:2, :] = jnp.zeros((1, LOCAL), f32)
    for n in range(BPD):
        beta_ref[n] = g_ref[1:2, n * BS : (n + 1) * BS]
    for n in range(BPD, YBLOCKS):
        source = from_ref[n]
        at = source % GROUP
        beta_ref[n] = jnp.where(source < GROUP, even_in[at, 0:1, :], odd_in[at, 0:1, :])
    weight_ref[...] = jnp.exp2(beta_ref[...] - shift)

    def body(step, carry):
        slot = list_ref[step]
        y, b = slot // BPD, slot % BPD
        beta = beta_ref[y]
        reach = jnp.maximum(high_of(beta) - shift, shift - low_of(beta))
        fits = reach[0, 0] <= left_ref[slot]
        term_copy(step).wait()

        @pl.when(fits)
        def _():
            weight = weight_ref[y]
            for c in range(0, BS, 64):
                span = pl.ds(pl.multiple_of(b * BS + c, 64), 64)
                part = acc_ref[span, :]
                for n in range(0, BS, 128):
                    part = part + terms_ref[step, c : c + 64, n : n + 128].astype(f32) * weight[:, n : n + 128]
                acc_ref[span, :] = part

        @pl.when(jnp.logical_not(fits))
        def _():
            load_pair(slot, x_ref, y_refs, x_buf, y_buf, sems)
            shifted_rows(x_buf, y_buf, beta, part_ref)
            add_part(part_ref, state_ref, b)

        return carry

    lax.fori_loop(0, live_ref[0], body, 0)
    total = lane_sums([acc_ref])
    top = jnp.where(total > 0.0, shift, lowest)
    top, total = merge(top, total, state_ref[0:1, :], state_ref[1:2, :])
    f_ref[...] = next_potential(x_rows_ref[0:1, :], x_rows_ref[1:2, :], logs(top, total), log_count)
    came = lambda n: (even_in, odd_in)[n // GROUP][n % GROUP, 1:2, :]
    total = jnp.concatenate([gathered(j, second_ref, came, who_ref) for j in range(BPD)], axis=1)
    g_next = next_potential(g_ref[0:1, :], y_rows_ref[1:2, :], total, log_count)
    g_out_ref[...] = moved_exact(g_next, y_rows_ref[2:3, :].astype(i32))


def slots_call(kernel, smem, front, kept, slow, x_blocks, y_list, outs, scratch, name):
    return pl.pallas_call(
        kernel,
        in_specs=[SMEM] * len(smem) + [VMEM] * len(front) + [HBM, HBM, ANY] + [ANY] * len(y_list),
        out_specs=[VMEM] * len(outs),
        scratch_shapes=scratch
        + [
            pltpu.VMEM((BS, 128), f32),
            pltpu.VMEM((BS, DIM), bf16),
            pltpu.VMEM((ROWS, DIM), bf16),
            pltpu.SemaphoreType.DMA((2,)),
            pltpu.VMEM((MOST, BS, BS), bf16),
            pltpu.SemaphoreType.DMA((MOST,)),
        ],
        out_shape=outs,
        compiler_params=params(),
        name=name,
    )(*smem, *front, kept, slow, x_blocks, *y_list)


def seat_tables():
    half = GROUP // 2
    offsets = np.zeros((GROUP, PEERS), np.int32)
    source = np.zeros((GROUP, YBLOCKS), np.int32)
    for seat in range(GROUP):
        odd_seat = (seat + half) % GROUP
        for other in range(GROUP):
            if other != seat and abs(other - seat) <= REACH:
                offsets[seat, other] = other - seat
            off = other - odd_seat
            if off != 0 and abs(off) <= REACH and not 0 <= seat + off < GROUP:
                offsets[seat, GROUP + other] = off
        for k, off in enumerate(ROUNDS[seat % 4]):
            source[seat, BPD + k] = list(offsets[seat]).index(off)
    index = np.full((GROUP, PEERS), -1, np.int32)
    for seat in range(GROUP):
        for k, off in enumerate(ROUNDS[seat % 4]):
            index[seat, offsets[seat] == off] = BPD + k
    return offsets, index, source


def swap(rows, devices, shift):
    groups = [[(GROUP * k + j + shift) % devices for j in range(GROUP)] for k in range(devices // GROUP)]
    return lax.all_to_all(rows, "blk", split_axis=0, concat_axis=0, tiled=True, axis_index_groups=groups)


def on_device(x_points, y_points, x_start, y_start, x_order, y_order, partners, counts):
    devices = lax.axis_size("blk")
    me = lax.axis_index("blk").astype(i32)
    log_count = math.log(LOCAL * devices)
    here = me[None]
    line = lambda v: v.reshape(1, LOCAL)

    y_sent, x_pos = pack_y(here, partners, counts, line(y_order), line(x_order), y_start, x_start, y_points, devices)
    y_came = lax.all_to_all(y_sent, "blk", split_axis=0, concat_axis=0, tiled=True)
    x_sent = pack_x(x_pos, x_points)
    x_came = lax.all_to_all(x_sent, "blk", split_axis=0, concat_axis=0, tiled=True)
    y_came, x_sent = lax.optimization_barrier((y_came, x_sent))
    y_rows, table, y_own, *y_sends = unpack_y(here, y_came, devices)

    def far_block(k):
        pairs = [(i, i + ROUNDS[i % 4][k]) for i in range(devices) if 0 <= i + ROUNDS[i % 4][k] < devices]
        return lax.ppermute(y_sends[k], "blk", pairs)

    y_far = [far_block(k) for k in range(EARLY)]
    x_came, y_far[1:], y_sends[EARLY:] = lax.optimization_barrier((x_came, y_far[1:], y_sends[EARLY:]))
    y_far += [far_block(k) for k in range(EARLY, FAR)]
    x_blocks, alpha, x_rows = unpack_x(x_came, table)

    offsets = lax.dynamic_slice(jnp.array(ROUNDS, i32), (me % 4, 0), (1, FAR))[0]
    live = jnp.arange(partners.shape[1], dtype=i32)[None, :] < counts[:, None]
    away = jnp.where(live, partners // BPD - me, devices)
    local_use = [((away == 0) & (partners % BPD == j)).any(axis=1) for j in range(BPD)]
    far = away[None, :, :] == offsets[:, None, None]
    use = jnp.concatenate([jnp.stack(local_use), far.any(axis=2)]).astype(i32).reshape(SLOTS)
    number = jnp.minimum(jnp.maximum(jnp.cumsum(use) - 1, 0), MOST - 1)
    count = jnp.minimum(jnp.sum(use), MOST)
    step = jnp.minimum(jnp.arange(MOST, dtype=i32), count - 1)
    at = (number[None, :] == step[:, None]) & (use[None, :] > 0)
    slots = jnp.sum(jnp.where(at, jnp.arange(SLOTS, dtype=i32)[None, :], 0), axis=1)
    lists = [slots, count[None]]

    peer_offsets, peer_index, peer_source = seat_tables()
    row = lambda t: lax.dynamic_slice(jnp.asarray(t), (me % GROUP, 0), (1, t.shape[1]))[0]
    peers, source, off = row(peer_index), row(peer_source), row(peer_offsets)
    peer = me + off
    wants = (table[:, 3 * (LOCAL // devices)] > 0.5).astype(i32)
    valid = (off != 0) & (peer >= 0) & (peer < devices)
    who = jnp.where(valid, wants[jnp.clip(peer, 0, devices - 1)], -1)

    common = (use, number, x_blocks, alpha, x_rows, y_rows)
    acc_0, *carried = sweep(common, [y_own], 0, None)
    acc_1, *carried = sweep(common, y_far[:EARLY], BPD, carried)
    acc_2, *carried, odd_out = sweep(common, y_far[EARLY:-1], BPD + EARLY, carried, peers, 1)
    acc_3, cols_first, left, kept, slow, even_out = sweep(common, y_far[-1:], YBLOCKS - 1, carried, peers, 0)
    y_all = [y_own] + y_far

    odd_in = swap(odd_out, devices, GROUP // 2)
    even_in = swap(even_out, devices, 0)
    accs = [acc_0, acc_1, acc_2, acc_3]
    x_next, cols_second = slots_call(
        functools.partial(columns_kernel, log_count=log_count, accs=len(accs)),
        lists + [use, left],
        accs + [x_rows, y_rows],
        kept,
        slow,
        x_blocks,
        y_all,
        [jax.ShapeDtypeStruct((8, LOCAL), f32), jax.ShapeDtypeStruct((YBLOCKS, 1, BS), f32)],
        [pltpu.VMEM((YBLOCKS, 8, BS), f32), pltpu.VMEM((LOCAL, 128), f32), pltpu.VMEM((8, LOCAL), f32)],
        "columns",
    )
    even_out, odd_out, g_one = home(who, peers, (even_in, odd_in), cols_first, cols_second, y_rows, log_count)
    rows_in = (swap(even_out, devices, 0), swap(odd_out, devices, GROUP // 2))
    f_two, g_two = slots_call(
        functools.partial(rows_kernel, log_count=log_count),
        lists + [use, left, source, who],
        [*rows_in, g_one, cols_second, y_rows, x_next],
        kept,
        slow,
        x_blocks,
        y_all,
        [jax.ShapeDtypeStruct((1, LOCAL), f32)] * 2,
        [
            pltpu.VMEM((LOCAL, 128), f32),
            pltpu.VMEM((YBLOCKS, 1, BS), f32),
            pltpu.VMEM((YBLOCKS, 1, BS), f32),
            pltpu.VMEM((8, LOCAL), f32),
        ],
        "rows",
    )
    return f_two.reshape(LOCAL), g_two.reshape(LOCAL)


def solution(mesh):
    placed_as = (
        P("blk", None),
        P("blk", None),
        P("blk"),
        P("blk"),
        P("blk"),
        P("blk"),
        P("blk", None),
        P("blk"),
    )
    return jax.shard_map(
        on_device, mesh=mesh, in_specs=placed_as, out_specs=(P("blk"), P("blk")), check_vma=False
    )
```

```python
import functools
import math

import jax
import jax.numpy as jnp
import numpy as np
from jax import lax
from jax.experimental import pallas as pl
from jax.experimental.pallas import tpu as pltpu
from jax.sharding import PartitionSpec as P

DIM = 512
BS = 1024
BPD = 2
REACH = 3
LOCAL = BPD * BS
EXTRA = 128
WIDE = DIM + EXTRA
TAIL = 16
ROWS = BS + TAIL
CHUNK = 512
PART = 256
ROUNDS = ((1, 3, -1, -2, -3, 2), (-1, -3, 1, -2, 3, 2), (1, 3, -1, 2, -3, -2), (-1, -3, 1, 2, 3, -2))
EARLY = 3
FAR = len(ROUNDS[0])
YBLOCKS = BPD + FAR
SLOTS = BPD * YBLOCKS
MOST = 12
GROUP = 8
PEERS = 2 * GROUP
X_LANES = EXTRA // 2

entropy_weight = 0.05
scale = math.log2(math.e) / entropy_weight
log_two = math.log(2.0)
lowest = -1e30
exponent_room = 112.0
mebi = 1024 * 1024

f32 = jnp.float32
bf16 = jnp.bfloat16
i32 = jnp.int32

SMEM = pl.BlockSpec(memory_space=pltpu.SMEM)
ANY = pl.BlockSpec(memory_space=pl.ANY)
VMEM = pl.BlockSpec(memory_space=pltpu.VMEM)
HBM = pl.BlockSpec(memory_space=pltpu.HBM)


def iota(shape, dim):
    return lax.broadcasted_iota(i32, shape, dim)


def dot(a, b):
    return jnp.dot(a, b, preferred_element_type=f32)


def nt_dot(a, b):
    return lax.dot_general(a, b, (((1,), (1,)), ((), ())), preferred_element_type=f32)


def ones_where(mask):
    return jnp.where(mask, 1.0, 0.0).astype(bf16)


def params():
    return pltpu.CompilerParams(vmem_limit_bytes=63 * mebi)


def whole(shape):
    return pl.BlockSpec(shape, lambda *t: (0,) * len(shape))


def laid_out(square):
    return jnp.concatenate([square[n : n + 1, :] for n in range(square.shape[0])], axis=1)


def down(row):
    parts = [jnp.broadcast_to(row[:, c : c + 128], (128, 128)).T for c in range(0, row.shape[1], 128)]
    return jnp.concatenate(parts, axis=0)


def moved(values, place):
    high = iota((16, LOCAL), 0) == lax.shift_right_logical(place, 7)
    low = ones_where(iota((128, LOCAL), 0) == jnp.bitwise_and(place, 127))
    stack = jnp.concatenate([jnp.where(high, v, 0.0) for v in values], axis=0).astype(bf16)
    out = nt_dot(stack, low)
    return [laid_out(out[16 * n : 16 * n + 16, :]) for n in range(len(values))]


def moved_exact(value, place):
    first = value.astype(bf16).astype(f32)
    second = (value - first).astype(bf16).astype(f32)
    parts = moved([first, second, value - first - second], place)
    return parts[0] + parts[1] + parts[2]


def before_matrix():
    return ones_where(iota((128, 128), 0) < iota((128, 128), 1))


def plan(order, start, devices, first_lane):
    share = LOCAL // devices
    target = lax.shift_right_logical(order, 11)
    hit = iota((devices, LOCAL), 0) == target
    hot = ones_where(hit)
    before = before_matrix()
    every = jnp.ones((128, 128), bf16)
    seen = jnp.zeros((devices, 128), f32)
    earlier = []
    for c in range(0, LOCAL, 128):
        piece = hot[:, c : c + 128]
        earlier.append(dot(piece, before) + seen)
        seen = seen + dot(piece, every)
    earlier = jnp.concatenate(earlier, axis=1)
    rank = jnp.sum(jnp.where(hit, earlier, 0.0), axis=0, keepdims=True).astype(i32)
    within = jnp.bitwise_and(order, LOCAL - 1)
    high = lax.shift_right_logical(within, 6).astype(f32)
    low = jnp.bitwise_and(within, 63).astype(f32)
    row = iota((EXTRA, LOCAL), 0) - first_lane
    field = row // share
    value = jnp.where(field == 0, high, jnp.where(field == 1, low, start))
    mine = (row >= 0) & (row < 3 * share) & (row % share == rank)
    return target * share + rank, nt_dot(hot, jnp.where(mine, value, 0.0).astype(bf16))


def partner_offsets(me):
    kind = jnp.bitwise_and(me, 3)
    out = []
    for k in range(FAR):
        value = jnp.int32(ROUNDS[0][k])
        for n in range(1, 4):
            value = jnp.where(kind == n, jnp.int32(ROUNDS[n][k]), value)
        out.append(value)
    return out


def pack_y_kernel(
    me_ref, partners_ref, counts_ref, y_order, x_order, y_start, x_start, points, out_ref, x_pos_ref, pos_ref, table_ref,
    *, devices
):
    step = pl.program_id(0)
    share = LOCAL // devices

    @pl.when(step == 0)
    def _():
        y_pos, y_table = plan(y_order[...], y_start[...].astype(f32).reshape(1, LOCAL), devices, 0)
        x_pos, x_table = plan(x_order[...], x_start[...].astype(f32).reshape(1, LOCAL), devices, X_LANES)
        pos_ref[...] = y_pos
        x_pos_ref[...] = x_pos
        me = me_ref[0]
        offsets = partner_offsets(me)
        need = [jnp.int32(0)] * FAR
        for b in range(BPD):
            for s in range(partners_ref.shape[1]):
                block = partners_ref[b, s]
                away = lax.shift_right_logical(block, 1) - me
                for k in range(FAR):
                    listed = (s < counts_ref[b]) & (away == offsets[k])
                    need[k] = jnp.where(listed, jnp.bitwise_and(block, 1), need[k])
        table = y_table + x_table
        row, lane = iota(table.shape, 0), iota(table.shape, 1)
        for k in range(FAR):
            table = jnp.where((row == me + offsets[k]) & (lane == 3 * share), need[k].astype(f32), table)
        table_ref[...] = table

    base = step * CHUNK
    hot = ones_where(iota((CHUNK, LOCAL), 0) + base == pos_ref[...])
    out_ref[:, :DIM] = dot(hot, points[...]).astype(bf16)
    some = CHUNK // share
    table = table_ref[pl.ds(pl.multiple_of(step * some, some), some), :]
    out_ref[:, DIM:] = jnp.broadcast_to(table[:, None, :], (some, share, EXTRA)).reshape(CHUNK, EXTRA).astype(bf16)


def pack_y(me, partners, counts, y_order, x_order, y_start, x_start, points, devices):
    row = whole((1, LOCAL))
    return pl.pallas_call(
        functools.partial(pack_y_kernel, devices=devices),
        grid=(LOCAL // CHUNK,),
        in_specs=[SMEM, SMEM, SMEM, row, row, whole((LOCAL,)), whole((LOCAL,)), whole((LOCAL, DIM))],
        out_specs=[pl.BlockSpec((CHUNK, WIDE), lambda t: (t, 0)), row],
        out_shape=[pltpu.HBM((LOCAL, WIDE), bf16), jax.ShapeDtypeStruct((1, LOCAL), i32)],
        scratch_shapes=[pltpu.VMEM((1, LOCAL), i32), pltpu.VMEM((devices, EXTRA), f32)],
        compiler_params=params(),
        name="pack_y",
    )(me, partners, counts, y_order, x_order, y_start, x_start, points)


def pack_x_kernel(pos_ref, points_ref, out_ref):
    base = pl.program_id(0) * CHUNK
    hot = ones_where(iota((CHUNK, LOCAL), 0) + base == pos_ref[...])
    out_ref[...] = dot(hot, points_ref[...]).astype(bf16)


def pack_x(pos, points):
    return pl.pallas_call(
        pack_x_kernel,
        grid=(LOCAL // CHUNK,),
        in_specs=[whole((1, LOCAL)), whole((LOCAL, DIM))],
        out_specs=pl.BlockSpec((CHUNK, DIM), lambda t: (t, 0)),
        out_shape=pltpu.HBM((LOCAL, DIM), bf16),
        compiler_params=params(),
        name="pack_x",
    )(pos, points)


WINDOW = PART + 16
HELD = BS + WINDOW + 16


def arrived(table, base, with_low):
    share = 16
    row, lane = iota((EXTRA, EXTRA), 0), iota((EXTRA, EXTRA), 1)
    pick = jnp.where(row == base + lane % share, 64.0 if with_low else 1.0, 0.0)
    if with_low:
        pick = jnp.where(row == base + share + lane % share, 1.0, pick)
    values = dot(table, pick.astype(bf16))
    values = jnp.where(row % (EXTRA // share) == lane // share, values, 0.0)
    return jnp.sum(values.reshape(LOCAL // 128, EXTRA // share, 128), axis=1)


def unpack_y_kernel(me_ref, came_ref, rows_ref, table_ref, own_ref, *rest, devices):
    sends = rest[:FAR]
    held, sems, own_sem, points_buf, extra_buf, in_sems = rest[FAR:]
    share = LOCAL // devices
    me = me_ref[0]
    extra_in = pltpu.make_async_copy(came_ref.at[:, pl.ds(DIM, EXTRA)], extra_buf, in_sems.at[0])
    points_in = pltpu.make_async_copy(came_ref.at[:, pl.ds(0, DIM)], points_buf, in_sems.at[1])
    extra_in.start()
    points_in.start()
    held[...] = jnp.zeros(held.shape, bf16)
    extra_in.wait()
    table = dot(ones_where(iota((devices, LOCAL), 1) == iota((devices, LOCAL), 0) * share), extra_buf[...])
    table_ref[...] = table
    place_square = arrived(table.astype(bf16), 0, True)
    place = laid_out(place_square)
    start = laid_out(arrived(table.astype(bf16), 2 * share, False))

    picks = []
    offsets = partner_offsets(me)
    small_row, small_lane = iota((devices, EXTRA), 0), iota((devices, EXTRA), 1)
    for k in range(FAR):
        here = (small_row == me + offsets[k]) & (small_lane == 3 * share)
        picks.append(jnp.sum(jnp.where(here, table, 0.0)) > 0.5)

    second = place >= float(BS)
    square = ones_where(place_square >= float(BS))
    totals = dot(square, jnp.ones((128, 128), bf16)).astype(bf16)
    earlier = dot(square, before_matrix()) + dot(ones_where(iota((16, 16), 1) < iota((16, 16), 0)), totals)
    ones_before = laid_out(earlier)
    dest = jnp.where(second, ones_before, iota((1, LOCAL), 1).astype(f32) - ones_before).astype(i32)
    seat = jnp.where(second, dest + BS, dest)
    position = place.astype(i32)
    start_row, high_row, low_row = moved(
        [start, lax.shift_right_logical(position, 6).astype(f32), jnp.bitwise_and(position, 63).astype(f32)], seat
    )
    rows_ref[0:1, :] = start_row
    rows_ref[2:3, :] = high_row * 64.0 + low_row
    rows_ref[3:8, :] = jnp.zeros((5, LOCAL), f32)
    sixteen, lane16 = iota((16, 128), 0), iota((16, 128), 1)
    points_in.wait()

    for j in range(BPD):
        here = jnp.where(second if j else jnp.logical_not(second), dest, -1)
        for c in range(LOCAL // PART):
            span = slice(c * PART, (c + 1) * PART)
            begin = jnp.sum(jnp.where((sixteen == c * PART // 128) & (lane16 == 0), earlier, 0.0)).astype(i32)
            if j == 0:
                begin = c * PART - begin
            begin = pl.multiple_of(lax.shift_left(lax.shift_right_logical(begin, 4), 4), 16)
            hot = ones_where(iota((WINDOW, PART), 0) + begin == here[:, span])
            part = dot(hot, points_buf[span, :]).astype(bf16)
            held[j, pl.ds(begin, WINDOW), :] = held[j, pl.ds(begin, WINDOW), :] + part
        half = []
        for c in range(0, BS, PART):
            points = held[j, c : c + PART, :].astype(f32)
            total = 0.5 * jnp.sum(points * points, axis=1, keepdims=True)
            half.append(jnp.broadcast_to(total, (PART, 128)).T[0:1, :])
        half = jnp.concatenate(half, axis=1)
        block = slice(j * BS, (j + 1) * BS)
        rows_ref[1:2, block] = half
        beta = start_row[:, block] - half
        first = beta.astype(bf16).astype(f32)
        next_part = (beta - first).astype(bf16).astype(f32)
        most = jnp.max(half, axis=1, keepdims=True) * 1.01
        sub = iota((TAIL, DIM), 0)
        tail = jnp.zeros((TAIL, DIM), f32) + most
        for n, piece in enumerate((first, next_part, beta - first - next_part)):
            tail = jnp.where(sub == 2 * n, piece[:, :DIM], tail)
            tail = jnp.where(sub == 2 * n + 1, piece[:, DIM:], tail)
        held[j, BS:ROWS, :] = tail.astype(bf16)
        done = held.at[j, pl.ds(0, ROWS), :]
        for k in range(FAR):
            wanted = picks[k] if j == 1 else jnp.logical_not(picks[k])

            @pl.when(wanted)
            def _():
                pltpu.make_async_copy(done, sends[k], sems.at[k]).start()

        pltpu.make_async_copy(done, own_ref.at[j], own_sem.at[j]).start()

    done = held.at[0, pl.ds(0, ROWS), :]
    for k in range(FAR):
        pltpu.make_async_copy(done, sends[k], sems.at[k]).wait()
    for j in range(BPD):
        pltpu.make_async_copy(done, own_ref.at[j], own_sem.at[j]).wait()


def unpack_y(me, came, devices):
    return pl.pallas_call(
        functools.partial(unpack_y_kernel, devices=devices),
        in_specs=[SMEM, ANY],
        out_specs=[VMEM, VMEM] + [HBM] * (1 + FAR),
        out_shape=[
            jax.ShapeDtypeStruct((8, LOCAL), f32),
            jax.ShapeDtypeStruct((devices, EXTRA), f32),
            pltpu.HBM((BPD, ROWS, DIM), bf16),
        ]
        + [pltpu.HBM((ROWS, DIM), bf16)] * FAR,
        scratch_shapes=[
            pltpu.VMEM((BPD, HELD, DIM), bf16),
            pltpu.SemaphoreType.DMA((FAR,)),
            pltpu.SemaphoreType.DMA((BPD,)),
            pltpu.VMEM((LOCAL, DIM), bf16),
            pltpu.VMEM((LOCAL, EXTRA), bf16),
            pltpu.SemaphoreType.DMA((2,)),
        ],
        compiler_params=params(),
        name="unpack_y",
    )(me, came)


def unpack_x_kernel(came_ref, table_ref, points_ref, alpha_ref, rows_ref, place_ref, start_ref):
    step = pl.program_id(0)

    @pl.when(step == 0)
    def _():
        table = table_ref[...].astype(bf16)
        place = laid_out(arrived(table, X_LANES, True)).astype(i32)
        place_ref[...] = place
        start_ref[...] = moved([laid_out(arrived(table, X_LANES + 32, False))], place)[0]

    base = step * CHUNK
    hot = ones_where(iota((CHUNK, LOCAL), 0) + base == place_ref[...])
    points = dot(hot, came_ref[...])
    points_ref[...] = points.astype(bf16)
    half = jnp.broadcast_to(0.5 * jnp.sum(points * points, axis=1, keepdims=True), (CHUNK, 128))
    start = start_ref[:, pl.ds(pl.multiple_of(base, CHUNK), CHUNK)]
    alpha_ref[...] = (down(start) - half) * scale
    rows_ref[0:1, :] = start
    rows_ref[1:8, :] = jnp.concatenate([half[c : c + 128, :].T[0:7, :] for c in range(0, CHUNK, 128)], axis=1)


def unpack_x(came, table):
    return pl.pallas_call(
        unpack_x_kernel,
        grid=(LOCAL // CHUNK,),
        in_specs=[whole((LOCAL, DIM)), whole((EXTRA, EXTRA))],
        out_specs=[
            pl.BlockSpec((CHUNK, DIM), lambda t: (t, 0)),
            pl.BlockSpec((CHUNK, 128), lambda t: (t, 0)),
            pl.BlockSpec((8, CHUNK), lambda t: (0, t)),
        ],
        out_shape=[
            pltpu.HBM((LOCAL, DIM), bf16),
            pltpu.HBM((LOCAL, 128), f32),
            jax.ShapeDtypeStruct((8, LOCAL), f32),
        ],
        scratch_shapes=[pltpu.VMEM((1, LOCAL), i32), pltpu.VMEM((1, LOCAL), f32)],
        compiler_params=params(),
        name="unpack_x",
    )(came, table)


def merge(top, total, other_top, other_total):
    new = jnp.maximum(top, other_top)
    return new, total * jnp.exp2(top - new) + other_total * jnp.exp2(other_top - new)


def logs(top, total):
    return jnp.where(total > 0.0, top + jnp.log2(total), lowest)


def high_of(row):
    return jnp.max(row, axis=1, keepdims=True)


def low_of(row):
    return jnp.min(row, axis=1, keepdims=True)


def put_cols(col_ref, y, part_top, part_total):
    top, total = merge(col_ref[y, 0:1, :], col_ref[y, 1:2, :], part_top, part_total)
    col_ref[y, 0:1, :] = top
    col_ref[y, 1:2, :] = total


def clear_cols(col_ref):
    col_ref[:, 0:1, :] = jnp.full((col_ref.shape[0], 1, BS), lowest, f32)
    col_ref[:, 1:2, :] = jnp.zeros((col_ref.shape[0], 1, BS), f32)


def shifted_rows(x_ref, y_ref, beta, part_ref):
    def body(c, carry):
        span = pl.ds(pl.multiple_of(c * PART, PART), PART)
        terms = nt_dot(x_ref[span, :], y_ref[0:BS, :]) * scale + beta
        top = jnp.max(terms, axis=1, keepdims=True)
        total = jnp.sum(jnp.exp2(terms - top), axis=1, keepdims=True)
        part_ref[span, :] = jnp.where(iota((PART, 128), 1) == 0, top, total)
        return carry

    lax.fori_loop(0, BS // PART, body, 0)


def shifted_cols(x_ref, y_ref, alpha_ref, col_ref, y):
    def body(c, carry):
        span = pl.ds(pl.multiple_of(c * PART, PART), PART)
        terms = nt_dot(x_ref[span, :], y_ref[0:BS, :]) * scale + alpha_ref[span, 0:1]
        top = jnp.max(terms, axis=0, keepdims=True)
        put_cols(col_ref, y, top, jnp.sum(jnp.exp2(terms - top), axis=0, keepdims=True))
        return carry

    lax.fori_loop(0, BS // PART, body, 0)


def add_part(part_ref, state_ref, b):
    for c in range(0, BS, 128):
        part = part_ref[c : c + 128, :].T
        span = pl.ds(pl.multiple_of(b * BS + c, 128), 128)
        top, total = merge(state_ref[0:1, span], state_ref[1:2, span], part[0:1, :], part[1:2, :])
        state_ref[0:1, span] = top
        state_ref[1:2, span] = total


def lane_sums(refs):
    out = []
    for c in range(0, LOCAL, 128):
        part = refs[0][c : c + 128, :]
        for ref in refs[1:]:
            part = part + ref[c : c + 128, :]
        out.append(jnp.sum(part.T, axis=0, keepdims=True))
    return jnp.concatenate(out, axis=1)


def fold(values):
    return jnp.sum(values.reshape(values.shape[0] // 8, 8, 128), axis=0)


def own_beta(y_rows_ref):
    return (y_rows_ref[0:1, :] - y_rows_ref[1:2, :]) * scale


def sweep_kernel(*refs, base, count, first, sends):
    use_ref, seat_of_ref, x_ref, alpha_ref, x_rows_ref, y_rows_ref = refs[:6]
    refs = refs[6:]
    if not first:
        cols_in, left_in = refs[:2]
        refs = refs[4:]
    if sends is not None:
        peers_ref = refs[0]
        refs = refs[1:]
    y_refs = refs[:1] if first else refs[:count]
    refs = refs[len(y_refs) :]
    acc_ref, cols_ref, left_ref, kept_ref, slow_ref = refs[:5]
    refs = refs[5:]
    if sends is not None:
        group_out = refs[0]
        refs = refs[1:]
    y_buf, sems, col_ref, weight_ref, part_ref, stat_ref, tiles, tile_sems, tile_count = refs

    def copy(n):
        source = y_refs[0].at[n] if first else y_refs[n]
        return pltpu.make_async_copy(source, y_buf.at[n % 2], sems.at[n % 2])

    copy(0).start()
    tile_count[0] = 0
    acc_ref[...] = jnp.zeros((LOCAL, 128), f32)

    def tile_copy(at, seat):
        return pltpu.make_async_copy(tiles.at[at], kept_ref.at[seat], tile_sems.at[at])

    if first:
        for n in range(SLOTS):
            left_ref[n] = -1.0
    else:
        for n in range(SLOTS):
            left_ref[n] = left_in[n]
        cols_ref[...] = cols_in[...]
    alpha = (x_rows_ref[0:1, :] - x_rows_ref[1:2, :]) * scale
    alpha_top = high_of(alpha)
    weight_ref[...] = jnp.exp2(alpha_ref[...] - alpha_top)
    lane = iota((8, 128), 1)
    beta_top = high_of(own_beta(y_rows_ref))
    most = high_of(x_rows_ref[1:2, :]) * 1.01
    spread = alpha_top - low_of(alpha)
    stat_ref[...] = jnp.where(lane == 0, alpha_top, jnp.where(lane == 1, spread, jnp.where(lane == 2, most, beta_top)))

    def body(step, carry):
        y, b = step // BPD, step % BPD
        slot = base * BPD + step
        for n in range(count):

            @pl.when(step == BPD * n)
            def _():
                copy(n).wait()
                if n + 1 < count:
                    copy(n + 1).start()

        @pl.when(b == 0)
        def _():
            clear_cols(col_ref)

        now = y_buf.at[y % 2]
        rows_from = b * BS

        @pl.when(use_ref[slot] > 0)
        def _():
            tail = now[BS:ROWS, :].astype(f32)
            halves = [tail[n : n + 1, :] + tail[n + 2 : n + 3, :] + tail[n + 4 : n + 5, :] for n in range(2)]
            beta = jnp.concatenate(halves, axis=1) * scale
            shift = stat_ref[0:1, 3:4]
            left = exponent_room - 2.0 * scale * jnp.sqrt(tail[6:7, 0:1] * stat_ref[0:1, 2:3])
            reach = jnp.maximum(stat_ref[0:1, 1:2], jnp.maximum(high_of(beta) - shift, shift - low_of(beta)))
            fits = (left - reach)[0, 0] >= 0.0

            @pl.when(fits)
            def _():
                left_ref[slot] = left[0, 0]
                done = tile_count[0]
                tile_count[0] = done + 1
                at = done % 2

                @pl.when(done > 1)
                def _():
                    tile_copy(at, 0).wait()

                weight = jnp.exp2(beta - shift)
                sums = jnp.zeros((8, BS), f32)
                for c in range(0, BS, PART):
                    span = pl.ds(pl.multiple_of(rows_from + c, PART), PART)
                    terms = jnp.exp2(nt_dot(x_ref[span, :], now[0:BS, :]) * scale)
                    tiles[at, c : c + PART, :] = terms.astype(bf16)
                    row_part = acc_ref[span, :]
                    col_parts = []
                    for n in range(0, BS, 128):
                        piece = terms[:, n : n + 128]
                        row_part = row_part + piece * weight[:, n : n + 128]
                        col_parts.append(fold(piece * weight_ref[span, :]))
                    acc_ref[span, :] = row_part
                    sums = sums + jnp.concatenate(col_parts, axis=1)
                tile_copy(at, seat_of_ref[slot]).start()
                put_cols(col_ref, 0, stat_ref[0:1, 0:1], jnp.sum(sums, axis=0, keepdims=True))

            @pl.when(jnp.logical_not(fits))
            def _():
                block = pl.ds(pl.multiple_of(rows_from, BS), BS)
                shifted_rows(x_ref.at[block, :], now, beta, part_ref)
                out = pltpu.make_async_copy(part_ref, slow_ref.at[slot], sems.at[2])
                out.start()
                shifted_cols(x_ref.at[block, :], now, alpha_ref.at[block, :], col_ref, 0)
                out.wait()

        @pl.when(b == BPD - 1)
        def _():
            cols_ref[base + y] = logs(col_ref[0, 0:1, :], col_ref[0, 1:2, :])

        return carry

    lax.fori_loop(0, BPD * count, body, 0)
    for n in range(2):

        @pl.when(tile_count[0] > n)
        def _():
            tile_copy(n, 0).wait()

    if sends is not None:
        for n in range(GROUP):
            group_out[n] = outgoing(cols_ref, peers_ref[sends * GROUP + n])


def outgoing(cols_ref, index):
    return jnp.where(index < 0, lowest, cols_ref[jnp.maximum(index, 0)])


def sweep(common, y_list, base, carried, peers=None, sends=None):
    first = carried is None
    count = BPD if first else len(y_list)
    in_specs = [SMEM, SMEM] + [VMEM] * 4
    operands = list(common)
    aliases = {}
    if not first:
        in_specs += [VMEM, SMEM, HBM, HBM]
        operands += list(carried)
        aliases = {8: 3, 9: 4}
    if sends is not None:
        in_specs.append(SMEM)
        operands.append(peers)
    in_specs += [ANY] * len(y_list)
    operands += y_list
    out_specs = [VMEM, VMEM, SMEM, HBM, HBM]
    out_shape = [
        jax.ShapeDtypeStruct((LOCAL, 128), f32),
        jax.ShapeDtypeStruct((YBLOCKS, 1, BS), f32),
        jax.ShapeDtypeStruct((SLOTS,), f32),
        pltpu.HBM((MOST, BS, BS), bf16),
        pltpu.HBM((SLOTS, BS, 128), f32),
    ]
    if sends is not None:
        out_specs.append(VMEM)
        out_shape.append(jax.ShapeDtypeStruct((GROUP, 1, BS), f32))
    return pl.pallas_call(
        functools.partial(sweep_kernel, base=base, count=count, first=first, sends=sends),
        in_specs=in_specs,
        out_specs=out_specs,
        out_shape=out_shape,
        scratch_shapes=[
            pltpu.VMEM((2, ROWS, DIM), bf16),
            pltpu.SemaphoreType.DMA((3,)),
            pltpu.VMEM((1, 8, BS), f32),
            pltpu.VMEM((LOCAL, 128), f32),
            pltpu.VMEM((BS, 128), f32),
            pltpu.VMEM((8, 128), f32),
            pltpu.VMEM((2, BS, BS), bf16),
            pltpu.SemaphoreType.DMA((2,)),
            pltpu.SMEM((1,), i32),
        ],
        input_output_aliases=aliases,
        compiler_params=params(),
        name=f"sweep_{base}",
    )(*operands)


def load_pair(slot, x_ref, y_refs, x_buf, y_buf, sems):
    rows = pl.ds(pl.multiple_of((slot % BPD) * BS, BS), BS)
    fetch = pltpu.make_async_copy(x_ref.at[rows, :], x_buf, sems.at[0])
    fetch.start()
    fetch.wait()
    for n in range(YBLOCKS):

        @pl.when(slot // BPD == n)
        def _():
            source = y_refs[0].at[n] if n < BPD else y_refs[n - BPD + 1]
            fetch = pltpu.make_async_copy(source, y_buf, sems.at[1])
            fetch.start()
            fetch.wait()


def next_potential(now, half, total, log_count):
    return 0.5 * (now + half + entropy_weight * (log_count - log_two * total))


def fetch_terms(kept_ref, terms_ref, sems, live):
    def term_copy(n):
        return pltpu.make_async_copy(kept_ref.at[n], terms_ref.at[n], sems.at[n])

    for n in range(MOST):

        @pl.when(n < live)
        def _():
            term_copy(n).start()

    return term_copy


def columns_kernel(list_ref, live_ref, use_ref, left_ref, *refs, log_count, accs):
    acc_refs = refs[:accs]
    x_rows_ref, y_rows_ref, kept_ref, slow_ref, x_ref = refs[accs : accs + 5]
    y_refs = refs[accs + 5 : accs + 6 + FAR]
    next_ref, out_ref, col_ref, weight_ref, state_ref, part_ref, x_buf, y_buf, sems, terms_ref, term_sems = refs[accs + 6 + FAR :]
    term_copy = fetch_terms(kept_ref, terms_ref, term_sems, live_ref[0])
    clear_cols(col_ref)
    total = lane_sums(acc_refs)
    state_ref[0:1, :] = jnp.where(total > 0.0, high_of(own_beta(y_rows_ref)), lowest)
    state_ref[1:2, :] = total
    for n in range(SLOTS):

        @pl.when((use_ref[n] > 0) & (left_ref[n] < 0.0))
        def _():
            fetch = pltpu.make_async_copy(slow_ref.at[n], part_ref, sems.at[0])
            fetch.start()
            fetch.wait()
            add_part(part_ref, state_ref, n % BPD)

    half = x_rows_ref[1:2, :]
    f_next = next_potential(x_rows_ref[0:1, :], half, logs(state_ref[0:1, :], state_ref[1:2, :]), log_count)
    next_ref[0:1, :] = f_next
    next_ref[1:2, :] = half
    next_ref[2:8, :] = jnp.zeros((6, LOCAL), f32)
    alpha = (f_next - half) * scale
    state_ref[2:3, :] = alpha
    top = high_of(alpha)
    weight_ref[...] = down(jnp.exp2(alpha - top))
    reach = (top - low_of(alpha))[0, 0]

    def body(step, carry):
        slot = list_ref[step]
        y, b = slot // BPD, slot % BPD
        fits = reach <= left_ref[slot]
        term_copy(step).wait()

        @pl.when(fits)
        def _():
            sums = jnp.zeros((8, BS), f32)
            for c in range(0, BS, 64):
                weight = weight_ref[pl.ds(pl.multiple_of(b * BS + c, 64), 64), :]
                parts = [fold(terms_ref[step, c : c + 64, n : n + 128].astype(f32) * weight) for n in range(0, BS, 128)]
                sums = sums + jnp.concatenate(parts, axis=1)
            put_cols(col_ref, y, top, jnp.sum(sums, axis=0, keepdims=True))

        @pl.when(jnp.logical_not(fits))
        def _():
            load_pair(slot, x_ref, y_refs, x_buf, y_buf, sems)
            for c in range(0, BS, 128):
                row = state_ref[2:3, pl.ds(pl.multiple_of(b * BS + c, 128), 128)]
                part_ref[c : c + 128, :] = jnp.broadcast_to(row, (128, 128)).T
            shifted_cols(x_buf, y_buf, part_ref, col_ref, y)

        return carry

    lax.fori_loop(0, live_ref[0], body, 0)
    for n in range(YBLOCKS):
        out_ref[n] = logs(col_ref[n, 0:1, :], col_ref[n, 1:2, :])


def gathered(j, own_ref, came, who_ref):
    terms = [own_ref[j]] + [jnp.where(who_ref[n] == j, came(n), lowest) for n in range(PEERS)]
    top = terms[0]
    for term in terms[1:]:
        top = jnp.maximum(top, term)
    total = jnp.exp2(terms[0] - top)
    for term in terms[1:]:
        total = total + jnp.exp2(term - top)
    return top + jnp.log2(total)


def home_kernel(who_ref, peers_ref, even_in, odd_in, first_ref, second_ref, y_rows_ref, even_out, odd_out, g_ref, *, log_count):
    came = lambda n: (even_in, odd_in)[n // GROUP][n % GROUP]
    betas = []
    for j in range(BPD):
        span = slice(j * BS, (j + 1) * BS)
        half = y_rows_ref[1:2, span]
        g_next = next_potential(y_rows_ref[0:1, span], half, gathered(j, first_ref, came, who_ref), log_count)
        g_ref[0:1, span] = g_next
        betas.append((g_next - half) * scale)
        g_ref[1:2, span] = betas[j]
    g_ref[2:8, :] = jnp.zeros((6, LOCAL), f32)
    for n in range(PEERS):
        out = (even_out, odd_out)[n // GROUP]
        out[n % GROUP, 0:1, :] = jnp.where(who_ref[n] == 1, betas[1], betas[0])
        out[n % GROUP, 1:2, :] = outgoing(second_ref, peers_ref[n])


def home(who, peers, rows_in, first, second, y_rows, log_count):
    return pl.pallas_call(
        functools.partial(home_kernel, log_count=log_count),
        in_specs=[SMEM, SMEM] + [VMEM] * 5,
        out_specs=[VMEM] * 3,
        out_shape=[jax.ShapeDtypeStruct((GROUP, 2, BS), f32)] * 2 + [jax.ShapeDtypeStruct((8, LOCAL), f32)],
        compiler_params=params(),
        name="home",
    )(who, peers, *rows_in, first, second, y_rows)


def rows_kernel(list_ref, live_ref, use_ref, left_ref, from_ref, who_ref, *refs, log_count):
    even_in, odd_in, g_ref, second_ref, y_rows_ref, x_rows_ref, kept_ref, slow_ref, x_ref = refs[:9]
    y_refs = refs[9 : 10 + FAR]
    f_ref, g_out_ref, acc_ref, beta_ref, weight_ref, state_ref, part_ref, x_buf, y_buf, sems, terms_ref, term_sems = refs[10 + FAR :]
    term_copy = fetch_terms(kept_ref, terms_ref, term_sems, live_ref[0])
    shift = high_of(g_ref[1:2, :])
    acc_ref[...] = jnp.zeros((LOCAL, 128), f32)
    state_ref[0:1, :] = jnp.full((1, LOCAL), lowest, f32)
    state_ref[1:2, :] = jnp.zeros((1, LOCAL), f32)
    for n in range(BPD):
        beta_ref[n] = g_ref[1:2, n * BS : (n + 1) * BS]
    for n in range(BPD, YBLOCKS):
        source = from_ref[n]
        at = source % GROUP
        beta_ref[n] = jnp.where(source < GROUP, even_in[at, 0:1, :], odd_in[at, 0:1, :])
    weight_ref[...] = jnp.exp2(beta_ref[...] - shift)

    def body(step, carry):
        slot = list_ref[step]
        y, b = slot // BPD, slot % BPD
        beta = beta_ref[y]
        reach = jnp.maximum(high_of(beta) - shift, shift - low_of(beta))
        fits = reach[0, 0] <= left_ref[slot]
        term_copy(step).wait()

        @pl.when(fits)
        def _():
            weight = weight_ref[y]
            for c in range(0, BS, 64):
                span = pl.ds(pl.multiple_of(b * BS + c, 64), 64)
                part = acc_ref[span, :]
                for n in range(0, BS, 128):
                    part = part + terms_ref[step, c : c + 64, n : n + 128].astype(f32) * weight[:, n : n + 128]
                acc_ref[span, :] = part

        @pl.when(jnp.logical_not(fits))
        def _():
            load_pair(slot, x_ref, y_refs, x_buf, y_buf, sems)
            shifted_rows(x_buf, y_buf, beta, part_ref)
            add_part(part_ref, state_ref, b)

        return carry

    lax.fori_loop(0, live_ref[0], body, 0)
    total = lane_sums([acc_ref])
    top = jnp.where(total > 0.0, shift, lowest)
    top, total = merge(top, total, state_ref[0:1, :], state_ref[1:2, :])
    f_ref[...] = next_potential(x_rows_ref[0:1, :], x_rows_ref[1:2, :], logs(top, total), log_count)
    came = lambda n: (even_in, odd_in)[n // GROUP][n % GROUP, 1:2, :]
    total = jnp.concatenate([gathered(j, second_ref, came, who_ref) for j in range(BPD)], axis=1)
    g_next = next_potential(g_ref[0:1, :], y_rows_ref[1:2, :], total, log_count)
    g_out_ref[...] = moved_exact(g_next, y_rows_ref[2:3, :].astype(i32))


def slots_call(kernel, smem, front, kept, slow, x_blocks, y_list, outs, scratch, name):
    return pl.pallas_call(
        kernel,
        in_specs=[SMEM] * len(smem) + [VMEM] * len(front) + [HBM, HBM, ANY] + [ANY] * len(y_list),
        out_specs=[VMEM] * len(outs),
        scratch_shapes=scratch
        + [
            pltpu.VMEM((BS, 128), f32),
            pltpu.VMEM((BS, DIM), bf16),
            pltpu.VMEM((ROWS, DIM), bf16),
            pltpu.SemaphoreType.DMA((2,)),
            pltpu.VMEM((MOST, BS, BS), bf16),
            pltpu.SemaphoreType.DMA((MOST,)),
        ],
        out_shape=outs,
        compiler_params=params(),
        name=name,
    )(*smem, *front, kept, slow, x_blocks, *y_list)


def seat_tables():
    half = GROUP // 2
    offsets = np.zeros((GROUP, PEERS), np.int32)
    source = np.zeros((GROUP, YBLOCKS), np.int32)
    for seat in range(GROUP):
        odd_seat = (seat + half) % GROUP
        for other in range(GROUP):
            if other != seat and abs(other - seat) <= REACH:
                offsets[seat, other] = other - seat
            off = other - odd_seat
            if off != 0 and abs(off) <= REACH and not 0 <= seat + off < GROUP:
                offsets[seat, GROUP + other] = off
        for k, off in enumerate(ROUNDS[seat % 4]):
            source[seat, BPD + k] = list(offsets[seat]).index(off)
    index = np.full((GROUP, PEERS), -1, np.int32)
    for seat in range(GROUP):
        for k, off in enumerate(ROUNDS[seat % 4]):
            index[seat, offsets[seat] == off] = BPD + k
    return offsets, index, source


def swap(rows, devices, shift):
    groups = [[(GROUP * k + j + shift) % devices for j in range(GROUP)] for k in range(devices // GROUP)]
    return lax.all_to_all(rows, "blk", split_axis=0, concat_axis=0, tiled=True, axis_index_groups=groups)


def on_device(x_points, y_points, x_start, y_start, x_order, y_order, partners, counts):
    devices = lax.axis_size("blk")
    me = lax.axis_index("blk").astype(i32)
    log_count = math.log(LOCAL * devices)
    here = me[None]
    line = lambda v: v.reshape(1, LOCAL)

    y_sent, x_pos = pack_y(here, partners, counts, line(y_order), line(x_order), y_start, x_start, y_points, devices)
    y_came = lax.all_to_all(y_sent, "blk", split_axis=0, concat_axis=0, tiled=True)
    x_sent = pack_x(x_pos, x_points)
    x_came = lax.all_to_all(x_sent, "blk", split_axis=0, concat_axis=0, tiled=True)
    y_came, x_sent = lax.optimization_barrier((y_came, x_sent))
    y_rows, table, y_own, *y_sends = unpack_y(here, y_came, devices)

    def far_block(k):
        pairs = [(i, i + ROUNDS[i % 4][k]) for i in range(devices) if 0 <= i + ROUNDS[i % 4][k] < devices]
        return lax.ppermute(y_sends[k], "blk", pairs)

    y_far = [far_block(k) for k in range(FAR)]
    x_blocks, alpha, x_rows = unpack_x(x_came, table)

    offsets = lax.dynamic_slice(jnp.array(ROUNDS, i32), (me % 4, 0), (1, FAR))[0]
    live = jnp.arange(partners.shape[1], dtype=i32)[None, :] < counts[:, None]
    away = jnp.where(live, partners // BPD - me, devices)
    local_use = [((away == 0) & (partners % BPD == j)).any(axis=1) for j in range(BPD)]
    far = away[None, :, :] == offsets[:, None, None]
    use = jnp.concatenate([jnp.stack(local_use), far.any(axis=2)]).astype(i32).reshape(SLOTS)
    number = jnp.minimum(jnp.maximum(jnp.cumsum(use) - 1, 0), MOST - 1)
    count = jnp.minimum(jnp.sum(use), MOST)
    step = jnp.minimum(jnp.arange(MOST, dtype=i32), count - 1)
    at = (number[None, :] == step[:, None]) & (use[None, :] > 0)
    slots = jnp.sum(jnp.where(at, jnp.arange(SLOTS, dtype=i32)[None, :], 0), axis=1)
    lists = [slots, count[None]]

    peer_offsets, peer_index, peer_source = seat_tables()
    row = lambda t: lax.dynamic_slice(jnp.asarray(t), (me % GROUP, 0), (1, t.shape[1]))[0]
    peers, source, off = row(peer_index), row(peer_source), row(peer_offsets)
    peer = me + off
    wants = (table[:, 3 * (LOCAL // devices)] > 0.5).astype(i32)
    valid = (off != 0) & (peer >= 0) & (peer < devices)
    who = jnp.where(valid, wants[jnp.clip(peer, 0, devices - 1)], -1)

    common = (use, number, x_blocks, alpha, x_rows, y_rows)
    acc_0, *carried = sweep(common, [y_own], 0, None)
    acc_1, *carried = sweep(common, y_far[:EARLY], BPD, carried)
    acc_2, *carried, odd_out = sweep(common, y_far[EARLY:-1], BPD + EARLY, carried, peers, 1)
    acc_3, cols_first, left, kept, slow, even_out = sweep(common, y_far[-1:], YBLOCKS - 1, carried, peers, 0)
    y_all = [y_own] + y_far

    odd_in = swap(odd_out, devices, GROUP // 2)
    even_in = swap(even_out, devices, 0)
    accs = [acc_0, acc_1, acc_2, acc_3]
    x_next, cols_second = slots_call(
        functools.partial(columns_kernel, log_count=log_count, accs=len(accs)),
        lists + [use, left],
        accs + [x_rows, y_rows],
        kept,
        slow,
        x_blocks,
        y_all,
        [jax.ShapeDtypeStruct((8, LOCAL), f32), jax.ShapeDtypeStruct((YBLOCKS, 1, BS), f32)],
        [pltpu.VMEM((YBLOCKS, 8, BS), f32), pltpu.VMEM((LOCAL, 128), f32), pltpu.VMEM((8, LOCAL), f32)],
        "columns",
    )
    even_out, odd_out, g_one = home(who, peers, (even_in, odd_in), cols_first, cols_second, y_rows, log_count)
    rows_in = (swap(even_out, devices, 0), swap(odd_out, devices, GROUP // 2))
    f_two, g_two = slots_call(
        functools.partial(rows_kernel, log_count=log_count),
        lists + [use, left, source, who],
        [*rows_in, g_one, cols_second, y_rows, x_next],
        kept,
        slow,
        x_blocks,
        y_all,
        [jax.ShapeDtypeStruct((1, LOCAL), f32)] * 2,
        [
            pltpu.VMEM((LOCAL, 128), f32),
            pltpu.VMEM((YBLOCKS, 1, BS), f32),
            pltpu.VMEM((YBLOCKS, 1, BS), f32),
            pltpu.VMEM((8, LOCAL), f32),
        ],
        "rows",
    )
    return f_two.reshape(LOCAL), g_two.reshape(LOCAL)


def solution(mesh):
    placed_as = (
        P("blk", None),
        P("blk", None),
        P("blk"),
        P("blk"),
        P("blk"),
        P("blk"),
        P("blk", None),
        P("blk"),
    )
    return jax.shard_map(
        on_device, mesh=mesh, in_specs=placed_as, out_specs=(P("blk"), P("blk")), check_vma=False
    )
```

```python
import functools
import math

import jax
import jax.numpy as jnp
import numpy as np
from jax import lax
from jax.experimental import pallas as pl
from jax.experimental.pallas import tpu as pltpu
from jax.sharding import PartitionSpec as P

DIM = 512
BS = 1024
BPD = 2
REACH = 3
LOCAL = BPD * BS
EXTRA = 128
WIDE = DIM + EXTRA
TAIL = 16
ROWS = BS + TAIL
CHUNK = 512
PART = 256
ROUNDS = ((1, 3, -1, -2, -3, 2), (-1, -3, 1, -2, 3, 2), (1, 3, -1, 2, -3, -2), (-1, -3, 1, 2, 3, -2))
EARLY = 3
FAR = len(ROUNDS[0])
YBLOCKS = BPD + FAR
SLOTS = BPD * YBLOCKS
MOST = 12
GROUP = 8
PEERS = 2 * GROUP
X_LANES = EXTRA // 2

entropy_weight = 0.05
scale = math.log2(math.e) / entropy_weight
log_two = math.log(2.0)
lowest = -1e30
exponent_room = 112.0
mebi = 1024 * 1024

f32 = jnp.float32
bf16 = jnp.bfloat16
i32 = jnp.int32

SMEM = pl.BlockSpec(memory_space=pltpu.SMEM)
ANY = pl.BlockSpec(memory_space=pl.ANY)
VMEM = pl.BlockSpec(memory_space=pltpu.VMEM)
HBM = pl.BlockSpec(memory_space=pltpu.HBM)


def iota(shape, dim):
    return lax.broadcasted_iota(i32, shape, dim)


def dot(a, b):
    return jnp.dot(a, b, preferred_element_type=f32)


def nt_dot(a, b):
    return lax.dot_general(a, b, (((1,), (1,)), ((), ())), preferred_element_type=f32)


def ones_where(mask):
    return jnp.where(mask, 1.0, 0.0).astype(bf16)


def params():
    return pltpu.CompilerParams(vmem_limit_bytes=64 * mebi)


def whole(shape):
    return pl.BlockSpec(shape, lambda *t: (0,) * len(shape))


def laid_out(square):
    return jnp.concatenate([square[n : n + 1, :] for n in range(square.shape[0])], axis=1)


def down(row):
    parts = [jnp.broadcast_to(row[:, c : c + 128], (128, 128)).T for c in range(0, row.shape[1], 128)]
    return jnp.concatenate(parts, axis=0)


def moved(values, place):
    high = iota((16, LOCAL), 0) == lax.shift_right_logical(place, 7)
    low = ones_where(iota((128, LOCAL), 0) == jnp.bitwise_and(place, 127))
    stack = jnp.concatenate([jnp.where(high, v, 0.0) for v in values], axis=0).astype(bf16)
    out = nt_dot(stack, low)
    return [laid_out(out[16 * n : 16 * n + 16, :]) for n in range(len(values))]


def moved_exact(value, place):
    first = value.astype(bf16).astype(f32)
    second = (value - first).astype(bf16).astype(f32)
    parts = moved([first, second, value - first - second], place)
    return parts[0] + parts[1] + parts[2]


def before_matrix():
    return ones_where(iota((128, 128), 0) < iota((128, 128), 1))


def plan(order, start, devices, first_lane):
    share = LOCAL // devices
    target = lax.shift_right_logical(order, 11)
    hit = iota((devices, LOCAL), 0) == target
    hot = ones_where(hit)
    before = before_matrix()
    every = jnp.ones((128, 128), bf16)
    seen = jnp.zeros((devices, 128), f32)
    earlier = []
    for c in range(0, LOCAL, 128):
        piece = hot[:, c : c + 128]
        earlier.append(dot(piece, before) + seen)
        seen = seen + dot(piece, every)
    earlier = jnp.concatenate(earlier, axis=1)
    rank = jnp.sum(jnp.where(hit, earlier, 0.0), axis=0, keepdims=True).astype(i32)
    within = jnp.bitwise_and(order, LOCAL - 1)
    high = lax.shift_right_logical(within, 6).astype(f32)
    low = jnp.bitwise_and(within, 63).astype(f32)
    row = iota((EXTRA, LOCAL), 0) - first_lane
    field = row // share
    value = jnp.where(field == 0, high, jnp.where(field == 1, low, start))
    mine = (row >= 0) & (row < 3 * share) & (row % share == rank)
    return target * share + rank, nt_dot(hot, jnp.where(mine, value, 0.0).astype(bf16))


def partner_offsets(me):
    kind = jnp.bitwise_and(me, 3)
    out = []
    for k in range(FAR):
        value = jnp.int32(ROUNDS[0][k])
        for n in range(1, 4):
            value = jnp.where(kind == n, jnp.int32(ROUNDS[n][k]), value)
        out.append(value)
    return out


def pack_y_kernel(
    me_ref, partners_ref, counts_ref, y_order, x_order, y_start, x_start, points, out_ref, x_pos_ref, pos_ref, table_ref,
    *, devices
):
    step = pl.program_id(0)
    share = LOCAL // devices

    @pl.when(step == 0)
    def _():
        y_pos, y_table = plan(y_order[...], y_start[...].astype(f32).reshape(1, LOCAL), devices, 0)
        x_pos, x_table = plan(x_order[...], x_start[...].astype(f32).reshape(1, LOCAL), devices, X_LANES)
        pos_ref[...] = y_pos
        x_pos_ref[...] = x_pos
        me = me_ref[0]
        offsets = partner_offsets(me)
        need = [jnp.int32(0)] * FAR
        for b in range(BPD):
            for s in range(partners_ref.shape[1]):
                block = partners_ref[b, s]
                away = lax.shift_right_logical(block, 1) - me
                for k in range(FAR):
                    listed = (s < counts_ref[b]) & (away == offsets[k])
                    need[k] = jnp.where(listed, jnp.bitwise_and(block, 1), need[k])
        table = y_table + x_table
        row, lane = iota(table.shape, 0), iota(table.shape, 1)
        for k in range(FAR):
            table = jnp.where((row == me + offsets[k]) & (lane == 3 * share), need[k].astype(f32), table)
        table_ref[...] = table

    base = step * CHUNK
    hot = ones_where(iota((CHUNK, LOCAL), 0) + base == pos_ref[...])
    out_ref[:, :DIM] = dot(hot, points[...]).astype(bf16)
    some = CHUNK // share
    table = table_ref[pl.ds(pl.multiple_of(step * some, some), some), :]
    out_ref[:, DIM:] = jnp.broadcast_to(table[:, None, :], (some, share, EXTRA)).reshape(CHUNK, EXTRA).astype(bf16)


def pack_y(me, partners, counts, y_order, x_order, y_start, x_start, points, devices):
    row = whole((1, LOCAL))
    return pl.pallas_call(
        functools.partial(pack_y_kernel, devices=devices),
        grid=(LOCAL // CHUNK,),
        in_specs=[SMEM, SMEM, SMEM, row, row, whole((LOCAL,)), whole((LOCAL,)), whole((LOCAL, DIM))],
        out_specs=[pl.BlockSpec((CHUNK, WIDE), lambda t: (t, 0)), row],
        out_shape=[pltpu.HBM((LOCAL, WIDE), bf16), jax.ShapeDtypeStruct((1, LOCAL), i32)],
        scratch_shapes=[pltpu.VMEM((1, LOCAL), i32), pltpu.VMEM((devices, EXTRA), f32)],
        compiler_params=params(),
        name="pack_y",
    )(me, partners, counts, y_order, x_order, y_start, x_start, points)


def pack_x_kernel(pos_ref, points_ref, out_ref):
    base = pl.program_id(0) * CHUNK
    hot = ones_where(iota((CHUNK, LOCAL), 0) + base == pos_ref[...])
    out_ref[...] = dot(hot, points_ref[...]).astype(bf16)


def pack_x(pos, points):
    return pl.pallas_call(
        pack_x_kernel,
        grid=(LOCAL // CHUNK,),
        in_specs=[whole((1, LOCAL)), whole((LOCAL, DIM))],
        out_specs=pl.BlockSpec((CHUNK, DIM), lambda t: (t, 0)),
        out_shape=pltpu.HBM((LOCAL, DIM), bf16),
        compiler_params=params(),
        name="pack_x",
    )(pos, points)


WINDOW = PART + 16
HELD = BS + WINDOW + 16


def arrived(table, base, with_low):
    share = 16
    row, lane = iota((EXTRA, EXTRA), 0), iota((EXTRA, EXTRA), 1)
    pick = jnp.where(row == base + lane % share, 64.0 if with_low else 1.0, 0.0)
    if with_low:
        pick = jnp.where(row == base + share + lane % share, 1.0, pick)
    values = dot(table, pick.astype(bf16))
    values = jnp.where(row % (EXTRA // share) == lane // share, values, 0.0)
    return jnp.sum(values.reshape(LOCAL // 128, EXTRA // share, 128), axis=1)


def unpack_y_kernel(me_ref, came_ref, rows_ref, table_ref, own_ref, *rest, devices):
    sends = rest[:FAR]
    held, sems, own_sem, points_buf, extra_buf, in_sems = rest[FAR:]
    share = LOCAL // devices
    me = me_ref[0]
    extra_in = pltpu.make_async_copy(came_ref.at[:, pl.ds(DIM, EXTRA)], extra_buf, in_sems.at[0])
    points_in = pltpu.make_async_copy(came_ref.at[:, pl.ds(0, DIM)], points_buf, in_sems.at[1])
    extra_in.start()
    points_in.start()
    held[...] = jnp.zeros(held.shape, bf16)
    extra_in.wait()
    table = dot(ones_where(iota((devices, LOCAL), 1) == iota((devices, LOCAL), 0) * share), extra_buf[...])
    table_ref[...] = table
    place_square = arrived(table.astype(bf16), 0, True)
    place = laid_out(place_square)
    start = laid_out(arrived(table.astype(bf16), 2 * share, False))

    picks = []
    offsets = partner_offsets(me)
    small_row, small_lane = iota((devices, EXTRA), 0), iota((devices, EXTRA), 1)
    for k in range(FAR):
        here = (small_row == me + offsets[k]) & (small_lane == 3 * share)
        picks.append(jnp.sum(jnp.where(here, table, 0.0)) > 0.5)

    second = place >= float(BS)
    square = ones_where(place_square >= float(BS))
    totals = dot(square, jnp.ones((128, 128), bf16)).astype(bf16)
    earlier = dot(square, before_matrix()) + dot(ones_where(iota((16, 16), 1) < iota((16, 16), 0)), totals)
    ones_before = laid_out(earlier)
    dest = jnp.where(second, ones_before, iota((1, LOCAL), 1).astype(f32) - ones_before).astype(i32)
    seat = jnp.where(second, dest + BS, dest)
    position = place.astype(i32)
    start_row, high_row, low_row = moved(
        [start, lax.shift_right_logical(position, 6).astype(f32), jnp.bitwise_and(position, 63).astype(f32)], seat
    )
    rows_ref[0:1, :] = start_row
    rows_ref[2:3, :] = high_row * 64.0 + low_row
    rows_ref[3:8, :] = jnp.zeros((5, LOCAL), f32)
    sixteen, lane16 = iota((16, 128), 0), iota((16, 128), 1)
    points_in.wait()

    for j in range(BPD):
        here = jnp.where(second if j else jnp.logical_not(second), dest, -1)
        for c in range(LOCAL // PART):
            span = slice(c * PART, (c + 1) * PART)
            begin = jnp.sum(jnp.where((sixteen == c * PART // 128) & (lane16 == 0), earlier, 0.0)).astype(i32)
            if j == 0:
                begin = c * PART - begin
            begin = pl.multiple_of(lax.shift_left(lax.shift_right_logical(begin, 4), 4), 16)
            hot = ones_where(iota((WINDOW, PART), 0) + begin == here[:, span])
            part = dot(hot, points_buf[span, :]).astype(bf16)
            held[j, pl.ds(begin, WINDOW), :] = held[j, pl.ds(begin, WINDOW), :] + part
        half = []
        for c in range(0, BS, PART):
            points = held[j, c : c + PART, :].astype(f32)
            total = 0.5 * jnp.sum(points * points, axis=1, keepdims=True)
            half.append(jnp.broadcast_to(total, (PART, 128)).T[0:1, :])
        half = jnp.concatenate(half, axis=1)
        block = slice(j * BS, (j + 1) * BS)
        rows_ref[1:2, block] = half
        beta = start_row[:, block] - half
        first = beta.astype(bf16).astype(f32)
        next_part = (beta - first).astype(bf16).astype(f32)
        most = jnp.max(half, axis=1, keepdims=True) * 1.01
        sub = iota((TAIL, DIM), 0)
        tail = jnp.zeros((TAIL, DIM), f32) + most
        for n, piece in enumerate((first, next_part, beta - first - next_part)):
            tail = jnp.where(sub == 2 * n, piece[:, :DIM], tail)
            tail = jnp.where(sub == 2 * n + 1, piece[:, DIM:], tail)
        held[j, BS:ROWS, :] = tail.astype(bf16)
        done = held.at[j, pl.ds(0, ROWS), :]
        for k in range(FAR):
            wanted = picks[k] if j == 1 else jnp.logical_not(picks[k])

            @pl.when(wanted)
            def _():
                pltpu.make_async_copy(done, sends[k], sems.at[k]).start()

        pltpu.make_async_copy(done, own_ref.at[j], own_sem.at[j]).start()

    done = held.at[0, pl.ds(0, ROWS), :]
    for k in range(FAR):
        pltpu.make_async_copy(done, sends[k], sems.at[k]).wait()
    for j in range(BPD):
        pltpu.make_async_copy(done, own_ref.at[j], own_sem.at[j]).wait()


def unpack_y(me, came, devices):
    return pl.pallas_call(
        functools.partial(unpack_y_kernel, devices=devices),
        in_specs=[SMEM, ANY],
        out_specs=[VMEM, VMEM] + [HBM] * (1 + FAR),
        out_shape=[
            jax.ShapeDtypeStruct((8, LOCAL), f32),
            jax.ShapeDtypeStruct((devices, EXTRA), f32),
            pltpu.HBM((BPD, ROWS, DIM), bf16),
        ]
        + [pltpu.HBM((ROWS, DIM), bf16)] * FAR,
        scratch_shapes=[
            pltpu.VMEM((BPD, HELD, DIM), bf16),
            pltpu.SemaphoreType.DMA((FAR,)),
            pltpu.SemaphoreType.DMA((BPD,)),
            pltpu.VMEM((LOCAL, DIM), bf16),
            pltpu.VMEM((LOCAL, EXTRA), bf16),
            pltpu.SemaphoreType.DMA((2,)),
        ],
        compiler_params=params(),
        name="unpack_y",
    )(me, came)


def unpack_x_kernel(came_ref, table_ref, points_ref, alpha_ref, rows_ref, place_ref, start_ref):
    step = pl.program_id(0)

    @pl.when(step == 0)
    def _():
        table = table_ref[...].astype(bf16)
        place = laid_out(arrived(table, X_LANES, True)).astype(i32)
        place_ref[...] = place
        start_ref[...] = moved([laid_out(arrived(table, X_LANES + 32, False))], place)[0]

    base = step * CHUNK
    hot = ones_where(iota((CHUNK, LOCAL), 0) + base == place_ref[...])
    points = dot(hot, came_ref[...])
    points_ref[...] = points.astype(bf16)
    half = jnp.broadcast_to(0.5 * jnp.sum(points * points, axis=1, keepdims=True), (CHUNK, 128))
    start = start_ref[:, pl.ds(pl.multiple_of(base, CHUNK), CHUNK)]
    alpha_ref[...] = (down(start) - half) * scale
    rows_ref[0:1, :] = start
    rows_ref[1:8, :] = jnp.concatenate([half[c : c + 128, :].T[0:7, :] for c in range(0, CHUNK, 128)], axis=1)


def unpack_x(came, table):
    return pl.pallas_call(
        unpack_x_kernel,
        grid=(LOCAL // CHUNK,),
        in_specs=[whole((LOCAL, DIM)), whole((EXTRA, EXTRA))],
        out_specs=[
            pl.BlockSpec((CHUNK, DIM), lambda t: (t, 0)),
            pl.BlockSpec((CHUNK, 128), lambda t: (t, 0)),
            pl.BlockSpec((8, CHUNK), lambda t: (0, t)),
        ],
        out_shape=[
            pltpu.HBM((LOCAL, DIM), bf16),
            pltpu.HBM((LOCAL, 128), f32),
            jax.ShapeDtypeStruct((8, LOCAL), f32),
        ],
        scratch_shapes=[pltpu.VMEM((1, LOCAL), i32), pltpu.VMEM((1, LOCAL), f32)],
        compiler_params=params(),
        name="unpack_x",
    )(came, table)


def merge(top, total, other_top, other_total):
    new = jnp.maximum(top, other_top)
    return new, total * jnp.exp2(top - new) + other_total * jnp.exp2(other_top - new)


def logs(top, total):
    return jnp.where(total > 0.0, top + jnp.log2(total), lowest)


def high_of(row):
    return jnp.max(row, axis=1, keepdims=True)


def low_of(row):
    return jnp.min(row, axis=1, keepdims=True)


def put_cols(col_ref, y, part_top, part_total):
    top, total = merge(col_ref[y, 0:1, :], col_ref[y, 1:2, :], part_top, part_total)
    col_ref[y, 0:1, :] = top
    col_ref[y, 1:2, :] = total


def clear_cols(col_ref):
    col_ref[:, 0:1, :] = jnp.full((col_ref.shape[0], 1, BS), lowest, f32)
    col_ref[:, 1:2, :] = jnp.zeros((col_ref.shape[0], 1, BS), f32)


def shifted_rows(x_ref, y_ref, beta, part_ref):
    def body(c, carry):
        span = pl.ds(pl.multiple_of(c * PART, PART), PART)
        terms = nt_dot(x_ref[span, :], y_ref[0:BS, :]) * scale + beta
        top = jnp.max(terms, axis=1, keepdims=True)
        total = jnp.sum(jnp.exp2(terms - top), axis=1, keepdims=True)
        part_ref[span, :] = jnp.where(iota((PART, 128), 1) == 0, top, total)
        return carry

    lax.fori_loop(0, BS // PART, body, 0)


def shifted_cols(x_ref, y_ref, alpha_ref, col_ref, y):
    def body(c, carry):
        span = pl.ds(pl.multiple_of(c * PART, PART), PART)
        terms = nt_dot(x_ref[span, :], y_ref[0:BS, :]) * scale + alpha_ref[span, 0:1]
        top = jnp.max(terms, axis=0, keepdims=True)
        put_cols(col_ref, y, top, jnp.sum(jnp.exp2(terms - top), axis=0, keepdims=True))
        return carry

    lax.fori_loop(0, BS // PART, body, 0)


def add_part(part_ref, state_ref, b):
    for c in range(0, BS, 128):
        part = part_ref[c : c + 128, :].T
        span = pl.ds(pl.multiple_of(b * BS + c, 128), 128)
        top, total = merge(state_ref[0:1, span], state_ref[1:2, span], part[0:1, :], part[1:2, :])
        state_ref[0:1, span] = top
        state_ref[1:2, span] = total


def lane_sums(refs):
    out = []
    for c in range(0, LOCAL, 128):
        part = refs[0][c : c + 128, :]
        for ref in refs[1:]:
            part = part + ref[c : c + 128, :]
        out.append(jnp.sum(part.T, axis=0, keepdims=True))
    return jnp.concatenate(out, axis=1)


def fold(values):
    return jnp.sum(values.reshape(values.shape[0] // 8, 8, 128), axis=0)


def own_beta(y_rows_ref):
    return (y_rows_ref[0:1, :] - y_rows_ref[1:2, :]) * scale


def sweep_kernel(*refs, base, count, first, sends):
    use_ref, seat_of_ref, x_ref, alpha_ref = refs[:4]
    refs = refs[4:]
    if first:
        x_rows_ref, y_rows_ref = refs[:2]
        refs = refs[2:]
    else:
        cols_in, left_in, stat_in = refs[:3]
        refs = refs[5:]
    if sends is not None:
        peers_ref = refs[0]
        refs = refs[1:]
    y_refs = refs[:1] if first else refs[:count]
    refs = refs[len(y_refs) :]
    acc_ref, cols_ref, left_ref, stat_ref, kept_ref, slow_ref = refs[:6]
    refs = refs[6:]
    if sends is not None:
        group_out = refs[0]
        refs = refs[1:]
    x_buf, alpha_buf, x_sems, y_buf, sems, col_ref, weight_ref, part_ref, beta_ref, fit_ref, room_ref, tiles, tile_sems, tile_count = refs

    def copy(n):
        source = y_refs[0].at[n] if first else y_refs[n]
        return pltpu.make_async_copy(source, y_buf.at[n % 2], sems.at[n % 2])

    def x_copies(n):
        rows = pl.ds(n * BS, BS)
        return (
            pltpu.make_async_copy(x_ref.at[rows, :], x_buf.at[rows, :], x_sems.at[n, 0]),
            pltpu.make_async_copy(alpha_ref.at[rows, :], alpha_buf.at[rows, :], x_sems.at[n, 1]),
        )

    copy(0).start()
    for n in range(BPD):
        for part in x_copies(n):
            part.start()
    tile_count[0] = 0
    acc_ref[...] = jnp.zeros((LOCAL, 128), f32)

    def tile_copy(at, seat):
        return pltpu.make_async_copy(tiles.at[at], kept_ref.at[seat], tile_sems.at[at])

    if first:
        for n in range(SLOTS):
            left_ref[n] = -1.0
        alpha = (x_rows_ref[0:1, :] - x_rows_ref[1:2, :]) * scale
        alpha_top = high_of(alpha)
        lane = iota((8, 128), 1)
        beta_top = high_of(own_beta(y_rows_ref))
        most = high_of(x_rows_ref[1:2, :]) * 1.01
        spread = alpha_top - low_of(alpha)
        stat_ref[...] = jnp.where(
            lane == 0, alpha_top, jnp.where(lane == 1, spread, jnp.where(lane == 2, most, beta_top))
        )
    else:
        for n in range(SLOTS):
            left_ref[n] = left_in[n]
        cols_ref[...] = cols_in[...]
        stat_ref[...] = stat_in[...]

    def body(step, carry):
        y, b = step // BPD, step % BPD
        slot = base * BPD + step
        for n in range(count):

            @pl.when(step == BPD * n)
            def _():
                copy(n).wait()
                if n + 1 < count:
                    copy(n + 1).start()

        for n in range(BPD):

            @pl.when(step == n)
            def _():
                for part in x_copies(n):
                    part.wait()
                rows = slice(n * BS, (n + 1) * BS)
                weight_ref[rows, :] = jnp.exp2(alpha_buf[rows, :] - stat_ref[0:1, 0:1])

        now = y_buf.at[y % 2]
        rows_from = b * BS

        @pl.when(b == 0)
        def _():
            clear_cols(col_ref)
            tail = now[BS:ROWS, :].astype(f32)
            halves = [tail[n : n + 1, :] + tail[n + 2 : n + 3, :] + tail[n + 4 : n + 5, :] for n in range(2)]
            beta = jnp.concatenate(halves, axis=1) * scale
            shift = stat_ref[0:1, 3:4]
            left = exponent_room - 2.0 * scale * jnp.sqrt(tail[6:7, 0:1] * stat_ref[0:1, 2:3])
            reach = jnp.maximum(stat_ref[0:1, 1:2], jnp.maximum(high_of(beta) - shift, shift - low_of(beta)))
            beta_ref[0:1, :] = beta
            beta_ref[1:2, :] = jnp.exp2(beta - shift)
            room_ref[0] = left[0, 0]
            fit_ref[0] = jnp.where((left - reach)[0, 0] >= 0.0, 1, 0)

        @pl.when(use_ref[slot] > 0)
        def _():
            fits = fit_ref[0] > 0

            @pl.when(fits)
            def _():
                left_ref[slot] = room_ref[0]
                done = tile_count[0]
                tile_count[0] = done + 1
                at = done % 2

                @pl.when(done > 1)
                def _():
                    tile_copy(at, 0).wait()

                weight = beta_ref[1:2, :]
                sums = jnp.zeros((8, BS), f32)
                for c in range(0, BS, PART):
                    span = pl.ds(pl.multiple_of(rows_from + c, PART), PART)
                    terms = jnp.exp2(nt_dot(x_buf[span, :], now[0:BS, :]) * scale)
                    tiles[at, c : c + PART, :] = terms.astype(bf16)
                    row_part = acc_ref[span, :]
                    col_parts = []
                    for n in range(0, BS, 128):
                        piece = terms[:, n : n + 128]
                        row_part = row_part + piece * weight[:, n : n + 128]
                        col_parts.append(fold(piece * weight_ref[span, :]))
                    acc_ref[span, :] = row_part
                    sums = sums + jnp.concatenate(col_parts, axis=1)
                tile_copy(at, seat_of_ref[slot]).start()
                put_cols(col_ref, 0, stat_ref[0:1, 0:1], jnp.sum(sums, axis=0, keepdims=True))

            @pl.when(jnp.logical_not(fits))
            def _():
                block = pl.ds(pl.multiple_of(rows_from, BS), BS)
                shifted_rows(x_buf.at[block, :], now, beta_ref[0:1, :], part_ref)
                out = pltpu.make_async_copy(part_ref, slow_ref.at[slot], sems.at[2])
                out.start()
                shifted_cols(x_buf.at[block, :], now, alpha_buf.at[block, :], col_ref, 0)
                out.wait()

        @pl.when(b == BPD - 1)
        def _():
            cols_ref[base + y] = logs(col_ref[0, 0:1, :], col_ref[0, 1:2, :])

        return carry

    lax.fori_loop(0, BPD * count, body, 0)
    for n in range(2):

        @pl.when(tile_count[0] > n)
        def _():
            tile_copy(n, 0).wait()

    if sends is not None:
        for n in range(GROUP):
            group_out[n] = outgoing(cols_ref, peers_ref[sends * GROUP + n])


def outgoing(cols_ref, index):
    return jnp.where(index < 0, lowest, cols_ref[jnp.maximum(index, 0)])


def sweep(common, y_list, base, carried, rows=None, peers=None, sends=None):
    first = carried is None
    count = BPD if first else len(y_list)
    in_specs = [SMEM, SMEM, HBM, HBM]
    operands = list(common)
    aliases = {}
    if first:
        in_specs += [VMEM, VMEM]
        operands += rows
    else:
        in_specs += [VMEM, SMEM, VMEM, HBM, HBM]
        operands += list(carried)
        aliases = {7: 4, 8: 5}
    if sends is not None:
        in_specs.append(SMEM)
        operands.append(peers)
    in_specs += [ANY] * len(y_list)
    operands += y_list
    out_specs = [VMEM, VMEM, SMEM, VMEM, HBM, HBM]
    out_shape = [
        jax.ShapeDtypeStruct((LOCAL, 128), f32),
        jax.ShapeDtypeStruct((YBLOCKS, 1, BS), f32),
        jax.ShapeDtypeStruct((SLOTS,), f32),
        jax.ShapeDtypeStruct((8, 128), f32),
        pltpu.HBM((MOST, BS, BS), bf16),
        pltpu.HBM((SLOTS, BS, 128), f32),
    ]
    if sends is not None:
        out_specs.append(VMEM)
        out_shape.append(jax.ShapeDtypeStruct((GROUP, 1, BS), f32))
    return pl.pallas_call(
        functools.partial(sweep_kernel, base=base, count=count, first=first, sends=sends),
        in_specs=in_specs,
        out_specs=out_specs,
        out_shape=out_shape,
        scratch_shapes=[
            pltpu.VMEM((LOCAL, DIM), bf16),
            pltpu.VMEM((LOCAL, 128), f32),
            pltpu.SemaphoreType.DMA((BPD, 2)),
            pltpu.VMEM((2, ROWS, DIM), bf16),
            pltpu.SemaphoreType.DMA((3,)),
            pltpu.VMEM((1, 8, BS), f32),
            pltpu.VMEM((LOCAL, 128), f32),
            pltpu.VMEM((BS, 128), f32),
            pltpu.VMEM((8, BS), f32),
            pltpu.SMEM((1,), i32),
            pltpu.SMEM((1,), f32),
            pltpu.VMEM((2, BS, BS), bf16),
            pltpu.SemaphoreType.DMA((2,)),
            pltpu.SMEM((1,), i32),
        ],
        input_output_aliases=aliases,
        compiler_params=params(),
        name=f"sweep_{base}",
    )(*operands)


def load_pair(slot, x_ref, y_refs, x_buf, y_buf, sems):
    rows = pl.ds(pl.multiple_of((slot % BPD) * BS, BS), BS)
    fetch = pltpu.make_async_copy(x_ref.at[rows, :], x_buf, sems.at[0])
    fetch.start()
    fetch.wait()
    for n in range(YBLOCKS):

        @pl.when(slot // BPD == n)
        def _():
            source = y_refs[0].at[n] if n < BPD else y_refs[n - BPD + 1]
            fetch = pltpu.make_async_copy(source, y_buf, sems.at[1])
            fetch.start()
            fetch.wait()


def next_potential(now, half, total, log_count):
    return 0.5 * (now + half + entropy_weight * (log_count - log_two * total))


def fetch_terms(kept_ref, terms_ref, sems, list_ref, seat_of_ref, start, stop):
    def term_copy(n):
        return pltpu.make_async_copy(kept_ref.at[seat_of_ref[list_ref[n]]], terms_ref.at[n], sems.at[n])

    for n in range(MOST):

        @pl.when((n >= start) & (n < stop))
        def _():
            term_copy(n).start()

    return term_copy


def columns_kernel(list_ref, live_ref, seat_of_ref, use_ref, left_ref, *refs, log_count, accs):
    start, stop = 0, live_ref[1]
    acc_refs = refs[:accs]
    x_rows_ref, y_rows_ref, kept_ref, slow_ref, x_ref = refs[accs : accs + 5]
    y_refs = refs[accs + 5 : accs + 6 + FAR]
    next_ref, out_ref, col_ref, weight_ref, state_ref, part_ref, x_buf, y_buf, sems, terms_ref, term_sems = refs[accs + 6 + FAR :]
    term_copy = fetch_terms(kept_ref, terms_ref, term_sems, list_ref, seat_of_ref, start, stop)
    clear_cols(col_ref)
    total = lane_sums(acc_refs)
    state_ref[0:1, :] = jnp.where(total > 0.0, high_of(own_beta(y_rows_ref)), lowest)
    state_ref[1:2, :] = total
    for n in range(SLOTS):

        @pl.when((use_ref[n] > 0) & (left_ref[n] < 0.0))
        def _():
            fetch = pltpu.make_async_copy(slow_ref.at[n], part_ref, sems.at[0])
            fetch.start()
            fetch.wait()
            add_part(part_ref, state_ref, n % BPD)

    half = x_rows_ref[1:2, :]
    f_next = next_potential(x_rows_ref[0:1, :], half, logs(state_ref[0:1, :], state_ref[1:2, :]), log_count)
    next_ref[0:1, :] = f_next
    next_ref[1:2, :] = half
    next_ref[2:8, :] = jnp.zeros((6, LOCAL), f32)
    alpha = (f_next - half) * scale
    state_ref[2:3, :] = alpha
    top = high_of(alpha)
    weight_ref[...] = down(jnp.exp2(alpha - top))
    reach = (top - low_of(alpha))[0, 0]

    def body(step, carry):
        slot = list_ref[step]
        y, b = slot // BPD, slot % BPD
        fits = reach <= left_ref[slot]
        term_copy(step).wait()

        @pl.when(fits)
        def _():
            sums = jnp.zeros((8, BS), f32)
            for c in range(0, BS, 64):
                weight = weight_ref[pl.ds(pl.multiple_of(b * BS + c, 64), 64), :]
                parts = [fold(terms_ref[step, c : c + 64, n : n + 128].astype(f32) * weight) for n in range(0, BS, 128)]
                sums = sums + jnp.concatenate(parts, axis=1)
            put_cols(col_ref, y, top, jnp.sum(sums, axis=0, keepdims=True))

        @pl.when(jnp.logical_not(fits))
        def _():
            load_pair(slot, x_ref, y_refs, x_buf, y_buf, sems)
            for c in range(0, BS, 128):
                row = state_ref[2:3, pl.ds(pl.multiple_of(b * BS + c, 128), 128)]
                part_ref[c : c + 128, :] = jnp.broadcast_to(row, (128, 128)).T
            shifted_cols(x_buf, y_buf, part_ref, col_ref, y)

        return carry

    lax.fori_loop(start, stop, body, 0)
    for n in range(YBLOCKS):
        out_ref[n] = logs(col_ref[n, 0:1, :], col_ref[n, 1:2, :])


def gathered(j, own_ref, came, who_ref):
    terms = [own_ref[j]] + [jnp.where(who_ref[n] == j, came(n), lowest) for n in range(PEERS)]
    top = terms[0]
    for term in terms[1:]:
        top = jnp.maximum(top, term)
    total = jnp.exp2(terms[0] - top)
    for term in terms[1:]:
        total = total + jnp.exp2(term - top)
    return top + jnp.log2(total)


def home_kernel(who_ref, peers_ref, even_in, odd_in, first_ref, second_ref, y_rows_ref, even_out, odd_out, g_ref, *, log_count):
    came = lambda n: (even_in, odd_in)[n // GROUP][n % GROUP]
    betas = []
    for j in range(BPD):
        span = slice(j * BS, (j + 1) * BS)
        half = y_rows_ref[1:2, span]
        g_next = next_potential(y_rows_ref[0:1, span], half, gathered(j, first_ref, came, who_ref), log_count)
        g_ref[0:1, span] = g_next
        betas.append((g_next - half) * scale)
        g_ref[1:2, span] = betas[j]
    g_ref[2:8, :] = jnp.zeros((6, LOCAL), f32)
    for n in range(PEERS):
        out = (even_out, odd_out)[n // GROUP]
        out[n % GROUP, 0:1, :] = jnp.where(who_ref[n] == 1, betas[1], betas[0])
        out[n % GROUP, 1:2, :] = outgoing(second_ref, peers_ref[n])


def home(who, peers, rows_in, first, second, y_rows, log_count):
    return pl.pallas_call(
        functools.partial(home_kernel, log_count=log_count),
        in_specs=[SMEM, SMEM] + [VMEM] * 5,
        out_specs=[VMEM] * 3,
        out_shape=[jax.ShapeDtypeStruct((GROUP, 2, BS), f32)] * 2 + [jax.ShapeDtypeStruct((8, LOCAL), f32)],
        compiler_params=params(),
        name="home",
    )(who, peers, *rows_in, first, second, y_rows)


def rows_kernel(list_ref, live_ref, seat_of_ref, use_ref, left_ref, *refs, log_count, last):
    if last:
        start, stop = live_ref[0], live_ref[1]
        from_ref, who_ref, acc_in, state_in, even_in, odd_in, g_ref, second_ref, y_rows_ref, x_rows_ref = refs[:10]
        refs = refs[10:]
    else:
        start, stop = 0, live_ref[0]
        from_ref, even_in, g_ref = refs[:3]
        refs = refs[3:]
    kept_ref, slow_ref, x_ref = refs[:3]
    y_refs = refs[3 : 4 + FAR]
    refs = refs[4 + FAR :]
    if last:
        f_ref, g_out_ref, acc_ref, state_ref = refs[:4]
        refs = refs[4:]
    else:
        acc_ref, state_ref = refs[:2]
        refs = refs[2:]
    beta_ref, weight_ref, part_ref, x_buf, y_buf, sems, terms_ref, term_sems = refs
    term_copy = fetch_terms(kept_ref, terms_ref, term_sems, list_ref, seat_of_ref, start, stop)
    shift = high_of(g_ref[1:2, :])
    if last:
        acc_ref[...] = acc_in[...]
        state_ref[...] = state_in[...]
    else:
        acc_ref[...] = jnp.zeros((LOCAL, 128), f32)
        state_ref[0:1, :] = jnp.full((1, LOCAL), lowest, f32)
        state_ref[1:8, :] = jnp.zeros((7, LOCAL), f32)
    for n in range(BPD):
        beta_ref[n] = g_ref[1:2, n * BS : (n + 1) * BS]
    for n in range(BPD, YBLOCKS):
        at = from_ref[n] % GROUP
        if last:
            beta_ref[n] = jnp.where(from_ref[n] < GROUP, even_in[at, 0:1, :], odd_in[at, 0:1, :])
        else:
            beta_ref[n] = even_in[at, 0:1, :]
    weight_ref[...] = jnp.exp2(beta_ref[...] - shift)

    def body(step, carry):
        slot = list_ref[step]
        y, b = slot // BPD, slot % BPD
        beta = beta_ref[y]
        reach = jnp.maximum(high_of(beta) - shift, shift - low_of(beta))
        fits = reach[0, 0] <= left_ref[slot]
        term_copy(step).wait()

        @pl.when(fits)
        def _():
            weight = weight_ref[y]
            for c in range(0, BS, 64):
                span = pl.ds(pl.multiple_of(b * BS + c, 64), 64)
                part = acc_ref[span, :]
                for n in range(0, BS, 128):
                    part = part + terms_ref[step, c : c + 64, n : n + 128].astype(f32) * weight[:, n : n + 128]
                acc_ref[span, :] = part

        @pl.when(jnp.logical_not(fits))
        def _():
            load_pair(slot, x_ref, y_refs, x_buf, y_buf, sems)
            shifted_rows(x_buf, y_buf, beta, part_ref)
            add_part(part_ref, state_ref, b)

        return carry

    lax.fori_loop(start, stop, body, 0)
    if not last:
        return
    total = lane_sums([acc_ref])
    top = jnp.where(total > 0.0, shift, lowest)
    top, total = merge(top, total, state_ref[0:1, :], state_ref[1:2, :])
    f_ref[...] = next_potential(x_rows_ref[0:1, :], x_rows_ref[1:2, :], logs(top, total), log_count)
    came = lambda n: (even_in, odd_in)[n // GROUP][n % GROUP, 1:2, :]
    total = jnp.concatenate([gathered(j, second_ref, came, who_ref) for j in range(BPD)], axis=1)
    g_next = next_potential(g_ref[0:1, :], y_rows_ref[1:2, :], total, log_count)
    g_out_ref[...] = moved_exact(g_next, y_rows_ref[2:3, :].astype(i32))


def slots_call(kernel, smem, front, kept, slow, x_blocks, y_list, outs, scratch, name):
    return pl.pallas_call(
        kernel,
        in_specs=[SMEM] * len(smem) + [VMEM] * len(front) + [HBM, HBM, ANY] + [ANY] * len(y_list),
        out_specs=[VMEM] * len(outs),
        scratch_shapes=scratch
        + [
            pltpu.VMEM((BS, 128), f32),
            pltpu.VMEM((BS, DIM), bf16),
            pltpu.VMEM((ROWS, DIM), bf16),
            pltpu.SemaphoreType.DMA((2,)),
            pltpu.VMEM((MOST, BS, BS), bf16),
            pltpu.SemaphoreType.DMA((MOST,)),
        ],
        out_shape=outs,
        compiler_params=params(),
        name=name,
    )(*smem, *front, kept, slow, x_blocks, *y_list)


def seat_tables():
    half = GROUP // 2
    offsets = np.zeros((GROUP, PEERS), np.int32)
    source = np.zeros((GROUP, YBLOCKS), np.int32)
    for seat in range(GROUP):
        odd_seat = (seat + half) % GROUP
        for other in range(GROUP):
            if other != seat and abs(other - seat) <= REACH:
                offsets[seat, other] = other - seat
            off = other - odd_seat
            if off != 0 and abs(off) <= REACH and not 0 <= seat + off < GROUP:
                offsets[seat, GROUP + other] = off
        for k, off in enumerate(ROUNDS[seat % 4]):
            source[seat, BPD + k] = list(offsets[seat]).index(off)
    index = np.full((GROUP, PEERS), -1, np.int32)
    for seat in range(GROUP):
        for k, off in enumerate(ROUNDS[seat % 4]):
            index[seat, offsets[seat] == off] = BPD + k
    return offsets, index, source


def swap(rows, devices, shift):
    groups = [[(GROUP * k + j + shift) % devices for j in range(GROUP)] for k in range(devices // GROUP)]
    return lax.all_to_all(rows, "blk", split_axis=0, concat_axis=0, tiled=True, axis_index_groups=groups)


def on_device(x_points, y_points, x_start, y_start, x_order, y_order, partners, counts):
    devices = lax.axis_size("blk")
    me = lax.axis_index("blk").astype(i32)
    log_count = math.log(LOCAL * devices)
    here = me[None]
    line = lambda v: v.reshape(1, LOCAL)

    y_sent, x_pos = pack_y(here, partners, counts, line(y_order), line(x_order), y_start, x_start, y_points, devices)
    y_came = lax.all_to_all(y_sent, "blk", split_axis=0, concat_axis=0, tiled=True)
    x_sent = pack_x(x_pos, x_points)
    x_came = lax.all_to_all(x_sent, "blk", split_axis=0, concat_axis=0, tiled=True)
    y_came, x_sent = lax.optimization_barrier((y_came, x_sent))
    y_rows, table, y_own, *y_sends = unpack_y(here, y_came, devices)

    def far_block(k):
        pairs = [(i, i + ROUNDS[i % 4][k]) for i in range(devices) if 0 <= i + ROUNDS[i % 4][k] < devices]
        return lax.ppermute(y_sends[k], "blk", pairs)

    y_far = [far_block(k) for k in range(FAR)]
    x_blocks, alpha, x_rows = unpack_x(x_came, table)

    offsets = lax.dynamic_slice(jnp.array(ROUNDS, i32), (me % 4, 0), (1, FAR))[0]
    live = jnp.arange(partners.shape[1], dtype=i32)[None, :] < counts[:, None]
    away = jnp.where(live, partners // BPD - me, devices)
    local_use = [((away == 0) & (partners % BPD == j)).any(axis=1) for j in range(BPD)]
    far = away[None, :, :] == offsets[:, None, None]
    use = jnp.concatenate([jnp.stack(local_use), far.any(axis=2)]).astype(i32).reshape(SLOTS)
    number = jnp.minimum(jnp.maximum(jnp.cumsum(use) - 1, 0), MOST - 1)

    peer_offsets, peer_index, peer_source = seat_tables()
    row = lambda t: lax.dynamic_slice(jnp.asarray(t), (me % GROUP, 0), (1, t.shape[1]))[0]
    peers, source, off = row(peer_index), row(peer_source), row(peer_offsets)
    peer = me + off
    wants = (table[:, 3 * (LOCAL // devices)] > 0.5).astype(i32)
    valid = (off != 0) & (peer >= 0) & (peer < devices)
    who = jnp.where(valid, wants[jnp.clip(peer, 0, devices - 1)], -1)

    far_slot = jnp.repeat(source >= GROUP, BPD).astype(i32)
    near = jnp.cumsum(use * (1 - far_slot))
    rank = jnp.where(far_slot > 0, near[-1] + jnp.cumsum(use * far_slot), near) - 1
    count = jnp.minimum(jnp.sum(use), MOST)
    step = jnp.minimum(jnp.arange(MOST, dtype=i32), count - 1)
    at = (rank[None, :] == step[:, None]) & (use[None, :] > 0)
    slots = jnp.sum(jnp.where(at, jnp.arange(SLOTS, dtype=i32)[None, :], 0), axis=1)
    live_counts = jnp.stack([jnp.minimum(near[-1], count), count])
    use, number, slots, live_counts, peers, source, who = lax.optimization_barrier(
        (use, number, slots, live_counts, peers, source, who)
    )
    lists = [slots, live_counts, number]

    common = (use, number, x_blocks, alpha)
    acc_0, *carried = sweep(common, [y_own], 0, None, [x_rows, y_rows])
    acc_1, *carried = sweep(common, y_far[:EARLY], BPD, carried)
    acc_2, *carried, odd_out = sweep(common, y_far[EARLY:-1], BPD + EARLY, carried, None, peers, 1)
    acc_3, cols_first, left, _, kept, slow, even_out = sweep(common, y_far[-1:], YBLOCKS - 1, carried, None, peers, 0)
    y_all = [y_own] + y_far

    odd_in = swap(odd_out, devices, GROUP // 2)
    even_in = swap(even_out, devices, 0)
    accs = [acc_0, acc_1, acc_2, acc_3]
    x_next, cols_second = slots_call(
        functools.partial(columns_kernel, log_count=log_count, accs=len(accs)),
        lists + [use, left],
        accs + [x_rows, y_rows],
        kept,
        slow,
        x_blocks,
        y_all,
        [jax.ShapeDtypeStruct((8, LOCAL), f32), jax.ShapeDtypeStruct((YBLOCKS, 1, BS), f32)],
        [pltpu.VMEM((YBLOCKS, 8, BS), f32), pltpu.VMEM((LOCAL, 128), f32), pltpu.VMEM((8, LOCAL), f32)],
        "columns",
    )
    even_out, odd_out, g_one = home(who, peers, (even_in, odd_in), cols_first, cols_second, y_rows, log_count)
    even_in = swap(even_out, devices, 0)
    odd_in = swap(odd_out, devices, GROUP // 2)
    row_scratch = [pltpu.VMEM((YBLOCKS, 1, BS), f32), pltpu.VMEM((YBLOCKS, 1, BS), f32)]
    acc, state = slots_call(
        functools.partial(rows_kernel, log_count=log_count, last=False),
        lists + [use, left, source],
        [even_in, g_one],
        kept,
        slow,
        x_blocks,
        y_all,
        [jax.ShapeDtypeStruct((LOCAL, 128), f32), jax.ShapeDtypeStruct((8, LOCAL), f32)],
        row_scratch,
        "rows_near",
    )
    f_two, g_two = slots_call(
        functools.partial(rows_kernel, log_count=log_count, last=True),
        lists + [use, left, source, who],
        [acc, state, even_in, odd_in, g_one, cols_second, y_rows, x_next],
        kept,
        slow,
        x_blocks,
        y_all,
        [jax.ShapeDtypeStruct((1, LOCAL), f32)] * 2,
        [pltpu.VMEM((LOCAL, 128), f32), pltpu.VMEM((8, LOCAL), f32)] + row_scratch,
        "rows_far",
    )
    return f_two.reshape(LOCAL), g_two.reshape(LOCAL)


def solution(mesh):
    placed_as = (
        P("blk", None),
        P("blk", None),
        P("blk"),
        P("blk"),
        P("blk"),
        P("blk"),
        P("blk", None),
        P("blk"),
    )
    return jax.shard_map(
        on_device, mesh=mesh, in_specs=placed_as, out_specs=(P("blk"), P("blk")), check_vma=False
    )
```

```python
import functools
import math

import jax
import jax.numpy as jnp
import numpy as np
from jax import lax
from jax.experimental import pallas as pl
from jax.experimental.pallas import tpu as pltpu
from jax.sharding import PartitionSpec as P

DIM = 512
BS = 1024
BPD = 2
REACH = 3
LOCAL = BPD * BS
EXTRA = 128
WIDE = DIM + EXTRA
TAIL = 16
ROWS = BS + TAIL
CHUNK = 512
PART = 256
ROUNDS = ((1, -3, 3, -1, -2, 2), (-1, 3, -3, 1, -2, 2), (1, -3, 3, -1, 2, -2), (-1, 3, -3, 1, 2, -2))
EARLY = 4
FAR = len(ROUNDS[0])
YBLOCKS = BPD + FAR
SLOTS = BPD * YBLOCKS
MOST = 12
GROUP = 8
PEERS = 2 * GROUP
X_LANES = EXTRA // 2

entropy_weight = 0.05
scale = math.log2(math.e) / entropy_weight
log_two = math.log(2.0)
lowest = -1e30
exponent_room = 112.0
mebi = 1024 * 1024

f32 = jnp.float32
bf16 = jnp.bfloat16
i32 = jnp.int32

SMEM = pl.BlockSpec(memory_space=pltpu.SMEM)
ANY = pl.BlockSpec(memory_space=pl.ANY)
VMEM = pl.BlockSpec(memory_space=pltpu.VMEM)
HBM = pl.BlockSpec(memory_space=pltpu.HBM)


def iota(shape, dim):
    return lax.broadcasted_iota(i32, shape, dim)


def dot(a, b):
    return jnp.dot(a, b, preferred_element_type=f32)


def nt_dot(a, b):
    return lax.dot_general(a, b, (((1,), (1,)), ((), ())), preferred_element_type=f32)


def ones_where(mask):
    return jnp.where(mask, 1.0, 0.0).astype(bf16)


def params():
    return pltpu.CompilerParams(vmem_limit_bytes=64 * mebi)


def whole(shape):
    return pl.BlockSpec(shape, lambda *t: (0,) * len(shape))


def laid_out(square):
    return jnp.concatenate([square[n : n + 1, :] for n in range(square.shape[0])], axis=1)


def down(row):
    parts = [jnp.broadcast_to(row[:, c : c + 128], (128, 128)).T for c in range(0, row.shape[1], 128)]
    return jnp.concatenate(parts, axis=0)


def moved(values, place):
    high = iota((16, LOCAL), 0) == lax.shift_right_logical(place, 7)
    low = ones_where(iota((128, LOCAL), 0) == jnp.bitwise_and(place, 127))
    stack = jnp.concatenate([jnp.where(high, v, 0.0) for v in values], axis=0).astype(bf16)
    out = nt_dot(stack, low)
    return [laid_out(out[16 * n : 16 * n + 16, :]) for n in range(len(values))]


def moved_exact(value, place):
    first = value.astype(bf16).astype(f32)
    second = (value - first).astype(bf16).astype(f32)
    parts = moved([first, second, value - first - second], place)
    return parts[0] + parts[1] + parts[2]


def before_matrix():
    return ones_where(iota((128, 128), 0) < iota((128, 128), 1))


def plan(order, start, devices, first_lane):
    share = LOCAL // devices
    target = lax.shift_right_logical(order, 11)
    hit = iota((devices, LOCAL), 0) == target
    hot = ones_where(hit)
    before = before_matrix()
    every = jnp.ones((128, 128), bf16)
    seen = jnp.zeros((devices, 128), f32)
    earlier = []
    for c in range(0, LOCAL, 128):
        piece = hot[:, c : c + 128]
        earlier.append(dot(piece, before) + seen)
        seen = seen + dot(piece, every)
    earlier = jnp.concatenate(earlier, axis=1)
    rank = jnp.sum(jnp.where(hit, earlier, 0.0), axis=0, keepdims=True).astype(i32)
    within = jnp.bitwise_and(order, LOCAL - 1)
    high = lax.shift_right_logical(within, 6).astype(f32)
    low = jnp.bitwise_and(within, 63).astype(f32)
    row = iota((EXTRA, LOCAL), 0) - first_lane
    field = row // share
    value = jnp.where(field == 0, high, jnp.where(field == 1, low, start))
    mine = (row >= 0) & (row < 3 * share) & (row % share == rank)
    return target * share + rank, nt_dot(hot, jnp.where(mine, value, 0.0).astype(bf16))


def partner_offsets(me):
    kind = jnp.bitwise_and(me, 3)
    out = []
    for k in range(FAR):
        value = jnp.int32(ROUNDS[0][k])
        for n in range(1, 4):
            value = jnp.where(kind == n, jnp.int32(ROUNDS[n][k]), value)
        out.append(value)
    return out


def pack_y_kernel(
    me_ref, partners_ref, counts_ref, y_order, x_order, y_start, x_start, points, out_ref, x_pos_ref, pos_ref, table_ref,
    *, devices
):
    step = pl.program_id(0)
    share = LOCAL // devices

    @pl.when(step == 0)
    def _():
        y_pos, y_table = plan(y_order[...], y_start[...].astype(f32).reshape(1, LOCAL), devices, 0)
        x_pos, x_table = plan(x_order[...], x_start[...].astype(f32).reshape(1, LOCAL), devices, X_LANES)
        pos_ref[...] = y_pos
        x_pos_ref[...] = x_pos
        me = me_ref[0]
        offsets = partner_offsets(me)
        need = [jnp.int32(0)] * FAR
        for b in range(BPD):
            for s in range(partners_ref.shape[1]):
                block = partners_ref[b, s]
                away = lax.shift_right_logical(block, 1) - me
                for k in range(FAR):
                    listed = (s < counts_ref[b]) & (away == offsets[k])
                    need[k] = jnp.where(listed, jnp.bitwise_and(block, 1), need[k])
        table = y_table + x_table
        row, lane = iota(table.shape, 0), iota(table.shape, 1)
        for k in range(FAR):
            table = jnp.where((row == me + offsets[k]) & (lane == 3 * share), need[k].astype(f32), table)
        table_ref[...] = table

    base = step * CHUNK
    hot = ones_where(iota((CHUNK, LOCAL), 0) + base == pos_ref[...])
    out_ref[:, :DIM] = dot(hot, points[...]).astype(bf16)
    some = CHUNK // share
    table = table_ref[pl.ds(pl.multiple_of(step * some, some), some), :]
    out_ref[:, DIM:] = jnp.broadcast_to(table[:, None, :], (some, share, EXTRA)).reshape(CHUNK, EXTRA).astype(bf16)


def pack_y(me, partners, counts, y_order, x_order, y_start, x_start, points, devices):
    row = whole((1, LOCAL))
    return pl.pallas_call(
        functools.partial(pack_y_kernel, devices=devices),
        grid=(LOCAL // CHUNK,),
        in_specs=[SMEM, SMEM, SMEM, row, row, whole((LOCAL,)), whole((LOCAL,)), whole((LOCAL, DIM))],
        out_specs=[pl.BlockSpec((CHUNK, WIDE), lambda t: (t, 0)), row],
        out_shape=[pltpu.HBM((LOCAL, WIDE), bf16), jax.ShapeDtypeStruct((1, LOCAL), i32)],
        scratch_shapes=[pltpu.VMEM((1, LOCAL), i32), pltpu.VMEM((devices, EXTRA), f32)],
        compiler_params=params(),
        name="pack_y",
    )(me, partners, counts, y_order, x_order, y_start, x_start, points)


def pack_x_kernel(pos_ref, points_ref, out_ref):
    base = pl.program_id(0) * CHUNK
    hot = ones_where(iota((CHUNK, LOCAL), 0) + base == pos_ref[...])
    out_ref[...] = dot(hot, points_ref[...]).astype(bf16)


def pack_x(pos, points):
    return pl.pallas_call(
        pack_x_kernel,
        grid=(LOCAL // CHUNK,),
        in_specs=[whole((1, LOCAL)), whole((LOCAL, DIM))],
        out_specs=pl.BlockSpec((CHUNK, DIM), lambda t: (t, 0)),
        out_shape=pltpu.HBM((LOCAL, DIM), bf16),
        compiler_params=params(),
        name="pack_x",
    )(pos, points)


WINDOW = PART + 16
HELD = BS + WINDOW + 16


def arrived(table, base, with_low):
    share = 16
    row, lane = iota((EXTRA, EXTRA), 0), iota((EXTRA, EXTRA), 1)
    pick = jnp.where(row == base + lane % share, 64.0 if with_low else 1.0, 0.0)
    if with_low:
        pick = jnp.where(row == base + share + lane % share, 1.0, pick)
    values = dot(table, pick.astype(bf16))
    values = jnp.where(row % (EXTRA // share) == lane // share, values, 0.0)
    return jnp.sum(values.reshape(LOCAL // 128, EXTRA // share, 128), axis=1)


def unpack_y_kernel(me_ref, came_ref, rows_ref, table_ref, own_ref, *rest, devices):
    sends = rest[:FAR]
    held, sems, own_sem, points_buf, extra_buf, in_sems = rest[FAR:]
    share = LOCAL // devices
    me = me_ref[0]
    extra_in = pltpu.make_async_copy(came_ref.at[:, pl.ds(DIM, EXTRA)], extra_buf, in_sems.at[0])
    points_in = pltpu.make_async_copy(came_ref.at[:, pl.ds(0, DIM)], points_buf, in_sems.at[1])
    extra_in.start()
    points_in.start()
    held[...] = jnp.zeros(held.shape, bf16)
    extra_in.wait()
    table = dot(ones_where(iota((devices, LOCAL), 1) == iota((devices, LOCAL), 0) * share), extra_buf[...])
    table_ref[...] = table
    place_square = arrived(table.astype(bf16), 0, True)
    place = laid_out(place_square)
    start = laid_out(arrived(table.astype(bf16), 2 * share, False))

    picks = []
    offsets = partner_offsets(me)
    small_row, small_lane = iota((devices, EXTRA), 0), iota((devices, EXTRA), 1)
    for k in range(FAR):
        here = (small_row == me + offsets[k]) & (small_lane == 3 * share)
        picks.append(jnp.sum(jnp.where(here, table, 0.0)) > 0.5)

    second = place >= float(BS)
    square = ones_where(place_square >= float(BS))
    totals = dot(square, jnp.ones((128, 128), bf16)).astype(bf16)
    earlier = dot(square, before_matrix()) + dot(ones_where(iota((16, 16), 1) < iota((16, 16), 0)), totals)
    ones_before = laid_out(earlier)
    dest = jnp.where(second, ones_before, iota((1, LOCAL), 1).astype(f32) - ones_before).astype(i32)
    seat = jnp.where(second, dest + BS, dest)
    position = place.astype(i32)
    start_row, high_row, low_row = moved(
        [start, lax.shift_right_logical(position, 6).astype(f32), jnp.bitwise_and(position, 63).astype(f32)], seat
    )
    rows_ref[0:1, :] = start_row
    rows_ref[2:3, :] = high_row * 64.0 + low_row
    rows_ref[3:8, :] = jnp.zeros((5, LOCAL), f32)
    sixteen, lane16 = iota((16, 128), 0), iota((16, 128), 1)
    points_in.wait()

    for j in range(BPD):
        here = jnp.where(second if j else jnp.logical_not(second), dest, -1)
        for c in range(LOCAL // PART):
            span = slice(c * PART, (c + 1) * PART)
            begin = jnp.sum(jnp.where((sixteen == c * PART // 128) & (lane16 == 0), earlier, 0.0)).astype(i32)
            if j == 0:
                begin = c * PART - begin
            begin = pl.multiple_of(lax.shift_left(lax.shift_right_logical(begin, 4), 4), 16)
            hot = ones_where(iota((WINDOW, PART), 0) + begin == here[:, span])
            part = dot(hot, points_buf[span, :]).astype(bf16)
            held[j, pl.ds(begin, WINDOW), :] = held[j, pl.ds(begin, WINDOW), :] + part
        half = []
        for c in range(0, BS, PART):
            points = held[j, c : c + PART, :].astype(f32)
            total = 0.5 * jnp.sum(points * points, axis=1, keepdims=True)
            half.append(jnp.broadcast_to(total, (PART, 128)).T[0:1, :])
        half = jnp.concatenate(half, axis=1)
        block = slice(j * BS, (j + 1) * BS)
        rows_ref[1:2, block] = half
        beta = start_row[:, block] - half
        first = beta.astype(bf16).astype(f32)
        next_part = (beta - first).astype(bf16).astype(f32)
        most = jnp.max(half, axis=1, keepdims=True) * 1.01
        sub = iota((TAIL, DIM), 0)
        tail = jnp.zeros((TAIL, DIM), f32) + most
        for n, piece in enumerate((first, next_part, beta - first - next_part)):
            tail = jnp.where(sub == 2 * n, piece[:, :DIM], tail)
            tail = jnp.where(sub == 2 * n + 1, piece[:, DIM:], tail)
        held[j, BS:ROWS, :] = tail.astype(bf16)
        done = held.at[j, pl.ds(0, ROWS), :]
        for k in range(FAR):
            wanted = picks[k] if j == 1 else jnp.logical_not(picks[k])

            @pl.when(wanted)
            def _():
                pltpu.make_async_copy(done, sends[k], sems.at[k]).start()

        pltpu.make_async_copy(done, own_ref.at[j], own_sem.at[j]).start()

    done = held.at[0, pl.ds(0, ROWS), :]
    for k in range(FAR):
        pltpu.make_async_copy(done, sends[k], sems.at[k]).wait()
    for j in range(BPD):
        pltpu.make_async_copy(done, own_ref.at[j], own_sem.at[j]).wait()


def unpack_y(me, came, devices):
    return pl.pallas_call(
        functools.partial(unpack_y_kernel, devices=devices),
        in_specs=[SMEM, ANY],
        out_specs=[VMEM, VMEM] + [HBM] * (1 + FAR),
        out_shape=[
            jax.ShapeDtypeStruct((8, LOCAL), f32),
            jax.ShapeDtypeStruct((devices, EXTRA), f32),
            pltpu.HBM((BPD, ROWS, DIM), bf16),
        ]
        + [pltpu.HBM((ROWS, DIM), bf16)] * FAR,
        scratch_shapes=[
            pltpu.VMEM((BPD, HELD, DIM), bf16),
            pltpu.SemaphoreType.DMA((FAR,)),
            pltpu.SemaphoreType.DMA((BPD,)),
            pltpu.VMEM((LOCAL, DIM), bf16),
            pltpu.VMEM((LOCAL, EXTRA), bf16),
            pltpu.SemaphoreType.DMA((2,)),
        ],
        compiler_params=params(),
        name="unpack_y",
    )(me, came)


def unpack_x_kernel(
    me_ref, peer_ref, came_ref, table_ref, points_ref, alpha_ref, rows_ref, who_ref, place_ref, start_ref, *, devices
):
    step = pl.program_id(0)

    @pl.when(step == 0)
    def _():
        table = table_ref[...].astype(bf16)
        place = laid_out(arrived(table, X_LANES, True)).astype(i32)
        place_ref[...] = place
        start_ref[...] = moved([laid_out(arrived(table, X_LANES + 32, False))], place)[0]
        row, lane = iota((EXTRA, EXTRA), 0), iota((EXTRA, EXTRA), 1)
        for n in range(PEERS):
            peer = me_ref[0] + peer_ref[n]
            wants = jnp.sum(jnp.where((row == peer) & (lane == 3 * LOCAL // devices), table_ref[...], 0.0)) > 0.5
            valid = (peer_ref[n] != 0) & (peer >= 0) & (peer < devices)
            who_ref[n] = jnp.where(valid, jnp.where(wants, 1, 0), -1)

    base = step * CHUNK
    hot = ones_where(iota((CHUNK, LOCAL), 0) + base == place_ref[...])
    points = dot(hot, came_ref[...])
    points_ref[...] = points.astype(bf16)
    half = jnp.broadcast_to(0.5 * jnp.sum(points * points, axis=1, keepdims=True), (CHUNK, 128))
    start = start_ref[:, pl.ds(pl.multiple_of(base, CHUNK), CHUNK)]
    alpha_ref[...] = (down(start) - half) * scale
    rows_ref[0:1, :] = start
    rows_ref[1:8, :] = jnp.concatenate([half[c : c + 128, :].T[0:7, :] for c in range(0, CHUNK, 128)], axis=1)


def unpack_x(me, peer_offsets, came, table, devices):
    return pl.pallas_call(
        functools.partial(unpack_x_kernel, devices=devices),
        grid=(LOCAL // CHUNK,),
        in_specs=[SMEM, SMEM, whole((LOCAL, DIM)), whole((EXTRA, EXTRA))],
        out_specs=[
            pl.BlockSpec((CHUNK, DIM), lambda t: (t, 0)),
            pl.BlockSpec((CHUNK, 128), lambda t: (t, 0)),
            pl.BlockSpec((8, CHUNK), lambda t: (0, t)),
            SMEM,
        ],
        out_shape=[
            pltpu.HBM((LOCAL, DIM), bf16),
            pltpu.HBM((LOCAL, 128), f32),
            jax.ShapeDtypeStruct((8, LOCAL), f32),
            jax.ShapeDtypeStruct((PEERS,), i32),
        ],
        scratch_shapes=[pltpu.VMEM((1, LOCAL), i32), pltpu.VMEM((1, LOCAL), f32)],
        compiler_params=params(),
        name="unpack_x",
    )(me, peer_offsets, came, table)


def merge(top, total, other_top, other_total):
    new = jnp.maximum(top, other_top)
    return new, total * jnp.exp2(top - new) + other_total * jnp.exp2(other_top - new)


def logs(top, total):
    return jnp.where(total > 0.0, top + jnp.log2(total), lowest)


def high_of(row):
    return jnp.max(row, axis=1, keepdims=True)


def low_of(row):
    return jnp.min(row, axis=1, keepdims=True)


def put_cols(col_ref, y, part_top, part_total):
    top, total = merge(col_ref[y, 0:1, :], col_ref[y, 1:2, :], part_top, part_total)
    col_ref[y, 0:1, :] = top
    col_ref[y, 1:2, :] = total


def clear_cols(col_ref):
    col_ref[:, 0:1, :] = jnp.full((col_ref.shape[0], 1, BS), lowest, f32)
    col_ref[:, 1:2, :] = jnp.zeros((col_ref.shape[0], 1, BS), f32)


def shifted_rows(x_ref, y_ref, beta, part_ref):
    def body(c, carry):
        span = pl.ds(pl.multiple_of(c * PART, PART), PART)
        terms = nt_dot(x_ref[span, :], y_ref[0:BS, :]) * scale + beta
        top = jnp.max(terms, axis=1, keepdims=True)
        total = jnp.sum(jnp.exp2(terms - top), axis=1, keepdims=True)
        part_ref[span, :] = jnp.where(iota((PART, 128), 1) == 0, top, total)
        return carry

    lax.fori_loop(0, BS // PART, body, 0)


def shifted_cols(x_ref, y_ref, alpha_ref, col_ref, y):
    def body(c, carry):
        span = pl.ds(pl.multiple_of(c * PART, PART), PART)
        terms = nt_dot(x_ref[span, :], y_ref[0:BS, :]) * scale + alpha_ref[span, 0:1]
        top = jnp.max(terms, axis=0, keepdims=True)
        put_cols(col_ref, y, top, jnp.sum(jnp.exp2(terms - top), axis=0, keepdims=True))
        return carry

    lax.fori_loop(0, BS // PART, body, 0)


def add_part(part_ref, state_ref, b):
    for c in range(0, BS, 128):
        part = part_ref[c : c + 128, :].T
        span = pl.ds(pl.multiple_of(b * BS + c, 128), 128)
        top, total = merge(state_ref[0:1, span], state_ref[1:2, span], part[0:1, :], part[1:2, :])
        state_ref[0:1, span] = top
        state_ref[1:2, span] = total


def lane_sums(refs):
    out = []
    for c in range(0, LOCAL, 128):
        part = refs[0][c : c + 128, :]
        for ref in refs[1:]:
            part = part + ref[c : c + 128, :]
        out.append(jnp.sum(part.T, axis=0, keepdims=True))
    return jnp.concatenate(out, axis=1)


def fold(values):
    return jnp.sum(values.reshape(values.shape[0] // 8, 8, 128), axis=0)


def own_beta(y_rows_ref):
    return (y_rows_ref[0:1, :] - y_rows_ref[1:2, :]) * scale


def sweep_kernel(*refs, base, count, first, sends):
    use_ref, seat_of_ref, x_ref, alpha_ref = refs[:4]
    refs = refs[4:]
    if first:
        x_rows_ref, y_rows_ref = refs[:2]
        refs = refs[2:]
    else:
        cols_in, left_in, stat_in = refs[:3]
        refs = refs[5:]
    if sends is not None:
        peers_ref = refs[0]
        refs = refs[1:]
    y_refs = refs[:1] if first else refs[:count]
    refs = refs[len(y_refs) :]
    acc_ref, cols_ref, left_ref, stat_ref, kept_ref, slow_ref = refs[:6]
    refs = refs[6:]
    if sends is not None:
        group_out = refs[0]
        refs = refs[1:]
    x_buf, alpha_buf, x_sems, y_buf, sems, col_ref, weight_ref, part_ref, beta_ref, fit_ref, room_ref, tiles, tile_sems, tile_count = refs

    def copy(n):
        source = y_refs[0].at[n] if first else y_refs[n]
        return pltpu.make_async_copy(source, y_buf.at[n % 2], sems.at[n % 2])

    def x_copies(n):
        rows = pl.ds(n * BS, BS)
        return (
            pltpu.make_async_copy(x_ref.at[rows, :], x_buf.at[rows, :], x_sems.at[n, 0]),
            pltpu.make_async_copy(alpha_ref.at[rows, :], alpha_buf.at[rows, :], x_sems.at[n, 1]),
        )

    copy(0).start()
    for n in range(BPD):
        for part in x_copies(n):
            part.start()
    tile_count[0] = 0
    acc_ref[...] = jnp.zeros((LOCAL, 128), f32)

    def tile_copy(at, seat):
        return pltpu.make_async_copy(tiles.at[at], kept_ref.at[seat], tile_sems.at[at])

    if first:
        for n in range(SLOTS):
            left_ref[n] = -1.0
        alpha = (x_rows_ref[0:1, :] - x_rows_ref[1:2, :]) * scale
        alpha_top = high_of(alpha)
        lane = iota((8, 128), 1)
        beta_top = high_of(own_beta(y_rows_ref))
        most = high_of(x_rows_ref[1:2, :]) * 1.01
        spread = alpha_top - low_of(alpha)
        stat_ref[...] = jnp.where(
            lane == 0, alpha_top, jnp.where(lane == 1, spread, jnp.where(lane == 2, most, beta_top))
        )
    else:
        for n in range(SLOTS):
            left_ref[n] = left_in[n]
        cols_ref[...] = cols_in[...]
        stat_ref[...] = stat_in[...]

    def body(step, carry):
        y, b = step // BPD, step % BPD
        slot = base * BPD + step
        for n in range(count):

            @pl.when(step == BPD * n)
            def _():
                copy(n).wait()
                if n + 1 < count:
                    copy(n + 1).start()

        for n in range(BPD):

            @pl.when(step == n)
            def _():
                for part in x_copies(n):
                    part.wait()
                rows = slice(n * BS, (n + 1) * BS)
                weight_ref[rows, :] = jnp.exp2(alpha_buf[rows, :] - stat_ref[0:1, 0:1])

        now = y_buf.at[y % 2]
        rows_from = b * BS

        @pl.when(b == 0)
        def _():
            clear_cols(col_ref)
            tail = now[BS:ROWS, :].astype(f32)
            halves = [tail[n : n + 1, :] + tail[n + 2 : n + 3, :] + tail[n + 4 : n + 5, :] for n in range(2)]
            beta = jnp.concatenate(halves, axis=1) * scale
            shift = stat_ref[0:1, 3:4]
            left = exponent_room - 2.0 * scale * jnp.sqrt(tail[6:7, 0:1] * stat_ref[0:1, 2:3])
            reach = jnp.maximum(stat_ref[0:1, 1:2], jnp.maximum(high_of(beta) - shift, shift - low_of(beta)))
            beta_ref[0:1, :] = beta
            beta_ref[1:2, :] = jnp.exp2(beta - shift)
            room_ref[0] = left[0, 0]
            fit_ref[0] = jnp.where((left - reach)[0, 0] >= 0.0, 1, 0)

        @pl.when(use_ref[slot] > 0)
        def _():
            fits = fit_ref[0] > 0

            @pl.when(fits)
            def _():
                left_ref[slot] = room_ref[0]
                done = tile_count[0]
                tile_count[0] = done + 1
                at = done % 2

                @pl.when(done > 1)
                def _():
                    tile_copy(at, 0).wait()

                weight = beta_ref[1:2, :]
                sums = jnp.zeros((8, BS), f32)
                for c in range(0, BS, PART):
                    span = pl.ds(pl.multiple_of(rows_from + c, PART), PART)
                    terms = jnp.exp2(nt_dot(x_buf[span, :], now[0:BS, :]) * scale)
                    tiles[at, c : c + PART, :] = terms.astype(bf16)
                    row_part = acc_ref[span, :]
                    col_parts = []
                    for n in range(0, BS, 128):
                        piece = terms[:, n : n + 128]
                        row_part = row_part + piece * weight[:, n : n + 128]
                        col_parts.append(fold(piece * weight_ref[span, :]))
                    acc_ref[span, :] = row_part
                    sums = sums + jnp.concatenate(col_parts, axis=1)
                tile_copy(at, seat_of_ref[slot]).start()
                put_cols(col_ref, 0, stat_ref[0:1, 0:1], jnp.sum(sums, axis=0, keepdims=True))

            @pl.when(jnp.logical_not(fits))
            def _():
                block = pl.ds(pl.multiple_of(rows_from, BS), BS)
                shifted_rows(x_buf.at[block, :], now, beta_ref[0:1, :], part_ref)
                out = pltpu.make_async_copy(part_ref, slow_ref.at[slot], sems.at[2])
                out.start()
                shifted_cols(x_buf.at[block, :], now, alpha_buf.at[block, :], col_ref, 0)
                out.wait()

        @pl.when(b == BPD - 1)
        def _():
            cols_ref[base + y] = logs(col_ref[0, 0:1, :], col_ref[0, 1:2, :])

        return carry

    lax.fori_loop(0, BPD * count, body, 0)
    for n in range(2):

        @pl.when(tile_count[0] > n)
        def _():
            tile_copy(n, 0).wait()

    if sends is not None:
        for n in range(GROUP):
            group_out[n] = outgoing(cols_ref, peers_ref[sends * GROUP + n])


def outgoing(cols_ref, index):
    return jnp.where(index < 0, lowest, cols_ref[jnp.maximum(index, 0)])


def sweep(common, y_list, base, carried, rows=None, peers=None, sends=None):
    first = carried is None
    count = BPD if first else len(y_list)
    in_specs = [SMEM, SMEM, HBM, HBM]
    operands = list(common)
    aliases = {}
    if first:
        in_specs += [VMEM, VMEM]
        operands += rows
    else:
        in_specs += [VMEM, SMEM, VMEM, HBM, HBM]
        operands += list(carried)
        aliases = {7: 4, 8: 5}
    if sends is not None:
        in_specs.append(SMEM)
        operands.append(peers)
    in_specs += [ANY] * len(y_list)
    operands += y_list
    out_specs = [VMEM, VMEM, SMEM, VMEM, HBM, HBM]
    out_shape = [
        jax.ShapeDtypeStruct((LOCAL, 128), f32),
        jax.ShapeDtypeStruct((YBLOCKS, 1, BS), f32),
        jax.ShapeDtypeStruct((SLOTS,), f32),
        jax.ShapeDtypeStruct((8, 128), f32),
        pltpu.HBM((MOST, BS, BS), bf16),
        pltpu.HBM((SLOTS, BS, 128), f32),
    ]
    if sends is not None:
        out_specs.append(VMEM)
        out_shape.append(jax.ShapeDtypeStruct((GROUP, 1, BS), f32))
    return pl.pallas_call(
        functools.partial(sweep_kernel, base=base, count=count, first=first, sends=sends),
        in_specs=in_specs,
        out_specs=out_specs,
        out_shape=out_shape,
        scratch_shapes=[
            pltpu.VMEM((LOCAL, DIM), bf16),
            pltpu.VMEM((LOCAL, 128), f32),
            pltpu.SemaphoreType.DMA((BPD, 2)),
            pltpu.VMEM((2, ROWS, DIM), bf16),
            pltpu.SemaphoreType.DMA((3,)),
            pltpu.VMEM((1, 8, BS), f32),
            pltpu.VMEM((LOCAL, 128), f32),
            pltpu.VMEM((BS, 128), f32),
            pltpu.VMEM((8, BS), f32),
            pltpu.SMEM((1,), i32),
            pltpu.SMEM((1,), f32),
            pltpu.VMEM((2, BS, BS), bf16),
            pltpu.SemaphoreType.DMA((2,)),
            pltpu.SMEM((1,), i32),
        ],
        input_output_aliases=aliases,
        compiler_params=params(),
        name=f"sweep_{base}",
    )(*operands)


def load_pair(slot, x_ref, y_refs, x_buf, y_buf, sems):
    rows = pl.ds(pl.multiple_of((slot % BPD) * BS, BS), BS)
    fetch = pltpu.make_async_copy(x_ref.at[rows, :], x_buf, sems.at[0])
    fetch.start()
    fetch.wait()
    for n in range(YBLOCKS):

        @pl.when(slot // BPD == n)
        def _():
            source = y_refs[0].at[n] if n < BPD else y_refs[n - BPD + 1]
            fetch = pltpu.make_async_copy(source, y_buf, sems.at[1])
            fetch.start()
            fetch.wait()


def next_potential(now, half, total, log_count):
    return 0.5 * (now + half + entropy_weight * (log_count - log_two * total))


def fetch_terms(kept_ref, terms_ref, sems, list_ref, seat_of_ref, start, stop):
    def term_copy(n):
        return pltpu.make_async_copy(kept_ref.at[seat_of_ref[list_ref[n]]], terms_ref.at[n], sems.at[n])

    for n in range(MOST):

        @pl.when((n >= start) & (n < stop))
        def _():
            term_copy(n).start()

    return term_copy


def columns_kernel(list_ref, live_ref, seat_of_ref, use_ref, left_ref, *refs, log_count, accs):
    start, stop = 0, live_ref[1]
    acc_refs = refs[:accs]
    x_rows_ref, y_rows_ref, kept_ref, slow_ref, x_ref = refs[accs : accs + 5]
    y_refs = refs[accs + 5 : accs + 6 + FAR]
    next_ref, out_ref, col_ref, weight_ref, state_ref, part_ref, x_buf, y_buf, sems, terms_ref, term_sems = refs[accs + 6 + FAR :]
    term_copy = fetch_terms(kept_ref, terms_ref, term_sems, list_ref, seat_of_ref, start, stop)
    clear_cols(col_ref)
    total = lane_sums(acc_refs)
    state_ref[0:1, :] = jnp.where(total > 0.0, high_of(own_beta(y_rows_ref)), lowest)
    state_ref[1:2, :] = total
    for n in range(SLOTS):

        @pl.when((use_ref[n] > 0) & (left_ref[n] < 0.0))
        def _():
            fetch = pltpu.make_async_copy(slow_ref.at[n], part_ref, sems.at[0])
            fetch.start()
            fetch.wait()
            add_part(part_ref, state_ref, n % BPD)

    half = x_rows_ref[1:2, :]
    f_next = next_potential(x_rows_ref[0:1, :], half, logs(state_ref[0:1, :], state_ref[1:2, :]), log_count)
    next_ref[0:1, :] = f_next
    next_ref[1:2, :] = half
    next_ref[2:8, :] = jnp.zeros((6, LOCAL), f32)
    alpha = (f_next - half) * scale
    state_ref[2:3, :] = alpha
    top = high_of(alpha)
    weight_ref[...] = down(jnp.exp2(alpha - top))
    reach = (top - low_of(alpha))[0, 0]

    def body(step, carry):
        slot = list_ref[step]
        y, b = slot // BPD, slot % BPD
        fits = reach <= left_ref[slot]
        term_copy(step).wait()

        @pl.when(fits)
        def _():
            sums = jnp.zeros((8, BS), f32)
            for c in range(0, BS, 64):
                weight = weight_ref[pl.ds(pl.multiple_of(b * BS + c, 64), 64), :]
                parts = [fold(terms_ref[step, c : c + 64, n : n + 128].astype(f32) * weight) for n in range(0, BS, 128)]
                sums = sums + jnp.concatenate(parts, axis=1)
            put_cols(col_ref, y, top, jnp.sum(sums, axis=0, keepdims=True))

        @pl.when(jnp.logical_not(fits))
        def _():
            load_pair(slot, x_ref, y_refs, x_buf, y_buf, sems)
            for c in range(0, BS, 128):
                row = state_ref[2:3, pl.ds(pl.multiple_of(b * BS + c, 128), 128)]
                part_ref[c : c + 128, :] = jnp.broadcast_to(row, (128, 128)).T
            shifted_cols(x_buf, y_buf, part_ref, col_ref, y)

        return carry

    lax.fori_loop(start, stop, body, 0)
    for n in range(YBLOCKS):
        out_ref[n] = logs(col_ref[n, 0:1, :], col_ref[n, 1:2, :])


def gathered(j, own_ref, came, who_ref):
    terms = [own_ref[j]] + [jnp.where(who_ref[n] == j, came(n), lowest) for n in range(PEERS)]
    top = terms[0]
    for term in terms[1:]:
        top = jnp.maximum(top, term)
    total = jnp.exp2(terms[0] - top)
    for term in terms[1:]:
        total = total + jnp.exp2(term - top)
    return top + jnp.log2(total)


def home_kernel(who_ref, peers_ref, even_in, odd_in, first_ref, second_ref, y_rows_ref, even_out, odd_out, g_ref, *, log_count):
    came = lambda n: (even_in, odd_in)[n // GROUP][n % GROUP]
    betas = []
    for j in range(BPD):
        span = slice(j * BS, (j + 1) * BS)
        half = y_rows_ref[1:2, span]
        g_next = next_potential(y_rows_ref[0:1, span], half, gathered(j, first_ref, came, who_ref), log_count)
        g_ref[0:1, span] = g_next
        betas.append((g_next - half) * scale)
        g_ref[1:2, span] = betas[j]
    g_ref[2:8, :] = jnp.zeros((6, LOCAL), f32)
    for n in range(PEERS):
        out = (even_out, odd_out)[n // GROUP]
        out[n % GROUP, 0:1, :] = jnp.where(who_ref[n] == 1, betas[1], betas[0])
        out[n % GROUP, 1:2, :] = outgoing(second_ref, peers_ref[n])


def home(who, peers, rows_in, first, second, y_rows, log_count):
    return pl.pallas_call(
        functools.partial(home_kernel, log_count=log_count),
        in_specs=[SMEM, SMEM] + [VMEM] * 5,
        out_specs=[VMEM] * 3,
        out_shape=[jax.ShapeDtypeStruct((GROUP, 2, BS), f32)] * 2 + [jax.ShapeDtypeStruct((8, LOCAL), f32)],
        compiler_params=params(),
        name="home",
    )(who, peers, *rows_in, first, second, y_rows)


def rows_kernel(list_ref, live_ref, seat_of_ref, use_ref, left_ref, *refs, log_count, last):
    if last:
        start, stop = live_ref[0], live_ref[1]
        from_ref, who_ref, acc_in, state_in, even_in, odd_in, g_ref, second_ref, y_rows_ref, x_rows_ref = refs[:10]
        refs = refs[10:]
    else:
        start, stop = 0, live_ref[0]
        from_ref, even_in, g_ref = refs[:3]
        refs = refs[3:]
    kept_ref, slow_ref, x_ref = refs[:3]
    y_refs = refs[3 : 4 + FAR]
    refs = refs[4 + FAR :]
    if last:
        f_ref, g_out_ref, acc_ref, state_ref = refs[:4]
        refs = refs[4:]
    else:
        acc_ref, state_ref = refs[:2]
        refs = refs[2:]
    beta_ref, weight_ref, part_ref, x_buf, y_buf, sems, terms_ref, term_sems = refs
    term_copy = fetch_terms(kept_ref, terms_ref, term_sems, list_ref, seat_of_ref, start, stop)
    shift = high_of(g_ref[1:2, :])
    if last:
        acc_ref[...] = acc_in[...]
        state_ref[...] = state_in[...]
    else:
        acc_ref[...] = jnp.zeros((LOCAL, 128), f32)
        state_ref[0:1, :] = jnp.full((1, LOCAL), lowest, f32)
        state_ref[1:8, :] = jnp.zeros((7, LOCAL), f32)
    for n in range(BPD):
        beta_ref[n] = g_ref[1:2, n * BS : (n + 1) * BS]
    for n in range(BPD, YBLOCKS):
        at = from_ref[n] % GROUP
        if last:
            beta_ref[n] = jnp.where(from_ref[n] < GROUP, even_in[at, 0:1, :], odd_in[at, 0:1, :])
        else:
            beta_ref[n] = even_in[at, 0:1, :]
    weight_ref[...] = jnp.exp2(beta_ref[...] - shift)

    def body(step, carry):
        slot = list_ref[step]
        y, b = slot // BPD, slot % BPD
        beta = beta_ref[y]
        reach = jnp.maximum(high_of(beta) - shift, shift - low_of(beta))
        fits = reach[0, 0] <= left_ref[slot]
        term_copy(step).wait()

        @pl.when(fits)
        def _():
            weight = weight_ref[y]
            for c in range(0, BS, 64):
                span = pl.ds(pl.multiple_of(b * BS + c, 64), 64)
                part = acc_ref[span, :]
                for n in range(0, BS, 128):
                    part = part + terms_ref[step, c : c + 64, n : n + 128].astype(f32) * weight[:, n : n + 128]
                acc_ref[span, :] = part

        @pl.when(jnp.logical_not(fits))
        def _():
            load_pair(slot, x_ref, y_refs, x_buf, y_buf, sems)
            shifted_rows(x_buf, y_buf, beta, part_ref)
            add_part(part_ref, state_ref, b)

        return carry

    lax.fori_loop(start, stop, body, 0)
    if not last:
        return
    total = lane_sums([acc_ref])
    top = jnp.where(total > 0.0, shift, lowest)
    top, total = merge(top, total, state_ref[0:1, :], state_ref[1:2, :])
    f_ref[...] = next_potential(x_rows_ref[0:1, :], x_rows_ref[1:2, :], logs(top, total), log_count)
    came = lambda n: (even_in, odd_in)[n // GROUP][n % GROUP, 1:2, :]
    total = jnp.concatenate([gathered(j, second_ref, came, who_ref) for j in range(BPD)], axis=1)
    g_next = next_potential(g_ref[0:1, :], y_rows_ref[1:2, :], total, log_count)
    g_out_ref[...] = moved_exact(g_next, y_rows_ref[2:3, :].astype(i32))


def slots_call(kernel, smem, front, kept, slow, x_blocks, y_list, outs, scratch, name):
    return pl.pallas_call(
        kernel,
        in_specs=[SMEM] * len(smem) + [VMEM] * len(front) + [HBM, HBM, ANY] + [ANY] * len(y_list),
        out_specs=[VMEM] * len(outs),
        scratch_shapes=scratch
        + [
            pltpu.VMEM((BS, 128), f32),
            pltpu.VMEM((BS, DIM), bf16),
            pltpu.VMEM((ROWS, DIM), bf16),
            pltpu.SemaphoreType.DMA((2,)),
            pltpu.VMEM((MOST, BS, BS), bf16),
            pltpu.SemaphoreType.DMA((MOST,)),
        ],
        out_shape=outs,
        compiler_params=params(),
        name=name,
    )(*smem, *front, kept, slow, x_blocks, *y_list)


def seat_tables():
    half = GROUP // 2
    offsets = np.zeros((GROUP, PEERS), np.int32)
    source = np.zeros((GROUP, YBLOCKS), np.int32)
    for seat in range(GROUP):
        odd_seat = (seat + half) % GROUP
        for other in range(GROUP):
            if other != seat and abs(other - seat) <= REACH:
                offsets[seat, other] = other - seat
            off = other - odd_seat
            if off != 0 and abs(off) <= REACH and not 0 <= seat + off < GROUP:
                offsets[seat, GROUP + other] = off
        for k, off in enumerate(ROUNDS[seat % 4]):
            source[seat, BPD + k] = list(offsets[seat]).index(off)
    index = np.full((GROUP, PEERS), -1, np.int32)
    for seat in range(GROUP):
        for k, off in enumerate(ROUNDS[seat % 4]):
            index[seat, offsets[seat] == off] = BPD + k
    return offsets, index, source


def swap(rows, devices, shift):
    groups = [[(GROUP * k + j + shift) % devices for j in range(GROUP)] for k in range(devices // GROUP)]
    return lax.all_to_all(rows, "blk", split_axis=0, concat_axis=0, tiled=True, axis_index_groups=groups)


def on_device(x_points, y_points, x_start, y_start, x_order, y_order, partners, counts):
    devices = lax.axis_size("blk")
    me = lax.axis_index("blk").astype(i32)
    log_count = math.log(LOCAL * devices)
    here = me[None]
    line = lambda v: v.reshape(1, LOCAL)

    y_sent, x_pos = pack_y(here, partners, counts, line(y_order), line(x_order), y_start, x_start, y_points, devices)
    y_came = lax.all_to_all(y_sent, "blk", split_axis=0, concat_axis=0, tiled=True)
    offsets = lax.dynamic_slice(jnp.array(ROUNDS, i32), (me % 4, 0), (1, FAR))[0]
    live = jnp.arange(partners.shape[1], dtype=i32)[None, :] < counts[:, None]
    away = jnp.where(live, partners // BPD - me, devices)
    local_use = [((away == 0) & (partners % BPD == j)).any(axis=1) for j in range(BPD)]
    far = away[None, :, :] == offsets[:, None, None]
    use = jnp.concatenate([jnp.stack(local_use), far.any(axis=2)]).astype(i32).reshape(SLOTS)
    number = jnp.minimum(jnp.maximum(jnp.cumsum(use) - 1, 0), MOST - 1)

    peer_offsets, peer_index, peer_source = seat_tables()
    row = lambda t: lax.dynamic_slice(jnp.asarray(t), (me % GROUP, 0), (1, t.shape[1]))[0]
    peers, source, off = row(peer_index), row(peer_source), row(peer_offsets)

    far_slot = jnp.repeat(source >= GROUP, BPD).astype(i32)
    near = jnp.cumsum(use * (1 - far_slot))
    rank = jnp.where(far_slot > 0, near[-1] + jnp.cumsum(use * far_slot), near) - 1
    count = jnp.minimum(jnp.sum(use), MOST)
    step = jnp.minimum(jnp.arange(MOST, dtype=i32), count - 1)
    at = (rank[None, :] == step[:, None]) & (use[None, :] > 0)
    slots = jnp.sum(jnp.where(at, jnp.arange(SLOTS, dtype=i32)[None, :], 0), axis=1)
    live_counts = jnp.stack([jnp.minimum(near[-1], count), count])
    x_pos, use, number, slots, live_counts, peers, source, off = lax.optimization_barrier((x_pos, use, number, slots, live_counts, peers, source, off))
    x_sent = pack_x(x_pos, x_points)
    y_came, x_sent = lax.optimization_barrier((y_came, x_sent))
    x_came = lax.all_to_all(x_sent, "blk", split_axis=0, concat_axis=0, tiled=True)
    lists = [slots, live_counts, number]
    y_rows, table, y_own, *y_sends = unpack_y(here, y_came, devices)

    def far_block(k):
        pairs = [(i, i + ROUNDS[i % 4][k]) for i in range(devices) if 0 <= i + ROUNDS[i % 4][k] < devices]
        return lax.ppermute(y_sends[k], "blk", pairs)

    y_far = [far_block(k) for k in range(FAR - 1)]
    x_came, y_far[0], y_sends[5] = lax.optimization_barrier((x_came, y_far[0], y_sends[5]))
    y_far.append(far_block(5))
    x_blocks, alpha, x_rows, who = unpack_x(here, off, x_came, table, devices)


    common = (use, number, x_blocks, alpha)
    acc_0, *carried = sweep(common, [y_own], 0, None, [x_rows, y_rows])
    acc_1, *carried = sweep(common, y_far[:EARLY], BPD, carried)
    acc_2, *carried, odd_out = sweep(common, y_far[EARLY:-1], BPD + EARLY, carried, None, peers, 1)
    acc_3, cols_first, left, _, kept, slow, even_out = sweep(common, y_far[-1:], YBLOCKS - 1, carried, None, peers, 0)
    y_all = [y_own] + y_far

    odd_in = swap(odd_out, devices, GROUP // 2)
    even_in = swap(even_out, devices, 0)
    accs = [acc_0, acc_1, acc_2, acc_3]
    x_next, cols_second = slots_call(
        functools.partial(columns_kernel, log_count=log_count, accs=len(accs)),
        lists + [use, left],
        accs + [x_rows, y_rows],
        kept,
        slow,
        x_blocks,
        y_all,
        [jax.ShapeDtypeStruct((8, LOCAL), f32), jax.ShapeDtypeStruct((YBLOCKS, 1, BS), f32)],
        [pltpu.VMEM((YBLOCKS, 8, BS), f32), pltpu.VMEM((LOCAL, 128), f32), pltpu.VMEM((8, LOCAL), f32)],
        "columns",
    )
    even_out, odd_out, g_one = home(who, peers, (even_in, odd_in), cols_first, cols_second, y_rows, log_count)
    even_in = swap(even_out, devices, 0)
    odd_in = swap(odd_out, devices, GROUP // 2)
    row_scratch = [pltpu.VMEM((YBLOCKS, 1, BS), f32), pltpu.VMEM((YBLOCKS, 1, BS), f32)]
    acc, state = slots_call(
        functools.partial(rows_kernel, log_count=log_count, last=False),
        lists + [use, left, source],
        [even_in, g_one],
        kept,
        slow,
        x_blocks,
        y_all,
        [jax.ShapeDtypeStruct((LOCAL, 128), f32), jax.ShapeDtypeStruct((8, LOCAL), f32)],
        row_scratch,
        "rows_near",
    )
    f_two, g_two = slots_call(
        functools.partial(rows_kernel, log_count=log_count, last=True),
        lists + [use, left, source, who],
        [acc, state, even_in, odd_in, g_one, cols_second, y_rows, x_next],
        kept,
        slow,
        x_blocks,
        y_all,
        [jax.ShapeDtypeStruct((1, LOCAL), f32)] * 2,
        [pltpu.VMEM((LOCAL, 128), f32), pltpu.VMEM((8, LOCAL), f32)] + row_scratch,
        "rows_far",
    )
    return f_two.reshape(LOCAL), g_two.reshape(LOCAL)


def solution(mesh):
    placed_as = (
        P("blk", None),
        P("blk", None),
        P("blk"),
        P("blk"),
        P("blk"),
        P("blk"),
        P("blk", None),
        P("blk"),
    )
    return jax.shard_map(
        on_device, mesh=mesh, in_specs=placed_as, out_specs=(P("blk"), P("blk")), check_vma=False
    )
```

```python
import functools
import math

import jax
import jax.numpy as jnp
import numpy as np
from jax import lax
from jax.experimental import pallas as pl
from jax.experimental.pallas import tpu as pltpu
from jax.sharding import PartitionSpec as P

DIM = 512
BS = 1024
BPD = 2
REACH = 3
LOCAL = BPD * BS
EXTRA = 128
WIDE = DIM + EXTRA
TAIL = 16
ROWS = BS + TAIL
CHUNK = 512
PART = 256
ROUNDS = ((1, -3, 3, -1, -2, 2), (-1, 3, -3, 1, -2, 2), (1, -3, 3, -1, 2, -2), (-1, 3, -3, 1, 2, -2))
EARLY = 4
FAR = len(ROUNDS[0])
YBLOCKS = BPD + FAR
SLOTS = BPD * YBLOCKS
MOST = 12
GROUP = 8
PEERS = 2 * GROUP
X_LANES = EXTRA // 2

entropy_weight = 0.05
scale = math.log2(math.e) / entropy_weight
log_two = math.log(2.0)
lowest = -1e30
exponent_room = 112.0
mebi = 1024 * 1024

f32 = jnp.float32
bf16 = jnp.bfloat16
i32 = jnp.int32

SMEM = pl.BlockSpec(memory_space=pltpu.SMEM)
ANY = pl.BlockSpec(memory_space=pl.ANY)
VMEM = pl.BlockSpec(memory_space=pltpu.VMEM)
HBM = pl.BlockSpec(memory_space=pltpu.HBM)


def iota(shape, dim):
    return lax.broadcasted_iota(i32, shape, dim)


def dot(a, b):
    return jnp.dot(a, b, preferred_element_type=f32)


def nt_dot(a, b):
    return lax.dot_general(a, b, (((1,), (1,)), ((), ())), preferred_element_type=f32)


def ones_where(mask):
    return jnp.where(mask, 1.0, 0.0).astype(bf16)


def params():
    return pltpu.CompilerParams(vmem_limit_bytes=64 * mebi)


def whole(shape):
    return pl.BlockSpec(shape, lambda *t: (0,) * len(shape))


def laid_out(square):
    return jnp.concatenate([square[n : n + 1, :] for n in range(square.shape[0])], axis=1)


def down(row):
    parts = [jnp.broadcast_to(row[:, c : c + 128], (128, 128)).T for c in range(0, row.shape[1], 128)]
    return jnp.concatenate(parts, axis=0)


def moved(values, place):
    high = iota((16, LOCAL), 0) == lax.shift_right_logical(place, 7)
    low = ones_where(iota((128, LOCAL), 0) == jnp.bitwise_and(place, 127))
    stack = jnp.concatenate([jnp.where(high, v, 0.0) for v in values], axis=0).astype(bf16)
    out = nt_dot(stack, low)
    return [laid_out(out[16 * n : 16 * n + 16, :]) for n in range(len(values))]


def moved_exact(value, place):
    first = value.astype(bf16).astype(f32)
    second = (value - first).astype(bf16).astype(f32)
    parts = moved([first, second, value - first - second], place)
    return parts[0] + parts[1] + parts[2]


def before_matrix():
    return ones_where(iota((128, 128), 0) < iota((128, 128), 1))


def plan(order, start, devices, first_lane):
    share = LOCAL // devices
    target = lax.shift_right_logical(order, 11)
    hit = iota((devices, LOCAL), 0) == target
    hot = ones_where(hit)
    before = before_matrix()
    every = jnp.ones((128, 128), bf16)
    seen = jnp.zeros((devices, 128), f32)
    earlier = []
    for c in range(0, LOCAL, 128):
        piece = hot[:, c : c + 128]
        earlier.append(dot(piece, before) + seen)
        seen = seen + dot(piece, every)
    earlier = jnp.concatenate(earlier, axis=1)
    rank = jnp.sum(jnp.where(hit, earlier, 0.0), axis=0, keepdims=True).astype(i32)
    within = jnp.bitwise_and(order, LOCAL - 1)
    high = lax.shift_right_logical(within, 6).astype(f32)
    low = jnp.bitwise_and(within, 63).astype(f32)
    row = iota((EXTRA, LOCAL), 0) - first_lane
    field = row // share
    value = jnp.where(field == 0, high, jnp.where(field == 1, low, start))
    mine = (row >= 0) & (row < 3 * share) & (row % share == rank)
    return target * share + rank, nt_dot(hot, jnp.where(mine, value, 0.0).astype(bf16))


def partner_offsets(me):
    kind = jnp.bitwise_and(me, 3)
    out = []
    for k in range(FAR):
        value = jnp.int32(ROUNDS[0][k])
        for n in range(1, 4):
            value = jnp.where(kind == n, jnp.int32(ROUNDS[n][k]), value)
        out.append(value)
    return out


def pack_y_kernel(
    me_ref, partners_ref, counts_ref, y_order, x_order, y_start, x_start, points, out_ref, x_pos_ref, pos_ref, table_ref,
    *, devices
):
    step = pl.program_id(0)
    share = LOCAL // devices

    @pl.when(step == 0)
    def _():
        y_pos, y_table = plan(y_order[...], y_start[...].astype(f32).reshape(1, LOCAL), devices, 0)
        x_pos, x_table = plan(x_order[...], x_start[...].astype(f32).reshape(1, LOCAL), devices, X_LANES)
        pos_ref[...] = y_pos
        x_pos_ref[...] = x_pos
        me = me_ref[0]
        offsets = partner_offsets(me)
        need = [jnp.int32(0)] * FAR
        for b in range(BPD):
            for s in range(partners_ref.shape[1]):
                block = partners_ref[b, s]
                away = lax.shift_right_logical(block, 1) - me
                for k in range(FAR):
                    listed = (s < counts_ref[b]) & (away == offsets[k])
                    need[k] = jnp.where(listed, jnp.bitwise_and(block, 1), need[k])
        table = y_table + x_table
        row, lane = iota(table.shape, 0), iota(table.shape, 1)
        for k in range(FAR):
            table = jnp.where((row == me + offsets[k]) & (lane == 3 * share), need[k].astype(f32), table)
        table_ref[...] = table

    base = step * CHUNK
    hot = ones_where(iota((CHUNK, LOCAL), 0) + base == pos_ref[...])
    out_ref[:, :DIM] = dot(hot, points[...]).astype(bf16)
    some = CHUNK // share
    table = table_ref[pl.ds(pl.multiple_of(step * some, some), some), :]
    out_ref[:, DIM:] = jnp.broadcast_to(table[:, None, :], (some, share, EXTRA)).reshape(CHUNK, EXTRA).astype(bf16)


def pack_y(me, partners, counts, y_order, x_order, y_start, x_start, points, devices):
    row = whole((1, LOCAL))
    return pl.pallas_call(
        functools.partial(pack_y_kernel, devices=devices),
        grid=(LOCAL // CHUNK,),
        in_specs=[SMEM, SMEM, SMEM, row, row, whole((LOCAL,)), whole((LOCAL,)), whole((LOCAL, DIM))],
        out_specs=[pl.BlockSpec((CHUNK, WIDE), lambda t: (t, 0)), row],
        out_shape=[pltpu.HBM((LOCAL, WIDE), bf16), jax.ShapeDtypeStruct((1, LOCAL), i32)],
        scratch_shapes=[pltpu.VMEM((1, LOCAL), i32), pltpu.VMEM((devices, EXTRA), f32)],
        compiler_params=params(),
        name="pack_y",
    )(me, partners, counts, y_order, x_order, y_start, x_start, points)


def pack_x_kernel(pos_ref, points_ref, out_ref):
    base = pl.program_id(0) * CHUNK
    hot = ones_where(iota((CHUNK, LOCAL), 0) + base == pos_ref[...])
    out_ref[...] = dot(hot, points_ref[...]).astype(bf16)


def pack_x(pos, points):
    return pl.pallas_call(
        pack_x_kernel,
        grid=(LOCAL // CHUNK,),
        in_specs=[whole((1, LOCAL)), whole((LOCAL, DIM))],
        out_specs=pl.BlockSpec((CHUNK, DIM), lambda t: (t, 0)),
        out_shape=pltpu.HBM((LOCAL, DIM), bf16),
        compiler_params=params(),
        name="pack_x",
    )(pos, points)


WINDOW = PART + 16
HELD = BS + WINDOW + 16


def arrived(table, base, with_low):
    share = 16
    row, lane = iota((EXTRA, EXTRA), 0), iota((EXTRA, EXTRA), 1)
    pick = jnp.where(row == base + lane % share, 64.0 if with_low else 1.0, 0.0)
    if with_low:
        pick = jnp.where(row == base + share + lane % share, 1.0, pick)
    values = dot(table, pick.astype(bf16))
    values = jnp.where(row % (EXTRA // share) == lane // share, values, 0.0)
    return jnp.sum(values.reshape(LOCAL // 128, EXTRA // share, 128), axis=1)


def unpack_y_kernel(me_ref, came_ref, rows_ref, table_ref, own_ref, *rest, devices):
    sends = rest[:FAR]
    held, sems, own_sem, points_buf, extra_buf, in_sems = rest[FAR:]
    share = LOCAL // devices
    me = me_ref[0]
    extra_in = pltpu.make_async_copy(came_ref.at[:, pl.ds(DIM, EXTRA)], extra_buf, in_sems.at[0])
    points_in = pltpu.make_async_copy(came_ref.at[:, pl.ds(0, DIM)], points_buf, in_sems.at[1])
    extra_in.start()
    points_in.start()
    held[...] = jnp.zeros(held.shape, bf16)
    extra_in.wait()
    table = dot(ones_where(iota((devices, LOCAL), 1) == iota((devices, LOCAL), 0) * share), extra_buf[...])
    table_ref[...] = table
    place_square = arrived(table.astype(bf16), 0, True)
    place = laid_out(place_square)
    start = laid_out(arrived(table.astype(bf16), 2 * share, False))

    picks = []
    offsets = partner_offsets(me)
    small_row, small_lane = iota((devices, EXTRA), 0), iota((devices, EXTRA), 1)
    for k in range(FAR):
        here = (small_row == me + offsets[k]) & (small_lane == 3 * share)
        picks.append(jnp.sum(jnp.where(here, table, 0.0)) > 0.5)

    second = place >= float(BS)
    square = ones_where(place_square >= float(BS))
    totals = dot(square, jnp.ones((128, 128), bf16)).astype(bf16)
    earlier = dot(square, before_matrix()) + dot(ones_where(iota((16, 16), 1) < iota((16, 16), 0)), totals)
    ones_before = laid_out(earlier)
    dest = jnp.where(second, ones_before, iota((1, LOCAL), 1).astype(f32) - ones_before).astype(i32)
    seat = jnp.where(second, dest + BS, dest)
    position = place.astype(i32)
    start_row, high_row, low_row = moved(
        [start, lax.shift_right_logical(position, 6).astype(f32), jnp.bitwise_and(position, 63).astype(f32)], seat
    )
    rows_ref[0:1, :] = start_row
    rows_ref[2:3, :] = high_row * 64.0 + low_row
    rows_ref[3:8, :] = jnp.zeros((5, LOCAL), f32)
    sixteen, lane16 = iota((16, 128), 0), iota((16, 128), 1)
    points_in.wait()

    for j in range(BPD):
        here = jnp.where(second if j else jnp.logical_not(second), dest, -1)
        for c in range(LOCAL // PART):
            span = slice(c * PART, (c + 1) * PART)
            begin = jnp.sum(jnp.where((sixteen == c * PART // 128) & (lane16 == 0), earlier, 0.0)).astype(i32)
            if j == 0:
                begin = c * PART - begin
            begin = pl.multiple_of(lax.shift_left(lax.shift_right_logical(begin, 4), 4), 16)
            hot = ones_where(iota((WINDOW, PART), 0) + begin == here[:, span])
            part = dot(hot, points_buf[span, :]).astype(bf16)
            held[j, pl.ds(begin, WINDOW), :] = held[j, pl.ds(begin, WINDOW), :] + part
        half = []
        for c in range(0, BS, PART):
            points = held[j, c : c + PART, :].astype(f32)
            total = 0.5 * jnp.sum(points * points, axis=1, keepdims=True)
            half.append(jnp.broadcast_to(total, (PART, 128)).T[0:1, :])
        half = jnp.concatenate(half, axis=1)
        block = slice(j * BS, (j + 1) * BS)
        rows_ref[1:2, block] = half
        beta = start_row[:, block] - half
        first = beta.astype(bf16).astype(f32)
        next_part = (beta - first).astype(bf16).astype(f32)
        most = jnp.max(half, axis=1, keepdims=True) * 1.01
        sub = iota((TAIL, DIM), 0)
        tail = jnp.zeros((TAIL, DIM), f32) + most
        for n, piece in enumerate((first, next_part, beta - first - next_part)):
            tail = jnp.where(sub == 2 * n, piece[:, :DIM], tail)
            tail = jnp.where(sub == 2 * n + 1, piece[:, DIM:], tail)
        held[j, BS:ROWS, :] = tail.astype(bf16)
        done = held.at[j, pl.ds(0, ROWS), :]
        for k in range(FAR):
            wanted = picks[k] if j == 1 else jnp.logical_not(picks[k])

            @pl.when(wanted)
            def _():
                pltpu.make_async_copy(done, sends[k], sems.at[k]).start()

        pltpu.make_async_copy(done, own_ref.at[j], own_sem.at[j]).start()

    done = held.at[0, pl.ds(0, ROWS), :]
    for k in range(FAR):
        pltpu.make_async_copy(done, sends[k], sems.at[k]).wait()
    for j in range(BPD):
        pltpu.make_async_copy(done, own_ref.at[j], own_sem.at[j]).wait()


def unpack_y(me, came, devices):
    return pl.pallas_call(
        functools.partial(unpack_y_kernel, devices=devices),
        in_specs=[SMEM, ANY],
        out_specs=[VMEM, VMEM] + [HBM] * (1 + FAR),
        out_shape=[
            jax.ShapeDtypeStruct((8, LOCAL), f32),
            jax.ShapeDtypeStruct((devices, EXTRA), f32),
            pltpu.HBM((BPD, ROWS, DIM), bf16),
        ]
        + [pltpu.HBM((ROWS, DIM), bf16)] * FAR,
        scratch_shapes=[
            pltpu.VMEM((BPD, HELD, DIM), bf16),
            pltpu.SemaphoreType.DMA((FAR,)),
            pltpu.SemaphoreType.DMA((BPD,)),
            pltpu.VMEM((LOCAL, DIM), bf16),
            pltpu.VMEM((LOCAL, EXTRA), bf16),
            pltpu.SemaphoreType.DMA((2,)),
        ],
        compiler_params=params(),
        name="unpack_y",
    )(me, came)


def unpack_x_kernel(
    me_ref, peer_ref, came_ref, table_ref, points_ref, alpha_ref, rows_ref, who_ref, place_ref, start_ref, *, devices
):
    step = pl.program_id(0)

    @pl.when(step == 0)
    def _():
        table = table_ref[...].astype(bf16)
        place = laid_out(arrived(table, X_LANES, True)).astype(i32)
        place_ref[...] = place
        start_ref[...] = moved([laid_out(arrived(table, X_LANES + 32, False))], place)[0]
        row, lane = iota((EXTRA, EXTRA), 0), iota((EXTRA, EXTRA), 1)
        for n in range(PEERS):
            peer = me_ref[0] + peer_ref[n]
            wants = jnp.sum(jnp.where((row == peer) & (lane == 3 * LOCAL // devices), table_ref[...], 0.0)) > 0.5
            valid = (peer_ref[n] != 0) & (peer >= 0) & (peer < devices)
            who_ref[n] = jnp.where(valid, jnp.where(wants, 1, 0), -1)

    base = step * CHUNK
    hot = ones_where(iota((CHUNK, LOCAL), 0) + base == place_ref[...])
    points = dot(hot, came_ref[...])
    points_ref[...] = points.astype(bf16)
    half = jnp.broadcast_to(0.5 * jnp.sum(points * points, axis=1, keepdims=True), (CHUNK, 128))
    start = start_ref[:, pl.ds(pl.multiple_of(base, CHUNK), CHUNK)]
    alpha_ref[...] = (down(start) - half) * scale
    rows_ref[0:1, :] = start
    rows_ref[1:8, :] = jnp.concatenate([half[c : c + 128, :].T[0:7, :] for c in range(0, CHUNK, 128)], axis=1)


def unpack_x(me, peer_offsets, came, table, devices):
    return pl.pallas_call(
        functools.partial(unpack_x_kernel, devices=devices),
        grid=(LOCAL // CHUNK,),
        in_specs=[SMEM, SMEM, whole((LOCAL, DIM)), whole((EXTRA, EXTRA))],
        out_specs=[
            pl.BlockSpec((CHUNK, DIM), lambda t: (t, 0)),
            pl.BlockSpec((CHUNK, 128), lambda t: (t, 0)),
            pl.BlockSpec((8, CHUNK), lambda t: (0, t)),
            SMEM,
        ],
        out_shape=[
            pltpu.HBM((LOCAL, DIM), bf16),
            pltpu.HBM((LOCAL, 128), f32),
            jax.ShapeDtypeStruct((8, LOCAL), f32),
            jax.ShapeDtypeStruct((PEERS,), i32),
        ],
        scratch_shapes=[pltpu.VMEM((1, LOCAL), i32), pltpu.VMEM((1, LOCAL), f32)],
        compiler_params=params(),
        name="unpack_x",
    )(me, peer_offsets, came, table)


def merge(top, total, other_top, other_total):
    new = jnp.maximum(top, other_top)
    return new, total * jnp.exp2(top - new) + other_total * jnp.exp2(other_top - new)


def logs(top, total):
    return jnp.where(total > 0.0, top + jnp.log2(total), lowest)


def high_of(row):
    return jnp.max(row, axis=1, keepdims=True)


def low_of(row):
    return jnp.min(row, axis=1, keepdims=True)


def put_cols(col_ref, y, part_top, part_total):
    top, total = merge(col_ref[y, 0:1, :], col_ref[y, 1:2, :], part_top, part_total)
    col_ref[y, 0:1, :] = top
    col_ref[y, 1:2, :] = total


def clear_cols(col_ref):
    col_ref[:, 0:1, :] = jnp.full((col_ref.shape[0], 1, BS), lowest, f32)
    col_ref[:, 1:2, :] = jnp.zeros((col_ref.shape[0], 1, BS), f32)


def shifted_rows(x_ref, y_ref, beta, part_ref):
    def body(c, carry):
        span = pl.ds(pl.multiple_of(c * PART, PART), PART)
        terms = nt_dot(x_ref[span, :], y_ref[0:BS, :]) * scale + beta
        top = jnp.max(terms, axis=1, keepdims=True)
        total = jnp.sum(jnp.exp2(terms - top), axis=1, keepdims=True)
        part_ref[span, :] = jnp.where(iota((PART, 128), 1) == 0, top, total)
        return carry

    lax.fori_loop(0, BS // PART, body, 0)


def shifted_cols(x_ref, y_ref, alpha_ref, col_ref, y):
    def body(c, carry):
        span = pl.ds(pl.multiple_of(c * PART, PART), PART)
        terms = nt_dot(x_ref[span, :], y_ref[0:BS, :]) * scale + alpha_ref[span, 0:1]
        top = jnp.max(terms, axis=0, keepdims=True)
        put_cols(col_ref, y, top, jnp.sum(jnp.exp2(terms - top), axis=0, keepdims=True))
        return carry

    lax.fori_loop(0, BS // PART, body, 0)


def add_part(part_ref, state_ref, b):
    for c in range(0, BS, 128):
        part = part_ref[c : c + 128, :].T
        span = pl.ds(pl.multiple_of(b * BS + c, 128), 128)
        top, total = merge(state_ref[0:1, span], state_ref[1:2, span], part[0:1, :], part[1:2, :])
        state_ref[0:1, span] = top
        state_ref[1:2, span] = total


def lane_sums(refs):
    out = []
    for c in range(0, LOCAL, 128):
        part = refs[0][c : c + 128, :]
        for ref in refs[1:]:
            part = part + ref[c : c + 128, :]
        out.append(jnp.sum(part.T, axis=0, keepdims=True))
    return jnp.concatenate(out, axis=1)


def fold(values):
    return jnp.sum(values.reshape(values.shape[0] // 8, 8, 128), axis=0)


def own_beta(y_rows_ref):
    return (y_rows_ref[0:1, :] - y_rows_ref[1:2, :]) * scale


def sweep_kernel(*refs, base, count, first, sends):
    use_ref, seat_of_ref, x_ref, alpha_ref = refs[:4]
    refs = refs[4:]
    if first:
        x_rows_ref, y_rows_ref = refs[:2]
        refs = refs[2:]
    else:
        cols_in, left_in, stat_in = refs[:3]
        refs = refs[5:]
    if sends is not None:
        peers_ref = refs[0]
        refs = refs[1:]
    y_refs = refs[:1] if first else refs[:count]
    refs = refs[len(y_refs) :]
    acc_ref, cols_ref, left_ref, stat_ref, kept_ref, slow_ref = refs[:6]
    refs = refs[6:]
    if sends is not None:
        group_out = refs[0]
        refs = refs[1:]
    x_buf, alpha_buf, x_sems, y_buf, sems, col_ref, weight_ref, part_ref, beta_ref, fit_ref, room_ref, tiles, tile_sems, tile_count = refs

    def copy(n):
        source = y_refs[0].at[n] if first else y_refs[n]
        return pltpu.make_async_copy(source, y_buf.at[n % 2], sems.at[n % 2])

    def x_copies(n):
        rows = pl.ds(n * BS, BS)
        return (
            pltpu.make_async_copy(x_ref.at[rows, :], x_buf.at[rows, :], x_sems.at[n, 0]),
            pltpu.make_async_copy(alpha_ref.at[rows, :], alpha_buf.at[rows, :], x_sems.at[n, 1]),
        )

    copy(0).start()
    for part in x_copies(0):
        part.start()
    tile_count[0] = 0
    acc_ref[...] = jnp.zeros((LOCAL, 128), f32)

    def tile_copy(at, seat):
        return pltpu.make_async_copy(tiles.at[at], kept_ref.at[seat], tile_sems.at[at])

    def part_copy(at, seat, c):
        rows = pl.ds(c, PART)
        return pltpu.make_async_copy(tiles.at[at, rows, :], kept_ref.at[seat, rows, :], tile_sems.at[at])

    if first:
        for n in range(SLOTS):
            left_ref[n] = -1.0
        alpha = (x_rows_ref[0:1, :] - x_rows_ref[1:2, :]) * scale
        alpha_top = high_of(alpha)
        lane = iota((8, 128), 1)
        beta_top = high_of(own_beta(y_rows_ref))
        most = high_of(x_rows_ref[1:2, :]) * 1.01
        spread = alpha_top - low_of(alpha)
        stat_ref[...] = jnp.where(
            lane == 0, alpha_top, jnp.where(lane == 1, spread, jnp.where(lane == 2, most, beta_top))
        )
    else:
        for n in range(SLOTS):
            left_ref[n] = left_in[n]
        cols_ref[...] = cols_in[...]
        stat_ref[...] = stat_in[...]

    def body(step, carry):
        y, b = step // BPD, step % BPD
        slot = base * BPD + step
        for n in range(count):

            @pl.when(step == BPD * n)
            def _():
                copy(n).wait()
                if n + 1 < count:
                    copy(n + 1).start()

        for n in range(BPD):

            @pl.when(step == n)
            def _():
                for part in x_copies(n):
                    part.wait()
                if n + 1 < BPD:
                    for part in x_copies(n + 1):
                        part.start()
                rows = slice(n * BS, (n + 1) * BS)
                weight_ref[rows, :] = jnp.exp2(alpha_buf[rows, :] - stat_ref[0:1, 0:1])

        now = y_buf.at[y % 2]
        rows_from = b * BS

        @pl.when(b == 0)
        def _():
            clear_cols(col_ref)
            tail = now[BS:ROWS, :].astype(f32)
            halves = [tail[n : n + 1, :] + tail[n + 2 : n + 3, :] + tail[n + 4 : n + 5, :] for n in range(2)]
            beta = jnp.concatenate(halves, axis=1) * scale
            shift = stat_ref[0:1, 3:4]
            left = exponent_room - 2.0 * scale * jnp.sqrt(tail[6:7, 0:1] * stat_ref[0:1, 2:3])
            reach = jnp.maximum(stat_ref[0:1, 1:2], jnp.maximum(high_of(beta) - shift, shift - low_of(beta)))
            beta_ref[0:1, :] = beta
            beta_ref[1:2, :] = jnp.exp2(beta - shift)
            room_ref[0] = left[0, 0]
            fit_ref[0] = jnp.where((left - reach)[0, 0] >= 0.0, 1, 0)

        @pl.when(use_ref[slot] > 0)
        def _():
            fits = fit_ref[0] > 0

            @pl.when(fits)
            def _():
                left_ref[slot] = room_ref[0]
                done = tile_count[0]
                tile_count[0] = done + 1
                at = done % 2

                @pl.when(done > 1)
                def _():
                    tile_copy(at, 0).wait()

                weight = beta_ref[1:2, :]
                sums = jnp.zeros((8, BS), f32)
                for c in range(0, BS, PART):
                    span = pl.ds(pl.multiple_of(rows_from + c, PART), PART)
                    terms = jnp.exp2(nt_dot(x_buf[span, :], now[0:BS, :]) * scale)
                    tiles[at, c : c + PART, :] = terms.astype(bf16)
                    part_copy(at, seat_of_ref[slot], c).start()
                    row_part = acc_ref[span, :]
                    col_parts = []
                    for n in range(0, BS, 128):
                        piece = terms[:, n : n + 128]
                        row_part = row_part + piece * weight[:, n : n + 128]
                        col_parts.append(fold(piece * weight_ref[span, :]))
                    acc_ref[span, :] = row_part
                    sums = sums + jnp.concatenate(col_parts, axis=1)
                put_cols(col_ref, 0, stat_ref[0:1, 0:1], jnp.sum(sums, axis=0, keepdims=True))

            @pl.when(jnp.logical_not(fits))
            def _():
                block = pl.ds(pl.multiple_of(rows_from, BS), BS)
                shifted_rows(x_buf.at[block, :], now, beta_ref[0:1, :], part_ref)
                out = pltpu.make_async_copy(part_ref, slow_ref.at[slot], sems.at[2])
                out.start()
                shifted_cols(x_buf.at[block, :], now, alpha_buf.at[block, :], col_ref, 0)
                out.wait()

        @pl.when(b == BPD - 1)
        def _():
            cols_ref[base + y] = logs(col_ref[0, 0:1, :], col_ref[0, 1:2, :])

        return carry

    lax.fori_loop(0, BPD * count, body, 0)
    for n in range(2):

        @pl.when(tile_count[0] > n)
        def _():
            tile_copy(n, 0).wait()

    if sends is not None:
        for n in range(GROUP):
            group_out[n] = outgoing(cols_ref, peers_ref[sends * GROUP + n])


def outgoing(cols_ref, index):
    return jnp.where(index < 0, lowest, cols_ref[jnp.maximum(index, 0)])


def sweep(common, y_list, base, carried, rows=None, peers=None, sends=None):
    first = carried is None
    count = BPD if first else len(y_list)
    in_specs = [SMEM, SMEM, HBM, HBM]
    operands = list(common)
    aliases = {}
    if first:
        in_specs += [VMEM, VMEM]
        operands += rows
    else:
        in_specs += [VMEM, SMEM, VMEM, HBM, HBM]
        operands += list(carried)
        aliases = {7: 4, 8: 5}
    if sends is not None:
        in_specs.append(SMEM)
        operands.append(peers)
    in_specs += [ANY] * len(y_list)
    operands += y_list
    out_specs = [VMEM, VMEM, SMEM, VMEM, HBM, HBM]
    out_shape = [
        jax.ShapeDtypeStruct((LOCAL, 128), f32),
        jax.ShapeDtypeStruct((YBLOCKS, 1, BS), f32),
        jax.ShapeDtypeStruct((SLOTS,), f32),
        jax.ShapeDtypeStruct((8, 128), f32),
        pltpu.HBM((MOST, BS, BS), bf16),
        pltpu.HBM((SLOTS, BS, 128), f32),
    ]
    if sends is not None:
        out_specs.append(VMEM)
        out_shape.append(jax.ShapeDtypeStruct((GROUP, 1, BS), f32))
    return pl.pallas_call(
        functools.partial(sweep_kernel, base=base, count=count, first=first, sends=sends),
        in_specs=in_specs,
        out_specs=out_specs,
        out_shape=out_shape,
        scratch_shapes=[
            pltpu.VMEM((LOCAL, DIM), bf16),
            pltpu.VMEM((LOCAL, 128), f32),
            pltpu.SemaphoreType.DMA((BPD, 2)),
            pltpu.VMEM((2, ROWS, DIM), bf16),
            pltpu.SemaphoreType.DMA((3,)),
            pltpu.VMEM((1, 8, BS), f32),
            pltpu.VMEM((LOCAL, 128), f32),
            pltpu.VMEM((BS, 128), f32),
            pltpu.VMEM((8, BS), f32),
            pltpu.SMEM((1,), i32),
            pltpu.SMEM((1,), f32),
            pltpu.VMEM((2, BS, BS), bf16),
            pltpu.SemaphoreType.DMA((2,)),
            pltpu.SMEM((1,), i32),
        ],
        input_output_aliases=aliases,
        compiler_params=params(),
        name=f"sweep_{base}",
    )(*operands)


def load_pair(slot, x_ref, y_refs, x_buf, y_buf, sems):
    rows = pl.ds(pl.multiple_of((slot % BPD) * BS, BS), BS)
    fetch = pltpu.make_async_copy(x_ref.at[rows, :], x_buf, sems.at[0])
    fetch.start()
    fetch.wait()
    for n in range(YBLOCKS):

        @pl.when(slot // BPD == n)
        def _():
            source = y_refs[0].at[n] if n < BPD else y_refs[n - BPD + 1]
            fetch = pltpu.make_async_copy(source, y_buf, sems.at[1])
            fetch.start()
            fetch.wait()


def next_potential(now, half, total, log_count):
    return 0.5 * (now + half + entropy_weight * (log_count - log_two * total))


def fetch_terms(kept_ref, terms_ref, sems, list_ref, seat_of_ref, start, stop):
    def term_copy(n):
        return pltpu.make_async_copy(kept_ref.at[seat_of_ref[list_ref[n]]], terms_ref.at[n], sems.at[n])

    for n in range(MOST):

        @pl.when((n >= start) & (n < stop))
        def _():
            term_copy(n).start()

    return term_copy


def columns_kernel(list_ref, live_ref, seat_of_ref, use_ref, left_ref, *refs, log_count, accs):
    start, stop = 0, live_ref[2]
    acc_refs = refs[:accs]
    x_rows_ref, y_rows_ref, kept_ref, slow_ref, x_ref = refs[accs : accs + 5]
    y_refs = refs[accs + 5 : accs + 6 + FAR]
    next_ref, out_ref, col_ref, weight_ref, state_ref, part_ref, x_buf, y_buf, sems, terms_ref, term_sems = refs[accs + 6 + FAR :]
    term_copy = fetch_terms(kept_ref, terms_ref, term_sems, list_ref, seat_of_ref, start, stop)
    clear_cols(col_ref)
    total = lane_sums(acc_refs)
    state_ref[0:1, :] = jnp.where(total > 0.0, high_of(own_beta(y_rows_ref)), lowest)
    state_ref[1:2, :] = total
    for n in range(SLOTS):

        @pl.when((use_ref[n] > 0) & (left_ref[n] < 0.0))
        def _():
            fetch = pltpu.make_async_copy(slow_ref.at[n], part_ref, sems.at[0])
            fetch.start()
            fetch.wait()
            add_part(part_ref, state_ref, n % BPD)

    half = x_rows_ref[1:2, :]
    f_next = next_potential(x_rows_ref[0:1, :], half, logs(state_ref[0:1, :], state_ref[1:2, :]), log_count)
    next_ref[0:1, :] = f_next
    next_ref[1:2, :] = half
    next_ref[2:8, :] = jnp.zeros((6, LOCAL), f32)
    alpha = (f_next - half) * scale
    state_ref[2:3, :] = alpha
    top = high_of(alpha)
    weight_ref[...] = down(jnp.exp2(alpha - top))
    reach = (top - low_of(alpha))[0, 0]

    def body(step, carry):
        slot = list_ref[step]
        y, b = slot // BPD, slot % BPD
        fits = reach <= left_ref[slot]
        term_copy(step).wait()

        @pl.when(fits)
        def _():
            sums = jnp.zeros((8, BS), f32)
            for c in range(0, BS, 64):
                weight = weight_ref[pl.ds(pl.multiple_of(b * BS + c, 64), 64), :]
                parts = [fold(terms_ref[step, c : c + 64, n : n + 128].astype(f32) * weight) for n in range(0, BS, 128)]
                sums = sums + jnp.concatenate(parts, axis=1)
            put_cols(col_ref, y, top, jnp.sum(sums, axis=0, keepdims=True))

        @pl.when(jnp.logical_not(fits))
        def _():
            load_pair(slot, x_ref, y_refs, x_buf, y_buf, sems)
            for c in range(0, BS, 128):
                row = state_ref[2:3, pl.ds(pl.multiple_of(b * BS + c, 128), 128)]
                part_ref[c : c + 128, :] = jnp.broadcast_to(row, (128, 128)).T
            shifted_cols(x_buf, y_buf, part_ref, col_ref, y)

        return carry

    lax.fori_loop(start, stop, body, 0)
    for n in range(YBLOCKS):
        out_ref[n] = logs(col_ref[n, 0:1, :], col_ref[n, 1:2, :])


def gathered(j, own_ref, came, who_ref):
    terms = [own_ref[j]] + [jnp.where(who_ref[n] == j, came(n), lowest) for n in range(PEERS)]
    top = terms[0]
    for term in terms[1:]:
        top = jnp.maximum(top, term)
    total = jnp.exp2(terms[0] - top)
    for term in terms[1:]:
        total = total + jnp.exp2(term - top)
    return top + jnp.log2(total)


def home_kernel(who_ref, peers_ref, even_in, odd_in, first_ref, second_ref, y_rows_ref, even_out, odd_out, g_ref, *, log_count):
    came = lambda n: (even_in, odd_in)[n // GROUP][n % GROUP]
    betas = []
    for j in range(BPD):
        span = slice(j * BS, (j + 1) * BS)
        half = y_rows_ref[1:2, span]
        g_next = next_potential(y_rows_ref[0:1, span], half, gathered(j, first_ref, came, who_ref), log_count)
        g_ref[0:1, span] = g_next
        betas.append((g_next - half) * scale)
        g_ref[1:2, span] = betas[j]
    g_ref[2:8, :] = jnp.zeros((6, LOCAL), f32)
    for n in range(PEERS):
        out = (even_out, odd_out)[n // GROUP]
        out[n % GROUP, 0:1, :] = jnp.where(who_ref[n] == 1, betas[1], betas[0])
        out[n % GROUP, 1:2, :] = outgoing(second_ref, peers_ref[n])


def home(who, peers, rows_in, first, second, y_rows, log_count):
    return pl.pallas_call(
        functools.partial(home_kernel, log_count=log_count),
        in_specs=[SMEM, SMEM] + [VMEM] * 5,
        out_specs=[VMEM] * 3,
        out_shape=[jax.ShapeDtypeStruct((GROUP, 2, BS), f32)] * 2 + [jax.ShapeDtypeStruct((8, LOCAL), f32)],
        compiler_params=params(),
        name="home",
    )(who, peers, *rows_in, first, second, y_rows)


def rows_kernel(list_ref, live_ref, seat_of_ref, use_ref, left_ref, *refs, log_count, phase):
    last = phase == 2
    start = live_ref[phase - 1] if phase else 0
    stop = live_ref[phase]
    if last:
        from_ref, who_ref, acc_in, state_in, even_in, odd_in, g_ref, second_ref, y_rows_ref, x_rows_ref = refs[:10]
        refs = refs[10:]
    elif phase:
        from_ref, acc_in, state_in, even_in, g_ref = refs[:5]
        refs = refs[5:]
    else:
        g_ref = refs[0]
        refs = refs[1:]
    kept_ref, slow_ref, x_ref = refs[:3]
    y_refs = refs[3 : 4 + FAR]
    refs = refs[4 + FAR :]
    if last:
        f_ref, g_out_ref, acc_ref, state_ref = refs[:4]
        refs = refs[4:]
    else:
        acc_ref, state_ref = refs[:2]
        refs = refs[2:]
    beta_ref, weight_ref, part_ref, x_buf, y_buf, sems, terms_ref, term_sems = refs
    term_copy = fetch_terms(kept_ref, terms_ref, term_sems, list_ref, seat_of_ref, start, stop)
    shift = high_of(g_ref[1:2, :])
    if phase:
        acc_ref[...] = acc_in[...]
        state_ref[...] = state_in[...]
    else:
        acc_ref[...] = jnp.zeros((LOCAL, 128), f32)
        state_ref[0:1, :] = jnp.full((1, LOCAL), lowest, f32)
        state_ref[1:8, :] = jnp.zeros((7, LOCAL), f32)
    for n in range(BPD):
        beta_ref[n] = g_ref[1:2, n * BS : (n + 1) * BS]
    for n in range(BPD, YBLOCKS if phase else BPD):
        at = from_ref[n] % GROUP
        if last:
            beta_ref[n] = jnp.where(from_ref[n] < GROUP, even_in[at, 0:1, :], odd_in[at, 0:1, :])
        else:
            beta_ref[n] = even_in[at, 0:1, :]
    some = YBLOCKS if phase else BPD
    weight_ref[0:some] = jnp.exp2(beta_ref[0:some] - shift)

    def body(step, carry):
        slot = list_ref[step]
        y, b = slot // BPD, slot % BPD
        beta = beta_ref[y]
        reach = jnp.maximum(high_of(beta) - shift, shift - low_of(beta))
        fits = reach[0, 0] <= left_ref[slot]
        term_copy(step).wait()

        @pl.when(fits)
        def _():
            weight = weight_ref[y]
            for c in range(0, BS, 64):
                span = pl.ds(pl.multiple_of(b * BS + c, 64), 64)
                part = acc_ref[span, :]
                for n in range(0, BS, 128):
                    part = part + terms_ref[step, c : c + 64, n : n + 128].astype(f32) * weight[:, n : n + 128]
                acc_ref[span, :] = part

        @pl.when(jnp.logical_not(fits))
        def _():
            load_pair(slot, x_ref, y_refs, x_buf, y_buf, sems)
            shifted_rows(x_buf, y_buf, beta, part_ref)
            add_part(part_ref, state_ref, b)

        return carry

    lax.fori_loop(start, stop, body, 0)
    if not last:
        return
    total = lane_sums([acc_ref])
    top = jnp.where(total > 0.0, shift, lowest)
    top, total = merge(top, total, state_ref[0:1, :], state_ref[1:2, :])
    f_ref[...] = next_potential(x_rows_ref[0:1, :], x_rows_ref[1:2, :], logs(top, total), log_count)
    came = lambda n: (even_in, odd_in)[n // GROUP][n % GROUP, 1:2, :]
    total = jnp.concatenate([gathered(j, second_ref, came, who_ref) for j in range(BPD)], axis=1)
    g_next = next_potential(g_ref[0:1, :], y_rows_ref[1:2, :], total, log_count)
    g_out_ref[...] = moved_exact(g_next, y_rows_ref[2:3, :].astype(i32))


def slots_call(kernel, smem, front, kept, slow, x_blocks, y_list, outs, scratch, name):
    return pl.pallas_call(
        kernel,
        in_specs=[SMEM] * len(smem) + [VMEM] * len(front) + [HBM, HBM, ANY] + [ANY] * len(y_list),
        out_specs=[VMEM] * len(outs),
        scratch_shapes=scratch
        + [
            pltpu.VMEM((BS, 128), f32),
            pltpu.VMEM((BS, DIM), bf16),
            pltpu.VMEM((ROWS, DIM), bf16),
            pltpu.SemaphoreType.DMA((2,)),
            pltpu.VMEM((MOST, BS, BS), bf16),
            pltpu.SemaphoreType.DMA((MOST,)),
        ],
        out_shape=outs,
        compiler_params=params(),
        name=name,
    )(*smem, *front, kept, slow, x_blocks, *y_list)


def seat_tables():
    half = GROUP // 2
    offsets = np.zeros((GROUP, PEERS), np.int32)
    source = np.zeros((GROUP, YBLOCKS), np.int32)
    for seat in range(GROUP):
        odd_seat = (seat + half) % GROUP
        for other in range(GROUP):
            if other != seat and abs(other - seat) <= REACH:
                offsets[seat, other] = other - seat
            off = other - odd_seat
            if off != 0 and abs(off) <= REACH and not 0 <= seat + off < GROUP:
                offsets[seat, GROUP + other] = off
        for k, off in enumerate(ROUNDS[seat % 4]):
            source[seat, BPD + k] = list(offsets[seat]).index(off)
    index = np.full((GROUP, PEERS), -1, np.int32)
    for seat in range(GROUP):
        for k, off in enumerate(ROUNDS[seat % 4]):
            index[seat, offsets[seat] == off] = BPD + k
    return offsets, index, source


def swap(rows, devices, shift):
    groups = [[(GROUP * k + j + shift) % devices for j in range(GROUP)] for k in range(devices // GROUP)]
    return lax.all_to_all(rows, "blk", split_axis=0, concat_axis=0, tiled=True, axis_index_groups=groups)


def on_device(x_points, y_points, x_start, y_start, x_order, y_order, partners, counts):
    devices = lax.axis_size("blk")
    me = lax.axis_index("blk").astype(i32)
    log_count = math.log(LOCAL * devices)
    here = me[None]
    line = lambda v: v.reshape(1, LOCAL)

    y_sent, x_pos = pack_y(here, partners, counts, line(y_order), line(x_order), y_start, x_start, y_points, devices)
    y_came = lax.all_to_all(y_sent, "blk", split_axis=0, concat_axis=0, tiled=True)
    offsets = lax.dynamic_slice(jnp.array(ROUNDS, i32), (me % 4, 0), (1, FAR))[0]
    live = jnp.arange(partners.shape[1], dtype=i32)[None, :] < counts[:, None]
    away = jnp.where(live, partners // BPD - me, devices)
    local_use = [((away == 0) & (partners % BPD == j)).any(axis=1) for j in range(BPD)]
    far = away[None, :, :] == offsets[:, None, None]
    use = jnp.concatenate([jnp.stack(local_use), far.any(axis=2)]).astype(i32).reshape(SLOTS)
    number = jnp.minimum(jnp.maximum(jnp.cumsum(use) - 1, 0), MOST - 1)

    peer_offsets, peer_index, peer_source = seat_tables()
    row = lambda t: lax.dynamic_slice(jnp.asarray(t), (me % GROUP, 0), (1, t.shape[1]))[0]
    peers, source, off = row(peer_index), row(peer_source), row(peer_offsets)

    far_slot = jnp.repeat(source >= GROUP, BPD).astype(i32)
    near = jnp.cumsum(use * (1 - far_slot))
    rank = jnp.where(far_slot > 0, near[-1] + jnp.cumsum(use * far_slot), near) - 1
    count = jnp.minimum(jnp.sum(use), MOST)
    step = jnp.minimum(jnp.arange(MOST, dtype=i32), count - 1)
    at = (rank[None, :] == step[:, None]) & (use[None, :] > 0)
    slots = jnp.sum(jnp.where(at, jnp.arange(SLOTS, dtype=i32)[None, :], 0), axis=1)
    own = jnp.sum(use[: BPD * BPD])
    live_counts = jnp.stack([own, jnp.minimum(near[-1], count), count])
    x_pos, use, number, slots, live_counts, peers, source, off = lax.optimization_barrier((x_pos, use, number, slots, live_counts, peers, source, off))
    x_sent = pack_x(x_pos, x_points)
    y_came, x_sent = lax.optimization_barrier((y_came, x_sent))
    x_came = lax.all_to_all(x_sent, "blk", split_axis=0, concat_axis=0, tiled=True)
    lists = [slots, live_counts, number]
    y_rows, table, y_own, *y_sends = unpack_y(here, y_came, devices)

    def far_block(k):
        pairs = [(i, i + ROUNDS[i % 4][k]) for i in range(devices) if 0 <= i + ROUNDS[i % 4][k] < devices]
        return lax.ppermute(y_sends[k], "blk", pairs)

    y_far = [far_block(k) for k in range(FAR - 1)]
    x_came, y_far[0], y_sends[5] = lax.optimization_barrier((x_came, y_far[0], y_sends[5]))
    y_far.append(far_block(5))
    x_blocks, alpha, x_rows, who = unpack_x(here, off, x_came, table, devices)


    common = (use, number, x_blocks, alpha)
    acc_0, *carried = sweep(common, [y_own], 0, None, [x_rows, y_rows])
    acc_1, *carried = sweep(common, y_far[:EARLY], BPD, carried)
    acc_2, *carried, odd_out = sweep(common, y_far[EARLY:-1], BPD + EARLY, carried, None, peers, 1)
    acc_3, cols_first, left, _, kept, slow, even_out = sweep(common, y_far[-1:], YBLOCKS - 1, carried, None, peers, 0)
    y_all = [y_own] + y_far

    odd_in = swap(odd_out, devices, GROUP // 2)
    even_in = swap(even_out, devices, 0)
    accs = [acc_0, acc_1, acc_2, acc_3]
    x_next, cols_second = slots_call(
        functools.partial(columns_kernel, log_count=log_count, accs=len(accs)),
        lists + [use, left],
        accs + [x_rows, y_rows],
        kept,
        slow,
        x_blocks,
        y_all,
        [jax.ShapeDtypeStruct((8, LOCAL), f32), jax.ShapeDtypeStruct((YBLOCKS, 1, BS), f32)],
        [pltpu.VMEM((YBLOCKS, 8, BS), f32), pltpu.VMEM((LOCAL, 128), f32), pltpu.VMEM((8, LOCAL), f32)],
        "columns",
    )
    even_out, odd_out, g_one = home(who, peers, (even_in, odd_in), cols_first, cols_second, y_rows, log_count)
    even_in = swap(even_out, devices, 0)
    row_scratch = [pltpu.VMEM((YBLOCKS, 1, BS), f32), pltpu.VMEM((YBLOCKS, 1, BS), f32)]
    sums = [jax.ShapeDtypeStruct((LOCAL, 128), f32), jax.ShapeDtypeStruct((8, LOCAL), f32)]

    def row_sums(phase, smem, front, outs, scratch):
        return slots_call(
            functools.partial(rows_kernel, log_count=log_count, phase=phase),
            lists + [use, left] + smem,
            front,
            kept,
            slow,
            x_blocks,
            y_all,
            outs,
            scratch + row_scratch,
            ("rows_own", "rows_even", "rows_odd")[phase],
        )

    acc, state = row_sums(0, [], [g_one], sums, [])
    odd_out, acc = lax.optimization_barrier((odd_out, acc))
    odd_in = swap(odd_out, devices, GROUP // 2)
    acc, state = row_sums(1, [source], [acc, state, even_in, g_one], sums, [])
    f_two, g_two = row_sums(
        2,
        [source, who],
        [acc, state, even_in, odd_in, g_one, cols_second, y_rows, x_next],
        [jax.ShapeDtypeStruct((1, LOCAL), f32)] * 2,
        [pltpu.VMEM((LOCAL, 128), f32), pltpu.VMEM((8, LOCAL), f32)],
    )
    return f_two.reshape(LOCAL), g_two.reshape(LOCAL)


def solution(mesh):
    placed_as = (
        P("blk", None),
        P("blk", None),
        P("blk"),
        P("blk"),
        P("blk"),
        P("blk"),
        P("blk", None),
        P("blk"),
    )
    return jax.shard_map(
        on_device, mesh=mesh, in_specs=placed_as, out_specs=(P("blk"), P("blk")), check_vma=False
    )
```

```python
import functools
import math

import jax
import jax.numpy as jnp
import numpy as np
from jax import lax
from jax.experimental import pallas as pl
from jax.experimental.pallas import tpu as pltpu
from jax.sharding import PartitionSpec as P

DIM = 512
BS = 1024
BPD = 2
REACH = 3
LOCAL = BPD * BS
EXTRA = 128
WIDE = DIM + EXTRA
TAIL = 16
ROWS = BS + TAIL
CHUNK = 512
PART = 256
ROUNDS = ((1, -3, 3, -1, -2, 2), (-1, 3, -3, 1, -2, 2), (1, -3, 3, -1, 2, -2), (-1, 3, -3, 1, 2, -2))
FAR = len(ROUNDS[0])
YBLOCKS = BPD + FAR
SLOTS = BPD * YBLOCKS
MOST = 12
GROUP = 8
PEERS = 2 * GROUP
X_LANES = EXTRA // 2

entropy_weight = 0.05
scale = math.log2(math.e) / entropy_weight
log_two = math.log(2.0)
lowest = -1e30
exponent_room = 112.0
mebi = 1024 * 1024

f32 = jnp.float32
bf16 = jnp.bfloat16
i32 = jnp.int32

SMEM = pl.BlockSpec(memory_space=pltpu.SMEM)
ANY = pl.BlockSpec(memory_space=pl.ANY)
VMEM = pl.BlockSpec(memory_space=pltpu.VMEM)
HBM = pl.BlockSpec(memory_space=pltpu.HBM)


def iota(shape, dim):
    return lax.broadcasted_iota(i32, shape, dim)


def dot(a, b):
    return jnp.dot(a, b, preferred_element_type=f32)


def nt_dot(a, b):
    return lax.dot_general(a, b, (((1,), (1,)), ((), ())), preferred_element_type=f32)


def ones_where(mask):
    return jnp.where(mask, 1.0, 0.0).astype(bf16)


def params():
    return pltpu.CompilerParams(vmem_limit_bytes=64 * mebi)


def whole(shape):
    return pl.BlockSpec(shape, lambda *t: (0,) * len(shape))


def laid_out(square):
    return jnp.concatenate([square[n : n + 1, :] for n in range(square.shape[0])], axis=1)


def down(row):
    parts = [jnp.broadcast_to(row[:, c : c + 128], (128, 128)).T for c in range(0, row.shape[1], 128)]
    return jnp.concatenate(parts, axis=0)


def moved(values, place):
    high = iota((16, LOCAL), 0) == lax.shift_right_logical(place, 7)
    low = ones_where(iota((128, LOCAL), 0) == jnp.bitwise_and(place, 127))
    stack = jnp.concatenate([jnp.where(high, v, 0.0) for v in values], axis=0).astype(bf16)
    out = nt_dot(stack, low)
    return [laid_out(out[16 * n : 16 * n + 16, :]) for n in range(len(values))]


def moved_exact(value, place):
    first = value.astype(bf16).astype(f32)
    second = (value - first).astype(bf16).astype(f32)
    parts = moved([first, second, value - first - second], place)
    return parts[0] + parts[1] + parts[2]


def before_matrix():
    return ones_where(iota((128, 128), 0) < iota((128, 128), 1))


def plan(order, start, devices, first_lane):
    share = LOCAL // devices
    target = lax.shift_right_logical(order, 11)
    hit = iota((devices, LOCAL), 0) == target
    hot = ones_where(hit)
    before = before_matrix()
    every = jnp.ones((128, 128), bf16)
    seen = jnp.zeros((devices, 128), f32)
    earlier = []
    for c in range(0, LOCAL, 128):
        piece = hot[:, c : c + 128]
        earlier.append(dot(piece, before) + seen)
        seen = seen + dot(piece, every)
    earlier = jnp.concatenate(earlier, axis=1)
    rank = jnp.sum(jnp.where(hit, earlier, 0.0), axis=0, keepdims=True).astype(i32)
    within = jnp.bitwise_and(order, LOCAL - 1)
    high = lax.shift_right_logical(within, 6).astype(f32)
    low = jnp.bitwise_and(within, 63).astype(f32)
    row = iota((EXTRA, LOCAL), 0) - first_lane
    field = row // share
    value = jnp.where(field == 0, high, jnp.where(field == 1, low, start))
    mine = (row >= 0) & (row < 3 * share) & (row % share == rank)
    return target * share + rank, nt_dot(hot, jnp.where(mine, value, 0.0).astype(bf16))


def partner_offsets(me):
    kind = jnp.bitwise_and(me, 3)
    out = []
    for k in range(FAR):
        value = jnp.int32(ROUNDS[0][k])
        for n in range(1, 4):
            value = jnp.where(kind == n, jnp.int32(ROUNDS[n][k]), value)
        out.append(value)
    return out


def pack_y_kernel(
    me_ref, partners_ref, counts_ref, y_order, x_order, y_start, x_start, points, out_ref, x_pos_ref, pos_ref, table_ref,
    *, devices
):
    step = pl.program_id(0)
    share = LOCAL // devices

    @pl.when(step == 0)
    def _():
        y_pos, y_table = plan(y_order[...], y_start[...].astype(f32).reshape(1, LOCAL), devices, 0)
        x_pos, x_table = plan(x_order[...], x_start[...].astype(f32).reshape(1, LOCAL), devices, X_LANES)
        pos_ref[...] = y_pos
        x_pos_ref[...] = x_pos
        me = me_ref[0]
        offsets = partner_offsets(me)
        need = [jnp.int32(0)] * FAR
        for b in range(BPD):
            for s in range(partners_ref.shape[1]):
                block = partners_ref[b, s]
                away = lax.shift_right_logical(block, 1) - me
                for k in range(FAR):
                    listed = (s < counts_ref[b]) & (away == offsets[k])
                    need[k] = jnp.where(listed, jnp.bitwise_and(block, 1), need[k])
        table = y_table + x_table
        row, lane = iota(table.shape, 0), iota(table.shape, 1)
        for k in range(FAR):
            table = jnp.where((row == me + offsets[k]) & (lane == 3 * share), need[k].astype(f32), table)
        table_ref[...] = table

    base = step * CHUNK
    hot = ones_where(iota((CHUNK, LOCAL), 0) + base == pos_ref[...])
    out_ref[:, :DIM] = dot(hot, points[...]).astype(bf16)
    some = CHUNK // share
    table = table_ref[pl.ds(pl.multiple_of(step * some, some), some), :]
    out_ref[:, DIM:] = jnp.broadcast_to(table[:, None, :], (some, share, EXTRA)).reshape(CHUNK, EXTRA).astype(bf16)


def pack_y(me, partners, counts, y_order, x_order, y_start, x_start, points, devices):
    row = whole((1, LOCAL))
    return pl.pallas_call(
        functools.partial(pack_y_kernel, devices=devices),
        grid=(LOCAL // CHUNK,),
        in_specs=[SMEM, SMEM, SMEM, row, row, whole((LOCAL,)), whole((LOCAL,)), whole((LOCAL, DIM))],
        out_specs=[pl.BlockSpec((CHUNK, WIDE), lambda t: (t, 0)), row],
        out_shape=[pltpu.HBM((LOCAL, WIDE), bf16), jax.ShapeDtypeStruct((1, LOCAL), i32)],
        scratch_shapes=[pltpu.VMEM((1, LOCAL), i32), pltpu.VMEM((devices, EXTRA), f32)],
        compiler_params=params(),
        name="pack_y",
    )(me, partners, counts, y_order, x_order, y_start, x_start, points)


def pack_x_kernel(pos_ref, points_ref, out_ref):
    base = pl.program_id(0) * CHUNK
    hot = ones_where(iota((CHUNK, LOCAL), 0) + base == pos_ref[...])
    out_ref[...] = dot(hot, points_ref[...]).astype(bf16)


def pack_x(pos, points):
    return pl.pallas_call(
        pack_x_kernel,
        grid=(LOCAL // CHUNK,),
        in_specs=[whole((1, LOCAL)), whole((LOCAL, DIM))],
        out_specs=pl.BlockSpec((CHUNK, DIM), lambda t: (t, 0)),
        out_shape=pltpu.HBM((LOCAL, DIM), bf16),
        compiler_params=params(),
        name="pack_x",
    )(pos, points)


WINDOW = PART + 16
HELD = BS + WINDOW + 16


def arrived(table, base, with_low):
    share = 16
    row, lane = iota((EXTRA, EXTRA), 0), iota((EXTRA, EXTRA), 1)
    pick = jnp.where(row == base + lane % share, 64.0 if with_low else 1.0, 0.0)
    if with_low:
        pick = jnp.where(row == base + share + lane % share, 1.0, pick)
    values = dot(table, pick.astype(bf16))
    values = jnp.where(row % (EXTRA // share) == lane // share, values, 0.0)
    return jnp.sum(values.reshape(LOCAL // 128, EXTRA // share, 128), axis=1)


def unpack_y_kernel(me_ref, came_ref, rows_ref, table_ref, own_ref, *rest, devices):
    sends = rest[:FAR]
    held, sems, own_sem, points_buf, extra_buf, in_sems = rest[FAR:]
    share = LOCAL // devices
    me = me_ref[0]
    extra_in = pltpu.make_async_copy(came_ref.at[:, pl.ds(DIM, EXTRA)], extra_buf, in_sems.at[0])
    points_in = pltpu.make_async_copy(came_ref.at[:, pl.ds(0, DIM)], points_buf, in_sems.at[1])
    extra_in.start()
    points_in.start()
    held[...] = jnp.zeros(held.shape, bf16)
    extra_in.wait()
    table = dot(ones_where(iota((devices, LOCAL), 1) == iota((devices, LOCAL), 0) * share), extra_buf[...])
    table_ref[...] = table
    place_square = arrived(table.astype(bf16), 0, True)
    place = laid_out(place_square)
    start = laid_out(arrived(table.astype(bf16), 2 * share, False))

    picks = []
    offsets = partner_offsets(me)
    small_row, small_lane = iota((devices, EXTRA), 0), iota((devices, EXTRA), 1)
    for k in range(FAR):
        here = (small_row == me + offsets[k]) & (small_lane == 3 * share)
        picks.append(jnp.sum(jnp.where(here, table, 0.0)) > 0.5)

    second = place >= float(BS)
    square = ones_where(place_square >= float(BS))
    totals = dot(square, jnp.ones((128, 128), bf16)).astype(bf16)
    earlier = dot(square, before_matrix()) + dot(ones_where(iota((16, 16), 1) < iota((16, 16), 0)), totals)
    ones_before = laid_out(earlier)
    dest = jnp.where(second, ones_before, iota((1, LOCAL), 1).astype(f32) - ones_before).astype(i32)
    seat = jnp.where(second, dest + BS, dest)
    position = place.astype(i32)
    start_row, high_row, low_row = moved(
        [start, lax.shift_right_logical(position, 6).astype(f32), jnp.bitwise_and(position, 63).astype(f32)], seat
    )
    rows_ref[0:1, :] = start_row
    rows_ref[2:3, :] = high_row * 64.0 + low_row
    rows_ref[3:8, :] = jnp.zeros((5, LOCAL), f32)
    sixteen, lane16 = iota((16, 128), 0), iota((16, 128), 1)
    points_in.wait()

    for j in range(BPD):
        here = jnp.where(second if j else jnp.logical_not(second), dest, -1)
        for c in range(LOCAL // PART):
            span = slice(c * PART, (c + 1) * PART)
            begin = jnp.sum(jnp.where((sixteen == c * PART // 128) & (lane16 == 0), earlier, 0.0)).astype(i32)
            if j == 0:
                begin = c * PART - begin
            begin = pl.multiple_of(lax.shift_left(lax.shift_right_logical(begin, 4), 4), 16)
            hot = ones_where(iota((WINDOW, PART), 0) + begin == here[:, span])
            part = dot(hot, points_buf[span, :]).astype(bf16)
            held[j, pl.ds(begin, WINDOW), :] = held[j, pl.ds(begin, WINDOW), :] + part
        half = []
        for c in range(0, BS, PART):
            points = held[j, c : c + PART, :].astype(f32)
            total = 0.5 * jnp.sum(points * points, axis=1, keepdims=True)
            half.append(jnp.broadcast_to(total, (PART, 128)).T[0:1, :])
        half = jnp.concatenate(half, axis=1)
        block = slice(j * BS, (j + 1) * BS)
        rows_ref[1:2, block] = half
        beta = start_row[:, block] - half
        first = beta.astype(bf16).astype(f32)
        next_part = (beta - first).astype(bf16).astype(f32)
        most = jnp.max(half, axis=1, keepdims=True) * 1.01
        sub = iota((TAIL, DIM), 0)
        tail = jnp.zeros((TAIL, DIM), f32) + most
        for n, piece in enumerate((first, next_part, beta - first - next_part)):
            tail = jnp.where(sub == 2 * n, piece[:, :DIM], tail)
            tail = jnp.where(sub == 2 * n + 1, piece[:, DIM:], tail)
        held[j, BS:ROWS, :] = tail.astype(bf16)
        done = held.at[j, pl.ds(0, ROWS), :]
        for k in range(FAR):
            wanted = picks[k] if j == 1 else jnp.logical_not(picks[k])

            @pl.when(wanted)
            def _():
                pltpu.make_async_copy(done, sends[k], sems.at[k]).start()

        pltpu.make_async_copy(done, own_ref.at[j], own_sem.at[j]).start()

    done = held.at[0, pl.ds(0, ROWS), :]
    for k in range(FAR):
        pltpu.make_async_copy(done, sends[k], sems.at[k]).wait()
    for j in range(BPD):
        pltpu.make_async_copy(done, own_ref.at[j], own_sem.at[j]).wait()


def unpack_y(me, came, devices):
    return pl.pallas_call(
        functools.partial(unpack_y_kernel, devices=devices),
        in_specs=[SMEM, ANY],
        out_specs=[VMEM, VMEM] + [HBM] * (1 + FAR),
        out_shape=[
            jax.ShapeDtypeStruct((8, LOCAL), f32),
            jax.ShapeDtypeStruct((devices, EXTRA), f32),
            pltpu.HBM((BPD, ROWS, DIM), bf16),
        ]
        + [pltpu.HBM((ROWS, DIM), bf16)] * FAR,
        scratch_shapes=[
            pltpu.VMEM((BPD, HELD, DIM), bf16),
            pltpu.SemaphoreType.DMA((FAR,)),
            pltpu.SemaphoreType.DMA((BPD,)),
            pltpu.VMEM((LOCAL, DIM), bf16),
            pltpu.VMEM((LOCAL, EXTRA), bf16),
            pltpu.SemaphoreType.DMA((2,)),
        ],
        compiler_params=params(),
        name="unpack_y",
    )(me, came)


def unpack_x_kernel(
    me_ref, peer_ref, came_ref, table_ref, points_ref, alpha_ref, rows_ref, who_ref, place_ref, start_ref, *, devices
):
    step = pl.program_id(0)

    @pl.when(step == 0)
    def _():
        table = table_ref[...].astype(bf16)
        place = laid_out(arrived(table, X_LANES, True)).astype(i32)
        place_ref[...] = place
        start_ref[...] = moved([laid_out(arrived(table, X_LANES + 32, False))], place)[0]
        row, lane = iota((EXTRA, EXTRA), 0), iota((EXTRA, EXTRA), 1)
        for n in range(PEERS):
            peer = me_ref[0] + peer_ref[n]
            wants = jnp.sum(jnp.where((row == peer) & (lane == 3 * LOCAL // devices), table_ref[...], 0.0)) > 0.5
            valid = (peer_ref[n] != 0) & (peer >= 0) & (peer < devices)
            who_ref[n] = jnp.where(valid, jnp.where(wants, 1, 0), -1)

    base = step * CHUNK
    hot = ones_where(iota((CHUNK, LOCAL), 0) + base == place_ref[...])
    points = dot(hot, came_ref[...])
    points_ref[...] = points.astype(bf16)
    half = jnp.broadcast_to(0.5 * jnp.sum(points * points, axis=1, keepdims=True), (CHUNK, 128))
    start = start_ref[:, pl.ds(pl.multiple_of(base, CHUNK), CHUNK)]
    alpha_ref[...] = (down(start) - half) * scale
    rows_ref[0:1, :] = start
    rows_ref[1:8, :] = jnp.concatenate([half[c : c + 128, :].T[0:7, :] for c in range(0, CHUNK, 128)], axis=1)


def unpack_x(me, peer_offsets, came, table, devices):
    return pl.pallas_call(
        functools.partial(unpack_x_kernel, devices=devices),
        grid=(LOCAL // CHUNK,),
        in_specs=[SMEM, SMEM, whole((LOCAL, DIM)), whole((EXTRA, EXTRA))],
        out_specs=[
            pl.BlockSpec((CHUNK, DIM), lambda t: (t, 0)),
            pl.BlockSpec((CHUNK, 128), lambda t: (t, 0)),
            pl.BlockSpec((8, CHUNK), lambda t: (0, t)),
            SMEM,
        ],
        out_shape=[
            pltpu.HBM((LOCAL, DIM), bf16),
            pltpu.HBM((LOCAL, 128), f32),
            jax.ShapeDtypeStruct((8, LOCAL), f32),
            jax.ShapeDtypeStruct((PEERS,), i32),
        ],
        scratch_shapes=[pltpu.VMEM((1, LOCAL), i32), pltpu.VMEM((1, LOCAL), f32)],
        compiler_params=params(),
        name="unpack_x",
    )(me, peer_offsets, came, table)


def merge(top, total, other_top, other_total):
    new = jnp.maximum(top, other_top)
    return new, total * jnp.exp2(top - new) + other_total * jnp.exp2(other_top - new)


def logs(top, total):
    return jnp.where(total > 0.0, top + jnp.log2(total), lowest)


def high_of(row):
    return jnp.max(row, axis=1, keepdims=True)


def low_of(row):
    return jnp.min(row, axis=1, keepdims=True)


def put_cols(col_ref, y, part_top, part_total):
    top, total = merge(col_ref[y, 0:1, :], col_ref[y, 1:2, :], part_top, part_total)
    col_ref[y, 0:1, :] = top
    col_ref[y, 1:2, :] = total


def clear_cols(col_ref):
    col_ref[:, 0:1, :] = jnp.full((col_ref.shape[0], 1, BS), lowest, f32)
    col_ref[:, 1:2, :] = jnp.zeros((col_ref.shape[0], 1, BS), f32)


def shifted_rows(x_ref, y_ref, beta, part_ref):
    def body(c, carry):
        span = pl.ds(pl.multiple_of(c * PART, PART), PART)
        terms = nt_dot(x_ref[span, :], y_ref[0:BS, :]) * scale + beta
        top = jnp.max(terms, axis=1, keepdims=True)
        total = jnp.sum(jnp.exp2(terms - top), axis=1, keepdims=True)
        part_ref[span, :] = jnp.where(iota((PART, 128), 1) == 0, top, total)
        return carry

    lax.fori_loop(0, BS // PART, body, 0)


def shifted_cols(x_ref, y_ref, alpha_ref, col_ref, y):
    def body(c, carry):
        span = pl.ds(pl.multiple_of(c * PART, PART), PART)
        terms = nt_dot(x_ref[span, :], y_ref[0:BS, :]) * scale + alpha_ref[span, 0:1]
        top = jnp.max(terms, axis=0, keepdims=True)
        put_cols(col_ref, y, top, jnp.sum(jnp.exp2(terms - top), axis=0, keepdims=True))
        return carry

    lax.fori_loop(0, BS // PART, body, 0)


def add_part(part_ref, state_ref, b):
    for c in range(0, BS, 128):
        part = part_ref[c : c + 128, :].T
        span = pl.ds(pl.multiple_of(b * BS + c, 128), 128)
        top, total = merge(state_ref[0:1, span], state_ref[1:2, span], part[0:1, :], part[1:2, :])
        state_ref[0:1, span] = top
        state_ref[1:2, span] = total


def lane_sums(refs):
    out = []
    for c in range(0, LOCAL, 128):
        part = refs[0][c : c + 128, :]
        for ref in refs[1:]:
            part = part + ref[c : c + 128, :]
        out.append(jnp.sum(part.T, axis=0, keepdims=True))
    return jnp.concatenate(out, axis=1)


def fold(values):
    return jnp.sum(values.reshape(values.shape[0] // 8, 8, 128), axis=0)


def own_beta(y_rows_ref):
    return (y_rows_ref[0:1, :] - y_rows_ref[1:2, :]) * scale


def sweep_kernel(*refs, base, count, first, sends, more):
    use_ref, seat_of_ref, x_ref, alpha_ref = refs[:4]
    refs = refs[4:]
    if first:
        x_rows_ref, y_rows_ref = refs[:2]
        refs = refs[2:]
    else:
        cols_in, left_in, stat_in = refs[:3]
        refs = refs[5:]
    if sends is not None:
        peers_ref = refs[0]
        refs = refs[1:]
    if more:
        acc_in = refs[0]
        refs = refs[1:]
    y_refs = refs[:1] if first else refs[:count]
    refs = refs[len(y_refs) :]
    acc_ref, cols_ref, left_ref, stat_ref, kept_ref, slow_ref = refs[:6]
    refs = refs[6:]
    if sends is not None:
        group_out = refs[0]
        refs = refs[1:]
    x_buf, alpha_buf, x_sems, y_buf, sems, col_ref, weight_ref, part_ref, beta_ref, fit_ref, room_ref, tiles, tile_sems, tile_count = refs

    def copy(n):
        source = y_refs[0].at[n] if first else y_refs[n]
        return pltpu.make_async_copy(source, y_buf.at[n % 2], sems.at[n % 2])

    def x_copies(n):
        rows = pl.ds(n * BS, BS)
        return (
            pltpu.make_async_copy(x_ref.at[rows, :], x_buf.at[rows, :], x_sems.at[n, 0]),
            pltpu.make_async_copy(alpha_ref.at[rows, :], alpha_buf.at[rows, :], x_sems.at[n, 1]),
        )

    copy(0).start()
    for part in x_copies(0):
        part.start()
    tile_count[0] = 0
    acc_ref[...] = acc_in[...] if more else jnp.zeros((LOCAL, 128), f32)

    def tile_copy(at, seat):
        return pltpu.make_async_copy(tiles.at[at], kept_ref.at[seat], tile_sems.at[at])

    def part_copy(at, seat, c):
        rows = pl.ds(c, PART)
        return pltpu.make_async_copy(tiles.at[at, rows, :], kept_ref.at[seat, rows, :], tile_sems.at[at])

    if first:
        for n in range(SLOTS):
            left_ref[n] = -1.0
        alpha = (x_rows_ref[0:1, :] - x_rows_ref[1:2, :]) * scale
        alpha_top = high_of(alpha)
        lane = iota((8, 128), 1)
        beta_top = high_of(own_beta(y_rows_ref))
        most = high_of(x_rows_ref[1:2, :]) * 1.01
        spread = alpha_top - low_of(alpha)
        stat_ref[...] = jnp.where(
            lane == 0, alpha_top, jnp.where(lane == 1, spread, jnp.where(lane == 2, most, beta_top))
        )
    else:
        for n in range(SLOTS):
            left_ref[n] = left_in[n]
        cols_ref[...] = cols_in[...]
        stat_ref[...] = stat_in[...]

    def body(step, carry):
        y, b = step // BPD, step % BPD
        slot = base * BPD + step
        for n in range(count):

            @pl.when(step == BPD * n)
            def _():
                copy(n).wait()
                if n + 1 < count:
                    copy(n + 1).start()

        for n in range(BPD):

            @pl.when(step == n)
            def _():
                for part in x_copies(n):
                    part.wait()
                if n + 1 < BPD:
                    for part in x_copies(n + 1):
                        part.start()
                rows = slice(n * BS, (n + 1) * BS)
                weight_ref[rows, :] = jnp.exp2(alpha_buf[rows, :] - stat_ref[0:1, 0:1])

        now = y_buf.at[y % 2]
        rows_from = b * BS

        @pl.when(b == 0)
        def _():
            clear_cols(col_ref)
            tail = now[BS:ROWS, :].astype(f32)
            halves = [tail[n : n + 1, :] + tail[n + 2 : n + 3, :] + tail[n + 4 : n + 5, :] for n in range(2)]
            beta = jnp.concatenate(halves, axis=1) * scale
            shift = stat_ref[0:1, 3:4]
            left = exponent_room - 2.0 * scale * jnp.sqrt(tail[6:7, 0:1] * stat_ref[0:1, 2:3])
            reach = jnp.maximum(stat_ref[0:1, 1:2], jnp.maximum(high_of(beta) - shift, shift - low_of(beta)))
            beta_ref[0:1, :] = beta
            beta_ref[1:2, :] = jnp.exp2(beta - shift)
            room_ref[0] = left[0, 0]
            fit_ref[0] = jnp.where((left - reach)[0, 0] >= 0.0, 1, 0)

        @pl.when(use_ref[slot] > 0)
        def _():
            fits = fit_ref[0] > 0

            @pl.when(fits)
            def _():
                left_ref[slot] = room_ref[0]
                done = tile_count[0]
                tile_count[0] = done + 1
                at = done % 2

                @pl.when(done > 1)
                def _():
                    tile_copy(at, 0).wait()

                weight = beta_ref[1:2, :]
                sums = jnp.zeros((8, BS), f32)
                for c in range(0, BS, PART):
                    span = pl.ds(pl.multiple_of(rows_from + c, PART), PART)
                    terms = jnp.exp2(nt_dot(x_buf[span, :], now[0:BS, :]) * scale)
                    tiles[at, c : c + PART, :] = terms.astype(bf16)
                    part_copy(at, seat_of_ref[slot], c).start()
                    row_part = acc_ref[span, :]
                    col_parts = []
                    for n in range(0, BS, 128):
                        piece = terms[:, n : n + 128]
                        row_part = row_part + piece * weight[:, n : n + 128]
                        col_parts.append(fold(piece * weight_ref[span, :]))
                    acc_ref[span, :] = row_part
                    sums = sums + jnp.concatenate(col_parts, axis=1)
                put_cols(col_ref, 0, stat_ref[0:1, 0:1], jnp.sum(sums, axis=0, keepdims=True))

            @pl.when(jnp.logical_not(fits))
            def _():
                block = pl.ds(pl.multiple_of(rows_from, BS), BS)
                shifted_rows(x_buf.at[block, :], now, beta_ref[0:1, :], part_ref)
                out = pltpu.make_async_copy(part_ref, slow_ref.at[slot], sems.at[2])
                out.start()
                shifted_cols(x_buf.at[block, :], now, alpha_buf.at[block, :], col_ref, 0)
                out.wait()

        @pl.when(b == BPD - 1)
        def _():
            cols_ref[base + y] = logs(col_ref[0, 0:1, :], col_ref[0, 1:2, :])

        return carry

    lax.fori_loop(0, BPD * count, body, 0)
    for n in range(2):

        @pl.when(tile_count[0] > n)
        def _():
            tile_copy(n, 0).wait()

    if sends is not None:
        for n in range(GROUP):
            group_out[n] = outgoing(cols_ref, peers_ref[sends * GROUP + n])


def outgoing(cols_ref, index):
    return jnp.where(index < 0, lowest, cols_ref[jnp.maximum(index, 0)])


def sweep(common, y_list, base, carried, rows=None, peers=None, sends=None, acc=None):
    first = carried is None
    count = BPD if first else len(y_list)
    in_specs = [SMEM, SMEM, HBM, HBM]
    operands = list(common)
    aliases = {}
    if first:
        in_specs += [VMEM, VMEM]
        operands += rows
    else:
        in_specs += [VMEM, SMEM, VMEM, HBM, HBM]
        operands += list(carried)
        aliases = {7: 4, 8: 5}
    if sends is not None:
        in_specs.append(SMEM)
        operands.append(peers)
    if acc is not None:
        in_specs.append(VMEM)
        operands.append(acc)
    in_specs += [ANY] * len(y_list)
    operands += y_list
    out_specs = [VMEM, VMEM, SMEM, VMEM, HBM, HBM]
    out_shape = [
        jax.ShapeDtypeStruct((LOCAL, 128), f32),
        jax.ShapeDtypeStruct((YBLOCKS, 1, BS), f32),
        jax.ShapeDtypeStruct((SLOTS,), f32),
        jax.ShapeDtypeStruct((8, 128), f32),
        pltpu.HBM((MOST, BS, BS), bf16),
        pltpu.HBM((SLOTS, BS, 128), f32),
    ]
    if sends is not None:
        out_specs.append(VMEM)
        out_shape.append(jax.ShapeDtypeStruct((GROUP, 1, BS), f32))
    return pl.pallas_call(
        functools.partial(sweep_kernel, base=base, count=count, first=first, sends=sends, more=acc is not None),
        in_specs=in_specs,
        out_specs=out_specs,
        out_shape=out_shape,
        scratch_shapes=[
            pltpu.VMEM((LOCAL, DIM), bf16),
            pltpu.VMEM((LOCAL, 128), f32),
            pltpu.SemaphoreType.DMA((BPD, 2)),
            pltpu.VMEM((2, ROWS, DIM), bf16),
            pltpu.SemaphoreType.DMA((3,)),
            pltpu.VMEM((1, 8, BS), f32),
            pltpu.VMEM((LOCAL, 128), f32),
            pltpu.VMEM((BS, 128), f32),
            pltpu.VMEM((8, BS), f32),
            pltpu.SMEM((1,), i32),
            pltpu.SMEM((1,), f32),
            pltpu.VMEM((2, BS, BS), bf16),
            pltpu.SemaphoreType.DMA((2,)),
            pltpu.SMEM((1,), i32),
        ],
        input_output_aliases=aliases,
        compiler_params=params(),
        name=f"sweep_{base}",
    )(*operands)


def load_pair(slot, x_ref, y_refs, x_buf, y_buf, sems):
    rows = pl.ds(pl.multiple_of((slot % BPD) * BS, BS), BS)
    fetch = pltpu.make_async_copy(x_ref.at[rows, :], x_buf, sems.at[0])
    fetch.start()
    fetch.wait()
    for n in range(YBLOCKS):

        @pl.when(slot // BPD == n)
        def _():
            source = y_refs[0].at[n] if n < BPD else y_refs[n - BPD + 1]
            fetch = pltpu.make_async_copy(source, y_buf, sems.at[1])
            fetch.start()
            fetch.wait()


def next_potential(now, half, total, log_count):
    return 0.5 * (now + half + entropy_weight * (log_count - log_two * total))


def fetch_terms(kept_ref, terms_ref, sems, list_ref, seat_of_ref, start, stop):
    def term_copy(n):
        return pltpu.make_async_copy(kept_ref.at[seat_of_ref[list_ref[n]]], terms_ref.at[n], sems.at[n])

    for n in range(MOST):

        @pl.when((n >= start) & (n < stop))
        def _():
            term_copy(n).start()

    return term_copy


def columns_kernel(list_ref, live_ref, seat_of_ref, use_ref, left_ref, *refs, log_count, accs):
    start, stop = 0, live_ref[2]
    acc_refs = refs[:accs]
    x_rows_ref, y_rows_ref, kept_ref, slow_ref, x_ref = refs[accs : accs + 5]
    y_refs = refs[accs + 5 : accs + 6 + FAR]
    next_ref, out_ref, col_ref, weight_ref, state_ref, part_ref, x_buf, y_buf, sems, terms_ref, term_sems = refs[accs + 6 + FAR :]
    term_copy = fetch_terms(kept_ref, terms_ref, term_sems, list_ref, seat_of_ref, start, stop)
    clear_cols(col_ref)
    total = lane_sums(acc_refs)
    state_ref[0:1, :] = jnp.where(total > 0.0, high_of(own_beta(y_rows_ref)), lowest)
    state_ref[1:2, :] = total
    for n in range(SLOTS):

        @pl.when((use_ref[n] > 0) & (left_ref[n] < 0.0))
        def _():
            fetch = pltpu.make_async_copy(slow_ref.at[n], part_ref, sems.at[0])
            fetch.start()
            fetch.wait()
            add_part(part_ref, state_ref, n % BPD)

    half = x_rows_ref[1:2, :]
    f_next = next_potential(x_rows_ref[0:1, :], half, logs(state_ref[0:1, :], state_ref[1:2, :]), log_count)
    next_ref[0:1, :] = f_next
    next_ref[1:2, :] = half
    next_ref[2:8, :] = jnp.zeros((6, LOCAL), f32)
    alpha = (f_next - half) * scale
    state_ref[2:3, :] = alpha
    top = high_of(alpha)
    weight_ref[...] = down(jnp.exp2(alpha - top))
    reach = (top - low_of(alpha))[0, 0]

    def body(step, carry):
        slot = list_ref[step]
        y, b = slot // BPD, slot % BPD
        fits = reach <= left_ref[slot]
        term_copy(step).wait()

        @pl.when(fits)
        def _():
            sums = jnp.zeros((8, BS), f32)
            for c in range(0, BS, 64):
                weight = weight_ref[pl.ds(pl.multiple_of(b * BS + c, 64), 64), :]
                parts = [fold(terms_ref[step, c : c + 64, n : n + 128].astype(f32) * weight) for n in range(0, BS, 128)]
                sums = sums + jnp.concatenate(parts, axis=1)
            put_cols(col_ref, y, top, jnp.sum(sums, axis=0, keepdims=True))

        @pl.when(jnp.logical_not(fits))
        def _():
            load_pair(slot, x_ref, y_refs, x_buf, y_buf, sems)
            for c in range(0, BS, 128):
                row = state_ref[2:3, pl.ds(pl.multiple_of(b * BS + c, 128), 128)]
                part_ref[c : c + 128, :] = jnp.broadcast_to(row, (128, 128)).T
            shifted_cols(x_buf, y_buf, part_ref, col_ref, y)

        return carry

    lax.fori_loop(start, stop, body, 0)
    for n in range(YBLOCKS):
        out_ref[n] = logs(col_ref[n, 0:1, :], col_ref[n, 1:2, :])


def gathered(j, own_ref, came, who_ref):
    terms = [own_ref[j]] + [jnp.where(who_ref[n] == j, came(n), lowest) for n in range(PEERS)]
    top = terms[0]
    for term in terms[1:]:
        top = jnp.maximum(top, term)
    total = jnp.exp2(terms[0] - top)
    for term in terms[1:]:
        total = total + jnp.exp2(term - top)
    return top + jnp.log2(total)


def home_kernel(who_ref, peers_ref, even_in, odd_in, first_ref, second_ref, y_rows_ref, even_out, odd_out, g_ref, *, log_count):
    came = lambda n: (even_in, odd_in)[n // GROUP][n % GROUP]
    betas = []
    for j in range(BPD):
        span = slice(j * BS, (j + 1) * BS)
        half = y_rows_ref[1:2, span]
        g_next = next_potential(y_rows_ref[0:1, span], half, gathered(j, first_ref, came, who_ref), log_count)
        g_ref[0:1, span] = g_next
        betas.append((g_next - half) * scale)
        g_ref[1:2, span] = betas[j]
    g_ref[2:8, :] = jnp.zeros((6, LOCAL), f32)
    for n in range(PEERS):
        out = (even_out, odd_out)[n // GROUP]
        out[n % GROUP, 0:1, :] = jnp.where(who_ref[n] == 1, betas[1], betas[0])
        out[n % GROUP, 1:2, :] = outgoing(second_ref, peers_ref[n])


def home(who, peers, rows_in, first, second, y_rows, log_count):
    return pl.pallas_call(
        functools.partial(home_kernel, log_count=log_count),
        in_specs=[SMEM, SMEM] + [VMEM] * 5,
        out_specs=[VMEM] * 3,
        out_shape=[jax.ShapeDtypeStruct((GROUP, 2, BS), f32)] * 2 + [jax.ShapeDtypeStruct((8, LOCAL), f32)],
        compiler_params=params(),
        name="home",
    )(who, peers, *rows_in, first, second, y_rows)


def rows_kernel(list_ref, live_ref, seat_of_ref, use_ref, left_ref, *refs, log_count, phase):
    last = phase == 2
    start = live_ref[phase - 1] if phase else 0
    stop = live_ref[phase]
    if last:
        from_ref, who_ref, acc_in, state_in, even_in, odd_in, g_ref, second_ref, y_rows_ref, x_rows_ref = refs[:10]
        refs = refs[10:]
    elif phase:
        from_ref, acc_in, state_in, even_in, g_ref = refs[:5]
        refs = refs[5:]
    else:
        g_ref = refs[0]
        refs = refs[1:]
    kept_ref, slow_ref, x_ref = refs[:3]
    y_refs = refs[3 : 4 + FAR]
    refs = refs[4 + FAR :]
    if last:
        f_ref, g_out_ref, acc_ref, state_ref = refs[:4]
        refs = refs[4:]
    else:
        acc_ref, state_ref = refs[:2]
        refs = refs[2:]
    beta_ref, weight_ref, part_ref, x_buf, y_buf, sems, terms_ref, term_sems = refs
    term_copy = fetch_terms(kept_ref, terms_ref, term_sems, list_ref, seat_of_ref, start, stop)
    shift = high_of(g_ref[1:2, :])
    if phase:
        acc_ref[...] = acc_in[...]
        state_ref[...] = state_in[...]
    else:
        acc_ref[...] = jnp.zeros((LOCAL, 128), f32)
        state_ref[0:1, :] = jnp.full((1, LOCAL), lowest, f32)
        state_ref[1:8, :] = jnp.zeros((7, LOCAL), f32)
    for n in range(BPD):
        beta_ref[n] = g_ref[1:2, n * BS : (n + 1) * BS]
    for n in range(BPD, YBLOCKS if phase else BPD):
        at = from_ref[n] % GROUP
        if last:
            beta_ref[n] = jnp.where(from_ref[n] < GROUP, even_in[at, 0:1, :], odd_in[at, 0:1, :])
        else:
            beta_ref[n] = even_in[at, 0:1, :]
    some = YBLOCKS if phase else BPD
    weight_ref[0:some] = jnp.exp2(beta_ref[0:some] - shift)

    def body(step, carry):
        slot = list_ref[step]
        y, b = slot // BPD, slot % BPD
        beta = beta_ref[y]
        reach = jnp.maximum(high_of(beta) - shift, shift - low_of(beta))
        fits = reach[0, 0] <= left_ref[slot]
        term_copy(step).wait()

        @pl.when(fits)
        def _():
            weight = weight_ref[y]
            for c in range(0, BS, 64):
                span = pl.ds(pl.multiple_of(b * BS + c, 64), 64)
                part = acc_ref[span, :]
                for n in range(0, BS, 128):
                    part = part + terms_ref[step, c : c + 64, n : n + 128].astype(f32) * weight[:, n : n + 128]
                acc_ref[span, :] = part

        @pl.when(jnp.logical_not(fits))
        def _():
            load_pair(slot, x_ref, y_refs, x_buf, y_buf, sems)
            shifted_rows(x_buf, y_buf, beta, part_ref)
            add_part(part_ref, state_ref, b)

        return carry

    lax.fori_loop(start, stop, body, 0)
    if not last:
        return
    total = lane_sums([acc_ref])
    top = jnp.where(total > 0.0, shift, lowest)
    top, total = merge(top, total, state_ref[0:1, :], state_ref[1:2, :])
    f_ref[...] = next_potential(x_rows_ref[0:1, :], x_rows_ref[1:2, :], logs(top, total), log_count)
    came = lambda n: (even_in, odd_in)[n // GROUP][n % GROUP, 1:2, :]
    total = jnp.concatenate([gathered(j, second_ref, came, who_ref) for j in range(BPD)], axis=1)
    g_next = next_potential(g_ref[0:1, :], y_rows_ref[1:2, :], total, log_count)
    g_out_ref[...] = moved_exact(g_next, y_rows_ref[2:3, :].astype(i32))


def slots_call(kernel, smem, front, kept, slow, x_blocks, y_list, outs, scratch, name):
    return pl.pallas_call(
        kernel,
        in_specs=[SMEM] * len(smem) + [VMEM] * len(front) + [HBM, HBM, ANY] + [ANY] * len(y_list),
        out_specs=[VMEM] * len(outs),
        scratch_shapes=scratch
        + [
            pltpu.VMEM((BS, 128), f32),
            pltpu.VMEM((BS, DIM), bf16),
            pltpu.VMEM((ROWS, DIM), bf16),
            pltpu.SemaphoreType.DMA((2,)),
            pltpu.VMEM((MOST, BS, BS), bf16),
            pltpu.SemaphoreType.DMA((MOST,)),
        ],
        out_shape=outs,
        compiler_params=params(),
        name=name,
    )(*smem, *front, kept, slow, x_blocks, *y_list)


def seat_tables():
    half = GROUP // 2
    offsets = np.zeros((GROUP, PEERS), np.int32)
    source = np.zeros((GROUP, YBLOCKS), np.int32)
    for seat in range(GROUP):
        odd_seat = (seat + half) % GROUP
        for other in range(GROUP):
            if other != seat and abs(other - seat) <= REACH:
                offsets[seat, other] = other - seat
            off = other - odd_seat
            if off != 0 and abs(off) <= REACH and not 0 <= seat + off < GROUP:
                offsets[seat, GROUP + other] = off
        for k, off in enumerate(ROUNDS[seat % 4]):
            source[seat, BPD + k] = list(offsets[seat]).index(off)
    index = np.full((GROUP, PEERS), -1, np.int32)
    for seat in range(GROUP):
        for k, off in enumerate(ROUNDS[seat % 4]):
            index[seat, offsets[seat] == off] = BPD + k
    return offsets, index, source


def swap(rows, devices, shift):
    groups = [[(GROUP * k + j + shift) % devices for j in range(GROUP)] for k in range(devices // GROUP)]
    return lax.all_to_all(rows, "blk", split_axis=0, concat_axis=0, tiled=True, axis_index_groups=groups)


def on_device(x_points, y_points, x_start, y_start, x_order, y_order, partners, counts):
    devices = lax.axis_size("blk")
    me = lax.axis_index("blk").astype(i32)
    log_count = math.log(LOCAL * devices)
    here = me[None]
    line = lambda v: v.reshape(1, LOCAL)

    y_sent, x_pos = pack_y(here, partners, counts, line(y_order), line(x_order), y_start, x_start, y_points, devices)
    y_came = lax.all_to_all(y_sent, "blk", split_axis=0, concat_axis=0, tiled=True)
    offsets = lax.dynamic_slice(jnp.array(ROUNDS, i32), (me % 4, 0), (1, FAR))[0]
    live = jnp.arange(partners.shape[1], dtype=i32)[None, :] < counts[:, None]
    away = jnp.where(live, partners // BPD - me, devices)
    local_use = [((away == 0) & (partners % BPD == j)).any(axis=1) for j in range(BPD)]
    far = away[None, :, :] == offsets[:, None, None]
    use = jnp.concatenate([jnp.stack(local_use), far.any(axis=2)]).astype(i32).reshape(SLOTS)
    number = jnp.minimum(jnp.maximum(jnp.cumsum(use) - 1, 0), MOST - 1)

    peer_offsets, peer_index, peer_source = seat_tables()
    row = lambda t: lax.dynamic_slice(jnp.asarray(t), (me % GROUP, 0), (1, t.shape[1]))[0]
    peers, source, off = row(peer_index), row(peer_source), row(peer_offsets)

    far_slot = jnp.repeat(source >= GROUP, BPD).astype(i32)
    near = jnp.cumsum(use * (1 - far_slot))
    rank = jnp.where(far_slot > 0, near[-1] + jnp.cumsum(use * far_slot), near) - 1
    count = jnp.minimum(jnp.sum(use), MOST)
    step = jnp.minimum(jnp.arange(MOST, dtype=i32), count - 1)
    at = (rank[None, :] == step[:, None]) & (use[None, :] > 0)
    slots = jnp.sum(jnp.where(at, jnp.arange(SLOTS, dtype=i32)[None, :], 0), axis=1)
    own = jnp.sum(use[: BPD * BPD])
    live_counts = jnp.stack([own, jnp.minimum(near[-1], count), count])
    x_pos, use, number, slots, live_counts, peers, source, off = lax.optimization_barrier((x_pos, use, number, slots, live_counts, peers, source, off))
    x_sent = pack_x(x_pos, x_points)
    y_came, x_sent = lax.optimization_barrier((y_came, x_sent))
    x_came = lax.all_to_all(x_sent, "blk", split_axis=0, concat_axis=0, tiled=True)
    lists = [slots, live_counts, number]
    y_rows, table, y_own, *y_sends = unpack_y(here, y_came, devices)

    def far_block(k):
        pairs = [(i, i + ROUNDS[i % 4][k]) for i in range(devices) if 0 <= i + ROUNDS[i % 4][k] < devices]
        return lax.ppermute(y_sends[k], "blk", pairs)

    y_far = [far_block(k) for k in range(FAR - 1)]
    x_came, y_far[0], y_sends[5] = lax.optimization_barrier((x_came, y_far[0], y_sends[5]))
    y_far.append(far_block(5))
    x_blocks, alpha, x_rows, who = unpack_x(here, off, x_came, table, devices)


    common = (use, number, x_blocks, alpha)
    acc, *carried = sweep(common, [y_own], 0, None, [x_rows, y_rows])
    acc, *carried = sweep(common, y_far[:2], BPD, carried, acc=acc)
    acc, *carried = sweep(common, y_far[2:4], BPD + 2, carried, acc=acc)
    acc_2, *carried, odd_out = sweep(common, y_far[4:5], BPD + 4, carried, None, peers, 1)
    acc_3, cols_first, left, _, kept, slow, even_out = sweep(common, y_far[5:], BPD + 5, carried, None, peers, 0)
    y_all = [y_own] + y_far

    odd_in = swap(odd_out, devices, GROUP // 2)
    even_in = swap(even_out, devices, 0)
    accs = [acc, acc_2, acc_3]
    x_next, cols_second = slots_call(
        functools.partial(columns_kernel, log_count=log_count, accs=len(accs)),
        lists + [use, left],
        accs + [x_rows, y_rows],
        kept,
        slow,
        x_blocks,
        y_all,
        [jax.ShapeDtypeStruct((8, LOCAL), f32), jax.ShapeDtypeStruct((YBLOCKS, 1, BS), f32)],
        [pltpu.VMEM((YBLOCKS, 8, BS), f32), pltpu.VMEM((LOCAL, 128), f32), pltpu.VMEM((8, LOCAL), f32)],
        "columns",
    )
    even_out, odd_out, g_one = home(who, peers, (even_in, odd_in), cols_first, cols_second, y_rows, log_count)
    even_in = swap(even_out, devices, 0)
    row_scratch = [pltpu.VMEM((YBLOCKS, 1, BS), f32), pltpu.VMEM((YBLOCKS, 1, BS), f32)]
    sums = [jax.ShapeDtypeStruct((LOCAL, 128), f32), jax.ShapeDtypeStruct((8, LOCAL), f32)]

    def row_sums(phase, smem, front, outs, scratch):
        return slots_call(
            functools.partial(rows_kernel, log_count=log_count, phase=phase),
            lists + [use, left] + smem,
            front,
            kept,
            slow,
            x_blocks,
            y_all,
            outs,
            scratch + row_scratch,
            ("rows_own", "rows_even", "rows_odd")[phase],
        )

    acc, state = row_sums(0, [], [g_one], sums, [])
    odd_out, acc = lax.optimization_barrier((odd_out, acc))
    odd_in = swap(odd_out, devices, GROUP // 2)
    acc, state = row_sums(1, [source], [acc, state, even_in, g_one], sums, [])
    f_two, g_two = row_sums(
        2,
        [source, who],
        [acc, state, even_in, odd_in, g_one, cols_second, y_rows, x_next],
        [jax.ShapeDtypeStruct((1, LOCAL), f32)] * 2,
        [pltpu.VMEM((LOCAL, 128), f32), pltpu.VMEM((8, LOCAL), f32)],
    )
    return f_two.reshape(LOCAL), g_two.reshape(LOCAL)


def solution(mesh):
    placed_as = (
        P("blk", None),
        P("blk", None),
        P("blk"),
        P("blk"),
        P("blk"),
        P("blk"),
        P("blk", None),
        P("blk"),
    )
    return jax.shard_map(
        on_device, mesh=mesh, in_specs=placed_as, out_specs=(P("blk"), P("blk")), check_vma=False
    )
```

```python
import functools
import math

import jax
import jax.numpy as jnp
import numpy as np
from jax import lax
from jax.experimental import pallas as pl
from jax.experimental.pallas import tpu as pltpu
from jax.sharding import PartitionSpec as P

DIM = 512
BS = 1024
BPD = 2
REACH = 3
LOCAL = BPD * BS
EXTRA = 128
WIDE = DIM + EXTRA
TAIL = 16
ROWS = BS + TAIL
CHUNK = 512
PART = 256
ROUNDS = ((1, -3, 3, -1, -2, 2), (-1, 3, -3, 1, -2, 2), (1, -3, 3, -1, 2, -2), (-1, 3, -3, 1, 2, -2))
FAR = len(ROUNDS[0])
YBLOCKS = BPD + FAR
SLOTS = BPD * YBLOCKS
MOST = 12
GROUP = 8
PEERS = 2 * GROUP
X_LANES = EXTRA // 2

entropy_weight = 0.05
scale = math.log2(math.e) / entropy_weight
log_two = math.log(2.0)
lowest = -1e30
exponent_room = 112.0
mebi = 1024 * 1024

f32 = jnp.float32
bf16 = jnp.bfloat16
i32 = jnp.int32

SMEM = pl.BlockSpec(memory_space=pltpu.SMEM)
ANY = pl.BlockSpec(memory_space=pl.ANY)
VMEM = pl.BlockSpec(memory_space=pltpu.VMEM)
HBM = pl.BlockSpec(memory_space=pltpu.HBM)


def iota(shape, dim):
    return lax.broadcasted_iota(i32, shape, dim)


def dot(a, b):
    return jnp.dot(a, b, preferred_element_type=f32)


def nt_dot(a, b):
    return lax.dot_general(a, b, (((1,), (1,)), ((), ())), preferred_element_type=f32)


def ones_where(mask):
    return jnp.where(mask, 1.0, 0.0).astype(bf16)


def params():
    return pltpu.CompilerParams(vmem_limit_bytes=64 * mebi)


def whole(shape):
    return pl.BlockSpec(shape, lambda *t: (0,) * len(shape))


def laid_out(square):
    return jnp.concatenate([square[n : n + 1, :] for n in range(square.shape[0])], axis=1)


def down(row):
    parts = [jnp.broadcast_to(row[:, c : c + 128], (128, 128)).T for c in range(0, row.shape[1], 128)]
    return jnp.concatenate(parts, axis=0)


def moved(values, place):
    high = iota((16, LOCAL), 0) == lax.shift_right_logical(place, 7)
    low = ones_where(iota((128, LOCAL), 0) == jnp.bitwise_and(place, 127))
    stack = jnp.concatenate([jnp.where(high, v, 0.0) for v in values], axis=0).astype(bf16)
    out = nt_dot(stack, low)
    return [laid_out(out[16 * n : 16 * n + 16, :]) for n in range(len(values))]


def moved_exact(value, place):
    first = value.astype(bf16).astype(f32)
    second = (value - first).astype(bf16).astype(f32)
    parts = moved([first, second, value - first - second], place)
    return parts[0] + parts[1] + parts[2]


def before_matrix():
    return ones_where(iota((128, 128), 0) < iota((128, 128), 1))


def plan(order, start, devices, first_lane):
    share = LOCAL // devices
    target = lax.shift_right_logical(order, 11)
    hit = iota((devices, LOCAL), 0) == target
    hot = ones_where(hit)
    before = before_matrix()
    every = jnp.ones((128, 128), bf16)
    seen = jnp.zeros((devices, 128), f32)
    earlier = []
    for c in range(0, LOCAL, 128):
        piece = hot[:, c : c + 128]
        earlier.append(dot(piece, before) + seen)
        seen = seen + dot(piece, every)
    earlier = jnp.concatenate(earlier, axis=1)
    rank = jnp.sum(jnp.where(hit, earlier, 0.0), axis=0, keepdims=True).astype(i32)
    within = jnp.bitwise_and(order, LOCAL - 1)
    high = lax.shift_right_logical(within, 6).astype(f32)
    low = jnp.bitwise_and(within, 63).astype(f32)
    row = iota((EXTRA, LOCAL), 0) - first_lane
    field = row // share
    value = jnp.where(field == 0, high, jnp.where(field == 1, low, start))
    mine = (row >= 0) & (row < 3 * share) & (row % share == rank)
    return target * share + rank, nt_dot(hot, jnp.where(mine, value, 0.0).astype(bf16))


def partner_offsets(me):
    kind = jnp.bitwise_and(me, 3)
    out = []
    for k in range(FAR):
        value = jnp.int32(ROUNDS[0][k])
        for n in range(1, 4):
            value = jnp.where(kind == n, jnp.int32(ROUNDS[n][k]), value)
        out.append(value)
    return out


def pack_y_kernel(
    me_ref, partners_ref, counts_ref, y_order, x_order, y_start, x_start, points, out_ref, x_pos_ref, pos_ref, table_ref,
    *, devices
):
    step = pl.program_id(0)
    share = LOCAL // devices

    @pl.when(step == 0)
    def _():
        y_pos, y_table = plan(y_order[...], y_start[...].astype(f32).reshape(1, LOCAL), devices, 0)
        x_pos, x_table = plan(x_order[...], x_start[...].astype(f32).reshape(1, LOCAL), devices, X_LANES)
        pos_ref[...] = y_pos
        x_pos_ref[...] = x_pos
        me = me_ref[0]
        offsets = partner_offsets(me)
        need = [jnp.int32(0)] * FAR
        for b in range(BPD):
            for s in range(partners_ref.shape[1]):
                block = partners_ref[b, s]
                away = lax.shift_right_logical(block, 1) - me
                for k in range(FAR):
                    listed = (s < counts_ref[b]) & (away == offsets[k])
                    need[k] = jnp.where(listed, jnp.bitwise_and(block, 1), need[k])
        table = y_table + x_table
        row, lane = iota(table.shape, 0), iota(table.shape, 1)
        for k in range(FAR):
            table = jnp.where((row == me + offsets[k]) & (lane == 3 * share), need[k].astype(f32), table)
        table_ref[...] = table

    base = step * CHUNK
    hot = ones_where(iota((CHUNK, LOCAL), 0) + base == pos_ref[...])
    out_ref[:, :DIM] = dot(hot, points[...]).astype(bf16)
    some = CHUNK // share
    table = table_ref[pl.ds(pl.multiple_of(step * some, some), some), :]
    out_ref[:, DIM:] = jnp.broadcast_to(table[:, None, :], (some, share, EXTRA)).reshape(CHUNK, EXTRA).astype(bf16)


def pack_y(me, partners, counts, y_order, x_order, y_start, x_start, points, devices):
    row = whole((1, LOCAL))
    return pl.pallas_call(
        functools.partial(pack_y_kernel, devices=devices),
        grid=(LOCAL // CHUNK,),
        in_specs=[SMEM, SMEM, SMEM, row, row, whole((LOCAL,)), whole((LOCAL,)), whole((LOCAL, DIM))],
        out_specs=[pl.BlockSpec((CHUNK, WIDE), lambda t: (t, 0)), row],
        out_shape=[pltpu.HBM((LOCAL, WIDE), bf16), jax.ShapeDtypeStruct((1, LOCAL), i32)],
        scratch_shapes=[pltpu.VMEM((1, LOCAL), i32), pltpu.VMEM((devices, EXTRA), f32)],
        compiler_params=params(),
        name="pack_y",
    )(me, partners, counts, y_order, x_order, y_start, x_start, points)


def pack_x_kernel(pos_ref, points_ref, out_ref):
    base = pl.program_id(0) * CHUNK
    hot = ones_where(iota((CHUNK, LOCAL), 0) + base == pos_ref[...])
    out_ref[...] = dot(hot, points_ref[...]).astype(bf16)


def pack_x(pos, points):
    return pl.pallas_call(
        pack_x_kernel,
        grid=(LOCAL // CHUNK,),
        in_specs=[whole((1, LOCAL)), whole((LOCAL, DIM))],
        out_specs=pl.BlockSpec((CHUNK, DIM), lambda t: (t, 0)),
        out_shape=pltpu.HBM((LOCAL, DIM), bf16),
        compiler_params=params(),
        name="pack_x",
    )(pos, points)


WINDOW = PART + 16
HELD = BS + WINDOW + 16


def arrived(table, base, with_low):
    share = 16
    row, lane = iota((EXTRA, EXTRA), 0), iota((EXTRA, EXTRA), 1)
    pick = jnp.where(row == base + lane % share, 64.0 if with_low else 1.0, 0.0)
    if with_low:
        pick = jnp.where(row == base + share + lane % share, 1.0, pick)
    values = dot(table, pick.astype(bf16))
    values = jnp.where(row % (EXTRA // share) == lane // share, values, 0.0)
    return jnp.sum(values.reshape(LOCAL // 128, EXTRA // share, 128), axis=1)


def unpack_y_kernel(me_ref, came_ref, rows_ref, table_ref, own_ref, *rest, devices):
    sends = rest[:FAR]
    held, sems, own_sem, points_buf, extra_buf, in_sems = rest[FAR:]
    share = LOCAL // devices
    me = me_ref[0]
    extra_in = pltpu.make_async_copy(came_ref.at[:, pl.ds(DIM, EXTRA)], extra_buf, in_sems.at[0])
    extra_in.start()
    points_in = []
    for c in range(LOCAL // PART):
        piece = pl.ds(c * PART, PART)
        points_in.append(
            pltpu.make_async_copy(came_ref.at[piece, pl.ds(0, DIM)], points_buf.at[piece, :], in_sems.at[1 + c])
        )
        points_in[c].start()
    extra_in.wait()
    table = dot(ones_where(iota((devices, LOCAL), 1) == iota((devices, LOCAL), 0) * share), extra_buf[...])
    table_ref[...] = table
    place_square = arrived(table.astype(bf16), 0, True)
    place = laid_out(place_square)
    start = laid_out(arrived(table.astype(bf16), 2 * share, False))

    picks = []
    offsets = partner_offsets(me)
    small_row, small_lane = iota((devices, EXTRA), 0), iota((devices, EXTRA), 1)
    for k in range(FAR):
        here = (small_row == me + offsets[k]) & (small_lane == 3 * share)
        picks.append(jnp.sum(jnp.where(here, table, 0.0)) > 0.5)

    second = place >= float(BS)
    square = ones_where(place_square >= float(BS))
    totals = dot(square, jnp.ones((128, 128), bf16)).astype(bf16)
    earlier = dot(square, before_matrix()) + dot(ones_where(iota((16, 16), 1) < iota((16, 16), 0)), totals)
    ones_before = laid_out(earlier)
    dest = jnp.where(second, ones_before, iota((1, LOCAL), 1).astype(f32) - ones_before).astype(i32)
    seat = jnp.where(second, dest + BS, dest)
    position = place.astype(i32)
    start_row, high_row, low_row = moved(
        [start, lax.shift_right_logical(position, 6).astype(f32), jnp.bitwise_and(position, 63).astype(f32)], seat
    )
    rows_ref[0:1, :] = start_row
    rows_ref[2:3, :] = high_row * 64.0 + low_row
    rows_ref[3:8, :] = jnp.zeros((5, LOCAL), f32)
    sixteen, lane16 = iota((16, 128), 0), iota((16, 128), 1)

    for j in range(BPD):
        held[j, 0:16, :] = jnp.zeros((16, DIM), bf16)
        here = jnp.where(second if j else jnp.logical_not(second), dest, -1)
        for c in range(LOCAL // PART):
            span = slice(c * PART, (c + 1) * PART)
            begin = jnp.sum(jnp.where((sixteen == c * PART // 128) & (lane16 == 0), earlier, 0.0)).astype(i32)
            if j == 0:
                begin = c * PART - begin
            begin = pl.multiple_of(lax.shift_left(lax.shift_right_logical(begin, 4), 4), 16)
            hot = ones_where(iota((WINDOW, PART), 0) + begin == here[:, span])
            if j == 0:
                points_in[c].wait()
            part = dot(hot, points_buf[span, :]).astype(bf16)
            first = pl.ds(begin, 16)
            held[j, first, :] = held[j, first, :] + part[0:16, :]
            held[j, pl.ds(pl.multiple_of(begin + 16, 16), PART), :] = part[16:, :]
        half = []
        for c in range(0, BS, PART):
            points = held[j, c : c + PART, :].astype(f32)
            total = 0.5 * jnp.sum(points * points, axis=1, keepdims=True)
            half.append(jnp.broadcast_to(total, (PART, 128)).T[0:1, :])
        half = jnp.concatenate(half, axis=1)
        block = slice(j * BS, (j + 1) * BS)
        rows_ref[1:2, block] = half
        beta = start_row[:, block] - half
        first = beta.astype(bf16).astype(f32)
        next_part = (beta - first).astype(bf16).astype(f32)
        most = jnp.max(half, axis=1, keepdims=True) * 1.01
        sub = iota((TAIL, DIM), 0)
        tail = jnp.zeros((TAIL, DIM), f32) + most
        for n, piece in enumerate((first, next_part, beta - first - next_part)):
            tail = jnp.where(sub == 2 * n, piece[:, :DIM], tail)
            tail = jnp.where(sub == 2 * n + 1, piece[:, DIM:], tail)
        held[j, BS:ROWS, :] = tail.astype(bf16)
        done = held.at[j, pl.ds(0, ROWS), :]
        for k in range(FAR):
            wanted = picks[k] if j == 1 else jnp.logical_not(picks[k])

            @pl.when(wanted)
            def _():
                pltpu.make_async_copy(done, sends[k], sems.at[k]).start()

        pltpu.make_async_copy(done, own_ref.at[j], own_sem.at[j]).start()

    done = held.at[0, pl.ds(0, ROWS), :]
    for k in range(FAR):
        pltpu.make_async_copy(done, sends[k], sems.at[k]).wait()
    for j in range(BPD):
        pltpu.make_async_copy(done, own_ref.at[j], own_sem.at[j]).wait()


def unpack_y(me, came, devices):
    return pl.pallas_call(
        functools.partial(unpack_y_kernel, devices=devices),
        in_specs=[SMEM, ANY],
        out_specs=[VMEM, VMEM] + [HBM] * (1 + FAR),
        out_shape=[
            jax.ShapeDtypeStruct((8, LOCAL), f32),
            jax.ShapeDtypeStruct((devices, EXTRA), f32),
            pltpu.HBM((BPD, ROWS, DIM), bf16),
        ]
        + [pltpu.HBM((ROWS, DIM), bf16)] * FAR,
        scratch_shapes=[
            pltpu.VMEM((BPD, HELD, DIM), bf16),
            pltpu.SemaphoreType.DMA((FAR,)),
            pltpu.SemaphoreType.DMA((BPD,)),
            pltpu.VMEM((LOCAL, DIM), bf16),
            pltpu.VMEM((LOCAL, EXTRA), bf16),
            pltpu.SemaphoreType.DMA((1 + LOCAL // PART,)),
        ],
        compiler_params=params(),
        name="unpack_y",
    )(me, came)


def unpack_x_kernel(
    me_ref, peer_ref, came_ref, table_ref, points_ref, alpha_ref, rows_ref, who_ref, place_ref, start_ref, *, devices
):
    step = pl.program_id(0)

    @pl.when(step == 0)
    def _():
        table = table_ref[...].astype(bf16)
        place = laid_out(arrived(table, X_LANES, True)).astype(i32)
        place_ref[...] = place
        start_ref[...] = moved([laid_out(arrived(table, X_LANES + 32, False))], place)[0]
        row, lane = iota((EXTRA, EXTRA), 0), iota((EXTRA, EXTRA), 1)
        for n in range(PEERS):
            peer = me_ref[0] + peer_ref[n]
            wants = jnp.sum(jnp.where((row == peer) & (lane == 3 * LOCAL // devices), table_ref[...], 0.0)) > 0.5
            valid = (peer_ref[n] != 0) & (peer >= 0) & (peer < devices)
            who_ref[n] = jnp.where(valid, jnp.where(wants, 1, 0), -1)

    base = step * CHUNK
    hot = ones_where(iota((CHUNK, LOCAL), 0) + base == place_ref[...])
    points = dot(hot, came_ref[...])
    points_ref[...] = points.astype(bf16)
    half = jnp.broadcast_to(0.5 * jnp.sum(points * points, axis=1, keepdims=True), (CHUNK, 128))
    start = start_ref[:, pl.ds(pl.multiple_of(base, CHUNK), CHUNK)]
    alpha_ref[...] = (down(start) - half) * scale
    rows_ref[0:1, :] = start
    rows_ref[1:8, :] = jnp.concatenate([half[c : c + 128, :].T[0:7, :] for c in range(0, CHUNK, 128)], axis=1)


def unpack_x(me, peer_offsets, came, table, devices):
    return pl.pallas_call(
        functools.partial(unpack_x_kernel, devices=devices),
        grid=(LOCAL // CHUNK,),
        in_specs=[SMEM, SMEM, whole((LOCAL, DIM)), whole((EXTRA, EXTRA))],
        out_specs=[
            pl.BlockSpec((CHUNK, DIM), lambda t: (t, 0)),
            pl.BlockSpec((CHUNK, 128), lambda t: (t, 0)),
            pl.BlockSpec((8, CHUNK), lambda t: (0, t)),
            SMEM,
        ],
        out_shape=[
            pltpu.HBM((LOCAL, DIM), bf16),
            pltpu.HBM((LOCAL, 128), f32),
            jax.ShapeDtypeStruct((8, LOCAL), f32),
            jax.ShapeDtypeStruct((PEERS,), i32),
        ],
        scratch_shapes=[pltpu.VMEM((1, LOCAL), i32), pltpu.VMEM((1, LOCAL), f32)],
        compiler_params=params(),
        name="unpack_x",
    )(me, peer_offsets, came, table)


def merge(top, total, other_top, other_total):
    new = jnp.maximum(top, other_top)
    return new, total * jnp.exp2(top - new) + other_total * jnp.exp2(other_top - new)


def logs(top, total):
    return jnp.where(total > 0.0, top + jnp.log2(total), lowest)


def high_of(row):
    return jnp.max(row, axis=1, keepdims=True)


def low_of(row):
    return jnp.min(row, axis=1, keepdims=True)


def put_cols(col_ref, y, part_top, part_total):
    top, total = merge(col_ref[y, 0:1, :], col_ref[y, 1:2, :], part_top, part_total)
    col_ref[y, 0:1, :] = top
    col_ref[y, 1:2, :] = total


def clear_cols(col_ref):
    col_ref[:, 0:1, :] = jnp.full((col_ref.shape[0], 1, BS), lowest, f32)
    col_ref[:, 1:2, :] = jnp.zeros((col_ref.shape[0], 1, BS), f32)


def shifted_rows(x_ref, y_ref, beta, part_ref):
    def body(c, carry):
        span = pl.ds(pl.multiple_of(c * PART, PART), PART)
        terms = nt_dot(x_ref[span, :], y_ref[0:BS, :]) * scale + beta
        top = jnp.max(terms, axis=1, keepdims=True)
        total = jnp.sum(jnp.exp2(terms - top), axis=1, keepdims=True)
        part_ref[span, :] = jnp.where(iota((PART, 128), 1) == 0, top, total)
        return carry

    lax.fori_loop(0, BS // PART, body, 0)


def shifted_cols(x_ref, y_ref, alpha_ref, col_ref, y):
    def body(c, carry):
        span = pl.ds(pl.multiple_of(c * PART, PART), PART)
        terms = nt_dot(x_ref[span, :], y_ref[0:BS, :]) * scale + alpha_ref[span, 0:1]
        top = jnp.max(terms, axis=0, keepdims=True)
        put_cols(col_ref, y, top, jnp.sum(jnp.exp2(terms - top), axis=0, keepdims=True))
        return carry

    lax.fori_loop(0, BS // PART, body, 0)


def add_part(part_ref, state_ref, b):
    for c in range(0, BS, 128):
        part = part_ref[c : c + 128, :].T
        span = pl.ds(pl.multiple_of(b * BS + c, 128), 128)
        top, total = merge(state_ref[0:1, span], state_ref[1:2, span], part[0:1, :], part[1:2, :])
        state_ref[0:1, span] = top
        state_ref[1:2, span] = total


def lane_sums(refs):
    out = []
    for c in range(0, LOCAL, 128):
        part = refs[0][c : c + 128, :]
        for ref in refs[1:]:
            part = part + ref[c : c + 128, :]
        out.append(jnp.sum(part.T, axis=0, keepdims=True))
    return jnp.concatenate(out, axis=1)


def fold(values):
    return jnp.sum(values.reshape(values.shape[0] // 8, 8, 128), axis=0)


def own_beta(y_rows_ref):
    return (y_rows_ref[0:1, :] - y_rows_ref[1:2, :]) * scale


def sweep_kernel(*refs, base, count, first, sends, more):
    use_ref, seat_of_ref, x_ref, alpha_ref = refs[:4]
    refs = refs[4:]
    if first:
        x_rows_ref, y_rows_ref = refs[:2]
        refs = refs[2:]
    else:
        cols_in, left_in, stat_in = refs[:3]
        refs = refs[5:]
    if sends is not None:
        peers_ref = refs[0]
        refs = refs[1:]
    if more:
        acc_in = refs[0]
        refs = refs[1:]
    y_refs = refs[:1] if first else refs[:count]
    refs = refs[len(y_refs) :]
    acc_ref, cols_ref, left_ref, stat_ref, kept_ref, slow_ref = refs[:6]
    refs = refs[6:]
    if sends is not None:
        group_out = refs[0]
        refs = refs[1:]
    x_buf, alpha_buf, x_sems, y_buf, sems, col_ref, weight_ref, part_ref, beta_ref, fit_ref, room_ref, tiles, tile_sems, tile_count = refs

    def copy(n):
        source = y_refs[0].at[n] if first else y_refs[n]
        return pltpu.make_async_copy(source, y_buf.at[n % 2], sems.at[n % 2])

    def x_copies(n):
        rows = pl.ds(n * BS, BS)
        return (
            pltpu.make_async_copy(x_ref.at[rows, :], x_buf.at[rows, :], x_sems.at[n, 0]),
            pltpu.make_async_copy(alpha_ref.at[rows, :], alpha_buf.at[rows, :], x_sems.at[n, 1]),
        )

    copy(0).start()
    for part in x_copies(0):
        part.start()
    tile_count[0] = 0
    acc_ref[...] = acc_in[...] if more else jnp.zeros((LOCAL, 128), f32)

    def tile_copy(at, seat):
        return pltpu.make_async_copy(tiles.at[at], kept_ref.at[seat], tile_sems.at[at])

    def part_copy(at, seat, c):
        rows = pl.ds(c, PART)
        return pltpu.make_async_copy(tiles.at[at, rows, :], kept_ref.at[seat, rows, :], tile_sems.at[at])

    if first:
        for n in range(SLOTS):
            left_ref[n] = -1.0
        alpha = (x_rows_ref[0:1, :] - x_rows_ref[1:2, :]) * scale
        alpha_top = high_of(alpha)
        lane = iota((8, 128), 1)
        beta_top = high_of(own_beta(y_rows_ref))
        most = high_of(x_rows_ref[1:2, :]) * 1.01
        spread = alpha_top - low_of(alpha)
        stat_ref[...] = jnp.where(
            lane == 0, alpha_top, jnp.where(lane == 1, spread, jnp.where(lane == 2, most, beta_top))
        )
    else:
        for n in range(SLOTS):
            left_ref[n] = left_in[n]
        cols_ref[...] = cols_in[...]
        stat_ref[...] = stat_in[...]

    def body(step, carry):
        y, b = step // BPD, step % BPD
        slot = base * BPD + step
        for n in range(count):

            @pl.when(step == BPD * n)
            def _():
                copy(n).wait()
                if n + 1 < count:
                    copy(n + 1).start()

        for n in range(BPD):

            @pl.when(step == n)
            def _():
                for part in x_copies(n):
                    part.wait()
                if n + 1 < BPD:
                    for part in x_copies(n + 1):
                        part.start()
                rows = slice(n * BS, (n + 1) * BS)
                weight_ref[rows, :] = jnp.exp2(alpha_buf[rows, :] - stat_ref[0:1, 0:1])

        now = y_buf.at[y % 2]
        rows_from = b * BS

        @pl.when(b == 0)
        def _():
            clear_cols(col_ref)
            tail = now[BS:ROWS, :].astype(f32)
            halves = [tail[n : n + 1, :] + tail[n + 2 : n + 3, :] + tail[n + 4 : n + 5, :] for n in range(2)]
            beta = jnp.concatenate(halves, axis=1) * scale
            shift = stat_ref[0:1, 3:4]
            left = exponent_room - 2.0 * scale * jnp.sqrt(tail[6:7, 0:1] * stat_ref[0:1, 2:3])
            reach = jnp.maximum(stat_ref[0:1, 1:2], jnp.maximum(high_of(beta) - shift, shift - low_of(beta)))
            beta_ref[0:1, :] = beta
            beta_ref[1:2, :] = jnp.exp2(beta - shift)
            room_ref[0] = left[0, 0]
            fit_ref[0] = jnp.where((left - reach)[0, 0] >= 0.0, 1, 0)

        @pl.when(use_ref[slot] > 0)
        def _():
            fits = fit_ref[0] > 0

            @pl.when(fits)
            def _():
                left_ref[slot] = room_ref[0]
                done = tile_count[0]
                tile_count[0] = done + 1
                at = done % 2

                @pl.when(done > 1)
                def _():
                    tile_copy(at, 0).wait()

                weight = beta_ref[1:2, :]
                sums = jnp.zeros((8, BS), f32)
                for c in range(0, BS, PART):
                    span = pl.ds(pl.multiple_of(rows_from + c, PART), PART)
                    terms = jnp.exp2(nt_dot(x_buf[span, :], now[0:BS, :]) * scale)
                    tiles[at, c : c + PART, :] = terms.astype(bf16)
                    part_copy(at, seat_of_ref[slot], c).start()
                    row_part = acc_ref[span, :]
                    col_parts = []
                    for n in range(0, BS, 128):
                        piece = terms[:, n : n + 128]
                        row_part = row_part + piece * weight[:, n : n + 128]
                        col_parts.append(fold(piece * weight_ref[span, :]))
                    acc_ref[span, :] = row_part
                    sums = sums + jnp.concatenate(col_parts, axis=1)
                put_cols(col_ref, 0, stat_ref[0:1, 0:1], jnp.sum(sums, axis=0, keepdims=True))

            @pl.when(jnp.logical_not(fits))
            def _():
                block = pl.ds(pl.multiple_of(rows_from, BS), BS)
                shifted_rows(x_buf.at[block, :], now, beta_ref[0:1, :], part_ref)
                out = pltpu.make_async_copy(part_ref, slow_ref.at[slot], sems.at[2])
                out.start()
                shifted_cols(x_buf.at[block, :], now, alpha_buf.at[block, :], col_ref, 0)
                out.wait()

        @pl.when(b == BPD - 1)
        def _():
            cols_ref[base + y] = logs(col_ref[0, 0:1, :], col_ref[0, 1:2, :])

        return carry

    lax.fori_loop(0, BPD * count, body, 0)
    for n in range(2):

        @pl.when(tile_count[0] > n)
        def _():
            tile_copy(n, 0).wait()

    if sends is not None:
        for n in range(GROUP):
            group_out[n] = outgoing(cols_ref, peers_ref[sends * GROUP + n])


def outgoing(cols_ref, index):
    return jnp.where(index < 0, lowest, cols_ref[jnp.maximum(index, 0)])


def sweep(common, y_list, base, carried, rows=None, peers=None, sends=None, acc=None):
    first = carried is None
    count = BPD if first else len(y_list)
    in_specs = [SMEM, SMEM, HBM, HBM]
    operands = list(common)
    aliases = {}
    if first:
        in_specs += [VMEM, VMEM]
        operands += rows
    else:
        in_specs += [VMEM, SMEM, VMEM, HBM, HBM]
        operands += list(carried)
        aliases = {7: 4, 8: 5}
    if sends is not None:
        in_specs.append(SMEM)
        operands.append(peers)
    if acc is not None:
        in_specs.append(VMEM)
        operands.append(acc)
    in_specs += [ANY] * len(y_list)
    operands += y_list
    out_specs = [VMEM, VMEM, SMEM, VMEM, HBM, HBM]
    out_shape = [
        jax.ShapeDtypeStruct((LOCAL, 128), f32),
        jax.ShapeDtypeStruct((YBLOCKS, 1, BS), f32),
        jax.ShapeDtypeStruct((SLOTS,), f32),
        jax.ShapeDtypeStruct((8, 128), f32),
        pltpu.HBM((MOST, BS, BS), bf16),
        pltpu.HBM((SLOTS, BS, 128), f32),
    ]
    if sends is not None:
        out_specs.append(VMEM)
        out_shape.append(jax.ShapeDtypeStruct((GROUP, 1, BS), f32))
    return pl.pallas_call(
        functools.partial(sweep_kernel, base=base, count=count, first=first, sends=sends, more=acc is not None),
        in_specs=in_specs,
        out_specs=out_specs,
        out_shape=out_shape,
        scratch_shapes=[
            pltpu.VMEM((LOCAL, DIM), bf16),
            pltpu.VMEM((LOCAL, 128), f32),
            pltpu.SemaphoreType.DMA((BPD, 2)),
            pltpu.VMEM((2, ROWS, DIM), bf16),
            pltpu.SemaphoreType.DMA((3,)),
            pltpu.VMEM((1, 8, BS), f32),
            pltpu.VMEM((LOCAL, 128), f32),
            pltpu.VMEM((BS, 128), f32),
            pltpu.VMEM((8, BS), f32),
            pltpu.SMEM((1,), i32),
            pltpu.SMEM((1,), f32),
            pltpu.VMEM((2, BS, BS), bf16),
            pltpu.SemaphoreType.DMA((2,)),
            pltpu.SMEM((1,), i32),
        ],
        input_output_aliases=aliases,
        compiler_params=params(),
        name=f"sweep_{base}",
    )(*operands)


def load_pair(slot, x_ref, y_refs, x_buf, y_buf, sems):
    rows = pl.ds(pl.multiple_of((slot % BPD) * BS, BS), BS)
    fetch = pltpu.make_async_copy(x_ref.at[rows, :], x_buf, sems.at[0])
    fetch.start()
    fetch.wait()
    for n in range(YBLOCKS):

        @pl.when(slot // BPD == n)
        def _():
            source = y_refs[0].at[n] if n < BPD else y_refs[n - BPD + 1]
            fetch = pltpu.make_async_copy(source, y_buf, sems.at[1])
            fetch.start()
            fetch.wait()


def next_potential(now, half, total, log_count):
    return 0.5 * (now + half + entropy_weight * (log_count - log_two * total))


def fetch_terms(kept_ref, terms_ref, sems, list_ref, seat_of_ref, start, stop):
    def term_copy(n):
        return pltpu.make_async_copy(kept_ref.at[seat_of_ref[list_ref[n]]], terms_ref.at[n], sems.at[n])

    for n in range(MOST):

        @pl.when((n >= start) & (n < stop))
        def _():
            term_copy(n).start()

    return term_copy


def columns_kernel(list_ref, live_ref, seat_of_ref, use_ref, left_ref, *refs, log_count, accs):
    start, stop = 0, live_ref[2]
    acc_refs = refs[:accs]
    x_rows_ref, y_rows_ref, kept_ref, slow_ref, x_ref = refs[accs : accs + 5]
    y_refs = refs[accs + 5 : accs + 6 + FAR]
    next_ref, out_ref, col_ref, weight_ref, state_ref, part_ref, x_buf, y_buf, sems, terms_ref, term_sems = refs[accs + 6 + FAR :]
    term_copy = fetch_terms(kept_ref, terms_ref, term_sems, list_ref, seat_of_ref, start, stop)
    clear_cols(col_ref)
    total = lane_sums(acc_refs)
    state_ref[0:1, :] = jnp.where(total > 0.0, high_of(own_beta(y_rows_ref)), lowest)
    state_ref[1:2, :] = total
    for n in range(SLOTS):

        @pl.when((use_ref[n] > 0) & (left_ref[n] < 0.0))
        def _():
            fetch = pltpu.make_async_copy(slow_ref.at[n], part_ref, sems.at[0])
            fetch.start()
            fetch.wait()
            add_part(part_ref, state_ref, n % BPD)

    half = x_rows_ref[1:2, :]
    f_next = next_potential(x_rows_ref[0:1, :], half, logs(state_ref[0:1, :], state_ref[1:2, :]), log_count)
    next_ref[0:1, :] = f_next
    next_ref[1:2, :] = half
    next_ref[2:8, :] = jnp.zeros((6, LOCAL), f32)
    alpha = (f_next - half) * scale
    state_ref[2:3, :] = alpha
    top = high_of(alpha)
    weight_ref[...] = down(jnp.exp2(alpha - top))
    reach = (top - low_of(alpha))[0, 0]

    def body(step, carry):
        slot = list_ref[step]
        y, b = slot // BPD, slot % BPD
        fits = reach <= left_ref[slot]
        term_copy(step).wait()

        @pl.when(fits)
        def _():
            sums = jnp.zeros((8, BS), f32)
            for c in range(0, BS, 64):
                weight = weight_ref[pl.ds(pl.multiple_of(b * BS + c, 64), 64), :]
                parts = [fold(terms_ref[step, c : c + 64, n : n + 128].astype(f32) * weight) for n in range(0, BS, 128)]
                sums = sums + jnp.concatenate(parts, axis=1)
            put_cols(col_ref, y, top, jnp.sum(sums, axis=0, keepdims=True))

        @pl.when(jnp.logical_not(fits))
        def _():
            load_pair(slot, x_ref, y_refs, x_buf, y_buf, sems)
            for c in range(0, BS, 128):
                row = state_ref[2:3, pl.ds(pl.multiple_of(b * BS + c, 128), 128)]
                part_ref[c : c + 128, :] = jnp.broadcast_to(row, (128, 128)).T
            shifted_cols(x_buf, y_buf, part_ref, col_ref, y)

        return carry

    lax.fori_loop(start, stop, body, 0)
    for n in range(YBLOCKS):
        out_ref[n] = logs(col_ref[n, 0:1, :], col_ref[n, 1:2, :])


def gathered(j, own_ref, came, who_ref):
    terms = [own_ref[j]] + [jnp.where(who_ref[n] == j, came(n), lowest) for n in range(PEERS)]
    top = terms[0]
    for term in terms[1:]:
        top = jnp.maximum(top, term)
    total = jnp.exp2(terms[0] - top)
    for term in terms[1:]:
        total = total + jnp.exp2(term - top)
    return top + jnp.log2(total)


def home_kernel(who_ref, peers_ref, even_in, odd_in, first_ref, second_ref, y_rows_ref, even_out, odd_out, g_ref, *, log_count):
    came = lambda n: (even_in, odd_in)[n // GROUP][n % GROUP]
    betas = []
    for j in range(BPD):
        span = slice(j * BS, (j + 1) * BS)
        half = y_rows_ref[1:2, span]
        g_next = next_potential(y_rows_ref[0:1, span], half, gathered(j, first_ref, came, who_ref), log_count)
        g_ref[0:1, span] = g_next
        betas.append((g_next - half) * scale)
        g_ref[1:2, span] = betas[j]
    g_ref[2:8, :] = jnp.zeros((6, LOCAL), f32)
    for n in range(PEERS):
        out = (even_out, odd_out)[n // GROUP]
        out[n % GROUP, 0:1, :] = jnp.where(who_ref[n] == 1, betas[1], betas[0])
        out[n % GROUP, 1:2, :] = outgoing(second_ref, peers_ref[n])


def home(who, peers, rows_in, first, second, y_rows, log_count):
    return pl.pallas_call(
        functools.partial(home_kernel, log_count=log_count),
        in_specs=[SMEM, SMEM] + [VMEM] * 5,
        out_specs=[VMEM] * 3,
        out_shape=[jax.ShapeDtypeStruct((GROUP, 2, BS), f32)] * 2 + [jax.ShapeDtypeStruct((8, LOCAL), f32)],
        compiler_params=params(),
        name="home",
    )(who, peers, *rows_in, first, second, y_rows)


def rows_kernel(list_ref, live_ref, seat_of_ref, use_ref, left_ref, *refs, log_count, phase):
    last = phase == 2
    start = live_ref[phase - 1] if phase else 0
    stop = live_ref[phase]
    if last:
        from_ref, who_ref, acc_in, state_in, even_in, odd_in, g_ref, second_ref, y_rows_ref, x_rows_ref = refs[:10]
        refs = refs[10:]
    elif phase:
        from_ref, acc_in, state_in, even_in, g_ref = refs[:5]
        refs = refs[5:]
    else:
        g_ref = refs[0]
        refs = refs[1:]
    kept_ref, slow_ref, x_ref = refs[:3]
    y_refs = refs[3 : 4 + FAR]
    refs = refs[4 + FAR :]
    if last:
        f_ref, g_out_ref, acc_ref, state_ref = refs[:4]
        refs = refs[4:]
    else:
        acc_ref, state_ref = refs[:2]
        refs = refs[2:]
    beta_ref, weight_ref, part_ref, x_buf, y_buf, sems, terms_ref, term_sems = refs
    term_copy = fetch_terms(kept_ref, terms_ref, term_sems, list_ref, seat_of_ref, start, stop)
    shift = high_of(g_ref[1:2, :])
    if phase:
        acc_ref[...] = acc_in[...]
        state_ref[...] = state_in[...]
    else:
        acc_ref[...] = jnp.zeros((LOCAL, 128), f32)
        state_ref[0:1, :] = jnp.full((1, LOCAL), lowest, f32)
        state_ref[1:8, :] = jnp.zeros((7, LOCAL), f32)
    for n in range(BPD):
        beta_ref[n] = g_ref[1:2, n * BS : (n + 1) * BS]
    for n in range(BPD, YBLOCKS if phase else BPD):
        at = from_ref[n] % GROUP
        if last:
            beta_ref[n] = jnp.where(from_ref[n] < GROUP, even_in[at, 0:1, :], odd_in[at, 0:1, :])
        else:
            beta_ref[n] = even_in[at, 0:1, :]
    some = YBLOCKS if phase else BPD
    weight_ref[0:some] = jnp.exp2(beta_ref[0:some] - shift)

    def body(step, carry):
        slot = list_ref[step]
        y, b = slot // BPD, slot % BPD
        beta = beta_ref[y]
        reach = jnp.maximum(high_of(beta) - shift, shift - low_of(beta))
        fits = reach[0, 0] <= left_ref[slot]
        term_copy(step).wait()

        @pl.when(fits)
        def _():
            weight = weight_ref[y]
            for c in range(0, BS, 64):
                span = pl.ds(pl.multiple_of(b * BS + c, 64), 64)
                part = acc_ref[span, :]
                for n in range(0, BS, 128):
                    part = part + terms_ref[step, c : c + 64, n : n + 128].astype(f32) * weight[:, n : n + 128]
                acc_ref[span, :] = part

        @pl.when(jnp.logical_not(fits))
        def _():
            load_pair(slot, x_ref, y_refs, x_buf, y_buf, sems)
            shifted_rows(x_buf, y_buf, beta, part_ref)
            add_part(part_ref, state_ref, b)

        return carry

    lax.fori_loop(start, stop, body, 0)
    if not last:
        return
    total = lane_sums([acc_ref])
    top = jnp.where(total > 0.0, shift, lowest)
    top, total = merge(top, total, state_ref[0:1, :], state_ref[1:2, :])
    f_ref[...] = next_potential(x_rows_ref[0:1, :], x_rows_ref[1:2, :], logs(top, total), log_count)
    came = lambda n: (even_in, odd_in)[n // GROUP][n % GROUP, 1:2, :]
    total = jnp.concatenate([gathered(j, second_ref, came, who_ref) for j in range(BPD)], axis=1)
    g_next = next_potential(g_ref[0:1, :], y_rows_ref[1:2, :], total, log_count)
    g_out_ref[...] = moved_exact(g_next, y_rows_ref[2:3, :].astype(i32))


def slots_call(kernel, smem, front, kept, slow, x_blocks, y_list, outs, scratch, name):
    return pl.pallas_call(
        kernel,
        in_specs=[SMEM] * len(smem) + [VMEM] * len(front) + [HBM, HBM, ANY] + [ANY] * len(y_list),
        out_specs=[VMEM] * len(outs),
        scratch_shapes=scratch
        + [
            pltpu.VMEM((BS, 128), f32),
            pltpu.VMEM((BS, DIM), bf16),
            pltpu.VMEM((ROWS, DIM), bf16),
            pltpu.SemaphoreType.DMA((2,)),
            pltpu.VMEM((MOST, BS, BS), bf16),
            pltpu.SemaphoreType.DMA((MOST,)),
        ],
        out_shape=outs,
        compiler_params=params(),
        name=name,
    )(*smem, *front, kept, slow, x_blocks, *y_list)


def seat_tables():
    half = GROUP // 2
    offsets = np.zeros((GROUP, PEERS), np.int32)
    source = np.zeros((GROUP, YBLOCKS), np.int32)
    for seat in range(GROUP):
        odd_seat = (seat + half) % GROUP
        for other in range(GROUP):
            if other != seat and abs(other - seat) <= REACH:
                offsets[seat, other] = other - seat
            off = other - odd_seat
            if off != 0 and abs(off) <= REACH and not 0 <= seat + off < GROUP:
                offsets[seat, GROUP + other] = off
        for k, off in enumerate(ROUNDS[seat % 4]):
            source[seat, BPD + k] = list(offsets[seat]).index(off)
    index = np.full((GROUP, PEERS), -1, np.int32)
    for seat in range(GROUP):
        for k, off in enumerate(ROUNDS[seat % 4]):
            index[seat, offsets[seat] == off] = BPD + k
    return offsets, index, source


def swap(rows, devices, shift):
    groups = [[(GROUP * k + j + shift) % devices for j in range(GROUP)] for k in range(devices // GROUP)]
    return lax.all_to_all(rows, "blk", split_axis=0, concat_axis=0, tiled=True, axis_index_groups=groups)


def on_device(x_points, y_points, x_start, y_start, x_order, y_order, partners, counts):
    devices = lax.axis_size("blk")
    me = lax.axis_index("blk").astype(i32)
    log_count = math.log(LOCAL * devices)
    here = me[None]
    line = lambda v: v.reshape(1, LOCAL)

    y_sent, x_pos = pack_y(here, partners, counts, line(y_order), line(x_order), y_start, x_start, y_points, devices)
    y_came = lax.all_to_all(y_sent, "blk", split_axis=0, concat_axis=0, tiled=True)
    offsets = lax.dynamic_slice(jnp.array(ROUNDS, i32), (me % 4, 0), (1, FAR))[0]
    live = jnp.arange(partners.shape[1], dtype=i32)[None, :] < counts[:, None]
    away = jnp.where(live, partners // BPD - me, devices)
    local_use = [((away == 0) & (partners % BPD == j)).any(axis=1) for j in range(BPD)]
    far = away[None, :, :] == offsets[:, None, None]
    use = jnp.concatenate([jnp.stack(local_use), far.any(axis=2)]).astype(i32).reshape(SLOTS)
    number = jnp.minimum(jnp.maximum(jnp.cumsum(use) - 1, 0), MOST - 1)

    peer_offsets, peer_index, peer_source = seat_tables()
    row = lambda t: lax.dynamic_slice(jnp.asarray(t), (me % GROUP, 0), (1, t.shape[1]))[0]
    peers, source, off = row(peer_index), row(peer_source), row(peer_offsets)

    far_slot = jnp.repeat(source >= GROUP, BPD).astype(i32)
    near = jnp.cumsum(use * (1 - far_slot))
    rank = jnp.where(far_slot > 0, near[-1] + jnp.cumsum(use * far_slot), near) - 1
    count = jnp.minimum(jnp.sum(use), MOST)
    step = jnp.minimum(jnp.arange(MOST, dtype=i32), count - 1)
    at = (rank[None, :] == step[:, None]) & (use[None, :] > 0)
    slots = jnp.sum(jnp.where(at, jnp.arange(SLOTS, dtype=i32)[None, :], 0), axis=1)
    own = jnp.sum(use[: BPD * BPD])
    live_counts = jnp.stack([own, jnp.minimum(near[-1], count), count])
    x_pos, use, number, slots, live_counts, peers, source, off = lax.optimization_barrier((x_pos, use, number, slots, live_counts, peers, source, off))
    x_sent = pack_x(x_pos, x_points)
    y_came, x_sent = lax.optimization_barrier((y_came, x_sent))
    x_came = lax.all_to_all(x_sent, "blk", split_axis=0, concat_axis=0, tiled=True)
    lists = [slots, live_counts, number]
    y_rows, table, y_own, *y_sends = unpack_y(here, y_came, devices)

    def far_block(k):
        pairs = [(i, i + ROUNDS[i % 4][k]) for i in range(devices) if 0 <= i + ROUNDS[i % 4][k] < devices]
        return lax.ppermute(y_sends[k], "blk", pairs)

    y_far = [far_block(k) for k in range(FAR - 1)]
    x_came, y_far[0], y_sends[5] = lax.optimization_barrier((x_came, y_far[0], y_sends[5]))
    y_far.append(far_block(5))
    x_blocks, alpha, x_rows, who = unpack_x(here, off, x_came, table, devices)


    common = (use, number, x_blocks, alpha)
    acc, *carried = sweep(common, [y_own], 0, None, [x_rows, y_rows])
    acc, *carried = sweep(common, y_far[:2], BPD, carried, acc=acc)
    acc, *carried = sweep(common, y_far[2:4], BPD + 2, carried, acc=acc)
    acc_2, *carried, odd_out = sweep(common, y_far[4:5], BPD + 4, carried, None, peers, 1)
    acc_3, cols_first, left, _, kept, slow, even_out = sweep(common, y_far[5:], BPD + 5, carried, None, peers, 0)
    y_all = [y_own] + y_far

    odd_in = swap(odd_out, devices, GROUP // 2)
    even_in = swap(even_out, devices, 0)
    accs = [acc, acc_2, acc_3]
    x_next, cols_second = slots_call(
        functools.partial(columns_kernel, log_count=log_count, accs=len(accs)),
        lists + [use, left],
        accs + [x_rows, y_rows],
        kept,
        slow,
        x_blocks,
        y_all,
        [jax.ShapeDtypeStruct((8, LOCAL), f32), jax.ShapeDtypeStruct((YBLOCKS, 1, BS), f32)],
        [pltpu.VMEM((YBLOCKS, 8, BS), f32), pltpu.VMEM((LOCAL, 128), f32), pltpu.VMEM((8, LOCAL), f32)],
        "columns",
    )
    even_out, odd_out, g_one = home(who, peers, (even_in, odd_in), cols_first, cols_second, y_rows, log_count)
    even_in = swap(even_out, devices, 0)
    row_scratch = [pltpu.VMEM((YBLOCKS, 1, BS), f32), pltpu.VMEM((YBLOCKS, 1, BS), f32)]
    sums = [jax.ShapeDtypeStruct((LOCAL, 128), f32), jax.ShapeDtypeStruct((8, LOCAL), f32)]

    def row_sums(phase, smem, front, outs, scratch):
        return slots_call(
            functools.partial(rows_kernel, log_count=log_count, phase=phase),
            lists + [use, left] + smem,
            front,
            kept,
            slow,
            x_blocks,
            y_all,
            outs,
            scratch + row_scratch,
            ("rows_own", "rows_even", "rows_odd")[phase],
        )

    acc, state = row_sums(0, [], [g_one], sums, [])
    odd_out, acc = lax.optimization_barrier((odd_out, acc))
    odd_in = swap(odd_out, devices, GROUP // 2)
    acc, state = row_sums(1, [source], [acc, state, even_in, g_one], sums, [])
    f_two, g_two = row_sums(
        2,
        [source, who],
        [acc, state, even_in, odd_in, g_one, cols_second, y_rows, x_next],
        [jax.ShapeDtypeStruct((1, LOCAL), f32)] * 2,
        [pltpu.VMEM((LOCAL, 128), f32), pltpu.VMEM((8, LOCAL), f32)],
    )
    return f_two.reshape(LOCAL), g_two.reshape(LOCAL)


def solution(mesh):
    placed_as = (
        P("blk", None),
        P("blk", None),
        P("blk"),
        P("blk"),
        P("blk"),
        P("blk"),
        P("blk", None),
        P("blk"),
    )
    return jax.shard_map(
        on_device, mesh=mesh, in_specs=placed_as, out_specs=(P("blk"), P("blk")), check_vma=False
    )
```

```python
import functools
import math

import jax
import jax.numpy as jnp
import numpy as np
from jax import lax
from jax.experimental import pallas as pl
from jax.experimental.pallas import tpu as pltpu
from jax.sharding import PartitionSpec as P

DIM = 512
BS = 1024
BPD = 2
REACH = 3
LOCAL = BPD * BS
EXTRA = 128
WIDE = DIM + EXTRA
TAIL = 16
ROWS = BS + TAIL
CHUNK = 512
PART = 256
ROUNDS = ((1, -3, 3, -1, -2, 2), (-1, 3, -3, 1, -2, 2), (1, -3, 3, -1, 2, -2), (-1, 3, -3, 1, 2, -2))
FAR = len(ROUNDS[0])
YBLOCKS = BPD + FAR
SLOTS = BPD * YBLOCKS
MOST = 12
GROUP = 8
PEERS = 2 * GROUP
X_LANES = EXTRA // 2

entropy_weight = 0.05
scale = math.log2(math.e) / entropy_weight
log_two = math.log(2.0)
lowest = -1e30
exponent_room = 112.0
mebi = 1024 * 1024

f32 = jnp.float32
bf16 = jnp.bfloat16
i32 = jnp.int32

SMEM = pl.BlockSpec(memory_space=pltpu.SMEM)
ANY = pl.BlockSpec(memory_space=pl.ANY)
VMEM = pl.BlockSpec(memory_space=pltpu.VMEM)
HBM = pl.BlockSpec(memory_space=pltpu.HBM)


def iota(shape, dim):
    return lax.broadcasted_iota(i32, shape, dim)


def dot(a, b):
    return jnp.dot(a, b, preferred_element_type=f32)


def nt_dot(a, b):
    return lax.dot_general(a, b, (((1,), (1,)), ((), ())), preferred_element_type=f32)


def ones_where(mask):
    return jnp.where(mask, 1.0, 0.0).astype(bf16)


def params():
    return pltpu.CompilerParams(vmem_limit_bytes=64 * mebi)


def whole(shape):
    return pl.BlockSpec(shape, lambda *t: (0,) * len(shape))


def laid_out(square):
    return jnp.concatenate([square[n : n + 1, :] for n in range(square.shape[0])], axis=1)


def down(row):
    parts = [jnp.broadcast_to(row[:, c : c + 128], (128, 128)).T for c in range(0, row.shape[1], 128)]
    return jnp.concatenate(parts, axis=0)


def moved(values, place):
    high = iota((16, LOCAL), 0) == lax.shift_right_logical(place, 7)
    low = ones_where(iota((128, LOCAL), 0) == jnp.bitwise_and(place, 127))
    stack = jnp.concatenate([jnp.where(high, v, 0.0) for v in values], axis=0).astype(bf16)
    out = nt_dot(stack, low)
    return [laid_out(out[16 * n : 16 * n + 16, :]) for n in range(len(values))]


def moved_exact(value, place):
    first = value.astype(bf16).astype(f32)
    second = (value - first).astype(bf16).astype(f32)
    parts = moved([first, second, value - first - second], place)
    return parts[0] + parts[1] + parts[2]


def before_matrix():
    return ones_where(iota((128, 128), 0) < iota((128, 128), 1))


def plan(order, start, devices, first_lane):
    share = LOCAL // devices
    target = lax.shift_right_logical(order, 11)
    hit = iota((devices, LOCAL), 0) == target
    hot = ones_where(hit)
    before = before_matrix()
    every = jnp.ones((128, 128), bf16)
    seen = jnp.zeros((devices, 128), f32)
    earlier = []
    for c in range(0, LOCAL, 128):
        piece = hot[:, c : c + 128]
        earlier.append(dot(piece, before) + seen)
        seen = seen + dot(piece, every)
    earlier = jnp.concatenate(earlier, axis=1)
    rank = jnp.sum(jnp.where(hit, earlier, 0.0), axis=0, keepdims=True).astype(i32)
    within = jnp.bitwise_and(order, LOCAL - 1)
    high = lax.shift_right_logical(within, 6).astype(f32)
    low = jnp.bitwise_and(within, 63).astype(f32)
    row = iota((EXTRA, LOCAL), 0) - first_lane
    field = row // share
    value = jnp.where(field == 0, high, jnp.where(field == 1, low, start))
    mine = (row >= 0) & (row < 3 * share) & (row % share == rank)
    return target * share + rank, nt_dot(hot, jnp.where(mine, value, 0.0).astype(bf16))


def partner_offsets(me):
    kind = jnp.bitwise_and(me, 3)
    out = []
    for k in range(FAR):
        value = jnp.int32(ROUNDS[0][k])
        for n in range(1, 4):
            value = jnp.where(kind == n, jnp.int32(ROUNDS[n][k]), value)
        out.append(value)
    return out


def pack_y_kernel(
    me_ref, partners_ref, counts_ref, y_order, x_order, y_start, x_start, points, out_ref, x_pos_ref, pos_ref, table_ref,
    *, devices
):
    step = pl.program_id(0)
    share = LOCAL // devices

    @pl.when(step == 0)
    def _():
        y_pos, y_table = plan(y_order[...], y_start[...].astype(f32).reshape(1, LOCAL), devices, 0)
        x_pos, x_table = plan(x_order[...], x_start[...].astype(f32).reshape(1, LOCAL), devices, X_LANES)
        pos_ref[...] = y_pos
        x_pos_ref[...] = x_pos
        me = me_ref[0]
        offsets = partner_offsets(me)
        need = [jnp.int32(0)] * FAR
        for b in range(BPD):
            for s in range(partners_ref.shape[1]):
                block = partners_ref[b, s]
                away = lax.shift_right_logical(block, 1) - me
                for k in range(FAR):
                    listed = (s < counts_ref[b]) & (away == offsets[k])
                    need[k] = jnp.where(listed, jnp.bitwise_and(block, 1), need[k])
        table = y_table + x_table
        row, lane = iota(table.shape, 0), iota(table.shape, 1)
        for k in range(FAR):
            table = jnp.where((row == me + offsets[k]) & (lane == 3 * share), need[k].astype(f32), table)
        table_ref[...] = table

    base = step * CHUNK
    hot = ones_where(iota((CHUNK, LOCAL), 0) + base == pos_ref[...])
    out_ref[:, :DIM] = dot(hot, points[...]).astype(bf16)
    some = CHUNK // share
    table = table_ref[pl.ds(pl.multiple_of(step * some, some), some), :]
    out_ref[:, DIM:] = jnp.broadcast_to(table[:, None, :], (some, share, EXTRA)).reshape(CHUNK, EXTRA).astype(bf16)


def pack_y(me, partners, counts, y_order, x_order, y_start, x_start, points, devices):
    row = whole((1, LOCAL))
    return pl.pallas_call(
        functools.partial(pack_y_kernel, devices=devices),
        grid=(LOCAL // CHUNK,),
        in_specs=[SMEM, SMEM, SMEM, row, row, whole((LOCAL,)), whole((LOCAL,)), whole((LOCAL, DIM))],
        out_specs=[pl.BlockSpec((CHUNK, WIDE), lambda t: (t, 0)), row],
        out_shape=[pltpu.HBM((LOCAL, WIDE), bf16), jax.ShapeDtypeStruct((1, LOCAL), i32)],
        scratch_shapes=[pltpu.VMEM((1, LOCAL), i32), pltpu.VMEM((devices, EXTRA), f32)],
        compiler_params=params(),
        name="pack_y",
    )(me, partners, counts, y_order, x_order, y_start, x_start, points)


def pack_x_kernel(pos_ref, points_ref, out_ref):
    base = pl.program_id(0) * CHUNK
    hot = ones_where(iota((CHUNK, LOCAL), 0) + base == pos_ref[...])
    out_ref[...] = dot(hot, points_ref[...]).astype(bf16)


def pack_x(pos, points):
    return pl.pallas_call(
        pack_x_kernel,
        grid=(LOCAL // CHUNK,),
        in_specs=[whole((1, LOCAL)), whole((LOCAL, DIM))],
        out_specs=pl.BlockSpec((CHUNK, DIM), lambda t: (t, 0)),
        out_shape=pltpu.HBM((LOCAL, DIM), bf16),
        compiler_params=params(),
        name="pack_x",
    )(pos, points)


WINDOW = PART + 16
HELD = BS + WINDOW + 16


def arrived(table, base, with_low):
    share = 16
    row, lane = iota((EXTRA, EXTRA), 0), iota((EXTRA, EXTRA), 1)
    pick = jnp.where(row == base + lane % share, 64.0 if with_low else 1.0, 0.0)
    if with_low:
        pick = jnp.where(row == base + share + lane % share, 1.0, pick)
    values = dot(table, pick.astype(bf16))
    values = jnp.where(row % (EXTRA // share) == lane // share, values, 0.0)
    return jnp.sum(values.reshape(LOCAL // 128, EXTRA // share, 128), axis=1)


def unpack_y_kernel(me_ref, came_ref, rows_ref, table_ref, own_ref, *rest, devices):
    sends = rest[:FAR]
    held, sems, own_sem, points_buf, extra_buf, in_sems = rest[FAR:]
    share = LOCAL // devices
    me = me_ref[0]
    extra_in = pltpu.make_async_copy(came_ref.at[:, pl.ds(DIM, EXTRA)], extra_buf, in_sems.at[0])
    points_in = pltpu.make_async_copy(came_ref.at[:, pl.ds(0, DIM)], points_buf, in_sems.at[1])
    extra_in.start()
    points_in.start()
    extra_in.wait()
    table = dot(ones_where(iota((devices, LOCAL), 1) == iota((devices, LOCAL), 0) * share), extra_buf[...])
    table_ref[...] = table
    place_square = arrived(table.astype(bf16), 0, True)
    place = laid_out(place_square)
    start = laid_out(arrived(table.astype(bf16), 2 * share, False))

    picks = []
    offsets = partner_offsets(me)
    small_row, small_lane = iota((devices, EXTRA), 0), iota((devices, EXTRA), 1)
    for k in range(FAR):
        here = (small_row == me + offsets[k]) & (small_lane == 3 * share)
        picks.append(jnp.sum(jnp.where(here, table, 0.0)) > 0.5)

    second = place >= float(BS)
    square = ones_where(place_square >= float(BS))
    totals = dot(square, jnp.ones((128, 128), bf16)).astype(bf16)
    earlier = dot(square, before_matrix()) + dot(ones_where(iota((16, 16), 1) < iota((16, 16), 0)), totals)
    ones_before = laid_out(earlier)
    dest = jnp.where(second, ones_before, iota((1, LOCAL), 1).astype(f32) - ones_before).astype(i32)
    seat = jnp.where(second, dest + BS, dest)
    position = place.astype(i32)
    start_row, high_row, low_row = moved(
        [start, lax.shift_right_logical(position, 6).astype(f32), jnp.bitwise_and(position, 63).astype(f32)], seat
    )
    rows_ref[0:1, :] = start_row
    rows_ref[2:3, :] = high_row * 64.0 + low_row
    rows_ref[3:8, :] = jnp.zeros((5, LOCAL), f32)
    sixteen, lane16 = iota((16, 128), 0), iota((16, 128), 1)
    points_in.wait()

    for j in range(BPD):
        held[j, 0:16, :] = jnp.zeros((16, DIM), bf16)
        here = jnp.where(second if j else jnp.logical_not(second), dest, -1)
        for c in range(LOCAL // PART):
            span = slice(c * PART, (c + 1) * PART)
            begin = jnp.sum(jnp.where((sixteen == c * PART // 128) & (lane16 == 0), earlier, 0.0)).astype(i32)
            if j == 0:
                begin = c * PART - begin
            begin = pl.multiple_of(lax.shift_left(lax.shift_right_logical(begin, 4), 4), 16)
            hot = ones_where(iota((WINDOW, PART), 0) + begin == here[:, span])
            part = dot(hot, points_buf[span, :]).astype(bf16)
            first = pl.ds(begin, 16)
            held[j, first, :] = held[j, first, :] + part[0:16, :]
            held[j, pl.ds(pl.multiple_of(begin + 16, 16), PART), :] = part[16:, :]
        half = []
        for c in range(0, BS, PART):
            points = held[j, c : c + PART, :].astype(f32)
            total = 0.5 * jnp.sum(points * points, axis=1, keepdims=True)
            half.append(jnp.broadcast_to(total, (PART, 128)).T[0:1, :])
        half = jnp.concatenate(half, axis=1)
        block = slice(j * BS, (j + 1) * BS)
        rows_ref[1:2, block] = half
        beta = start_row[:, block] - half
        first = beta.astype(bf16).astype(f32)
        next_part = (beta - first).astype(bf16).astype(f32)
        most = jnp.max(half, axis=1, keepdims=True) * 1.01
        sub = iota((TAIL, DIM), 0)
        tail = jnp.zeros((TAIL, DIM), f32) + most
        for n, piece in enumerate((first, next_part, beta - first - next_part)):
            tail = jnp.where(sub == 2 * n, piece[:, :DIM], tail)
            tail = jnp.where(sub == 2 * n + 1, piece[:, DIM:], tail)
        held[j, BS:ROWS, :] = tail.astype(bf16)
        done = held.at[j, pl.ds(0, ROWS), :]
        for k in range(FAR):
            wanted = picks[k] if j == 1 else jnp.logical_not(picks[k])

            @pl.when(wanted)
            def _():
                pltpu.make_async_copy(done, sends[k], sems.at[k]).start()

        pltpu.make_async_copy(done, own_ref.at[j], own_sem.at[j]).start()

    done = held.at[0, pl.ds(0, ROWS), :]
    for k in range(FAR):
        pltpu.make_async_copy(done, sends[k], sems.at[k]).wait()
    for j in range(BPD):
        pltpu.make_async_copy(done, own_ref.at[j], own_sem.at[j]).wait()


def unpack_y(me, came, devices):
    return pl.pallas_call(
        functools.partial(unpack_y_kernel, devices=devices),
        in_specs=[SMEM, ANY],
        out_specs=[VMEM, VMEM] + [HBM] * (1 + FAR),
        out_shape=[
            jax.ShapeDtypeStruct((8, LOCAL), f32),
            jax.ShapeDtypeStruct((devices, EXTRA), f32),
            pltpu.HBM((BPD, ROWS, DIM), bf16),
        ]
        + [pltpu.HBM((ROWS, DIM), bf16)] * FAR,
        scratch_shapes=[
            pltpu.VMEM((BPD, HELD, DIM), bf16),
            pltpu.SemaphoreType.DMA((FAR,)),
            pltpu.SemaphoreType.DMA((BPD,)),
            pltpu.VMEM((LOCAL, DIM), bf16),
            pltpu.VMEM((LOCAL, EXTRA), bf16),
            pltpu.SemaphoreType.DMA((2,)),
        ],
        compiler_params=params(),
        name="unpack_y",
    )(me, came)


def unpack_x_kernel(
    me_ref, peer_ref, came_ref, table_ref, points_ref, alpha_ref, rows_ref, who_ref, place_ref, start_ref, *, devices
):
    step = pl.program_id(0)

    @pl.when(step == 0)
    def _():
        table = table_ref[...].astype(bf16)
        place = laid_out(arrived(table, X_LANES, True)).astype(i32)
        place_ref[...] = place
        start_ref[...] = moved([laid_out(arrived(table, X_LANES + 32, False))], place)[0]
        row, lane = iota((EXTRA, EXTRA), 0), iota((EXTRA, EXTRA), 1)
        for n in range(PEERS):
            peer = me_ref[0] + peer_ref[n]
            wants = jnp.sum(jnp.where((row == peer) & (lane == 3 * LOCAL // devices), table_ref[...], 0.0)) > 0.5
            valid = (peer_ref[n] != 0) & (peer >= 0) & (peer < devices)
            who_ref[n] = jnp.where(valid, jnp.where(wants, 1, 0), -1)

    base = step * CHUNK
    hot = ones_where(iota((CHUNK, LOCAL), 0) + base == place_ref[...])
    points = dot(hot, came_ref[...])
    points_ref[...] = points.astype(bf16)
    half = jnp.broadcast_to(0.5 * jnp.sum(points * points, axis=1, keepdims=True), (CHUNK, 128))
    start = start_ref[:, pl.ds(pl.multiple_of(base, CHUNK), CHUNK)]
    alpha_ref[...] = (down(start) - half) * scale
    rows_ref[0:1, :] = start
    rows_ref[1:8, :] = jnp.concatenate([half[c : c + 128, :].T[0:7, :] for c in range(0, CHUNK, 128)], axis=1)


def unpack_x(me, peer_offsets, came, table, devices):
    return pl.pallas_call(
        functools.partial(unpack_x_kernel, devices=devices),
        grid=(LOCAL // CHUNK,),
        in_specs=[SMEM, SMEM, whole((LOCAL, DIM)), whole((EXTRA, EXTRA))],
        out_specs=[
            pl.BlockSpec((CHUNK, DIM), lambda t: (t, 0)),
            pl.BlockSpec((CHUNK, 128), lambda t: (t, 0)),
            pl.BlockSpec((8, CHUNK), lambda t: (0, t)),
            SMEM,
        ],
        out_shape=[
            pltpu.HBM((LOCAL, DIM), bf16),
            pltpu.HBM((LOCAL, 128), f32),
            jax.ShapeDtypeStruct((8, LOCAL), f32),
            jax.ShapeDtypeStruct((PEERS,), i32),
        ],
        scratch_shapes=[pltpu.VMEM((1, LOCAL), i32), pltpu.VMEM((1, LOCAL), f32)],
        compiler_params=params(),
        name="unpack_x",
    )(me, peer_offsets, came, table)


def merge(top, total, other_top, other_total):
    new = jnp.maximum(top, other_top)
    return new, total * jnp.exp2(top - new) + other_total * jnp.exp2(other_top - new)


def logs(top, total):
    return jnp.where(total > 0.0, top + jnp.log2(total), lowest)


def high_of(row):
    return jnp.max(row, axis=1, keepdims=True)


def low_of(row):
    return jnp.min(row, axis=1, keepdims=True)


def put_cols(col_ref, y, part_top, part_total):
    top, total = merge(col_ref[y, 0:1, :], col_ref[y, 1:2, :], part_top, part_total)
    col_ref[y, 0:1, :] = top
    col_ref[y, 1:2, :] = total


def clear_cols(col_ref):
    col_ref[:, 0:1, :] = jnp.full((col_ref.shape[0], 1, BS), lowest, f32)
    col_ref[:, 1:2, :] = jnp.zeros((col_ref.shape[0], 1, BS), f32)


def shifted_rows(x_ref, y_ref, beta, part_ref):
    def body(c, carry):
        span = pl.ds(pl.multiple_of(c * PART, PART), PART)
        terms = nt_dot(x_ref[span, :], y_ref[0:BS, :]) * scale + beta
        top = jnp.max(terms, axis=1, keepdims=True)
        total = jnp.sum(jnp.exp2(terms - top), axis=1, keepdims=True)
        part_ref[span, :] = jnp.where(iota((PART, 128), 1) == 0, top, total)
        return carry

    lax.fori_loop(0, BS // PART, body, 0)


def shifted_cols(x_ref, y_ref, alpha_ref, col_ref, y):
    def body(c, carry):
        span = pl.ds(pl.multiple_of(c * PART, PART), PART)
        terms = nt_dot(x_ref[span, :], y_ref[0:BS, :]) * scale + alpha_ref[span, 0:1]
        top = jnp.max(terms, axis=0, keepdims=True)
        put_cols(col_ref, y, top, jnp.sum(jnp.exp2(terms - top), axis=0, keepdims=True))
        return carry

    lax.fori_loop(0, BS // PART, body, 0)


def add_part(part_ref, state_ref, b):
    for c in range(0, BS, 128):
        part = part_ref[c : c + 128, :].T
        span = pl.ds(pl.multiple_of(b * BS + c, 128), 128)
        top, total = merge(state_ref[0:1, span], state_ref[1:2, span], part[0:1, :], part[1:2, :])
        state_ref[0:1, span] = top
        state_ref[1:2, span] = total


def lane_sums(refs):
    out = []
    for c in range(0, LOCAL, 128):
        part = refs[0][c : c + 128, :]
        for ref in refs[1:]:
            part = part + ref[c : c + 128, :]
        out.append(jnp.sum(part.T, axis=0, keepdims=True))
    return jnp.concatenate(out, axis=1)


def fold(values):
    return jnp.sum(values.reshape(values.shape[0] // 8, 8, 128), axis=0)


def own_beta(y_rows_ref):
    return (y_rows_ref[0:1, :] - y_rows_ref[1:2, :]) * scale


def sweep_kernel(*refs, base, count, first, sends, more):
    use_ref, seat_of_ref, x_ref, alpha_ref = refs[:4]
    refs = refs[4:]
    if first:
        x_rows_ref, y_rows_ref = refs[:2]
        refs = refs[2:]
    else:
        cols_in, left_in, stat_in = refs[:3]
        refs = refs[5:]
    if sends is not None:
        peers_ref = refs[0]
        refs = refs[1:]
    if more:
        acc_in = refs[0]
        refs = refs[1:]
    y_refs = refs[:1] if first else refs[:count]
    refs = refs[len(y_refs) :]
    acc_ref, cols_ref, left_ref, stat_ref, kept_ref, slow_ref = refs[:6]
    refs = refs[6:]
    if sends is not None:
        group_out = refs[0]
        refs = refs[1:]
    x_buf, alpha_buf, x_sems, y_buf, sems, col_ref, weight_ref, part_ref, beta_ref, fit_ref, room_ref, tiles, tile_sems, tile_count = refs

    def copy(n):
        source = y_refs[0].at[n] if first else y_refs[n]
        return pltpu.make_async_copy(source, y_buf.at[n % 2], sems.at[n % 2])

    def x_copies(n):
        rows = pl.ds(n * BS, BS)
        return (
            pltpu.make_async_copy(x_ref.at[rows, :], x_buf.at[rows, :], x_sems.at[n, 0]),
            pltpu.make_async_copy(alpha_ref.at[rows, :], alpha_buf.at[rows, :], x_sems.at[n, 1]),
        )

    copy(0).start()
    for part in x_copies(0):
        part.start()
    tile_count[0] = 0
    acc_ref[...] = acc_in[...] if more else jnp.zeros((LOCAL, 128), f32)

    def tile_copy(at, seat):
        return pltpu.make_async_copy(tiles.at[at], kept_ref.at[seat], tile_sems.at[at])

    def part_copy(at, seat, c):
        rows = pl.ds(c, PART)
        return pltpu.make_async_copy(tiles.at[at, rows, :], kept_ref.at[seat, rows, :], tile_sems.at[at])

    if first:
        for n in range(SLOTS):
            left_ref[n] = -1.0
        alpha = (x_rows_ref[0:1, :] - x_rows_ref[1:2, :]) * scale
        alpha_top = high_of(alpha)
        lane = iota((8, 128), 1)
        beta_top = high_of(own_beta(y_rows_ref))
        most = high_of(x_rows_ref[1:2, :]) * 1.01
        spread = alpha_top - low_of(alpha)
        stat_ref[...] = jnp.where(
            lane == 0, alpha_top, jnp.where(lane == 1, spread, jnp.where(lane == 2, most, beta_top))
        )
    else:
        for n in range(SLOTS):
            left_ref[n] = left_in[n]
        cols_ref[...] = cols_in[...]
        stat_ref[...] = stat_in[...]

    def body(step, carry):
        y, b = step // BPD, step % BPD
        slot = base * BPD + step
        for n in range(count):

            @pl.when(step == BPD * n)
            def _():
                copy(n).wait()
                if n + 1 < count:
                    copy(n + 1).start()

        for n in range(BPD):

            @pl.when(step == n)
            def _():
                for part in x_copies(n):
                    part.wait()
                if n + 1 < BPD:
                    for part in x_copies(n + 1):
                        part.start()
                rows = slice(n * BS, (n + 1) * BS)
                weight_ref[rows, :] = jnp.exp2(alpha_buf[rows, :] - stat_ref[0:1, 0:1])

        now = y_buf.at[y % 2]
        rows_from = b * BS

        @pl.when(b == 0)
        def _():
            clear_cols(col_ref)
            tail = now[BS:ROWS, :].astype(f32)
            halves = [tail[n : n + 1, :] + tail[n + 2 : n + 3, :] + tail[n + 4 : n + 5, :] for n in range(2)]
            beta = jnp.concatenate(halves, axis=1) * scale
            shift = stat_ref[0:1, 3:4]
            left = exponent_room - 2.0 * scale * jnp.sqrt(tail[6:7, 0:1] * stat_ref[0:1, 2:3])
            reach = jnp.maximum(stat_ref[0:1, 1:2], jnp.maximum(high_of(beta) - shift, shift - low_of(beta)))
            beta_ref[0:1, :] = beta
            beta_ref[1:2, :] = jnp.exp2(beta - shift)
            room_ref[0] = left[0, 0]
            fit_ref[0] = jnp.where((left - reach)[0, 0] >= 0.0, 1, 0)

        @pl.when(use_ref[slot] > 0)
        def _():
            fits = fit_ref[0] > 0

            @pl.when(fits)
            def _():
                left_ref[slot] = room_ref[0]
                done = tile_count[0]
                tile_count[0] = done + 1
                at = done % 2

                @pl.when(done > 1)
                def _():
                    tile_copy(at, 0).wait()

                weight = beta_ref[1:2, :]
                sums = jnp.zeros((8, BS), f32)
                for c in range(0, BS, PART):
                    span = pl.ds(pl.multiple_of(rows_from + c, PART), PART)
                    terms = jnp.exp2(nt_dot(x_buf[span, :], now[0:BS, :]) * scale)
                    tiles[at, c : c + PART, :] = terms.astype(bf16)
                    part_copy(at, seat_of_ref[slot], c).start()
                    row_part = acc_ref[span, :]
                    col_parts = []
                    for n in range(0, BS, 128):
                        piece = terms[:, n : n + 128]
                        row_part = row_part + piece * weight[:, n : n + 128]
                        col_parts.append(fold(piece * weight_ref[span, :]))
                    acc_ref[span, :] = row_part
                    sums = sums + jnp.concatenate(col_parts, axis=1)
                put_cols(col_ref, 0, stat_ref[0:1, 0:1], jnp.sum(sums, axis=0, keepdims=True))

            @pl.when(jnp.logical_not(fits))
            def _():
                block = pl.ds(pl.multiple_of(rows_from, BS), BS)
                shifted_rows(x_buf.at[block, :], now, beta_ref[0:1, :], part_ref)
                out = pltpu.make_async_copy(part_ref, slow_ref.at[slot], sems.at[2])
                out.start()
                shifted_cols(x_buf.at[block, :], now, alpha_buf.at[block, :], col_ref, 0)
                out.wait()

        @pl.when(b == BPD - 1)
        def _():
            cols_ref[base + y] = logs(col_ref[0, 0:1, :], col_ref[0, 1:2, :])

        return carry

    lax.fori_loop(0, BPD * count, body, 0)
    for n in range(2):

        @pl.when(tile_count[0] > n)
        def _():
            tile_copy(n, 0).wait()

    if sends is not None:
        for n in range(GROUP):
            group_out[n] = outgoing(cols_ref, peers_ref[sends * GROUP + n])


def outgoing(cols_ref, index):
    return jnp.where(index < 0, lowest, cols_ref[jnp.maximum(index, 0)])


def sweep(common, y_list, base, carried, rows=None, peers=None, sends=None, acc=None):
    first = carried is None
    count = BPD if first else len(y_list)
    in_specs = [SMEM, SMEM, HBM, HBM]
    operands = list(common)
    aliases = {}
    if first:
        in_specs += [VMEM, VMEM]
        operands += rows
    else:
        in_specs += [VMEM, SMEM, VMEM, HBM, HBM]
        operands += list(carried)
        aliases = {7: 4, 8: 5}
    if sends is not None:
        in_specs.append(SMEM)
        operands.append(peers)
    if acc is not None:
        in_specs.append(VMEM)
        operands.append(acc)
    in_specs += [ANY] * len(y_list)
    operands += y_list
    out_specs = [VMEM, VMEM, SMEM, VMEM, HBM, HBM]
    out_shape = [
        jax.ShapeDtypeStruct((LOCAL, 128), f32),
        jax.ShapeDtypeStruct((YBLOCKS, 1, BS), f32),
        jax.ShapeDtypeStruct((SLOTS,), f32),
        jax.ShapeDtypeStruct((8, 128), f32),
        pltpu.HBM((MOST, BS, BS), bf16),
        pltpu.HBM((SLOTS, BS, 128), f32),
    ]
    if sends is not None:
        out_specs.append(VMEM)
        out_shape.append(jax.ShapeDtypeStruct((GROUP, 1, BS), f32))
    return pl.pallas_call(
        functools.partial(sweep_kernel, base=base, count=count, first=first, sends=sends, more=acc is not None),
        in_specs=in_specs,
        out_specs=out_specs,
        out_shape=out_shape,
        scratch_shapes=[
            pltpu.VMEM((LOCAL, DIM), bf16),
            pltpu.VMEM((LOCAL, 128), f32),
            pltpu.SemaphoreType.DMA((BPD, 2)),
            pltpu.VMEM((2, ROWS, DIM), bf16),
            pltpu.SemaphoreType.DMA((3,)),
            pltpu.VMEM((1, 8, BS), f32),
            pltpu.VMEM((LOCAL, 128), f32),
            pltpu.VMEM((BS, 128), f32),
            pltpu.VMEM((8, BS), f32),
            pltpu.SMEM((1,), i32),
            pltpu.SMEM((1,), f32),
            pltpu.VMEM((2, BS, BS), bf16),
            pltpu.SemaphoreType.DMA((2,)),
            pltpu.SMEM((1,), i32),
        ],
        input_output_aliases=aliases,
        compiler_params=params(),
        name=f"sweep_{base}",
    )(*operands)


def load_pair(slot, x_ref, y_refs, x_buf, y_buf, sems):
    rows = pl.ds(pl.multiple_of((slot % BPD) * BS, BS), BS)
    fetch = pltpu.make_async_copy(x_ref.at[rows, :], x_buf, sems.at[0])
    fetch.start()
    fetch.wait()
    for n in range(YBLOCKS):

        @pl.when(slot // BPD == n)
        def _():
            source = y_refs[0].at[n] if n < BPD else y_refs[n - BPD + 1]
            fetch = pltpu.make_async_copy(source, y_buf, sems.at[1])
            fetch.start()
            fetch.wait()


def next_potential(now, half, total, log_count):
    return 0.5 * (now + half + entropy_weight * (log_count - log_two * total))


def fetch_terms(kept_ref, terms_ref, sems, list_ref, seat_of_ref, start, stop):
    def term_copy(n):
        return pltpu.make_async_copy(kept_ref.at[seat_of_ref[list_ref[n]]], terms_ref.at[n], sems.at[n])

    for n in range(MOST):

        @pl.when((n >= start) & (n < stop))
        def _():
            term_copy(n).start()

    return term_copy


def columns_kernel(list_ref, live_ref, seat_of_ref, use_ref, left_ref, *refs, log_count, accs):
    start, stop = 0, live_ref[2]
    acc_refs = refs[:accs]
    x_rows_ref, y_rows_ref, kept_ref, slow_ref, x_ref = refs[accs : accs + 5]
    y_refs = refs[accs + 5 : accs + 6 + FAR]
    next_ref, out_ref, col_ref, weight_ref, state_ref, part_ref, x_buf, y_buf, sems, terms_ref, term_sems = refs[accs + 6 + FAR :]
    term_copy = fetch_terms(kept_ref, terms_ref, term_sems, list_ref, seat_of_ref, start, stop)
    clear_cols(col_ref)
    total = lane_sums(acc_refs)
    state_ref[0:1, :] = jnp.where(total > 0.0, high_of(own_beta(y_rows_ref)), lowest)
    state_ref[1:2, :] = total
    for n in range(SLOTS):

        @pl.when((use_ref[n] > 0) & (left_ref[n] < 0.0))
        def _():
            fetch = pltpu.make_async_copy(slow_ref.at[n], part_ref, sems.at[0])
            fetch.start()
            fetch.wait()
            add_part(part_ref, state_ref, n % BPD)

    half = x_rows_ref[1:2, :]
    f_next = next_potential(x_rows_ref[0:1, :], half, logs(state_ref[0:1, :], state_ref[1:2, :]), log_count)
    next_ref[0:1, :] = f_next
    next_ref[1:2, :] = half
    next_ref[2:8, :] = jnp.zeros((6, LOCAL), f32)
    alpha = (f_next - half) * scale
    state_ref[2:3, :] = alpha
    top = high_of(alpha)
    weight_ref[...] = down(jnp.exp2(alpha - top))
    reach = (top - low_of(alpha))[0, 0]

    def body(step, carry):
        slot = list_ref[step]
        y, b = slot // BPD, slot % BPD
        fits = reach <= left_ref[slot]
        term_copy(step).wait()

        @pl.when(fits)
        def _():
            sums = jnp.zeros((8, BS), f32)
            for c in range(0, BS, 64):
                weight = weight_ref[pl.ds(pl.multiple_of(b * BS + c, 64), 64), :]
                parts = [fold(terms_ref[step, c : c + 64, n : n + 128].astype(f32) * weight) for n in range(0, BS, 128)]
                sums = sums + jnp.concatenate(parts, axis=1)
            put_cols(col_ref, y, top, jnp.sum(sums, axis=0, keepdims=True))

        @pl.when(jnp.logical_not(fits))
        def _():
            load_pair(slot, x_ref, y_refs, x_buf, y_buf, sems)
            for c in range(0, BS, 128):
                row = state_ref[2:3, pl.ds(pl.multiple_of(b * BS + c, 128), 128)]
                part_ref[c : c + 128, :] = jnp.broadcast_to(row, (128, 128)).T
            shifted_cols(x_buf, y_buf, part_ref, col_ref, y)

        return carry

    lax.fori_loop(start, stop, body, 0)
    for n in range(YBLOCKS):
        out_ref[n] = logs(col_ref[n, 0:1, :], col_ref[n, 1:2, :])


def gathered(j, own_ref, came, who_ref):
    terms = [own_ref[j]] + [jnp.where(who_ref[n] == j, came(n), lowest) for n in range(PEERS)]
    top = terms[0]
    for term in terms[1:]:
        top = jnp.maximum(top, term)
    total = jnp.exp2(terms[0] - top)
    for term in terms[1:]:
        total = total + jnp.exp2(term - top)
    return top + jnp.log2(total)


def home_kernel(who_ref, peers_ref, even_in, odd_in, first_ref, second_ref, y_rows_ref, even_out, odd_out, g_ref, *, log_count):
    came = lambda n: (even_in, odd_in)[n // GROUP][n % GROUP]
    betas = []
    for j in range(BPD):
        span = slice(j * BS, (j + 1) * BS)
        half = y_rows_ref[1:2, span]
        g_next = next_potential(y_rows_ref[0:1, span], half, gathered(j, first_ref, came, who_ref), log_count)
        g_ref[0:1, span] = g_next
        betas.append((g_next - half) * scale)
        g_ref[1:2, span] = betas[j]
    g_ref[2:8, :] = jnp.zeros((6, LOCAL), f32)
    for n in range(PEERS):
        out = (even_out, odd_out)[n // GROUP]
        out[n % GROUP, 0:1, :] = jnp.where(who_ref[n] == 1, betas[1], betas[0])
        out[n % GROUP, 1:2, :] = outgoing(second_ref, peers_ref[n])


def home(who, peers, rows_in, first, second, y_rows, log_count):
    return pl.pallas_call(
        functools.partial(home_kernel, log_count=log_count),
        in_specs=[SMEM, SMEM] + [VMEM] * 5,
        out_specs=[VMEM] * 3,
        out_shape=[jax.ShapeDtypeStruct((GROUP, 2, BS), f32)] * 2 + [jax.ShapeDtypeStruct((8, LOCAL), f32)],
        compiler_params=params(),
        name="home",
    )(who, peers, *rows_in, first, second, y_rows)


def rows_kernel(list_ref, live_ref, seat_of_ref, use_ref, left_ref, *refs, log_count, phase):
    last = phase == 2
    start = live_ref[phase - 1] if phase else 0
    stop = live_ref[phase]
    if last:
        from_ref, who_ref, acc_in, state_in, even_in, odd_in, g_ref, second_ref, y_rows_ref, x_rows_ref = refs[:10]
        refs = refs[10:]
    elif phase:
        from_ref, acc_in, state_in, even_in, g_ref = refs[:5]
        refs = refs[5:]
    else:
        g_ref = refs[0]
        refs = refs[1:]
    kept_ref, slow_ref, x_ref = refs[:3]
    y_refs = refs[3 : 4 + FAR]
    refs = refs[4 + FAR :]
    if last:
        f_ref, g_out_ref, acc_ref, state_ref = refs[:4]
        refs = refs[4:]
    else:
        acc_ref, state_ref = refs[:2]
        refs = refs[2:]
    beta_ref, weight_ref, part_ref, x_buf, y_buf, sems, terms_ref, term_sems = refs
    term_copy = fetch_terms(kept_ref, terms_ref, term_sems, list_ref, seat_of_ref, start, stop)
    shift = high_of(g_ref[1:2, :])
    if phase:
        acc_ref[...] = acc_in[...]
        state_ref[...] = state_in[...]
    else:
        acc_ref[...] = jnp.zeros((LOCAL, 128), f32)
        state_ref[0:1, :] = jnp.full((1, LOCAL), lowest, f32)
        state_ref[1:8, :] = jnp.zeros((7, LOCAL), f32)
    for n in range(BPD):
        beta_ref[n] = g_ref[1:2, n * BS : (n + 1) * BS]
    for n in range(BPD, YBLOCKS if phase else BPD):
        at = from_ref[n] % GROUP
        if last:
            beta_ref[n] = jnp.where(from_ref[n] < GROUP, even_in[at, 0:1, :], odd_in[at, 0:1, :])
        else:
            beta_ref[n] = even_in[at, 0:1, :]
    some = YBLOCKS if phase else BPD
    weight_ref[0:some] = jnp.exp2(beta_ref[0:some] - shift)

    def body(step, carry):
        slot = list_ref[step]
        y, b = slot // BPD, slot % BPD
        beta = beta_ref[y]
        reach = jnp.maximum(high_of(beta) - shift, shift - low_of(beta))
        fits = reach[0, 0] <= left_ref[slot]
        term_copy(step).wait()

        @pl.when(fits)
        def _():
            weight = weight_ref[y]
            for c in range(0, BS, 64):
                span = pl.ds(pl.multiple_of(b * BS + c, 64), 64)
                part = acc_ref[span, :]
                for n in range(0, BS, 128):
                    part = part + terms_ref[step, c : c + 64, n : n + 128].astype(f32) * weight[:, n : n + 128]
                acc_ref[span, :] = part

        @pl.when(jnp.logical_not(fits))
        def _():
            load_pair(slot, x_ref, y_refs, x_buf, y_buf, sems)
            shifted_rows(x_buf, y_buf, beta, part_ref)
            add_part(part_ref, state_ref, b)

        return carry

    lax.fori_loop(start, stop, body, 0)
    if not last:
        return
    total = lane_sums([acc_ref])
    top = jnp.where(total > 0.0, shift, lowest)
    top, total = merge(top, total, state_ref[0:1, :], state_ref[1:2, :])
    f_ref[...] = next_potential(x_rows_ref[0:1, :], x_rows_ref[1:2, :], logs(top, total), log_count)
    came = lambda n: (even_in, odd_in)[n // GROUP][n % GROUP, 1:2, :]
    total = jnp.concatenate([gathered(j, second_ref, came, who_ref) for j in range(BPD)], axis=1)
    g_next = next_potential(g_ref[0:1, :], y_rows_ref[1:2, :], total, log_count)
    g_out_ref[...] = moved_exact(g_next, y_rows_ref[2:3, :].astype(i32))


def slots_call(kernel, smem, front, kept, slow, x_blocks, y_list, outs, scratch, name):
    return pl.pallas_call(
        kernel,
        in_specs=[SMEM] * len(smem) + [VMEM] * len(front) + [HBM, HBM, ANY] + [ANY] * len(y_list),
        out_specs=[VMEM] * len(outs),
        scratch_shapes=scratch
        + [
            pltpu.VMEM((BS, 128), f32),
            pltpu.VMEM((BS, DIM), bf16),
            pltpu.VMEM((ROWS, DIM), bf16),
            pltpu.SemaphoreType.DMA((2,)),
            pltpu.VMEM((MOST, BS, BS), bf16),
            pltpu.SemaphoreType.DMA((MOST,)),
        ],
        out_shape=outs,
        compiler_params=params(),
        name=name,
    )(*smem, *front, kept, slow, x_blocks, *y_list)


def seat_tables():
    half = GROUP // 2
    offsets = np.zeros((GROUP, PEERS), np.int32)
    source = np.zeros((GROUP, YBLOCKS), np.int32)
    for seat in range(GROUP):
        odd_seat = (seat + half) % GROUP
        for other in range(GROUP):
            if other != seat and abs(other - seat) <= REACH:
                offsets[seat, other] = other - seat
            off = other - odd_seat
            if off != 0 and abs(off) <= REACH and not 0 <= seat + off < GROUP:
                offsets[seat, GROUP + other] = off
        for k, off in enumerate(ROUNDS[seat % 4]):
            source[seat, BPD + k] = list(offsets[seat]).index(off)
    index = np.full((GROUP, PEERS), -1, np.int32)
    for seat in range(GROUP):
        for k, off in enumerate(ROUNDS[seat % 4]):
            index[seat, offsets[seat] == off] = BPD + k
    return offsets, index, source


def swap(rows, devices, shift):
    groups = [[(GROUP * k + j + shift) % devices for j in range(GROUP)] for k in range(devices // GROUP)]
    return lax.all_to_all(rows, "blk", split_axis=0, concat_axis=0, tiled=True, axis_index_groups=groups)


def on_device(x_points, y_points, x_start, y_start, x_order, y_order, partners, counts):
    devices = lax.axis_size("blk")
    me = lax.axis_index("blk").astype(i32)
    log_count = math.log(LOCAL * devices)
    here = me[None]
    line = lambda v: v.reshape(1, LOCAL)

    y_sent, x_pos = pack_y(here, partners, counts, line(y_order), line(x_order), y_start, x_start, y_points, devices)
    y_came = lax.all_to_all(y_sent, "blk", split_axis=0, concat_axis=0, tiled=True)
    offsets = lax.dynamic_slice(jnp.array(ROUNDS, i32), (me % 4, 0), (1, FAR))[0]
    live = jnp.arange(partners.shape[1], dtype=i32)[None, :] < counts[:, None]
    away = jnp.where(live, partners // BPD - me, devices)
    local_use = [((away == 0) & (partners % BPD == j)).any(axis=1) for j in range(BPD)]
    far = away[None, :, :] == offsets[:, None, None]
    use = jnp.concatenate([jnp.stack(local_use), far.any(axis=2)]).astype(i32).reshape(SLOTS)
    number = jnp.minimum(jnp.maximum(jnp.cumsum(use) - 1, 0), MOST - 1)

    peer_offsets, peer_index, peer_source = seat_tables()
    row = lambda t: lax.dynamic_slice(jnp.asarray(t), (me % GROUP, 0), (1, t.shape[1]))[0]
    peers, source, off = row(peer_index), row(peer_source), row(peer_offsets)

    far_slot = jnp.repeat(source >= GROUP, BPD).astype(i32)
    near = jnp.cumsum(use * (1 - far_slot))
    rank = jnp.where(far_slot > 0, near[-1] + jnp.cumsum(use * far_slot), near) - 1
    count = jnp.minimum(jnp.sum(use), MOST)
    step = jnp.minimum(jnp.arange(MOST, dtype=i32), count - 1)
    at = (rank[None, :] == step[:, None]) & (use[None, :] > 0)
    slots = jnp.sum(jnp.where(at, jnp.arange(SLOTS, dtype=i32)[None, :], 0), axis=1)
    own = jnp.sum(use[: BPD * BPD])
    live_counts = jnp.stack([own, jnp.minimum(near[-1], count), count])
    x_pos, use, number, slots, live_counts, peers, source, off = lax.optimization_barrier((x_pos, use, number, slots, live_counts, peers, source, off))
    x_sent = pack_x(x_pos, x_points)
    y_came, x_sent = lax.optimization_barrier((y_came, x_sent))
    x_came = lax.all_to_all(x_sent, "blk", split_axis=0, concat_axis=0, tiled=True)
    lists = [slots, live_counts, number]
    y_rows, table, y_own, *y_sends = unpack_y(here, y_came, devices)

    def far_block(k):
        pairs = [(i, i + ROUNDS[i % 4][k]) for i in range(devices) if 0 <= i + ROUNDS[i % 4][k] < devices]
        return lax.ppermute(y_sends[k], "blk", pairs)

    y_far = [far_block(k) for k in range(FAR - 1)]
    x_came, y_far[0], y_sends[5] = lax.optimization_barrier((x_came, y_far[0], y_sends[5]))
    y_far.append(far_block(5))
    x_blocks, alpha, x_rows, who = unpack_x(here, off, x_came, table, devices)


    common = (use, number, x_blocks, alpha)
    acc, *carried = sweep(common, [y_own], 0, None, [x_rows, y_rows])
    acc, *carried = sweep(common, y_far[:2], BPD, carried, acc=acc)
    acc, *carried = sweep(common, y_far[2:4], BPD + 2, carried, acc=acc)
    acc_2, *carried, odd_out = sweep(common, y_far[4:5], BPD + 4, carried, None, peers, 1)
    acc_3, cols_first, left, _, kept, slow, even_out = sweep(common, y_far[5:], BPD + 5, carried, None, peers, 0)
    y_all = [y_own] + y_far

    odd_in = swap(odd_out, devices, GROUP // 2)
    even_in = swap(even_out, devices, 0)
    accs = [acc, acc_2, acc_3]
    x_next, cols_second = slots_call(
        functools.partial(columns_kernel, log_count=log_count, accs=len(accs)),
        lists + [use, left],
        accs + [x_rows, y_rows],
        kept,
        slow,
        x_blocks,
        y_all,
        [jax.ShapeDtypeStruct((8, LOCAL), f32), jax.ShapeDtypeStruct((YBLOCKS, 1, BS), f32)],
        [pltpu.VMEM((YBLOCKS, 8, BS), f32), pltpu.VMEM((LOCAL, 128), f32), pltpu.VMEM((8, LOCAL), f32)],
        "columns",
    )
    even_out, odd_out, g_one = home(who, peers, (even_in, odd_in), cols_first, cols_second, y_rows, log_count)
    even_in = swap(even_out, devices, 0)
    row_scratch = [pltpu.VMEM((YBLOCKS, 1, BS), f32), pltpu.VMEM((YBLOCKS, 1, BS), f32)]
    sums = [jax.ShapeDtypeStruct((LOCAL, 128), f32), jax.ShapeDtypeStruct((8, LOCAL), f32)]

    def row_sums(phase, smem, front, outs, scratch):
        return slots_call(
            functools.partial(rows_kernel, log_count=log_count, phase=phase),
            lists + [use, left] + smem,
            front,
            kept,
            slow,
            x_blocks,
            y_all,
            outs,
            scratch + row_scratch,
            ("rows_own", "rows_even", "rows_odd")[phase],
        )

    acc, state = row_sums(0, [], [g_one], sums, [])
    odd_out, acc = lax.optimization_barrier((odd_out, acc))
    odd_in = swap(odd_out, devices, GROUP // 2)
    acc, state = row_sums(1, [source], [acc, state, even_in, g_one], sums, [])
    f_two, g_two = row_sums(
        2,
        [source, who],
        [acc, state, even_in, odd_in, g_one, cols_second, y_rows, x_next],
        [jax.ShapeDtypeStruct((1, LOCAL), f32)] * 2,
        [pltpu.VMEM((LOCAL, 128), f32), pltpu.VMEM((8, LOCAL), f32)],
    )
    return f_two.reshape(LOCAL), g_two.reshape(LOCAL)


def solution(mesh):
    placed_as = (
        P("blk", None),
        P("blk", None),
        P("blk"),
        P("blk"),
        P("blk"),
        P("blk"),
        P("blk", None),
        P("blk"),
    )
    return jax.shard_map(
        on_device, mesh=mesh, in_specs=placed_as, out_specs=(P("blk"), P("blk")), check_vma=False
    )
```
